32 devices in a mesh: section: 2 (over core), dp: 16 (over z, y, x).
Axes of the slice: x: 2, y: 2, z: 4, core: 2. Of those that a mesh axis runs over, the one named last changes fastest.
Arguments:
- tokens: bfloat16 [64, 512, 512], P('dp', 'section'), may hold values from -6 to 6
- memory: bfloat16 [64, 64, 512], P('dp', 'section'), may hold values from -6 to 6
- lengths: int32 [32], P('dp'), may hold values from 256 to 1024, as said below
- w_qkv: bfloat16 [2, 512, 1536], P('section', 'dp'), may hold values from -0.25 to 0.25
- w_out: bfloat16 [2, 512, 512], P('section', 'dp'), may hold values from -1 to 1
- w_up: bfloat16 [2, 512, 2048], P('section', 'dp'), may hold values from -0.25 to 0.25
- w_down: bfloat16 [2, 2048, 512], P('section', 'dp'), may hold values from -0.125 to 0.125
- gain_attn: bfloat16 [2, 512], P('section', 'dp'), may hold values from 0.5 to 1.5
- gain_ffn: bfloat16 [2, 512], P('section', 'dp'), may hold values from 0.5 to 1.5
- forget_bias: bfloat16 [2, 512], P('section', 'dp'), may hold values from -4 to 4
- grad_tokens: bfloat16 [64, 512, 512], P('dp', 'section'), may hold values from -6 to 6
- grad_memory: bfloat16 [64, 64, 512], P('dp', 'section'), may hold values from -6 to 6
Outputs:
- out_tokens: bfloat16 [64, 512, 512], P('dp', 'section')
- out_memory: bfloat16 [64, 64, 512], P('dp', 'section')
- grad_in_tokens: bfloat16 [64, 512, 512], P('dp', 'section')
- grad_in_memory: bfloat16 [64, 64, 512], P('dp', 'section')
- grad_w_qkv: float32 [2, 512, 1536], P('section', 'dp')
- grad_w_out: float32 [2, 512, 512], P('section', 'dp')
- grad_w_up: float32 [2, 512, 2048], P('section', 'dp')
- grad_w_down: float32 [2, 2048, 512], P('section', 'dp')
- grad_gain_attn: float32 [2, 512], P('section', 'dp')
- grad_gain_ffn: float32 [2, 512], P('section', 'dp')
- grad_forget_bias: float32 [2, 512], P('section', 'dp')
- rms: float32 [2, 3], replicated
The draws below stay inside these ranges and needn't reach their ends.
Inputs may be any that keep to these rules, and one draw needn't show every extreme that they name: `lengths`: in every draw some document has exactly 1024 tokens.
All inputs are finite; a program needn't handle non-finite values.
Results may differ from the reference program's by a relative error of at most 0.018.
Values may be sent and summed in bfloat16 or wider, within the bound.
A program may use at most 192 MiB of HBM per device.

```python
import jax
import jax.numpy as jnp
from jax import lax

D = 512
H = 8
HD = 64
FF = 2048
SLOTS = 64
SEG = 512
SEG_DOC = 2
DOCS = 32
SEGMENTS = 64
DOC_MAX = 1024
ROWS = 576


def draw_lengths(key, part):
    key = jax.random.fold_in(key, 7)
    draw_key, pick_key = jax.random.split(key)
    drawn = jax.random.randint(draw_key, (DOCS,), SEG // 2, DOC_MAX + 1)
    chosen = jax.random.randint(pick_key, (), 0, DOCS)
    return jnp.where(jnp.arange(DOCS) == chosen, DOC_MAX, drawn).astype(jnp.int32)


def steps_of(stream_key, shape, shards, low, high):
    def one(dim, parts):
        draws = jax.random.uniform(jax.random.fold_in(jax.random.fold_in(stream_key, 6), dim), (parts,), jnp.float32, low / len(shards), high / len(shards))
        return jnp.repeat(jnp.exp(draws), shape[dim] // parts).reshape((-1,) + (1,) * (len(shape) - dim - 1))

    factor_of = one(*shards[0])
    for cut in shards[1:]:
        factor_of = factor_of * one(*cut)
    return factor_of


def noise(own_key, dims, spread, most, shards=(), kind=jnp.bfloat16):
    values = jax.random.normal(own_key, dims, jnp.float32) * spread
    if len(shards) > 0:
        values = steps_of(own_key, dims, shards, -0.22, 0.18) * values
    return jnp.clip(values, min=-most, max=most).astype(kind)


def setup_inputs(seed: int = 0) -> dict:
    arg_keys = jax.random.split(jax.random.key(seed), 13)
    tokens = noise(arg_keys[0], (SEGMENTS, SEG, D), 1.0, 6.0, ((0, 16), (1, 2)))
    memory = noise(arg_keys[1], (SEGMENTS, SLOTS, D), 1.0, 6.0, ((0, 16), (1, 2)))
    lengths = draw_lengths(jax.random.fold_in(arg_keys[12], 71), 0)
    w_qkv = noise(arg_keys[3], (2, D, 3 * D), D ** -0.5, 0.25, ((0, 2), (1, 16)))
    w_out = noise(arg_keys[4], (2, D, D), (D // 16) ** -0.5, 1.0, ((0, 2), (1, 16)))
    w_up = noise(arg_keys[5], (2, D, FF), D ** -0.5, 0.25, ((0, 2), (1, 16)))
    w_down = noise(arg_keys[6], (2, FF, D), FF ** -0.5, 0.125, ((0, 2), (1, 16)))
    gain_attn = jnp.clip(1.0 + 0.1 * jax.random.normal(arg_keys[7], (2, D), jnp.float32), 0.5, 1.5).astype(jnp.bfloat16)
    gain_ffn = jnp.clip(1.0 + 0.1 * jax.random.normal(arg_keys[8], (2, D), jnp.float32), 0.5, 1.5).astype(jnp.bfloat16)
    forget_bias = noise(arg_keys[9], (2, SLOTS * H), 1.0, 4.0, ((0, 2), (1, 16)))
    grad_tokens = noise(arg_keys[10], (SEGMENTS, SEG, D), 1.0, 6.0, ((0, 16), (1, 2)))
    grad_memory = noise(arg_keys[11], (SEGMENTS, SLOTS, D), 1.0, 6.0, ((0, 16), (1, 2)))
    return dict(tokens=tokens, memory=memory, lengths=lengths, w_qkv=w_qkv, w_out=w_out, w_up=w_up, w_down=w_down, gain_attn=gain_attn, gain_ffn=gain_ffn, forget_bias=forget_bias, grad_tokens=grad_tokens, grad_memory=grad_memory)


norm_eps = 1e-06
score_scale = 0.125
masked_score = -1000000000.0

@jax.custom_vjp
def low(v):
    return lax.optimization_barrier(v.astype(jnp.bfloat16)).astype(jnp.float32)

@jax.custom_vjp
def low_back(v):
    return v

def low_keep(v):
    return (low(v), None)

def low_pass(kept, grad):
    return (grad,)

def back_keep(v):
    return (v, None)

def back_low(kept, grad):
    return (low(grad),)
low.defvjp(low_keep, low_pass)
low_back.defvjp(back_keep, back_low)

def wide_dot(left_mat, right_mat):
    return jnp.dot(left_mat, right_mat, precision=lax.Precision.HIGHEST, preferred_element_type=jnp.float32)

def rms_scale(row_vals, gain_vec):
    return row_vals * lax.rsqrt(lax.optimization_barrier(jnp.mean(row_vals * row_vals, axis=-1, keepdims=True)) + norm_eps) * gain_vec

def token_squares(values, valid_rows):
    token_part = values[SLOTS:]
    return jnp.sum(lax.optimization_barrier(jnp.sum(token_part * token_part, axis=1)) * valid_rows[SLOTS:].astype(jnp.float32))

def layer_pass(layer_in, valid_rows, layer_weights):
    w_qkv, w_out, w_up, w_down, gain_attn, gain_ffn, forget_bias = layer_weights
    normed = low(rms_scale(layer_in, gain_attn))
    project = low(low_back(wide_dot(normed, w_qkv)))
    queries = project[:, :D].reshape(ROWS, H, HD)
    keys_h = project[:, D:2 * D].reshape(ROWS, H, HD)
    values_h = project[:, 2 * D:].reshape(ROWS, H, HD)
    bias_rows = jnp.concatenate([forget_bias.reshape(SLOTS, H).T, jnp.zeros((H, SEG), jnp.float32)], axis=1)
    raw_scores = jnp.einsum('qhd,khd->hqk', queries, keys_h, precision=lax.Precision.HIGHEST) * score_scale + bias_rows[:, None, :]
    scores = low_back(jnp.where(valid_rows[None, None, :], raw_scores, masked_score))
    attn_probs = low(jax.nn.softmax(scores, axis=-1))
    attended = low(low_back(jnp.einsum('hqk,khd->qhd', attn_probs, values_h, precision=lax.Precision.HIGHEST).reshape(ROWS, D)))
    branch = low_back(wide_dot(attended, w_out))
    middle = layer_in + branch
    normed_two = low(rms_scale(middle, gain_ffn))
    before = low_back(wide_dot(normed_two, w_up))
    active = low(jax.nn.gelu(before, approximate=True))
    ffn_out = low_back(wide_dot(active, w_down))
    squares = jnp.stack([token_squares(layer_in, valid_rows), token_squares(branch, valid_rows), token_squares(ffn_out, valid_rows)])
    return (middle + ffn_out, squares)

def both_layers(token_rows, memory_rows, stacked, valid_rows):
    first_weights = tuple((piece[0] for piece in stacked))
    second_weights = tuple((piece[1] for piece in stacked))
    first_out, first_sq = layer_pass(jnp.concatenate([memory_rows, token_rows], axis=0), valid_rows, first_weights)
    second_in = low(low_back(first_out))
    second_out, second_sq = layer_pass(second_in, valid_rows, second_weights)
    return (second_out, jnp.stack([first_sq, second_sq]))

def reference(tokens, memory, lengths, w_qkv, w_out, w_up, w_down, gain_attn, gain_ffn, forget_bias, grad_tokens, grad_memory):
    stacked = tuple((source_arr.astype(jnp.float32) for source_arr in (w_qkv, w_out, w_up, w_down, gain_attn, gain_ffn, forget_bias)))
    positions = jnp.arange(SEG, dtype=jnp.int32)
    slot_valid = jnp.ones((SLOTS,), dtype=bool)

    def segment_step(carry, seg_index):
        grad_sums, stat_sums = carry
        doc_index = seg_index // SEG_DOC
        seg_part = seg_index % SEG_DOC
        valid_rows = jnp.concatenate([slot_valid, seg_part * SEG + positions < lengths[doc_index]])
        token_rows = tokens[seg_index].astype(jnp.float32)
        memory_rows = memory[seg_index].astype(jnp.float32)

        def run_layers(token_arg, memory_arg, weight_arg):
            return both_layers(token_arg, memory_arg, weight_arg, valid_rows)
        out_rows, pull_back, squares = jax.vjp(run_layers, token_rows, memory_rows, stacked, has_aux=True)
        cotangent = jnp.concatenate([grad_memory[seg_index].astype(jnp.float32), grad_tokens[seg_index].astype(jnp.float32)], axis=0)
        grad_tok, grad_mem, grad_par = pull_back(cotangent)
        grad_sums = jax.tree.map(jnp.add, grad_sums, grad_par)
        results = (out_rows[SLOTS:].astype(jnp.bfloat16), out_rows[:SLOTS].astype(jnp.bfloat16), grad_tok.astype(jnp.bfloat16), grad_mem.astype(jnp.bfloat16))
        return ((grad_sums, stat_sums + squares), results)
    zero_grads = tuple((jnp.zeros_like(piece) for piece in stacked))
    start_carry = (zero_grads, jnp.zeros((2, 3), jnp.float32))
    (grad_sums, stat_sums), results = lax.scan(segment_step, start_carry, jnp.arange(SEGMENTS, dtype=jnp.int32))
    token_count = jnp.sum(lengths).astype(jnp.float32)
    rms = jnp.sqrt(stat_sums / (token_count * D))
    return (results[0], results[1], results[2], results[3], grad_sums[0], grad_sums[1], grad_sums[2], grad_sums[3], grad_sums[4], grad_sums[5], grad_sums[6], rms)
```

```python
from functools import partial

import jax
import jax.numpy as jnp
from jax import lax
from jax.experimental import pallas as pl
from jax.experimental.pallas import tpu as pltpu
from jax.sharding import PartitionSpec as P

norm_eps = 1e-06
score_scale = 0.125
log2_e = 1.4426950408889634
masked_score = -1000000000.0
gelu_c = 0.7978845608028654
gelu_k = 0.044715
f32 = jnp.float32
bf16 = jnp.bfloat16
lanes = 128
chunk = 512


def mm(a, b, ca=1, cb=0):
    return lax.dot_general(a, b, (((ca,), (cb,)), ((), ())), preferred_element_type=f32)


def nt(a, b):
    return mm(a, b, 1, 1)


def tn(a, b):
    return mm(a, b, 0, 0)


def lane_marks(head_size, side):
    lane = lax.broadcasted_iota(jnp.int32, (1, lanes), 1)
    own = ((lane // head_size) == side).astype(f32)
    first = (1 - side) * head_size
    marks = [(lane == first + k).astype(f32) for k in range(3)]
    return own, marks


def fused_layers(dims, *refs):
    segs, rows, width, ff, slots, heads = dims
    (
        len_ref, u0_ref, dout_ref, gain_a, gain_f, bias_ref,
        wq_in, wo_in, wu_in, wd_in,
        y_ref, du_ref, gq_out, go_out, gu_out, gd_out,
        dga_ref, dgf_ref, dbias_ref, stat_ref,
        qkv_hbm, e_hbm, o_hbm, il_hbm, pre_hbm,
        wq, wo, wu, wd, ub, dy, qkv, ebuf, obuf, ilbuf, hbuf, pre, doa, dn, n2buf,
        sem_w, sem_spill, sem_back, sem_g, sem_io,
    ) = refs
    head_size = width // heads
    pairs = width // lanes
    all_rows = segs * rows
    tok_rows = rows - slots
    doc_len = len_ref[0]

    def weight_copies(layer, picks=range(4)):
        return [
            pltpu.make_async_copy(src.at[layer], dst.at[layer], sem_w.at[layer, k])
            for k, (src, dst) in enumerate(((wq_in, wq), (wo_in, wo), (wu_in, wu), (wd_in, wd)))
            if k in picks
        ]

    for layer in range(2):
        for copy in weight_copies(layer):
            copy.start()

    def seg_rows(s):
        return pl.ds(pl.multiple_of(s * rows, rows), rows)

    def spill_copies(s, back, picks=range(5)):
        at = seg_rows(s)
        pairs_of = (
            (qkv.at[at], qkv_hbm.at[at]),
            (ebuf.at[s], e_hbm.at[s]),
            (obuf.at[at], o_hbm.at[at]),
            (ilbuf.at[at], il_hbm.at[at]),
            (pre.at[at], pre_hbm.at[at]),
        )
        if back:
            return [
                pltpu.make_async_copy(hbm, vmem, sem_back.at[s, k])
                for k, (vmem, hbm) in enumerate(pairs_of)
                if k in picks
            ]
        return [
            pltpu.make_async_copy(vmem, hbm, sem_spill.at[s, k])
            for k, (vmem, hbm) in enumerate(pairs_of)
            if k in picks
        ]

    def valid_col(s):
        row = lax.broadcasted_iota(jnp.int32, (rows, 1), 0)
        return jnp.where(
            (row >= slots) & (s * tok_rows + row - slots < doc_len), 1.0, 0.0
        ).astype(f32)

    def mask_col(s):
        row = lax.broadcasted_iota(jnp.int32, (rows, 1), 0)
        return jnp.where(
            (row >= slots) & (s * tok_rows + row - slots >= doc_len), masked_score, 0.0
        ).astype(f32)

    loads = [
        pltpu.make_async_copy(u0_ref, ub.at[0], sem_io.at[0]),
        pltpu.make_async_copy(dout_ref, dy, sem_io.at[1]),
    ]
    y_copy = pltpu.make_async_copy(ub.at[2], y_ref, sem_io.at[2])
    du_copy = pltpu.make_async_copy(dy, du_ref, sem_io.at[3])
    for copy in loads:
        copy.start()
    stat_ref[...] = jnp.zeros_like(stat_ref)
    dga_ref[...] = jnp.zeros_like(dga_ref)
    dgf_ref[...] = jnp.zeros_like(dgf_ref)
    dbias_ref[...] = jnp.zeros_like(dbias_ref)

    for copy in loads:
        copy.wait()

    def add_stat(layer, k, row_sums, valid):
        total = jnp.sum(row_sums * valid, axis=0, keepdims=True)
        stat_ref[layer, k : k + 1, :] += jnp.broadcast_to(total, (1, lanes))

    def forward_attention(layer, s):
        at = seg_rows(s)
        mask = mask_col(s)
        for p in range(pairs):
            cols = slice(p * lanes, (p + 1) * lanes)
            qp = qkv[at, cols]
            kp = qkv[at, slice(width + p * lanes, width + (p + 1) * lanes)]
            vp = qkv[at, slice(2 * width + p * lanes, 2 * width + (p + 1) * lanes)]
            outs = []
            for side in range(2):
                h = 2 * p + side
                own, marks = lane_marks(head_size, side)
                bias = jnp.broadcast_to(bias_ref[layer, :, h : h + 1], (slots, lanes))
                hi = bias.astype(bf16).astype(f32)
                aux = jnp.concatenate([hi * marks[1] + (bias - hi) * marks[2], jnp.zeros((tok_rows, lanes), f32)], axis=0)
                aux = aux + mask * marks[0]
                every = marks[0] + marks[1] + marks[2]
                ka = kp * own.astype(bf16) + aux.astype(bf16)
                qa = qp * (1.0 - every).astype(bf16) + every.astype(bf16)
                scores = nt(qa, ka)
                top = jnp.max(scores, axis=1, keepdims=True)
                weights = jnp.exp2(scores - top).astype(bf16)
                ebuf[s, h] = weights
                va = vp * own.astype(bf16) + (1.0 - own).astype(bf16)
                outs.append(mm(weights, va))
            own, _ = lane_marks(head_size, 0)
            raw = jnp.where(own > 0, outs[0], outs[1])
            sums = pltpu.roll(jnp.where(own > 0, outs[1], outs[0]), head_size, 1)
            inv = 1.0 / sums
            ilbuf[at, cols] = inv.astype(ilbuf.dtype)
            obuf[at, cols] = (raw * inv).astype(bf16)

    def forward_seg(layer, s):
        at = seg_rows(s)

        @pl.when(layer == 1)
        def _():
            for copy in spill_copies(s, False):
                copy.wait()

        @pl.when(s == 0)
        def _():
            weight_copies(layer, (0,))[0].wait()

        valid = valid_col(s)
        x = ub[layer, at, :].astype(f32)
        squares = jnp.sum(x * x, axis=1, keepdims=True)
        add_stat(layer, 0, squares, valid)
        n1 = (x * lax.rsqrt(squares / width + norm_eps) * gain_a[layer]).astype(bf16)
        for k in range(3):
            part = mm(n1, wq[layer, :, k * width : (k + 1) * width])
            if k == 0:
                part = part * (score_scale * log2_e)
            qkv[at, k * width : (k + 1) * width] = part.astype(bf16)
        forward_attention(layer, s)

        @pl.when(layer == 0)
        def _():
            for copy in spill_copies(s, False, range(4)):
                copy.start()

        @pl.when(s == 0)
        def _():
            for copy in weight_copies(layer, (1, 2, 3)):
                copy.wait()

        z = mm(obuf[at, :], wo[layer])
        add_stat(layer, 1, jnp.sum(z * z, axis=1, keepdims=True), valid)
        h = ub[layer, at, :].astype(f32) + z
        hbuf[layer, at, :] = h.astype(bf16)
        dn[at, :] = h
        n2 = (h * lax.rsqrt(jnp.mean(h * h, axis=1, keepdims=True) + norm_eps) * gain_f[layer]).astype(bf16)
        n2buf[at, :] = n2
        out = None
        for c in range(ff // chunk):
            cols = slice(c * chunk, (c + 1) * chunk)
            before = mm(n2buf[at, :], wu[layer, :, cols])
            pre[at, cols] = before.astype(bf16)
            gate = 0.5 + 0.5 * jnp.tanh(before * (gelu_c + (gelu_c * gelu_k) * (before * before)))
            part = mm((before * gate).astype(bf16), wd[layer, cols, :])
            out = part if out is None else out + part
        add_stat(layer, 2, jnp.sum(out * out, axis=1, keepdims=True), valid)
        ub[layer + 1, at, :] = (dn[at, :] + out).astype(bf16)

        @pl.when(layer == 0)
        def _():
            spill_copies(s, False, (4,))[0].start()

    @pl.loop(0, 2 * segs)
    def _(step):
        forward_seg(step // segs, step % segs)

    y_copy.start()

    def norm_back(x, gain, grad):
        inv = lax.rsqrt(jnp.mean(x * x, axis=1, keepdims=True) + norm_eps)
        hat = x * inv
        dgain = jnp.sum(grad * hat, axis=0, keepdims=True)
        scaled = grad * gain
        return inv * (scaled - hat * jnp.mean(scaled * hat, axis=1, keepdims=True)), dgain

    def backward_ffn(layer):
        slot = layer + 1

        @pl.loop(0, segs)
        def _(s):
            at = seg_rows(s)
            h = hbuf[layer, at, :].astype(f32)
            n2buf[at, :] = (h * lax.rsqrt(jnp.mean(h * h, axis=1, keepdims=True) + norm_eps) * gain_f[layer]).astype(bf16)

        dn[...] = jnp.zeros_like(dn)

        @pl.loop(0, ff // chunk)
        def _(c):
            cols = pl.ds(pl.multiple_of(c * chunk, chunk), chunk)
            d_act = nt(dy[...], wd[layer, cols, :])
            x = pre[:, cols].astype(f32)
            sq = x * x
            gate = 0.5 + 0.5 * jnp.tanh(x * (gelu_c + (gelu_c * gelu_k) * sq))
            act = x * gate
            slope = gate + act * (1.0 - gate) * (2.0 * gelu_c + (6.0 * gelu_c * gelu_k) * sq)
            d_pre = (d_act * slope).astype(bf16)
            pre[:, cols] = d_pre
            wd[slot, cols, :] = tn(act.astype(bf16), dy[...]).astype(bf16)
            wu[slot, :, cols] = tn(n2buf[...], d_pre).astype(bf16)
            dn[...] += nt(d_pre, wu[layer, :, cols])

    def backward_middle(layer, s):
        at = seg_rows(s)
        dh, dgain = norm_back(hbuf[layer, at, :].astype(f32), gain_f[layer], dn[at, :])
        dgf_ref[layer] += dgain
        dh = dh + dy[at, :].astype(f32)
        dn[at, :] = dh
        dz = dh.astype(bf16)
        dy[at, :] = dz
        do = nt(dz, wo[layer]) * ilbuf[at, :].astype(f32)
        prod = do.astype(bf16).astype(f32) * obuf[at, :].astype(f32)
        for p in range(pairs):
            cols = slice(p * lanes, (p + 1) * lanes)
            for side in range(2):
                own, marks = lane_marks(head_size, side)
                delta = -jnp.sum(prod[:, cols] * own, axis=1, keepdims=True)
                hi = delta.astype(bf16).astype(f32)
                fill = hi * marks[0] + (delta - hi) * marks[1]
                doa[side, at, cols] = (do[:, cols] * (1.0 - marks[0] - marks[1]) + fill).astype(bf16)

    def backward_attention(layer, s):
        at = seg_rows(s)
        for p in range(pairs):
            cols = slice(p * lanes, (p + 1) * lanes)
            kcols = slice(width + p * lanes, width + (p + 1) * lanes)
            vcols = slice(2 * width + p * lanes, 2 * width + (p + 1) * lanes)
            qp = qkv[at, cols]
            kp = qkv[at, kcols]
            vp = qkv[at, vcols]
            q_turned = qp.T
            dq, dk, dv = [], [], []
            for side in range(2):
                h = 2 * p + side
                own, marks = lane_marks(head_size, side)
                do_h = doa[side, at, cols]
                va = vp * own.astype(bf16) + (marks[0] + marks[1]).astype(bf16)
                weights = ebuf[s, h]
                d_scores = weights.astype(f32) * nt(do_h, va)
                dbias_ref[layer, h : h + 1, :] += jnp.sum(d_scores[:, :lanes], axis=0, keepdims=True)
                d_scores = d_scores.astype(bf16)
                half = slice(side * head_size, (side + 1) * head_size)
                dq.append(mm(d_scores, kp))
                dk.append(mm(q_turned[half, :], d_scores))
                dv.append(mm(do_h.T[half, :], weights))
            own, _ = lane_marks(head_size, 0)
            qkv[at, cols] = (jnp.where(own > 0, dq[0], dq[1]) * score_scale).astype(bf16)
            qkv[at, kcols] = (jnp.concatenate(dk, axis=0).T * (1.0 / log2_e)).astype(bf16)
            qkv[at, vcols] = jnp.concatenate(dv, axis=0).T.astype(bf16)

    def backward_input(layer, s):
        at = seg_rows(s)
        x = ub[layer, at, :].astype(f32)
        du, dgain = norm_back(x, gain_a[layer], nt(qkv[at, :], wq[layer]))
        dga_ref[layer] += dgain
        dy[at, :] = (du + dn[at, :]).astype(bf16)
        n2buf[at, :] = (x * lax.rsqrt(jnp.mean(x * x, axis=1, keepdims=True) + norm_eps) * gain_a[layer]).astype(bf16)

    def grad_copies(layer, picks=range(4)):
        slot = layer + 1
        return [
            pltpu.make_async_copy(src.at[slot], dst.at[layer], sem_g.at[layer, k])
            for k, (src, dst) in enumerate(((wq, gq_out), (wo, go_out), (wu, gu_out), (wd, gd_out)))
            if k in picks
        ]

    @pl.loop(0, 2)
    def _(step):
        layer = 1 - step
        slot = layer + 1

        @pl.when(layer == 0)
        def _():
            for s in range(segs):
                for copy in spill_copies(s, True, (2, 3, 4)):
                    copy.wait()

        backward_ffn(layer)

        @pl.loop(0, segs)
        def _(s):
            backward_middle(layer, s)

        wo[slot] = tn(obuf[...], dy[...]).astype(bf16)
        for copy in grad_copies(layer, (1, 2, 3)):
            copy.start()

        @pl.when(layer == 1)
        def _():
            for s in range(segs):
                for copy in spill_copies(s, True, (2, 3, 4)):
                    copy.start()

        @pl.loop(0, segs)
        def _(s):
            @pl.when(layer == 0)
            def _():
                for copy in spill_copies(s, True, (0, 1)):
                    copy.wait()

            backward_attention(layer, s)

            @pl.when(layer == 1)
            def _():
                spill_copies(s, True, (1,))[0].start()

        @pl.loop(0, segs)
        def _(s):
            backward_input(layer, s)

        for k in range(3):
            part = slice(k * width, (k + 1) * width)
            wq[slot, :, part] = tn(n2buf[...], qkv[:, part]).astype(bf16)
        grad_copies(layer, (0,))[0].start()

        @pl.when(layer == 1)
        def _():
            for s in range(segs):
                spill_copies(s, True, (0,))[0].start()

        for copy in grad_copies(layer):
            copy.wait()

    du_copy.start()
    du_copy.wait()
    y_copy.wait()


def run_layers(doc_len, u0, dout, gains, bias, weights, heads, slots, segs):
    all_rows, width = u0.shape
    rows = all_rows // segs
    ff = weights[2].shape[2]
    dims = (segs, rows, width, ff, slots, heads)
    vmem = pl.BlockSpec(memory_space=pltpu.VMEM)
    smem = pl.BlockSpec(memory_space=pltpu.SMEM)
    hbm = pl.BlockSpec(memory_space=pl.ANY)
    shape = jax.ShapeDtypeStruct
    wide = (all_rows, width)
    spills = [
        shape((all_rows, 3 * width), bf16),
        shape((segs, heads, rows, rows), bf16),
        shape(wide, bf16),
        shape(wide, bf16),
        shape((all_rows, ff), bf16),
    ]
    out_shape = [
        shape(wide, bf16),
        shape(wide, bf16),
        shape((2, width, 3 * width), bf16),
        shape((2, width, width), bf16),
        shape((2, width, ff), bf16),
        shape((2, ff, width), bf16),
        shape((2, 1, width), f32),
        shape((2, 1, width), f32),
        shape((2, heads, lanes), f32),
        shape((2, 8, lanes), f32),
    ] + spills
    scratch = [
        pltpu.VMEM((3, width, 3 * width), bf16),
        pltpu.VMEM((3, width, width), bf16),
        pltpu.VMEM((3, width, ff), bf16),
        pltpu.VMEM((3, ff, width), bf16),
        pltpu.VMEM((3, *wide), bf16),
        pltpu.VMEM(wide, bf16),
        pltpu.VMEM((all_rows, 3 * width), bf16),
        pltpu.VMEM((segs, heads, rows, rows), bf16),
        pltpu.VMEM(wide, bf16),
        pltpu.VMEM(wide, bf16),
        pltpu.VMEM((2, *wide), bf16),
        pltpu.VMEM((all_rows, ff), bf16),
        pltpu.VMEM((2, *wide), bf16),
        pltpu.VMEM(wide, f32),
        pltpu.VMEM(wide, bf16),
        pltpu.SemaphoreType.DMA((2, 4)),
        pltpu.SemaphoreType.DMA((segs, 5)),
        pltpu.SemaphoreType.DMA((segs, 5)),
        pltpu.SemaphoreType.DMA((2, 4)),
        pltpu.SemaphoreType.DMA((4,)),
    ]
    return pl.pallas_call(
        partial(fused_layers, dims),
        out_shape=out_shape,
        in_specs=[smem] + [hbm] * 2 + [vmem] * 3 + [hbm] * 4,
        out_specs=[hbm] * 6 + [vmem] * 4 + [hbm] * 5,
        scratch_shapes=scratch,
        compiler_params=pltpu.CompilerParams(vmem_limit_bytes=63 * 2**20),
    )(doc_len, u0, dout, *gains, bias, *weights)[:10]


def swap(block):
    return lax.ppermute(block, "section", [(0, 1), (1, 0)])


def body(
    tokens,
    memory,
    lengths,
    w_qkv,
    w_out,
    w_up,
    w_down,
    gain_attn,
    gain_ffn,
    forget_bias,
    grad_tokens,
    grad_memory,
):
    section = lax.axis_index("section")
    is_first = section == 0
    micro = tokens.shape[0]
    segs = micro // 2
    half_tok = tokens.shape[1]
    half_mem = memory.shape[1]
    slots = 2 * half_mem
    seg_len = 2 * half_tok
    rows = slots + seg_len
    width = tokens.shape[2]

    def own_segs(halves):
        return lax.dynamic_slice_in_dim(halves, section * segs, segs, 0)

    def other_segs(halves):
        return lax.dynamic_slice_in_dim(halves, (1 - section) * segs, segs, 0)

    def both(kept, got):
        return jnp.concatenate(
            [jnp.where(is_first, kept, got), jnp.where(is_first, got, kept)], axis=1
        )

    inputs = (tokens, memory, grad_tokens, grad_memory)
    got = swap(tuple(other_segs(part) for part in inputs))
    full = [both(own_segs(part), other) for part, other in zip(inputs, got)]
    u0 = jnp.concatenate([full[1], full[0]], axis=1).reshape(segs * rows, width)
    dout = jnp.concatenate([full[3], full[2]], axis=1).reshape(segs * rows, width)

    def gather(piece):
        return lax.all_gather(piece, ("section", "dp"), axis=1, tiled=True).reshape(2, -1, *piece.shape[2:])

    weights = tuple(gather(piece) for piece in (w_qkv, w_out, w_up, w_down))
    gains = [gather(piece).astype(f32)[:, None, :] for piece in (gain_attn, gain_ffn)]
    bias_flat = gather(forget_bias).astype(f32)
    heads = bias_flat.shape[1] // slots
    bias = jnp.pad(bias_flat.reshape(2, slots, heads) * log2_e, ((0, 0), (0, 0), (0, lanes - heads)))
    per_doc = micro // lengths.shape[0]
    own_len = lax.dynamic_slice_in_dim(lengths, section * segs // per_doc, 1, 0)
    y, du, gq, go, gu, gd, dga, dgf, dbias, stats = run_layers(
        own_len, u0, dout, gains, bias, weights, heads, slots, segs
    )

    def scatter(grad):
        mine = lax.dynamic_index_in_dim(grad, section, 0, keepdims=True)
        other = lax.dynamic_index_in_dim(grad, 1 - section, 0, keepdims=True)
        chip = (mine.astype(f32) + swap(other).astype(f32)).astype(grad.dtype)
        return lax.psum_scatter(chip, "dp", scatter_dimension=1, tiled=True).astype(f32)

    grad_bias = jnp.swapaxes(dbias[:, :, :slots], 1, 2).reshape(2, slots * heads)
    shares = tuple(scatter(grad) for grad in (gq, go, gu, gd, dga[:, 0], dgf[:, 0], grad_bias))
    token_count = jnp.sum(own_len).astype(f32)
    sums = jnp.concatenate([stats[:, :3, 0].reshape(6), token_count[None]])
    totals = lax.psum(sums, ("section", "dp"))
    rms = jnp.sqrt(totals[:6].reshape(2, 3) / (totals[6] * width))

    result = jnp.stack([y.reshape(segs, rows, width), du.reshape(segs, rows, width)])

    def half_of(which):
        tok = lax.dynamic_slice_in_dim(result, slots + which * half_tok, half_tok, 2)
        mem = lax.dynamic_slice_in_dim(result, which * half_mem, half_mem, 2)
        return tok, mem

    kept = half_of(section)
    got = swap(half_of(1 - section))

    def order(mine, other):
        return jnp.concatenate(
            [jnp.where(is_first, mine, other), jnp.where(is_first, other, mine)], axis=0
        )

    toks = [order(kept[0][k], got[0][k]) for k in range(2)]
    mems = [order(kept[1][k], got[1][k]) for k in range(2)]
    return (toks[0], mems[0], toks[1], mems[1], *shares, rms)


def solution(mesh):
    rows = P("dp", "section", None)
    mats = P("section", "dp", None)
    vecs = P("section", "dp")
    return jax.shard_map(
        body,
        mesh=mesh,
        in_specs=(rows, rows, P("dp"), mats, mats, mats, mats, vecs, vecs, vecs, rows, rows),
        out_specs=(rows, rows, rows, rows, mats, mats, mats, mats, vecs, vecs, vecs, P()),
        check_vma=False,
    )
```

```python
from functools import partial

import jax
import jax.numpy as jnp
from jax import lax
from jax.experimental import pallas as pl
from jax.experimental.pallas import tpu as pltpu
from jax.sharding import PartitionSpec as P

norm_eps = 1e-06
score_scale = 0.125
log2_e = 1.4426950408889634
masked_score = -1000000000.0
gelu_c = 0.7978845608028654
gelu_k = 0.044715
f32 = jnp.float32
bf16 = jnp.bfloat16
lanes = 128
chunk = 512


def mm(a, b, ca=1, cb=0):
    return lax.dot_general(a, b, (((ca,), (cb,)), ((), ())), preferred_element_type=f32)


def nt(a, b):
    return mm(a, b, 1, 1)


def tn(a, b):
    return mm(a, b, 0, 0)


def lane_marks(head_size, side):
    lane = lax.broadcasted_iota(jnp.int32, (1, lanes), 1)
    own = ((lane // head_size) == side).astype(f32)
    first = (1 - side) * head_size
    marks = [(lane == first + k).astype(f32) for k in range(3)]
    return own, marks


def fused_layers(dims, routed, *refs):
    segs, rows, width, ff, slots, heads = dims
    (
        len_ref, u0_ref, dout_ref, wq_in, wo_in, wu_in, wd_in,
        y_ref, du_ref, gq_out, go_out, gu_out, gd_out,
        dga_ref, dgf_ref, dbias_ref, stat_ref,
        qkv_hbm, e_hbm, o_hbm, il_hbm, pre_hbm,
        wq, wo, wu, wd, ub, dy, qkv, ebuf, obuf, ilbuf, hbuf, pre, doa, dn, n2buf,
        gains, bias_rows, ext, sem_spill, sem_back, sem_g, sem_io,
        sem_own, sem_send, sem_recv,
    ) = refs
    head_size = width // heads
    pairs = width // lanes
    tok_rows = rows - slots
    doc_len = len_ref[0]
    weight_in = (wq_in, wo_in, wu_in, wd_in)
    weight_buf = (wq, wo, wu, wd)
    every = slice(None)

    def units_of(layer):
        half_ff, half_deep = ff // 2, ff // 64
        lead = [
            (0, slice(0, lanes + width), every),
            (0, slice(lanes + width, lanes + 2 * width), every),
            (0, slice(lanes + 2 * width, lanes + 3 * width), every),
        ]
        if layer == 1:
            lead = [(0, every, every)]
        rest = [(1, every, every)]
        rest += [(2, slice(k * half_ff, (k + 1) * half_ff), every) for k in range(2)]
        rest += [(3, every, slice(k * half_deep, (k + 1) * half_deep)) for k in range(2)]
        return [(layer, *unit) for unit in lead + rest]

    units = units_of(0) + units_of(1)
    first_units = [k for k, unit in enumerate(units) if unit[1] == 0]
    later_units = [k for k, unit in enumerate(units) if unit[1] != 0]

    def view(n, z, y, x, c):
        layer, which, cols, part = units[n]
        return weight_buf[which].at[layer, z, y, x, c, part, cols]

    if routed:
        core = lax.axis_index("section")
        chip = lax.axis_index("dp")
        z, y, x = chip // 4, (chip // 2) % 2, chip % 2
        other = 1 - core

        def place(pz, py, px):
            return pz * 4 + py * 2 + px

        mate = (other, chip)
        near_x = (core, place(z, y, 1 - x))
        near_y = (core, place(z, 1 - y, x))
        along_z = [(core, place((z + k) % 4, y, x)) for k in range(1, 4)]

        def remote(src, dst, n, k, target):
            return pltpu.make_async_remote_copy(
                src_ref=src,
                dst_ref=dst,
                send_sem=sem_send.at[n, k],
                recv_sem=sem_recv.at[n, k],
                device_id=target,
                device_id_type=pl.DeviceIdType.MESH,
            )

        def own_shard(n):
            layer, which, cols, part = units[n]
            src = weight_in[which].at[every, part, cols]
            return src, view(n, z, y, x, every)

        def z_copy(n, k):
            spot = view(n, z, y, x, core)
            return remote(spot, spot, n, k, along_z[k - 1])

        def plane_copy(n, k, x_first):
            if k == 4:
                spot = view(n, every, y, x, core)
                return remote(spot, spot, n, 4, near_x if x_first else near_y)
            spot = view(n, every, y, every, core) if x_first else view(n, every, every, x, core)
            return remote(spot, spot, n, 5, near_y if x_first else near_x)

        def mate_copy(n, k, x_first, half):
            if k < 9:
                from_z = (z + 4 - (k - 5)) % 4
                spot = view(n, from_z, y, x, half)
            elif k == 9:
                spot = view(n, every, y, 1 - x, half) if x_first else view(n, every, 1 - y, x, half)
            else:
                spot = view(n, every, 1 - y, every, half) if x_first else view(n, every, every, 1 - x, half)
            return remote(spot, spot, n, k, mate)

        def by_route(n, act):
            for side in range(2):
                @pl.when(core == side)
                def _(side=side):
                    act((side + n) % 2 == 0)

        def share_own(n):
            src, dst = own_shard(n)

            @pl.when(core == units[n][0])
            def _():
                pltpu.make_async_copy(src, dst, sem_own.at[n]).start()
                remote(src, dst, n, 0, mate).start()

        def start_z(n):
            src, dst = own_shard(n)

            @pl.when(core == units[n][0])
            def _():
                pltpu.make_async_copy(src, dst, sem_own.at[n]).wait()

            @pl.when(core != units[n][0])
            def _():
                remote(src, dst, n, 0, mate).wait_recv()

            for k in range(1, 4):
                z_copy(n, k).start()

        def first_hop(n):
            for k in range(1, 4):
                z_copy(n, k).wait_recv()

            def act(x_first):
                plane_copy(n, 4, x_first).start()
                for k in range(6, 9):
                    mate_copy(n, k, x_first, core).start()

            by_route(n, act)

        def second_hop(n):
            def act(x_first):
                plane_copy(n, 4, x_first).wait_recv()
                plane_copy(n, 5, x_first).start()
                mate_copy(n, 9, x_first, core).start()

            by_route(n, act)

        def last_share(n):
            def act(x_first):
                plane_copy(n, 5, x_first).wait_recv()
                mate_copy(n, 10, x_first, core).start()

            by_route(n, act)

        def complete(n):
            def act(x_first):
                for k in range(6, 11):
                    mate_copy(n, k, not x_first, other).wait_recv()

            by_route(n, act)

        def drain(n):
            src, dst = own_shard(n)

            @pl.when(core == units[n][0])
            def _():
                remote(src, dst, n, 0, mate).wait_send()

            for k in range(1, 4):
                z_copy(n, k).wait_send()

            def act(x_first):
                for k in (4, 5):
                    plane_copy(n, k, x_first).wait_send()
                for k in range(6, 11):
                    mate_copy(n, k, x_first, core).wait_send()

            by_route(n, act)

        def tick(t):
            if 0 <= t - 4 < len(units):
                last_share(t - 4)
            if 0 <= t - 2 < len(units):
                second_hop(t - 2)
            if 0 <= t < len(units):
                first_hop(t)
            ahead = t + 4
            if ahead < len(units) and ahead >= lead_units:
                start_z(ahead)

        lead_units = 6
        ticks_at = {
            (0, 0, "qkv"): [7], (0, 0, "quad0"): [8], (0, 0, "quad1"): [9],
            (0, 1, "qkv"): [10], (0, 1, "quad0"): [11], (0, 1, "quad1"): [12],
            (0, 0, "ffn"): [13], (0, 1, "ffn"): [14],
            (1, 0, "qkv"): [15], (1, 0, "quad0"): [16], (1, 0, "quad1"): [17],
        }
    else:
        ticks_at = {}

        def weight_copy(n):
            layer, which, cols, part = units[n]
            src = weight_in[which].at[layer, every, every, every, every, part, cols]
            return pltpu.make_async_copy(src, view(n, every, every, every, every), sem_own.at[n])

        def complete(n):
            weight_copy(n).wait()

    def after(layer, s, point):
        for (at_layer, at_s, at_point), ticks in ticks_at.items():
            if at_point == point:
                @pl.when((layer == at_layer) & (s == at_s))
                def _(ticks=ticks):
                    for t in ticks:
                        tick(t)

    def need(layer, picks):
        for at_layer in range(2):
            @pl.when(layer == at_layer)
            def _(at_layer=at_layer):
                for n in picks:
                    if units[n][0] == at_layer:
                        complete(n)

    def mat(which, slot, cols=every, planes=None):
        if planes is None:
            value = weight_buf[which][slot, :, :, :, :, :, cols]
        else:
            value = weight_buf[which][slot, planes, :, :, :, :, cols]
        deep = 1
        for size in value.shape[:-1]:
            deep *= size
        return value.reshape(deep, value.shape[-1])

    def put_mat(which, slot, value, cols=every, planes=None):
        buf = weight_buf[which]
        shape = buf.shape[1:-1]
        if planes is None:
            buf[slot, :, :, :, :, :, cols] = value.reshape(*shape, value.shape[-1])
        else:
            buf[slot, planes] = value.reshape(1, *shape[1:], value.shape[-1])

    def qkv_cols(k):
        return slice(lanes + k * width, lanes + (k + 1) * width)

    def seg_rows(s):
        return pl.ds(pl.multiple_of(s * rows, rows), rows)

    def spill_copies(s, back, picks=range(5)):
        at = seg_rows(s)
        pairs_of = (
            (qkv.at[at], qkv_hbm.at[at]),
            (ebuf.at[s], e_hbm.at[s]),
            (obuf.at[at], o_hbm.at[at]),
            (ilbuf.at[at], il_hbm.at[at]),
            (pre.at[at], pre_hbm.at[at]),
        )
        if back:
            return [
                pltpu.make_async_copy(hbm, vmem, sem_back.at[s, k])
                for k, (vmem, hbm) in enumerate(pairs_of)
                if k in picks
            ]
        return [
            pltpu.make_async_copy(vmem, hbm, sem_spill.at[s, k])
            for k, (vmem, hbm) in enumerate(pairs_of)
            if k in picks
        ]

    def valid_col(s):
        row = lax.broadcasted_iota(jnp.int32, (rows, 1), 0)
        return jnp.where(
            (row >= slots) & (s * tok_rows + row - slots < doc_len), 1.0, 0.0
        ).astype(f32)

    def mask_col(s):
        row = lax.broadcasted_iota(jnp.int32, (rows, 1), 0)
        return jnp.where(
            (row >= slots) & (s * tok_rows + row - slots >= doc_len), masked_score, 0.0
        ).astype(f32)

    loads = [
        pltpu.make_async_copy(u0_ref, ub.at[0], sem_io.at[0]),
        pltpu.make_async_copy(dout_ref, dy, sem_io.at[1]),
    ]
    y_copy = pltpu.make_async_copy(ub.at[2], y_ref, sem_io.at[2])
    du_copy = pltpu.make_async_copy(dy, du_ref, sem_io.at[3])
    for copy in loads:
        copy.start()
    if routed:
        barrier = pltpu.get_barrier_semaphore()
        peers = [mate, near_x, near_y, *along_z]
        for peer in peers:
            pl.semaphore_signal(barrier, inc=1, device_id=peer, device_id_type=pl.DeviceIdType.MESH)
        pl.semaphore_wait(barrier, len(peers))
        for n in range(len(units)):
            share_own(n)
        for n in range(lead_units):
            start_z(n)
        for t in range(7):
            tick(t)
    else:
        for n in range(len(units)):
            weight_copy(n).start()
    stat_ref[...] = jnp.zeros_like(stat_ref)
    dga_ref[...] = jnp.zeros_like(dga_ref)
    dgf_ref[...] = jnp.zeros_like(dgf_ref)
    dbias_ref[...] = jnp.zeros_like(dbias_ref)

    for copy in loads:
        copy.wait()

    def add_stat(layer, k, row_sums, valid):
        total = jnp.sum(row_sums * valid, axis=0, keepdims=True)
        stat_ref[layer, k : k + 1, :] += jnp.broadcast_to(total, (1, lanes))

    def forward_attention(layer, s):
        at = seg_rows(s)
        mask = mask_col(s)
        for p in range(pairs):
            cols = slice(p * lanes, (p + 1) * lanes)
            qp = qkv[at, cols]
            kp = qkv[at, slice(width + p * lanes, width + (p + 1) * lanes)]
            vp = qkv[at, slice(2 * width + p * lanes, 2 * width + (p + 1) * lanes)]
            outs = []
            for side in range(2):
                h = 2 * p + side
                own, marks = lane_marks(head_size, side)
                bias = bias_rows[layer, h]
                hi = bias.astype(bf16).astype(f32)
                aux = jnp.concatenate([hi * marks[1] + (bias - hi) * marks[2], jnp.zeros((tok_rows, lanes), f32)], axis=0)
                aux = aux + mask * marks[0]
                extra = marks[0] + marks[1] + marks[2]
                ka = kp * own.astype(bf16) + aux.astype(bf16)
                qa = qp * (1.0 - extra).astype(bf16) + extra.astype(bf16)
                scores = nt(qa, ka)
                top = jnp.max(scores, axis=1, keepdims=True)
                weights = jnp.exp2(scores - top).astype(bf16)
                ebuf[s, h] = weights
                va = vp * own.astype(bf16) + (1.0 - own).astype(bf16)
                outs.append(mm(weights, va))
            own, _ = lane_marks(head_size, 0)
            raw = jnp.where(own > 0, outs[0], outs[1])
            sums = pltpu.roll(jnp.where(own > 0, outs[1], outs[0]), head_size, 1)
            inv = 1.0 / sums
            ilbuf[at, cols] = inv.astype(ilbuf.dtype)
            obuf[at, cols] = (raw * inv).astype(bf16)
            if p % 2 == 1:
                after(layer, s, "quad" + str(p // 2))

    def unpack_small(layer):
        ext[...] = mat(0, layer, slice(0, lanes)).astype(f32)
        turned = ext[...].T
        for k in range(2):
            gains[layer, k] = turned[k : k + 1, :]
        for h in range(heads):
            column = ext[pl.ds(h, slots, stride=heads), :][:, 2:3]
            bias_rows[layer, h] = jnp.broadcast_to(column * log2_e, (slots, lanes))

    def forward_attn(layer, s):
        at = seg_rows(s)

        @pl.when(layer == 1)
        def _():
            for copy in spill_copies(s, False):
                copy.wait()

        valid = valid_col(s)
        x = ub[layer, at, :].astype(f32)
        squares = jnp.sum(x * x, axis=1, keepdims=True)
        add_stat(layer, 0, squares, valid)
        n1 = (x * lax.rsqrt(squares / width + norm_eps) * gains[layer, 0]).astype(bf16)
        for k in range(3):
            part = mm(n1, mat(0, layer, qkv_cols(k)))
            if k == 0:
                part = part * (score_scale * log2_e)
            qkv[at, k * width : (k + 1) * width] = part.astype(bf16)
        after(layer, s, "qkv")
        forward_attention(layer, s)

        @pl.when(layer == 0)
        def _():
            for copy in spill_copies(s, False, range(4)):
                copy.start()

    def forward_ffn(layer, s):
        at = seg_rows(s)
        valid = valid_col(s)
        z = mm(obuf[at, :], mat(1, layer))
        add_stat(layer, 1, jnp.sum(z * z, axis=1, keepdims=True), valid)
        h = ub[layer, at, :].astype(f32) + z
        hbuf[layer, at, :] = h.astype(bf16)
        dn[at, :] = h
        n2 = (h * lax.rsqrt(jnp.mean(h * h, axis=1, keepdims=True) + norm_eps) * gains[layer, 1]).astype(bf16)
        n2buf[at, :] = n2
        out = None
        for c in range(ff // chunk):
            cols = slice(c * chunk, (c + 1) * chunk)
            before = mm(n2buf[at, :], mat(2, layer, cols))
            pre[at, cols] = before.astype(bf16)
            gate = 0.5 + 0.5 * jnp.tanh(before * (gelu_c + (gelu_c * gelu_k) * (before * before)))
            part = mm((before * gate).astype(bf16), mat(3, layer, planes=slice(c, c + 1)))
            out = part if out is None else out + part
        add_stat(layer, 2, jnp.sum(out * out, axis=1, keepdims=True), valid)
        ub[layer + 1, at, :] = (dn[at, :] + out).astype(bf16)

        @pl.when(layer == 0)
        def _():
            spill_copies(s, False, (4,))[0].start()

        after(layer, s, "ffn")

    @pl.loop(0, 2)
    def _(layer):
        need(layer, first_units)
        unpack_small(layer)

        @pl.loop(0, segs)
        def _(s):
            forward_attn(layer, s)

        need(layer, later_units)

        @pl.loop(0, segs)
        def _(s):
            forward_ffn(layer, s)

    if routed:
        for n in range(len(units)):
            drain(n)
    y_copy.start()

    def norm_back(x, gain, grad):
        inv = lax.rsqrt(jnp.mean(x * x, axis=1, keepdims=True) + norm_eps)
        hat = x * inv
        dgain = jnp.sum(grad * hat, axis=0, keepdims=True)
        scaled = grad * gain
        return inv * (scaled - hat * jnp.mean(scaled * hat, axis=1, keepdims=True)), dgain

    def backward_ffn(layer):
        slot = layer + 1

        @pl.loop(0, segs)
        def _(s):
            at = seg_rows(s)
            h = hbuf[layer, at, :].astype(f32)
            n2buf[at, :] = (h * lax.rsqrt(jnp.mean(h * h, axis=1, keepdims=True) + norm_eps) * gains[layer, 1]).astype(bf16)

        dn[...] = jnp.zeros_like(dn)

        @pl.loop(0, ff // chunk)
        def _(c):
            cols = pl.ds(pl.multiple_of(c * chunk, chunk), chunk)
            planes = pl.ds(c, 1)
            d_act = nt(dy[...], mat(3, layer, planes=planes))
            x = pre[:, cols].astype(f32)
            sq = x * x
            gate = 0.5 + 0.5 * jnp.tanh(x * (gelu_c + (gelu_c * gelu_k) * sq))
            act = x * gate
            slope = gate + act * (1.0 - gate) * (2.0 * gelu_c + (6.0 * gelu_c * gelu_k) * sq)
            d_pre = (d_act * slope).astype(bf16)
            pre[:, cols] = d_pre
            put_mat(3, slot, tn(act.astype(bf16), dy[...]).astype(bf16), planes=planes)
            put_mat(2, slot, tn(n2buf[...], d_pre).astype(bf16), cols)
            dn[...] += nt(d_pre, mat(2, layer, cols))

    def backward_middle(layer, s):
        at = seg_rows(s)
        dh, dgain = norm_back(hbuf[layer, at, :].astype(f32), gains[layer, 1], dn[at, :])
        dgf_ref[layer] += dgain
        dh = dh + dy[at, :].astype(f32)
        dn[at, :] = dh
        dz = dh.astype(bf16)
        dy[at, :] = dz
        do = nt(dz, mat(1, layer)) * ilbuf[at, :].astype(f32)
        prod = do.astype(bf16).astype(f32) * obuf[at, :].astype(f32)
        for p in range(pairs):
            cols = slice(p * lanes, (p + 1) * lanes)
            for side in range(2):
                own, marks = lane_marks(head_size, side)
                delta = -jnp.sum(prod[:, cols] * own, axis=1, keepdims=True)
                hi = delta.astype(bf16).astype(f32)
                fill = hi * marks[0] + (delta - hi) * marks[1]
                doa[side, at, cols] = (do[:, cols] * (1.0 - marks[0] - marks[1]) + fill).astype(bf16)

    def backward_attention(layer, s):
        at = seg_rows(s)
        for p in range(pairs):
            cols = slice(p * lanes, (p + 1) * lanes)
            kcols = slice(width + p * lanes, width + (p + 1) * lanes)
            vcols = slice(2 * width + p * lanes, 2 * width + (p + 1) * lanes)
            qp = qkv[at, cols]
            kp = qkv[at, kcols]
            vp = qkv[at, vcols]
            q_turned = qp.T
            dq, dk, dv = [], [], []
            for side in range(2):
                h = 2 * p + side
                own, marks = lane_marks(head_size, side)
                do_h = doa[side, at, cols]
                va = vp * own.astype(bf16) + (marks[0] + marks[1]).astype(bf16)
                weights = ebuf[s, h]
                d_scores = weights.astype(f32) * nt(do_h, va)
                dbias_ref[layer, h : h + 1, :] += jnp.sum(d_scores[:, :lanes], axis=0, keepdims=True)
                d_scores = d_scores.astype(bf16)
                half = slice(side * head_size, (side + 1) * head_size)
                dq.append(mm(d_scores, kp))
                dk.append(mm(q_turned[half, :], d_scores))
                dv.append(mm(do_h.T[half, :], weights))
            own, _ = lane_marks(head_size, 0)
            qkv[at, cols] = (jnp.where(own > 0, dq[0], dq[1]) * score_scale).astype(bf16)
            qkv[at, kcols] = (jnp.concatenate(dk, axis=0).T * (1.0 / log2_e)).astype(bf16)
            qkv[at, vcols] = jnp.concatenate(dv, axis=0).T.astype(bf16)

    def backward_input(layer, s):
        at = seg_rows(s)
        x = ub[layer, at, :].astype(f32)
        du, dgain = norm_back(x, gains[layer, 0], nt(qkv[at, :], mat(0, layer, slice(lanes, lanes + 3 * width))))
        dga_ref[layer] += dgain
        dy[at, :] = (du + dn[at, :]).astype(bf16)
        n2buf[at, :] = (x * lax.rsqrt(jnp.mean(x * x, axis=1, keepdims=True) + norm_eps) * gains[layer, 0]).astype(bf16)

    def grad_copies(layer, picks=range(4)):
        slot = layer + 1
        return [
            pltpu.make_async_copy(src.at[slot], dst.at[layer], sem_g.at[layer, k])
            for k, (src, dst) in enumerate(((wq, gq_out), (wo, go_out), (wu, gu_out), (wd, gd_out)))
            if k in picks
        ]

    @pl.loop(0, 2)
    def _(step):
        layer = 1 - step
        slot = layer + 1

        @pl.when(layer == 0)
        def _():
            for s in range(segs):
                for copy in spill_copies(s, True, (2, 3, 4)):
                    copy.wait()

        backward_ffn(layer)

        @pl.loop(0, segs)
        def _(s):
            backward_middle(layer, s)

        put_mat(1, slot, tn(obuf[...], dy[...]).astype(bf16))
        for copy in grad_copies(layer, (1, 2, 3)):
            copy.start()

        @pl.when(layer == 1)
        def _():
            for s in range(segs):
                for copy in spill_copies(s, True, (2, 3, 4)):
                    copy.start()

        @pl.loop(0, segs)
        def _(s):
            @pl.when(layer == 0)
            def _():
                for copy in spill_copies(s, True, (0, 1)):
                    copy.wait()

            backward_attention(layer, s)

            @pl.when(layer == 1)
            def _():
                spill_copies(s, True, (1,))[0].start()

        @pl.loop(0, segs)
        def _(s):
            backward_input(layer, s)

        for k in range(3):
            part = slice(k * width, (k + 1) * width)
            put_mat(0, slot, tn(n2buf[...], qkv[:, part]).astype(bf16), qkv_cols(k))
        grad_copies(layer, (0,))[0].start()

        @pl.when(layer == 1)
        def _():
            for s in range(segs):
                spill_copies(s, True, (0,))[0].start()

        for copy in grad_copies(layer):
            copy.wait()

    du_copy.start()
    du_copy.wait()
    y_copy.wait()


def run_layers(doc_len, u0, dout, weights, routed, heads, slots, segs):
    all_rows, width = u0.shape
    rows = all_rows // segs
    ff = weights[2].shape[-1]
    dims = (segs, rows, width, ff, slots, heads)
    vmem = pl.BlockSpec(memory_space=pltpu.VMEM)
    smem = pl.BlockSpec(memory_space=pltpu.SMEM)
    hbm = pl.BlockSpec(memory_space=pl.ANY)
    shape = jax.ShapeDtypeStruct
    wide = (all_rows, width)
    grid = (4, 2, 2, 2)
    mats = [
        (*grid, width // 32, lanes + 3 * width),
        (*grid, width // 32, width),
        (*grid, width // 32, ff),
        (*grid, ff // 32, width),
    ]
    spills = [
        shape((all_rows, 3 * width), bf16),
        shape((segs, heads, rows, rows), bf16),
        shape(wide, bf16),
        shape(wide, bf16),
        shape((all_rows, ff), bf16),
    ]
    out_shape = [shape(wide, bf16)] * 2
    out_shape += [shape((2, *mat), bf16) for mat in mats]
    out_shape += [
        shape((2, 1, width), f32),
        shape((2, 1, width), f32),
        shape((2, heads, lanes), f32),
        shape((2, 8, lanes), f32),
    ] + spills
    unit_count = 16
    scratch = [pltpu.VMEM((3, *mat), bf16) for mat in mats]
    scratch += [
        pltpu.VMEM((3, *wide), bf16),
        pltpu.VMEM(wide, bf16),
        pltpu.VMEM((all_rows, 3 * width), bf16),
        pltpu.VMEM((segs, heads, rows, rows), bf16),
        pltpu.VMEM(wide, bf16),
        pltpu.VMEM(wide, bf16),
        pltpu.VMEM((2, *wide), bf16),
        pltpu.VMEM((all_rows, ff), bf16),
        pltpu.VMEM((2, *wide), bf16),
        pltpu.VMEM(wide, f32),
        pltpu.VMEM(wide, bf16),
        pltpu.VMEM((2, 2, 1, width), f32),
        pltpu.VMEM((2, heads, slots, lanes), f32),
        pltpu.VMEM((width, lanes), f32),
        pltpu.SemaphoreType.DMA((segs, 5)),
        pltpu.SemaphoreType.DMA((segs, 5)),
        pltpu.SemaphoreType.DMA((2, 4)),
        pltpu.SemaphoreType.DMA((4,)),
        pltpu.SemaphoreType.DMA((unit_count,)),
        pltpu.SemaphoreType.DMA((unit_count, 11)),
        pltpu.SemaphoreType.DMA((unit_count, 11)),
    ]
    params = dict(vmem_limit_bytes=63 * 2**20)
    if routed:
        params.update(collective_id=0, has_side_effects=True)
    return pl.pallas_call(
        partial(fused_layers, dims, routed),
        out_shape=out_shape,
        in_specs=[smem] + [hbm] * 6,
        out_specs=[hbm] * 6 + [vmem] * 4 + [hbm] * 5,
        scratch_shapes=scratch,
        compiler_params=pltpu.CompilerParams(**params),
    )(doc_len, u0, dout, *weights)[:10]


def swap(block):
    return lax.ppermute(block, "section", [(0, 1), (1, 0)])


def body(
    tokens,
    memory,
    lengths,
    w_qkv,
    w_out,
    w_up,
    w_down,
    gain_attn,
    gain_ffn,
    forget_bias,
    grad_tokens,
    grad_memory,
):
    section = lax.axis_index("section")
    is_first = section == 0
    micro = tokens.shape[0]
    segs = micro // 2
    half_tok = tokens.shape[1]
    half_mem = memory.shape[1]
    slots = 2 * half_mem
    seg_len = 2 * half_tok
    rows = slots + seg_len
    width = tokens.shape[2]

    def own_segs(halves):
        return lax.dynamic_slice_in_dim(halves, section * segs, segs, 0)

    def other_segs(halves):
        return lax.dynamic_slice_in_dim(halves, (1 - section) * segs, segs, 0)

    def both(kept, got):
        return jnp.concatenate(
            [jnp.where(is_first, kept, got), jnp.where(is_first, got, kept)], axis=1
        )

    inputs = (tokens, memory, grad_tokens, grad_memory)
    got = swap(tuple(other_segs(part) for part in inputs))
    full = [both(own_segs(part), other) for part, other in zip(inputs, got)]
    u0 = jnp.concatenate([full[1], full[0]], axis=1).reshape(segs * rows, width)
    dout = jnp.concatenate([full[3], full[2]], axis=1).reshape(segs * rows, width)

    heads = forget_bias.shape[1] * lax.axis_size("dp") // slots
    small = jnp.stack([gain_attn, gain_ffn, forget_bias], axis=2)
    small = jnp.pad(small, ((0, 0), (0, 0), (0, lanes - 3)))
    pieces = (jnp.concatenate([small, w_qkv], axis=2), w_out, w_up, w_down)
    routed = lax.axis_size("dp") == 16 and width == 512

    def gather(piece):
        whole = lax.all_gather(piece, ("section", "dp"), axis=1, tiled=True)
        return whole.reshape(2, 4, 2, 2, 2, -1, piece.shape[2])

    if routed:
        weights = [piece.reshape(2, -1, piece.shape[2]) for piece in pieces]
    else:
        weights = [gather(piece) for piece in pieces]
    per_doc = micro // lengths.shape[0]
    own_len = lax.dynamic_slice_in_dim(lengths, section * segs // per_doc, 1, 0)
    y, du, gq, go, gu, gd, dga, dgf, dbias, stats = run_layers(
        own_len, u0, dout, weights, routed, heads, slots, segs
    )

    def scatter(grad):
        mine = lax.dynamic_index_in_dim(grad, section, 0, keepdims=True)
        other = lax.dynamic_index_in_dim(grad, 1 - section, 0, keepdims=True)
        chip = (mine.astype(f32) + swap(other).astype(f32)).astype(grad.dtype)
        return lax.psum_scatter(chip, "dp", scatter_dimension=1, tiled=True).astype(f32)

    gq, go, gu, gd = (
        grad.reshape(2, -1, grad.shape[-1]) for grad in (gq[..., lanes:], go, gu, gd)
    )
    grad_bias = jnp.swapaxes(dbias[:, :, :slots], 1, 2).reshape(2, slots * heads)
    shares = tuple(scatter(grad) for grad in (gq, go, gu, gd, dga[:, 0], dgf[:, 0], grad_bias))
    token_count = jnp.sum(own_len).astype(f32)
    sums = jnp.concatenate([stats[:, :3, 0].reshape(6), token_count[None]])
    totals = lax.psum(sums, ("section", "dp"))
    rms = jnp.sqrt(totals[:6].reshape(2, 3) / (totals[6] * width))

    result = jnp.stack([y.reshape(segs, rows, width), du.reshape(segs, rows, width)])

    def half_of(which):
        tok = lax.dynamic_slice_in_dim(result, slots + which * half_tok, half_tok, 2)
        mem = lax.dynamic_slice_in_dim(result, which * half_mem, half_mem, 2)
        return tok, mem

    kept = half_of(section)
    got = swap(half_of(1 - section))

    def order(mine, other):
        return jnp.concatenate(
            [jnp.where(is_first, mine, other), jnp.where(is_first, other, mine)], axis=0
        )

    toks = [order(kept[0][k], got[0][k]) for k in range(2)]
    mems = [order(kept[1][k], got[1][k]) for k in range(2)]
    return (toks[0], mems[0], toks[1], mems[1], *shares, rms)


def solution(mesh):
    rows = P("dp", "section", None)
    mats = P("section", "dp", None)
    vecs = P("section", "dp")
    return jax.shard_map(
        body,
        mesh=mesh,
        in_specs=(rows, rows, P("dp"), mats, mats, mats, mats, vecs, vecs, vecs, rows, rows),
        out_specs=(rows, rows, rows, rows, mats, mats, mats, mats, vecs, vecs, vecs, P()),
        check_vma=False,
    )
```

```python
from functools import partial

import jax
import jax.numpy as jnp
from jax import lax
from jax.experimental import pallas as pl
from jax.experimental.pallas import tpu as pltpu
from jax.sharding import PartitionSpec as P

norm_eps = 1e-06
score_scale = 0.125
log2_e = 1.4426950408889634
masked_score = -1000000000.0
gelu_c = 0.7978845608028654
gelu_k = 0.044715
f32 = jnp.float32
bf16 = jnp.bfloat16
lanes = 128
chunk = 512


def mm(a, b, ca=1, cb=0):
    return lax.dot_general(a, b, (((ca,), (cb,)), ((), ())), preferred_element_type=f32)


def nt(a, b):
    return mm(a, b, 1, 1)


def tn(a, b):
    return mm(a, b, 0, 0)


def lane_marks(head_size, side):
    lane = lax.broadcasted_iota(jnp.int32, (1, lanes), 1)
    own = ((lane // head_size) == side).astype(f32)
    first = (1 - side) * head_size
    marks = [(lane == first + k).astype(f32) for k in range(3)]
    return own, marks


def fused_layers(dims, routed, *refs):
    segs, rows, width, ff, slots, heads = dims
    refs = list(refs)

    def take(count):
        picked = refs[:count]
        del refs[:count]
        return picked

    (len_ref,) = take(1)
    rows_in = take(4 if routed else 2)
    weight_in = take(4)
    rows_out = take(4 if routed else 2)
    grads_out = take(4)
    (stat_out,) = take(1)
    spill_hbm = take(5)
    lands = [take(4) for _ in range(4)] if routed else None
    weight_buf = take(4)
    ub, dy, qkv, ebuf, obuf, ilbuf, hbuf, pre, doa, dn = take(10)
    gains, bias_rows, ext, gain_sums, dbias, stat_ref = take(6)
    sem_spill, sem_back, sem_g, sem_io, sem_own, sem_send, sem_recv = take(7)
    if routed:
        stage, fin = take(4), take(4)
        stat_sum, stat_land = take(2)
        sem_stage, rs_send, rs_recv, io_send, io_recv, stat_send, stat_recv = take(7)
    head_size = width // heads
    pairs = width // lanes
    tok_rows = rows - slots
    doc_len = len_ref[0]
    every = slice(None)

    def units_of(layer):
        half_ff, half_deep = ff // 2, ff // 64
        lead = [
            (0, slice(0, lanes + width), every),
            (0, slice(lanes + width, lanes + 2 * width), every),
            (0, slice(lanes + 2 * width, lanes + 3 * width), every),
        ]
        if layer == 1:
            lead = [(0, every, every)]
        rest = [(1, every, every)]
        rest += [(2, slice(k * half_ff, (k + 1) * half_ff), every) for k in range(2)]
        rest += [(3, every, slice(k * half_deep, (k + 1) * half_deep)) for k in range(2)]
        return [(layer, *unit) for unit in lead + rest]

    units = units_of(0) + units_of(1)
    first_units = [k for k, unit in enumerate(units) if unit[1] == 0]
    later_units = [k for k, unit in enumerate(units) if unit[1] != 0]

    def view(n, z, y, x, c):
        layer, which, cols, part = units[n]
        return weight_buf[which].at[layer, z, y, x, c, part, cols]

    if routed:
        core = lax.axis_index("section")
        chip = lax.axis_index("dp")
        z, y, x = chip // 4, (chip // 2) % 2, chip % 2
        other = 1 - core

        def place(pz, py, px):
            return pz * 4 + py * 2 + px

        mate = (other, chip)
        near_x = (core, place(z, y, 1 - x))
        near_y = (core, place(z, 1 - y, x))
        along_z = [(core, place((z + k) % 4, y, x)) for k in range(1, 4)]

        def remote(src, dst, n, k, target):
            return pltpu.make_async_remote_copy(
                src_ref=src,
                dst_ref=dst,
                send_sem=sem_send.at[n, k],
                recv_sem=sem_recv.at[n, k],
                device_id=target,
                device_id_type=pl.DeviceIdType.MESH,
            )

        def own_shard(n):
            layer, which, cols, part = units[n]
            src = weight_in[which].at[every, part, cols]
            return src, view(n, z, y, x, every)

        def z_copy(n, k):
            spot = view(n, z, y, x, core)
            return remote(spot, spot, n, k, along_z[k - 1])

        def plane_copy(n, k, x_first):
            if k == 4:
                spot = view(n, every, y, x, core)
                return remote(spot, spot, n, 4, near_x if x_first else near_y)
            spot = view(n, every, y, every, core) if x_first else view(n, every, every, x, core)
            return remote(spot, spot, n, 5, near_y if x_first else near_x)

        def mate_copy(n, k, x_first, half):
            if k < 9:
                from_z = (z + 4 - (k - 5)) % 4
                spot = view(n, from_z, y, x, half)
            elif k == 9:
                spot = view(n, every, y, 1 - x, half) if x_first else view(n, every, 1 - y, x, half)
            else:
                spot = view(n, every, 1 - y, every, half) if x_first else view(n, every, every, 1 - x, half)
            return remote(spot, spot, n, k, mate)

        def by_route(n, act):
            for side in range(2):
                @pl.when(core == side)
                def _(side=side):
                    act((side + n) % 2 == 0)

        def share_own(n):
            src, dst = own_shard(n)

            @pl.when(core == units[n][0])
            def _():
                pltpu.make_async_copy(src, dst, sem_own.at[n]).start()
                remote(src, dst, n, 0, mate).start()

        def start_z(n):
            src, dst = own_shard(n)

            @pl.when(core == units[n][0])
            def _():
                pltpu.make_async_copy(src, dst, sem_own.at[n]).wait()

            @pl.when(core != units[n][0])
            def _():
                remote(src, dst, n, 0, mate).wait_recv()

            for k in range(1, 4):
                z_copy(n, k).start()

        def first_hop(n):
            for k in range(1, 4):
                z_copy(n, k).wait_recv()

            def act(x_first):
                plane_copy(n, 4, x_first).start()
                for k in range(6, 9):
                    mate_copy(n, k, x_first, core).start()

            by_route(n, act)

        def second_hop(n):
            def act(x_first):
                plane_copy(n, 4, x_first).wait_recv()
                plane_copy(n, 5, x_first).start()
                mate_copy(n, 9, x_first, core).start()

            by_route(n, act)

        def last_share(n):
            def act(x_first):
                plane_copy(n, 5, x_first).wait_recv()
                mate_copy(n, 10, x_first, core).start()

            by_route(n, act)

        def complete(n):
            def act(x_first):
                for k in range(6, 11):
                    mate_copy(n, k, not x_first, other).wait_recv()

            by_route(n, act)

        def drain(n):
            src, dst = own_shard(n)

            @pl.when(core == units[n][0])
            def _():
                remote(src, dst, n, 0, mate).wait_send()

            for k in range(1, 4):
                z_copy(n, k).wait_send()

            def act(x_first):
                for k in (4, 5):
                    plane_copy(n, k, x_first).wait_send()
                for k in range(6, 11):
                    mate_copy(n, k, x_first, core).wait_send()

            by_route(n, act)

        def tick(t):
            if 0 <= t - 4 < len(units):
                last_share(t - 4)
            if 0 <= t - 2 < len(units):
                second_hop(t - 2)
            if 0 <= t < len(units):
                first_hop(t)
            ahead = t + 4
            if ahead < len(units) and ahead >= lead_units:
                start_z(ahead)

        lead_units = 6
        ticks_at = {
            (0, 0, "qkv"): [7], (0, 0, "quad0"): [8], (0, 0, "quad1"): [9],
            (0, 1, "qkv"): [10], (0, 1, "quad0"): [11], (0, 1, "quad1"): [12],
            (0, 0, "ffn"): [13], (0, 1, "ffn"): [14],
            (1, 0, "qkv"): [15], (1, 0, "quad0"): [16], (1, 0, "quad1"): [17],
        }
    else:
        ticks_at = {}

        def weight_copy(n):
            layer, which, cols, part = units[n]
            src = weight_in[which].at[layer, every, every, every, every, part, cols]
            return pltpu.make_async_copy(src, view(n, every, every, every, every), sem_own.at[n])

        def complete(n):
            weight_copy(n).wait()

    def after(layer, s, point):
        for (at_layer, at_s, at_point), ticks in ticks_at.items():
            if at_point == point:
                @pl.when((layer == at_layer) & (s == at_s))
                def _(ticks=ticks):
                    for t in ticks:
                        tick(t)

    def need(layer, picks):
        for at_layer in range(2):
            @pl.when(layer == at_layer)
            def _(at_layer=at_layer):
                for n in picks:
                    if units[n][0] == at_layer:
                        complete(n)

    def mat(which, slot, cols=every, planes=None):
        if planes is None:
            value = weight_buf[which][slot, :, :, :, :, :, cols]
        else:
            value = weight_buf[which][slot, planes, :, :, :, :, cols]
        deep = 1
        for size in value.shape[:-1]:
            deep *= size
        return value.reshape(deep, value.shape[-1])

    def put_mat(which, slot, value, cols=every, planes=None):
        buf = weight_buf[which]
        shape = buf.shape[1:-1]
        if planes is None:
            buf[slot, :, :, :, :, :, cols] = value.reshape(*shape, value.shape[-1])
        else:
            buf[slot, planes] = value.reshape(1, *shape[1:], value.shape[-1])

    def qkv_cols(k):
        return slice(lanes + k * width, lanes + (k + 1) * width)

    def seg_rows(s):
        return pl.ds(pl.multiple_of(s * rows, rows), rows)

    def spill_copies(s, back, picks=range(5)):
        at = seg_rows(s)
        kept = (qkv.at[at], ebuf.at[s], obuf.at[at], ilbuf.at[at], pre.at[at])
        pairs_of = [
            (vmem, hbm.at[s] if k == 1 else hbm.at[at])
            for k, (vmem, hbm) in enumerate(zip(kept, spill_hbm))
        ]
        if back:
            return [
                pltpu.make_async_copy(hbm, vmem, sem_back.at[s, k])
                for k, (vmem, hbm) in enumerate(pairs_of)
                if k in picks
            ]
        return [
            pltpu.make_async_copy(vmem, hbm, sem_spill.at[s, k])
            for k, (vmem, hbm) in enumerate(pairs_of)
            if k in picks
        ]

    def valid_col(s):
        row = lax.broadcasted_iota(jnp.int32, (rows, 1), 0)
        return jnp.where(
            (row >= slots) & (s * tok_rows + row - slots < doc_len), 1.0, 0.0
        ).astype(f32)

    def mask_col(s):
        row = lax.broadcasted_iota(jnp.int32, (rows, 1), 0)
        return jnp.where(
            (row >= slots) & (s * tok_rows + row - slots >= doc_len), masked_score, 0.0
        ).astype(f32)

    if routed:
        half_tok, half_mem = tok_rows // 2, slots // 2

        def io_copies(buf, tok_ref, mem_ref, first, outward):
            local, away = [], []
            k = first
            for s in range(segs):
                mine, theirs = core * segs + s, other * segs + s
                for ref, base, size in ((tok_ref, slots, half_tok), (mem_ref, 0, half_mem)):
                    def rows_of(half):
                        return buf.at[pl.ds(pl.multiple_of(s * rows + base + half * size, 16), size)]

                    if outward:
                        local.append(pltpu.make_async_copy(rows_of(core), ref.at[mine], sem_io.at[k]))
                        src, dst = rows_of(other), ref.at[mine]
                    else:
                        local.append(pltpu.make_async_copy(ref.at[mine], rows_of(core), sem_io.at[k]))
                        src, dst = ref.at[theirs], rows_of(core)
                    away.append(
                        pltpu.make_async_remote_copy(
                            src_ref=src,
                            dst_ref=dst,
                            send_sem=io_send.at[k],
                            recv_sem=io_recv.at[k],
                            device_id=mate,
                            device_id_type=pl.DeviceIdType.MESH,
                        )
                    )
                    k += 1
            return local, away

        loads, shares = io_copies(ub.at[0], rows_in[0], rows_in[1], 0, False)
        more = io_copies(dy, rows_in[2], rows_in[3], 2 * segs, False)
        loads, shares = loads + more[0], shares + more[1]
        y_copies = io_copies(doa.at[1], rows_out[0], rows_out[1], 4 * segs, True)
        du_copies = io_copies(dy, rows_out[2], rows_out[3], 6 * segs, True)
    else:
        loads = [
            pltpu.make_async_copy(rows_in[0], ub.at[0], sem_io.at[0]),
            pltpu.make_async_copy(rows_in[1], dy, sem_io.at[1]),
        ]
        shares = []
        y_copies = [pltpu.make_async_copy(doa.at[1], rows_out[0], sem_io.at[2])], []
        du_copies = [pltpu.make_async_copy(dy, rows_out[1], sem_io.at[3])], []
    for copy in loads:
        copy.start()
    if routed:
        barrier = pltpu.get_barrier_semaphore()
        peers = [mate, near_x, near_y, *along_z]
        for peer in peers:
            pl.semaphore_signal(barrier, inc=1, device_id=peer, device_id_type=pl.DeviceIdType.MESH)
        pl.semaphore_wait(barrier, len(peers))
        for n in range(len(units)):
            share_own(n)
        for copy in shares:
            copy.start()
        for n in range(lead_units):
            start_z(n)
        for t in range(7):
            tick(t)
    else:
        for n in range(len(units)):
            weight_copy(n).start()
    stat_ref[...] = jnp.zeros_like(stat_ref)

    for copy in loads:
        copy.wait()
    for copy in shares:
        copy.wait()

    def add_stat(layer, k, row_sums, valid):
        total = jnp.sum(row_sums * valid, axis=0, keepdims=True)
        stat_ref[layer, k : k + 1, :] += jnp.broadcast_to(total, (1, lanes))

    def forward_attention(layer, s):
        at = seg_rows(s)
        mask = mask_col(s)
        for p in range(pairs):
            cols = slice(p * lanes, (p + 1) * lanes)
            qp = qkv[at, cols]
            kp = qkv[at, slice(width + p * lanes, width + (p + 1) * lanes)]
            vp = qkv[at, slice(2 * width + p * lanes, 2 * width + (p + 1) * lanes)]
            outs = []
            for side in range(2):
                h = 2 * p + side
                own, marks = lane_marks(head_size, side)
                bias = bias_rows[layer, h]
                hi = bias.astype(bf16).astype(f32)
                aux = jnp.concatenate([hi * marks[1] + (bias - hi) * marks[2], jnp.zeros((tok_rows, lanes), f32)], axis=0)
                aux = aux + mask * marks[0]
                extra = marks[0] + marks[1] + marks[2]
                ka = kp * own.astype(bf16) + aux.astype(bf16)
                qa = qp * (1.0 - extra).astype(bf16) + extra.astype(bf16)
                scores = nt(qa, ka)
                top = jnp.max(scores, axis=1, keepdims=True)
                weights = jnp.exp2(scores - top).astype(bf16)
                ebuf[s, h] = weights
                va = vp * own.astype(bf16) + (1.0 - own).astype(bf16)
                outs.append(mm(weights, va))
            own, _ = lane_marks(head_size, 0)
            raw = jnp.where(own > 0, outs[0], outs[1])
            sums = pltpu.roll(jnp.where(own > 0, outs[1], outs[0]), head_size, 1)
            inv = 1.0 / sums
            ilbuf[at, cols] = inv.astype(ilbuf.dtype)
            obuf[at, cols] = (raw * inv).astype(bf16)
            if p % 2 == 1:
                after(layer, s, "quad" + str(p // 2))

    def unpack_small(layer):
        ext[...] = mat(0, layer, slice(0, lanes)).astype(f32)
        turned = ext[...].T
        for k in range(2):
            gains[layer, k] = turned[k : k + 1, :]
        for h in range(heads):
            column = ext[pl.ds(h, slots, stride=heads), :][:, 2:3]
            bias_rows[layer, h] = jnp.broadcast_to(column * log2_e, (slots, lanes))

    def forward_attn(layer, s):
        at = seg_rows(s)

        @pl.when(layer == 1)
        def _():
            for copy in spill_copies(s, False):
                copy.wait()

        valid = valid_col(s)
        x = ub[layer, at, :].astype(f32)
        squares = jnp.sum(x * x, axis=1, keepdims=True)
        add_stat(layer, 0, squares, valid)
        add_stat(layer, 3, valid, valid)
        n1 = (x * lax.rsqrt(squares / width + norm_eps) * gains[layer, 0]).astype(bf16)
        for k in range(3):
            part = mm(n1, mat(0, layer, qkv_cols(k)))
            if k == 0:
                part = part * (score_scale * log2_e)
            qkv[at, k * width : (k + 1) * width] = part.astype(bf16)
        after(layer, s, "qkv")
        forward_attention(layer, s)

        @pl.when(layer == 0)
        def _():
            for copy in spill_copies(s, False, range(4)):
                copy.start()

    def forward_ffn(layer, s):
        at = seg_rows(s)
        valid = valid_col(s)
        z = mm(obuf[at, :], mat(1, layer))
        add_stat(layer, 1, jnp.sum(z * z, axis=1, keepdims=True), valid)
        h = ub[layer, at, :].astype(f32) + z
        hbuf[layer, at, :] = h.astype(bf16)
        dn[at, :] = h
        doa[0, at, :] = (h * lax.rsqrt(jnp.mean(h * h, axis=1, keepdims=True) + norm_eps) * gains[layer, 1]).astype(bf16)
        out = None
        for c in range(ff // chunk):
            cols = slice(c * chunk, (c + 1) * chunk)
            before = mm(doa[0, at, :], mat(2, layer, cols))
            pre[at, cols] = before.astype(bf16)
            gate = 0.5 + 0.5 * jnp.tanh(before * (gelu_c + (gelu_c * gelu_k) * (before * before)))
            part = mm((before * gate).astype(bf16), mat(3, layer, planes=slice(c, c + 1)))
            out = part if out is None else out + part
        add_stat(layer, 2, jnp.sum(out * out, axis=1, keepdims=True), valid)
        result = (dn[at, :] + out).astype(bf16)

        @pl.when(layer == 0)
        def _():
            ub[1, at, :] = result

        @pl.when(layer == 1)
        def _():
            doa[1, at, :] = result

        @pl.when(layer == 0)
        def _():
            spill_copies(s, False, (4,))[0].start()

        after(layer, s, "ffn")

    @pl.loop(0, 2)
    def _(layer):
        need(layer, first_units)
        unpack_small(layer)

        @pl.loop(0, segs)
        def _(s):
            forward_attn(layer, s)

        need(layer, later_units)

        @pl.loop(0, segs)
        def _(s):
            forward_ffn(layer, s)

    if routed:
        for n in range(len(units)):
            drain(n)
    for copies in y_copies:
        for copy in copies:
            copy.start()

    if routed:
        def rs_copy(src, dst, layer, u, k, target):
            return pltpu.make_async_remote_copy(
                src_ref=src,
                dst_ref=dst,
                send_sem=rs_send.at[layer, u, k],
                recv_sem=rs_recv.at[layer, u, k],
                device_id=target,
                device_id_type=pl.DeviceIdType.MESH,
            )

        def part(layer, u, pz, py, px, c):
            return weight_buf[u].at[layer + 1, pz, py, px, c]

        def rs_sends(layer, u, step, y_first):
            land = lands[u][step].at[layer] if step < 4 else None
            if step == 0:
                return [rs_copy(part(layer, u, every, every, every, other), land, layer, u, 0, mate)]
            if step == 1:
                spot = part(layer, u, every, 1 - y, every, core) if y_first else part(layer, u, every, every, 1 - x, core)
                return [rs_copy(spot, land, layer, u, 1, near_y if y_first else near_x)]
            if step == 2:
                spot = part(layer, u, every, y, 1 - x, core) if y_first else part(layer, u, every, 1 - y, x, core)
                return [rs_copy(spot, land, layer, u, 2, near_x if y_first else near_y)]
            if step == 3:
                return [
                    rs_copy(part(layer, u, (z + k) % 4, y, x, core), land.at[k - 1], layer, u, 2 + k, along_z[k - 1])
                    for k in range(1, 4)
                ]
            return [rs_copy(fin[u].at[layer], grads_out[u].at[core], layer, u, 6, mate)]

        def rs_route(u, act):
            for side in range(2):
                @pl.when(core == side)
                def _(side=side):
                    act((side + u) % 2 == 0)

        def rs_start(layer, u, step):
            def act(y_first):
                for copy in rs_sends(layer, u, step, y_first):
                    copy.start()

            if step in (1, 2):
                rs_route(u, act)
            else:
                act(True)

        def stage_part(u, step):
            if step == 0:
                return stage[u]
            if step == 1:
                return stage[u].at[:, :, 0]
            if step == 2:
                return stage[u].at[:, 0, 0]
            return stage[u].at[0:3, 0, 0]

        def stage_copy(layer, u, step):
            return pltpu.make_async_copy(lands[u][step].at[layer], stage_part(u, step), sem_stage.at[u])

        def rs_arrive(layer, u, step):
            def act(y_first):
                for copy in rs_sends(layer, u, step, y_first):
                    copy.wait_recv()

            if step in (1, 2):
                rs_route(u, act)
            else:
                act(True)
            stage_copy(layer, u, step).start()

        def rs_merge(layer, u, step):
            stage_copy(layer, u, step).wait()
            slot = layer + 1
            buf, got = weight_buf[u], stage[u]
            if step == 3:
                total = buf[slot, z, y, x, core].astype(f32)
                for k in range(3):
                    total = total + got[k, 0, 0].astype(f32)
                fin[u][layer] = total

                @pl.when(core == layer)
                def _():
                    pltpu.make_async_copy(fin[u].at[layer], grads_out[u].at[core], sem_g.at[layer, u]).start()

                @pl.when(core != layer)
                def _():
                    rs_start(layer, u, 4)

                return

            @pl.loop(0, 4)
            def _(pz):
                if step == 0:
                    buf[slot, pz, :, :, core] += got[pz]
                elif step == 2:
                    buf[slot, pz, y, x, core] += got[pz, 0, 0]
                else:
                    def act(y_first):
                        if y_first:
                            buf[slot, pz, y, :, core] += got[pz, :, 0]
                        else:
                            buf[slot, pz, :, x, core] += got[pz, :, 0]

                    rs_route(u, act)

            rs_start(layer, u, step + 1)

        def rs_finish(layer, u):
            @pl.when(core == layer)
            def _():
                pltpu.make_async_copy(fin[u].at[layer], grads_out[u].at[core], sem_g.at[layer, u]).wait()
                rs_sends(layer, u, 4, True)[0].wait_recv()

            @pl.when(core != layer)
            def _():
                rs_sends(layer, u, 4, True)[0].wait_send()

            for step in range(4):
                def act(y_first, step=step):
                    for copy in rs_sends(layer, u, step, y_first):
                        copy.wait_send()

                if step in (1, 2):
                    rs_route(u, act)
                else:
                    act(True)

        def stat_copy(step, k=0):
            target = (mate, near_y, near_x)[step] if step < 3 else along_z[k]
            spot = step if step < 3 else 3 + z
            return pltpu.make_async_remote_copy(
                src_ref=stat_sum.at[step],
                dst_ref=stat_land.at[spot],
                send_sem=stat_send.at[step + k],
                recv_sem=stat_recv.at[step + k],
                device_id=target,
                device_id_type=pl.DeviceIdType.MESH,
            )

        def stat_step(step):
            if step == 0:
                stat_sum[0] = stat_ref[...]
            elif step < 4:
                stat_copy(step - 1).wait()
                stat_sum[step] = stat_sum[step - 1] + stat_land[step - 1]
            if step < 3:
                stat_copy(step).start()
            elif step == 3:
                stat_land[3 + z] = stat_sum[3]
                for k in range(3):
                    stat_copy(3, k).start()
            else:
                for k in range(3):
                    stat_copy(3, k).wait()
                total = stat_land[3] + stat_land[4] + stat_land[5] + stat_land[6]
                stat_ref[...] = total
                stat_done()

        stat_step(0)
        wq_u, wo_u, wu_u, wd_u = range(4)

        def arrive(layer, step, *us):
            return [partial(rs_arrive, layer, u, step) for u in us]

        def merge(layer, step, *us):
            return [partial(rs_merge, layer, u, step) for u in us]

        def send(layer, *us):
            return [partial(rs_start, layer, u, 0) for u in us]

        back_points = {
            (1, "ffn0"): [partial(stat_step, 1)],
            (1, "ffn1"): [partial(stat_step, 2)],
            (1, "ffn2"): [partial(stat_step, 3)],
            (1, "ffn3"): [partial(stat_step, 4)] + send(1, wd_u, wu_u),
            (1, "mid"): arrive(1, 0, wd_u, wu_u),
            (1, "wo"): merge(1, 0, wd_u, wu_u) + send(1, wo_u),
            (1, "att0"): arrive(1, 0, wo_u),
            (1, "quad"): merge(1, 0, wo_u),
            (1, "att1"): arrive(1, 1, wd_u, wu_u),
            (1, "wq"): send(1, wq_u) + merge(1, 1, wd_u, wu_u),
            (1, "in0"): arrive(1, 1, wo_u),
            (1, "in1"): merge(1, 1, wo_u) + arrive(1, 0, wq_u),
            (0, "ffn0"): merge(1, 0, wq_u) + arrive(1, 2, wd_u, wu_u),
            (0, "ffn1"): merge(1, 2, wd_u, wu_u) + arrive(1, 2, wo_u),
            (0, "ffn2"): merge(1, 2, wo_u) + arrive(1, 1, wq_u),
            (0, "ffn3"): merge(1, 1, wq_u) + arrive(1, 3, wd_u, wu_u, wo_u) + send(0, wd_u, wu_u),
            (0, "mid"): merge(1, 3, wd_u, wu_u, wo_u) + arrive(1, 2, wq_u) + arrive(0, 0, wd_u, wu_u),
            (0, "wo"): merge(1, 2, wq_u) + merge(0, 0, wd_u, wu_u) + send(0, wo_u),
            (0, "att0"): arrive(0, 0, wo_u) + arrive(1, 3, wq_u),
            (0, "quad"): merge(0, 0, wo_u) + merge(1, 3, wq_u) + arrive(0, 1, wd_u, wu_u),
            (0, "att1"): merge(0, 1, wd_u, wu_u) + arrive(0, 1, wo_u),
            (0, "wq"): send(0, wq_u) + merge(0, 1, wo_u),
            (0, "in0"): arrive(0, 2, wd_u, wu_u),
            (0, "in1"): merge(0, 2, wd_u, wu_u) + arrive(0, 0, wq_u) + arrive(0, 2, wo_u),
            (0, "end"): merge(0, 0, wq_u)
            + merge(0, 2, wo_u)
            + arrive(0, 3, wd_u, wu_u)
            + merge(0, 3, wd_u, wu_u)
            + arrive(0, 1, wq_u)
            + merge(0, 1, wq_u)
            + arrive(0, 3, wo_u)
            + merge(0, 3, wo_u)
            + arrive(0, 2, wq_u)
            + merge(0, 2, wq_u)
            + arrive(0, 3, wq_u)
            + merge(0, 3, wq_u),
        }
    else:
        back_points = {}

    def stat_done():
        totals = stat_ref[...]
        stat_out[...] = totals if not routed else jnp.sqrt(totals / (totals[0:1, 3:4, :] * width))

    if not routed:
        stat_done()

    def back_point(layer, point, s=None, at=None):
        for (at_layer, at_point), actions in back_points.items():
            if at_point == point:
                here = layer == at_layer
                if s is not None:
                    here = here & (s == at)

                @pl.when(here)
                def _(actions=actions):
                    for action in actions:
                        action()

    def norm_back(x, gain, grad):
        inv = lax.rsqrt(jnp.mean(x * x, axis=1, keepdims=True) + norm_eps)
        hat = x * inv
        scaled = grad * gain
        return inv * (scaled - hat * jnp.mean(scaled * hat, axis=1, keepdims=True))

    def add_gain(k, d_weight, weight):
        for p in range(d_weight.shape[1] // lanes):
            cols = slice(p * lanes, (p + 1) * lanes)
            gain_sums[k] += d_weight[:, cols] * weight[:, cols].astype(f32)

    def pack_small(layer):
        turned = dbias[...].T
        for h in range(heads):
            ext[pl.ds(h, slots, stride=heads), :] = jnp.broadcast_to(turned[:slots, h : h + 1], (slots, lanes))
        lane = lax.broadcasted_iota(jnp.int32, (width, lanes), 1)
        gain = mat(0, layer, slice(0, lanes)).astype(f32)
        sums = [jnp.sum(gain_sums[k], axis=1, keepdims=True) for k in range(2)]
        safe = jnp.where(lane < 2, gain, 1.0)
        value = jnp.where(lane == 0, sums[0], jnp.where(lane == 1, sums[1], 0.0)) / safe
        value = jnp.where(lane == 2, ext[...], value)
        put_mat(0, layer + 1, value.astype(bf16), slice(0, lanes))

    def backward_ffn(layer):
        slot = layer + 1

        @pl.loop(0, segs)
        def _(s):
            at = seg_rows(s)
            h = hbuf[layer, at, :].astype(f32)
            doa[0, at, :] = (h * lax.rsqrt(jnp.mean(h * h, axis=1, keepdims=True) + norm_eps) * gains[layer, 1]).astype(bf16)

        dn[...] = jnp.zeros_like(dn)
        gain_sums[...] = jnp.zeros_like(gain_sums)
        dbias[...] = jnp.zeros_like(dbias)

        @pl.loop(0, ff // chunk)
        def _(c):
            cols = pl.ds(pl.multiple_of(c * chunk, chunk), chunk)
            planes = pl.ds(c, 1)
            d_act = nt(dy[...], mat(3, layer, planes=planes))
            x = pre[:, cols].astype(f32)
            sq = x * x
            gate = 0.5 + 0.5 * jnp.tanh(x * (gelu_c + (gelu_c * gelu_k) * sq))
            act = x * gate
            slope = gate + act * (1.0 - gate) * (2.0 * gelu_c + (6.0 * gelu_c * gelu_k) * sq)
            d_pre = (d_act * slope).astype(bf16)
            pre[:, cols] = d_pre
            put_mat(3, slot, tn(act.astype(bf16), dy[...]).astype(bf16), planes=planes)
            d_up = tn(doa[0], d_pre)
            add_gain(1, d_up, mat(2, layer, cols))
            put_mat(2, slot, d_up.astype(bf16), cols)
            dn[...] += nt(d_pre, mat(2, layer, cols))
            for k in range(ff // chunk):
                back_point(layer, "ffn" + str(k), c, k)

    def backward_middle(layer, s):
        at = seg_rows(s)
        dh = norm_back(hbuf[layer, at, :].astype(f32), gains[layer, 1], dn[at, :])
        dh = dh + dy[at, :].astype(f32)
        dn[at, :] = dh
        dz = dh.astype(bf16)
        dy[at, :] = dz
        do = nt(dz, mat(1, layer)) * ilbuf[at, :].astype(f32)
        prod = do.astype(bf16).astype(f32) * obuf[at, :].astype(f32)
        for p in range(pairs):
            cols = slice(p * lanes, (p + 1) * lanes)
            for side in range(2):
                own, marks = lane_marks(head_size, side)
                delta = -jnp.sum(prod[:, cols] * own, axis=1, keepdims=True)
                hi = delta.astype(bf16).astype(f32)
                fill = hi * marks[0] + (delta - hi) * marks[1]
                doa[side, at, cols] = (do[:, cols] * (1.0 - marks[0] - marks[1]) + fill).astype(bf16)

    def backward_attention(layer, s):
        at = seg_rows(s)
        for p in range(pairs):
            cols = slice(p * lanes, (p + 1) * lanes)
            kcols = slice(width + p * lanes, width + (p + 1) * lanes)
            vcols = slice(2 * width + p * lanes, 2 * width + (p + 1) * lanes)
            qp = qkv[at, cols]
            kp = qkv[at, kcols]
            vp = qkv[at, vcols]
            q_turned = qp.T
            dq, dk, dv = [], [], []
            for side in range(2):
                h = 2 * p + side
                own, marks = lane_marks(head_size, side)
                do_h = doa[side, at, cols]
                va = vp * own.astype(bf16) + (marks[0] + marks[1]).astype(bf16)
                weights = ebuf[s, h]
                d_scores = weights.astype(f32) * nt(do_h, va)
                dbias[h : h + 1, :] += jnp.sum(d_scores[:, :lanes], axis=0, keepdims=True)
                d_scores = d_scores.astype(bf16)
                half = slice(side * head_size, (side + 1) * head_size)
                dq.append(mm(d_scores, kp))
                dk.append(mm(q_turned[half, :], d_scores))
                dv.append(mm(do_h.T[half, :], weights))
            own, _ = lane_marks(head_size, 0)
            qkv[at, cols] = (jnp.where(own > 0, dq[0], dq[1]) * score_scale).astype(bf16)
            qkv[at, kcols] = (jnp.concatenate(dk, axis=0).T * (1.0 / log2_e)).astype(bf16)
            qkv[at, vcols] = jnp.concatenate(dv, axis=0).T.astype(bf16)
            if p == pairs // 2 - 1:
                back_point(layer, "quad", s, 1)

    def backward_input(layer, s):
        at = seg_rows(s)
        x = ub[layer, at, :].astype(f32)
        du = norm_back(x, gains[layer, 0], nt(qkv[at, :], mat(0, layer, slice(lanes, lanes + 3 * width))))
        dy[at, :] = (du + dn[at, :]).astype(bf16)

    def grad_copies(layer):
        return [
            pltpu.make_async_copy(buf.at[layer + 1], out.at[layer], sem_g.at[layer, k])
            for k, (buf, out) in enumerate(zip(weight_buf, grads_out))
        ]

    @pl.loop(0, 2)
    def _(step):
        layer = 1 - step
        slot = layer + 1

        @pl.when(layer == 0)
        def _():
            for s in range(segs):
                for copy in spill_copies(s, True, (2, 3, 4)):
                    copy.wait()

        backward_ffn(layer)

        @pl.when(layer == 1)
        def _():
            for copies in y_copies:
                for copy in copies:
                    copy.wait()

        @pl.loop(0, segs)
        def _(s):
            backward_middle(layer, s)

        back_point(layer, "mid")
        put_mat(1, slot, tn(obuf[...], dy[...]).astype(bf16))
        back_point(layer, "wo")

        @pl.when(layer == 1)
        def _():
            for s in range(segs):
                for copy in spill_copies(s, True, (2, 3, 4)):
                    copy.start()

        @pl.loop(0, segs)
        def _(s):
            @pl.when(layer == 0)
            def _():
                for copy in spill_copies(s, True, (0, 1)):
                    copy.wait()

            backward_attention(layer, s)

            @pl.when(layer == 1)
            def _():
                spill_copies(s, True, (1,))[0].start()

            for k in range(segs):
                back_point(layer, "att" + str(k), s, k)

        @pl.loop(0, segs)
        def _(s):
            at = seg_rows(s)
            v = ub[layer, at, :].astype(f32)
            doa[0, at, :] = (v * lax.rsqrt(jnp.mean(v * v, axis=1, keepdims=True) + norm_eps) * gains[layer, 0]).astype(bf16)

        for k in range(3):
            cols = slice(k * width, (k + 1) * width)
            d_weight = tn(doa[0], qkv[:, cols])
            add_gain(0, d_weight, mat(0, layer, qkv_cols(k)))
            put_mat(0, slot, d_weight.astype(bf16), qkv_cols(k))
        pack_small(layer)
        back_point(layer, "wq")

        @pl.loop(0, segs)
        def _(s):
            backward_input(layer, s)
            for k in range(segs):
                back_point(layer, "in" + str(k), s, k)

        @pl.when(layer == 1)
        def _():
            for s in range(segs):
                spill_copies(s, True, (0,))[0].start()

        if not routed:
            for copy in grad_copies(layer):
                copy.start()
            for copy in grad_copies(layer):
                copy.wait()

    for copies in du_copies:
        for copy in copies:
            copy.start()
    back_point(0, "end")
    if routed:
        for layer in (1, 0):
            for u in range(4):
                rs_finish(layer, u)
    for copies in du_copies:
        for copy in copies:
            copy.wait()


def run_layers(dims, routed, doc_len, row_args, weights):
    segs, rows, width, ff, slots, heads = dims
    all_rows = segs * rows
    vmem = pl.BlockSpec(memory_space=pltpu.VMEM)
    smem = pl.BlockSpec(memory_space=pltpu.SMEM)
    hbm = pl.BlockSpec(memory_space=pl.ANY)
    shape = jax.ShapeDtypeStruct
    dma = pltpu.SemaphoreType.DMA
    wide = (all_rows, width)
    tiles = [
        (width // 32, lanes + 3 * width),
        (width // 32, width),
        (width // 32, ff),
        (ff // 32, width),
    ]
    out_shape = [shape(part.shape, bf16) for part in row_args]
    if routed:
        out_shape += [shape((2, *tile), f32) for tile in tiles]
    else:
        out_shape += [shape((2, 4, 2, 2, 2, *tile), bf16) for tile in tiles]
    row_outs = len(out_shape)
    out_shape += [shape((2, 8, lanes), f32)]
    out_shape += [
        shape((all_rows, 3 * width), bf16),
        shape((segs, heads, rows, rows), bf16),
        shape(wide, bf16),
        shape(wide, bf16),
        shape((all_rows, ff), bf16),
    ]
    if routed:
        for tile in tiles:
            out_shape += [shape((2, *lead, *tile), bf16) for lead in ((4, 2, 2), (4, 2), (4,), (3,))]
    unit_count = 16
    scratch = [pltpu.VMEM((3, 4, 2, 2, 2, *tile), bf16) for tile in tiles]
    scratch += [
        pltpu.VMEM((2, *wide), bf16),
        pltpu.VMEM(wide, bf16),
        pltpu.VMEM((all_rows, 3 * width), bf16),
        pltpu.VMEM((segs, heads, rows, rows), bf16),
        pltpu.VMEM(wide, bf16),
        pltpu.VMEM(wide, bf16),
        pltpu.VMEM((2, *wide), bf16),
        pltpu.VMEM((all_rows, ff), bf16),
        pltpu.VMEM((2, *wide), bf16),
        pltpu.VMEM(wide, f32),
        pltpu.VMEM((2, 2, 1, width), f32),
        pltpu.VMEM((2, heads, slots, lanes), f32),
        pltpu.VMEM((width, lanes), f32),
        pltpu.VMEM((2, width, lanes), f32),
        pltpu.VMEM((heads, lanes), f32),
        pltpu.VMEM((2, 8, lanes), f32),
        dma((segs, 5)),
        dma((segs, 5)),
        dma((2, 4)),
        dma((8 * segs,)),
        dma((unit_count,)),
        dma((unit_count, 11)),
        dma((unit_count, 11)),
    ]
    params = dict(vmem_limit_bytes=63 * 2**20)
    if routed:
        params.update(collective_id=0, has_side_effects=True)
        scratch += [pltpu.VMEM((4, 2, 2, *tile), bf16) for tile in tiles]
        scratch += [pltpu.VMEM((2, *tile), f32) for tile in tiles]
        scratch += [
            pltpu.VMEM((4, 2, 8, lanes), f32),
            pltpu.VMEM((7, 2, 8, lanes), f32),
            dma((4,)),
            dma((2, 4, 7)),
            dma((2, 4, 7)),
            dma((8 * segs,)),
            dma((8 * segs,)),
            dma((6,)),
            dma((6,)),
        ]
    return pl.pallas_call(
        partial(fused_layers, dims, routed),
        out_shape=out_shape,
        in_specs=[smem] + [hbm] * (len(row_args) + 4),
        out_specs=[hbm] * row_outs + [vmem] + [hbm] * (len(out_shape) - row_outs - 1),
        scratch_shapes=scratch,
        compiler_params=pltpu.CompilerParams(**params),
    )(doc_len, *row_args, *weights)[: row_outs + 1]


def swap(block):
    return lax.ppermute(block, "section", [(0, 1), (1, 0)])


def body(
    tokens,
    memory,
    lengths,
    w_qkv,
    w_out,
    w_up,
    w_down,
    gain_attn,
    gain_ffn,
    forget_bias,
    grad_tokens,
    grad_memory,
):
    section = lax.axis_index("section")
    is_first = section == 0
    micro = tokens.shape[0]
    segs = micro // 2
    half_tok = tokens.shape[1]
    half_mem = memory.shape[1]
    slots = 2 * half_mem
    rows = slots + 2 * half_tok
    width = tokens.shape[2]
    ff = w_up.shape[2]
    heads = forget_bias.shape[1] * lax.axis_size("dp") // slots
    per_doc = micro // lengths.shape[0]
    dims = (segs, rows, width, ff, slots, heads)
    own_len = lax.dynamic_slice_in_dim(lengths, section * segs // per_doc, 1, 0)
    small = jnp.stack([gain_attn, gain_ffn, forget_bias], axis=2)
    small = jnp.pad(small, ((0, 0), (0, 0), (0, lanes - 3)))
    pieces = (jnp.concatenate([small, w_qkv], axis=2), w_out, w_up, w_down)

    def unpack(grads):
        grad_q = grads[0]
        return (grad_q[:, :, lanes:], *grads[1:], *(grad_q[:, :, k] for k in range(3)))

    if lax.axis_size("dp") == 16 and w_qkv.shape[1] == 32:
        weights = [piece.reshape(2, -1, piece.shape[2]) for piece in pieces]
        *outs, rms = run_layers(dims, True, own_len, (tokens, memory, grad_tokens, grad_memory), weights)
        grads = [grad.reshape(1, -1, grad.shape[2]) for grad in outs[4:]]
        return (*outs[:4], *unpack(grads), rms[:, :3, 0])

    def own_segs(halves):
        return lax.dynamic_slice_in_dim(halves, section * segs, segs, 0)

    def other_segs(halves):
        return lax.dynamic_slice_in_dim(halves, (1 - section) * segs, segs, 0)

    def both(kept, got):
        return jnp.concatenate(
            [jnp.where(is_first, kept, got), jnp.where(is_first, got, kept)], axis=1
        )

    inputs = (tokens, memory, grad_tokens, grad_memory)
    got = swap(tuple(other_segs(part) for part in inputs))
    full = [both(own_segs(part), other) for part, other in zip(inputs, got)]
    u0 = jnp.concatenate([full[1], full[0]], axis=1).reshape(segs * rows, width)
    dout = jnp.concatenate([full[3], full[2]], axis=1).reshape(segs * rows, width)

    def gather(piece):
        whole = lax.all_gather(piece, ("section", "dp"), axis=1, tiled=True)
        return whole.reshape(2, 4, 2, 2, 2, -1, piece.shape[2])

    y, du, *grads, stats = run_layers(dims, False, own_len, (u0, dout), [gather(piece) for piece in pieces])

    def scatter(grad):
        grad = grad.reshape(2, -1, grad.shape[-1])
        mine = lax.dynamic_index_in_dim(grad, section, 0, keepdims=True)
        other = lax.dynamic_index_in_dim(grad, 1 - section, 0, keepdims=True)
        chip = (mine.astype(f32) + swap(other).astype(f32)).astype(grad.dtype)
        return lax.psum_scatter(chip, "dp", scatter_dimension=1, tiled=True).astype(f32)

    shares = unpack([scatter(grad) for grad in grads])
    totals = lax.psum(stats[:, :4, 0], ("section", "dp"))
    rms = jnp.sqrt(totals[:, :3] / (totals[0, 3] * width))
    result = jnp.stack([y.reshape(segs, rows, width), du.reshape(segs, rows, width)])

    def half_of(which):
        tok = lax.dynamic_slice_in_dim(result, slots + which * half_tok, half_tok, 2)
        mem = lax.dynamic_slice_in_dim(result, which * half_mem, half_mem, 2)
        return tok, mem

    kept = half_of(section)
    got = swap(half_of(1 - section))

    def order(mine, other):
        return jnp.concatenate(
            [jnp.where(is_first, mine, other), jnp.where(is_first, other, mine)], axis=0
        )

    toks = [order(kept[0][k], got[0][k]) for k in range(2)]
    mems = [order(kept[1][k], got[1][k]) for k in range(2)]
    return (toks[0], mems[0], toks[1], mems[1], *shares, rms)


def solution(mesh):
    rows = P("dp", "section", None)
    mats = P("section", "dp", None)
    vecs = P("section", "dp")
    return jax.shard_map(
        body,
        mesh=mesh,
        in_specs=(rows, rows, P("dp"), mats, mats, mats, mats, vecs, vecs, vecs, rows, rows),
        out_specs=(rows, rows, rows, rows, mats, mats, mats, mats, vecs, vecs, vecs, P()),
        check_vma=False,
    )
```

```python
from functools import partial

import jax
import jax.numpy as jnp
from jax import lax
from jax.experimental import pallas as pl
from jax.experimental.pallas import tpu as pltpu
from jax.sharding import PartitionSpec as P

norm_eps = 1e-06
score_scale = 0.125
log2_e = 1.4426950408889634
masked_score = -1000000000.0
gelu_c = 0.7978845608028654
gelu_k = 0.044715
f32 = jnp.float32
bf16 = jnp.bfloat16
lanes = 128
chunk = 512


def mm(a, b, ca=1, cb=0):
    return lax.dot_general(a, b, (((ca,), (cb,)), ((), ())), preferred_element_type=f32)


def nt(a, b):
    return mm(a, b, 1, 1)


def tn(a, b):
    return mm(a, b, 0, 0)


def lane_marks(head_size, side):
    lane = lax.broadcasted_iota(jnp.int32, (1, lanes), 1)
    own = ((lane // head_size) == side).astype(f32)
    first = (1 - side) * head_size
    marks = [(lane == first + k).astype(f32) for k in range(3)]
    return own, marks


def fused_layers(dims, routed, *refs):
    segs, rows, width, ff, slots, heads, per_doc = dims
    refs = list(refs)

    def take(count):
        picked = refs[:count]
        del refs[:count]
        return picked

    (len_ref,) = take(1)
    rows_in = take(4 if routed else 2)
    weight_in = take(5 if routed else 4)
    rows_out = take(4 if routed else 2)
    grads_out = take(5 if routed else 4)
    (stat_out,) = take(1)
    spill_hbm = take(8)
    weight_buf = take(4)
    ub, dy, qkv, ebuf, obuf, ilbuf, hbuf, slope, active, doa, dn = take(11)
    gains, bias_rows, ext, gain_sums, dbias, stat_ref = take(6)
    sem_spill, sem_back, sem_g, sem_io, sem_own, sem_send, sem_recv = take(7)
    if routed:
        lands = [take(4) for _ in range(5)]
        fin = take(5)
        stat_sum, stat_land = take(2)
        rs_send, rs_recv, rs_free, io_send, io_recv, stat_send, stat_recv = take(7)
    head_size = width // heads
    pairs = width // lanes
    tok_rows = rows - slots
    quads = width // (2 * lanes)
    quad = 2 * lanes
    first_doc = lax.axis_index("section") * segs // per_doc if routed else 0
    every = slice(None)

    def units_of(layer):
        half_ff, half_deep = ff // 2, ff // 64
        lead = [
            (0, slice(0, lanes + width), every),
            (0, slice(lanes + width, lanes + 2 * width), every),
            (0, slice(lanes + 2 * width, lanes + 3 * width), every),
        ]
        rest = [(1, every, every)]
        rest += [(3, every, slice(k * half_deep, (k + 1) * half_deep)) for k in range(2)]
        rest += [(2, slice(k * half_ff, (k + 1) * half_ff), every) for k in range(2)]
        return [(layer, *unit) for unit in lead + rest]

    units = units_of(0) + units_of(1)
    first_units = [k for k, unit in enumerate(units) if unit[1] == 0]
    last_units = [7, 15]
    later_units = [k for k, unit in enumerate(units) if unit[1] != 0 and k not in last_units]
    plane_first = (11, 15)

    def view(n, z, y, x, c):
        layer, which, cols, part = units[n]
        return weight_buf[which].at[layer, z, y, x, c, part, cols]

    if routed:
        core = lax.axis_index("section")
        chip = lax.axis_index("dp")
        z, y, x = chip // 4, (chip // 2) % 2, chip % 2
        other = 1 - core

        def place(pz, py, px):
            return pz * 4 + py * 2 + px

        mate = (other, chip)
        near_x = (core, place(z, y, 1 - x))
        near_y = (core, place(z, 1 - y, x))
        along_z = [(core, place((z + k) % 4, y, x)) for k in range(1, 4)]

        def remote(src, dst, n, k, target):
            return pltpu.make_async_remote_copy(
                src_ref=src,
                dst_ref=dst,
                send_sem=sem_send.at[n, k],
                recv_sem=sem_recv.at[n, k],
                device_id=target,
                device_id_type=pl.DeviceIdType.MESH,
            )

        def own_shards(n):
            layer, which, cols, part = units[n]
            home = weight_buf[which].at[layer, z, y, x]
            if which > 0:
                return [(weight_in[which].at[every, part, cols], home.at[every, part, cols], 0)]
            start = max(cols.start - lanes, 0)
            matrix = slice(start, cols.stop - lanes)
            pairs_of = [(weight_in[0].at[every, every, matrix], home.at[every, every, slice(start + lanes, cols.stop)], 0)]
            if cols.start == 0:
                pairs_of.append((weight_in[4], home.at[every, every, slice(0, lanes)], 11))
            return pairs_of

        def z_copy(n, k):
            where = view(n, z, every, every, core) if n in plane_first else view(n, z, y, x, core)
            return remote(where, where, n, k, along_z[k - 1])

        def plane_copy(n, k, x_first):
            planes = z if n in plane_first else every
            if k == 4:
                where = view(n, planes, y, x, core)
                return remote(where, where, n, 4, near_x if x_first else near_y)
            where = view(n, planes, y, every, core) if x_first else view(n, planes, every, x, core)
            return remote(where, where, n, 5, near_y if x_first else near_x)

        def mate_copy(n, k, x_first, half):
            planes = z if n in plane_first else every
            if k < 9:
                from_z = (z + 4 - (k - 5)) % 4
                where = view(n, from_z, every, every, half) if n in plane_first else view(n, from_z, y, x, half)
            elif k == 9:
                where = view(n, planes, y, 1 - x, half) if x_first else view(n, planes, 1 - y, x, half)
            else:
                where = view(n, planes, 1 - y, every, half) if x_first else view(n, planes, every, 1 - x, half)
            return remote(where, where, n, k, mate)

        def by_route(n, act):
            for side in range(2):
                @pl.when(core == side)
                def _(side=side):
                    act((side + n) % 2 == 0)

        def share_own(n):
            @pl.when(core == units[n][0])
            def _():
                for i, (src, dst, k) in enumerate(own_shards(n)):
                    pltpu.make_async_copy(src, dst, sem_own.at[n, i]).start()
                    remote(src, dst, n, k, mate).start()

        def start_z(n):
            @pl.when(core == units[n][0])
            def _():
                for i, (src, dst, k) in enumerate(own_shards(n)):
                    pltpu.make_async_copy(src, dst, sem_own.at[n, i]).wait()

            @pl.when(core != units[n][0])
            def _():
                for src, dst, k in own_shards(n):
                    remote(src, dst, n, k, mate).wait_recv()

            if n in plane_first:
                by_route(n, lambda x_first: plane_copy(n, 4, x_first).start())
            else:
                for k in range(1, 4):
                    z_copy(n, k).start()

        def first_hop(n):
            if n not in plane_first:
                for k in range(1, 4):
                    z_copy(n, k).wait_recv()

            def act(x_first):
                if n in plane_first:
                    plane_copy(n, 4, x_first).wait_recv()
                    plane_copy(n, 5, x_first).start()
                    mate_copy(n, 9, x_first, core).start()
                else:
                    plane_copy(n, 4, x_first).start()
                    for k in range(6, 9):
                        mate_copy(n, k, x_first, core).start()

            by_route(n, act)

        def second_hop(n):
            def act(x_first):
                if n in plane_first:
                    plane_copy(n, 5, x_first).wait_recv()
                    for k in range(1, 4):
                        z_copy(n, k).start()
                    mate_copy(n, 10, x_first, core).start()
                else:
                    plane_copy(n, 4, x_first).wait_recv()
                    plane_copy(n, 5, x_first).start()
                    mate_copy(n, 9, x_first, core).start()

            by_route(n, act)

        def last_share(n):
            def act(x_first):
                if n in plane_first:
                    for k in range(1, 4):
                        z_copy(n, k).wait_recv()
                        mate_copy(n, 5 + k, x_first, core).start()
                else:
                    plane_copy(n, 5, x_first).wait_recv()
                    mate_copy(n, 10, x_first, core).start()

            by_route(n, act)

        def complete(n):
            def act(x_first):
                for k in range(6, 11):
                    mate_copy(n, k, not x_first, other).wait_recv()

            by_route(n, act)

        def drain(n):
            @pl.when(core == units[n][0])
            def _():
                for src, dst, k in own_shards(n):
                    remote(src, dst, n, k, mate).wait_send()

            for k in range(1, 4):
                z_copy(n, k).wait_send()

            def act(x_first):
                for k in (4, 5):
                    plane_copy(n, k, x_first).wait_send()
                for k in range(6, 11):
                    mate_copy(n, k, x_first, core).wait_send()

            by_route(n, act)

        def hops(text):
            kinds = dict(z=start_z, f=first_hop, s=second_hop, l=last_share)
            for word in text.split():
                kinds[word[0]](int(word[1:]))

        opening = "z0 z1 z2 z3 z4 z5 f0 f1 s0 z6 f2 s1 z7 f3 s2 l0 f4 s3 l1 f5 s4 f6 l2"
        hops_at = {
            (0, 0, "qkv"): "s5 f7 z8 z9 z11 z15", (0, 0, "quad0"): "s6 z10 z12", (0, 0, "quad1"): "f8 z13 f11",
            (0, 1, "qkv"): "s7 f9", (0, 1, "quad0"): "s8 f10 z14 f15", (0, 1, "quad1"): "s9 s11",
            (0, 0, "gate"): "l3 l4 l5 l6 f12", (0, 0, "ffna"): "s10 f13", (0, 1, "ffna"): "s12 s15",
            (0, 0, "last"): "l7", (0, 0, "ffnb"): "s13 f14 l8", (0, 1, "ffnb"): "l9 l10",
            (1, 0, "qkv"): "s14",
            (1, 0, "gate"): "l11 l12 l13 l14", (1, 0, "last"): "l15",
        }
    else:
        hops_at = {}

        def weight_copy(n):
            layer, which, cols, part = units[n]
            src = weight_in[which].at[layer, every, every, every, every, part, cols]
            return pltpu.make_async_copy(src, view(n, every, every, every, every), sem_own.at[n, 0])

        def complete(n):
            weight_copy(n).wait()

    def after(layer, s, point):
        for (at_layer, at_s, at_point), text in hops_at.items():
            if at_point == point:
                @pl.when((layer == at_layer) & (s == at_s))
                def _(text=text):
                    hops(text)

    def need(layer, picks):
        for at_layer in range(2):
            @pl.when(layer == at_layer)
            def _(at_layer=at_layer):
                for n in picks:
                    if units[n][0] == at_layer:
                        complete(n)

    def mat(which, slot, cols=every, planes=None):
        if planes is None:
            value = weight_buf[which][slot, :, :, :, :, :, cols]
        else:
            value = weight_buf[which][slot, planes, :, :, :, :, cols]
        deep = 1
        for size in value.shape[:-1]:
            deep *= size
        return value.reshape(deep, value.shape[-1])

    def put_mat(which, slot, value, cols=every, planes=None):
        buf = weight_buf[which]
        shape = buf.shape[1:-1]
        if planes is None:
            buf[slot, :, :, :, :, :, cols] = value.reshape(*shape, value.shape[-1])
        else:
            buf[slot, planes] = value.reshape(1, *shape[1:], value.shape[-1])

    def qkv_cols(k):
        return slice(lanes + k * width, lanes + (k + 1) * width)

    def seg_rows(s):
        return pl.ds(pl.multiple_of(s * rows, rows), rows)

    def spill_copies(s, back, picks=range(7)):
        at = seg_rows(s)
        kept = (qkv.at[at], ebuf.at[s], obuf.at[at], ilbuf.at[at], slope.at[at], active.at[at], hbuf.at[at], ub.at[at])
        pairs_of = [
            (vmem, hbm.at[s] if k == 1 else hbm.at[at])
            for k, (vmem, hbm) in enumerate(zip(kept, spill_hbm))
        ]
        if back:
            return [
                pltpu.make_async_copy(hbm, vmem, sem_back.at[s, k])
                for k, (vmem, hbm) in enumerate(pairs_of)
                if k in picks
            ]
        return [
            pltpu.make_async_copy(vmem, hbm, sem_spill.at[s, k])
            for k, (vmem, hbm) in enumerate(pairs_of)
            if k in picks
        ]

    def doc_end(s):
        return len_ref[first_doc + s // per_doc] - (s % per_doc) * tok_rows

    def valid_col(s):
        row = lax.broadcasted_iota(jnp.int32, (rows, 1), 0)
        return jnp.where(
            (row >= slots) & (row - slots < doc_end(s)), 1.0, 0.0
        ).astype(f32)

    def mask_col(s):
        row = lax.broadcasted_iota(jnp.int32, (rows, 1), 0)
        return jnp.where(
            (row >= slots) & (row - slots >= doc_end(s)), masked_score, 0.0
        ).astype(f32)

    if routed:
        half_tok, half_mem = tok_rows // 2, slots // 2

        def io_copies(buf, tok_ref, mem_ref, first, outward):
            local, away = [], []
            k = first
            for s in range(segs):
                mine, theirs = core * segs + s, other * segs + s
                for ref, base, size in ((tok_ref, slots, half_tok), (mem_ref, 0, half_mem)):
                    def rows_of(half):
                        return buf.at[pl.ds(pl.multiple_of(s * rows + base + half * size, 16), size)]

                    if outward:
                        local.append(pltpu.make_async_copy(rows_of(core), ref.at[mine], sem_io.at[k]))
                        src, dst = rows_of(other), ref.at[mine]
                    else:
                        local.append(pltpu.make_async_copy(ref.at[mine], rows_of(core), sem_io.at[k]))
                        src, dst = ref.at[theirs], rows_of(core)
                    away.append(
                        pltpu.make_async_remote_copy(
                            src_ref=src,
                            dst_ref=dst,
                            send_sem=io_send.at[k],
                            recv_sem=io_recv.at[k],
                            device_id=mate,
                            device_id_type=pl.DeviceIdType.MESH,
                        )
                    )
                    k += 1
            return local, away

        loads, shares = io_copies(ub, rows_in[0], rows_in[1], 0, False)
        more = io_copies(dy, rows_in[2], rows_in[3], 2 * segs, False)
        loads, shares = loads + more[0], shares + more[1]
        y_copies = io_copies(doa.at[1], rows_out[0], rows_out[1], 4 * segs, True)
        du_copies = io_copies(dy, rows_out[2], rows_out[3], 6 * segs, True)
    else:
        loads = [
            pltpu.make_async_copy(rows_in[0], ub, sem_io.at[0]),
            pltpu.make_async_copy(rows_in[1], dy, sem_io.at[1]),
        ]
        shares = []
        y_copies = [pltpu.make_async_copy(doa.at[1], rows_out[0], sem_io.at[2])], []
        du_copies = [pltpu.make_async_copy(dy, rows_out[1], sem_io.at[3])], []
    for copy in loads:
        copy.start()
    if routed:
        barrier = pltpu.get_barrier_semaphore()
        peers = [mate, near_x, near_y, (core, place(z, 1 - y, 1 - x)), *along_z]
        peers += [(other, place((z + k) % 4, y, x)) for k in range(1, 4)]
        for peer in peers:
            pl.semaphore_signal(barrier, inc=1, device_id=peer, device_id_type=pl.DeviceIdType.MESH)
        pl.semaphore_wait(barrier, len(peers))
        for n in range(8):
            share_own(n)
        for copy in shares:
            copy.start()
        for n in range(8, len(units)):
            share_own(n)
        hops(opening)
    else:
        for n in range(len(units)):
            weight_copy(n).start()
    stat_ref[...] = jnp.zeros_like(stat_ref)

    for copy in loads:
        copy.wait()
    for copy in shares:
        copy.wait()

    def add_stat(layer, k, row_sums, valid):
        total = jnp.sum(row_sums * valid, axis=0, keepdims=True)
        stat_ref[layer, k : k + 1, :] += jnp.broadcast_to(total, (1, lanes))

    def forward_attention(layer, s):
        at = seg_rows(s)
        mask = mask_col(s)
        for p in range(pairs):
            cols = slice(p * lanes, (p + 1) * lanes)
            qp = qkv[at, cols]
            kp = qkv[at, slice(width + p * lanes, width + (p + 1) * lanes)]
            vp = qkv[at, slice(2 * width + p * lanes, 2 * width + (p + 1) * lanes)]
            outs = []
            for side in range(2):
                h = 2 * p + side
                own, marks = lane_marks(head_size, side)
                bias = bias_rows[h]
                hi = bias.astype(bf16).astype(f32)
                aux = jnp.concatenate([hi * marks[1] + (bias - hi) * marks[2], jnp.zeros((tok_rows, lanes), f32)], axis=0)
                aux = aux + mask * marks[0]
                extra = marks[0] + marks[1] + marks[2]
                ka = kp * own.astype(bf16) + aux.astype(bf16)
                qa = qp * (1.0 - extra).astype(bf16) + extra.astype(bf16)
                scores = nt(qa, ka)
                top = jnp.max(scores, axis=1, keepdims=True)
                weights = jnp.exp2(scores - top).astype(bf16)
                ebuf[s, h] = weights
                va = vp * own.astype(bf16) + (1.0 - own).astype(bf16)
                outs.append(mm(weights, va))
            own, _ = lane_marks(head_size, 0)
            raw = jnp.where(own > 0, outs[0], outs[1])
            sums = pltpu.roll(jnp.where(own > 0, outs[1], outs[0]), head_size, 1)
            inv = 1.0 / sums
            ilbuf[at, cols] = inv.astype(ilbuf.dtype)
            obuf[at, cols] = (raw * inv).astype(bf16)
            if p % 2 == 1:
                after(layer, s, "quad" + str(p // 2))

    def unpack_small(layer):
        ext[...] = mat(0, layer, slice(0, lanes)).astype(f32)
        turned = ext[...].T
        for k in range(2):
            gains[layer, k] = turned[k : k + 1, :]
        for h in range(heads):
            column = ext[pl.ds(h, slots, stride=heads), :][:, 2:3]
            bias_rows[h] = jnp.broadcast_to(column * log2_e, (slots, lanes))

    def forward_attn(layer, s):
        at = seg_rows(s)

        @pl.when(layer == 1)
        def _():
            for copy in spill_copies(s, False):
                copy.wait()

        @pl.when(layer == 0)
        def _():
            spill_copies(s, False, (7,))[0].start()

        valid = valid_col(s)
        x = ub[at, :].astype(f32)
        squares = jnp.sum(x * x, axis=1, keepdims=True)
        add_stat(layer, 0, squares, valid)
        add_stat(layer, 3, valid, valid)
        n1 = (x * lax.rsqrt(squares / width + norm_eps) * gains[layer, 0]).astype(bf16)
        for k in range(3):
            part = mm(n1, mat(0, layer, qkv_cols(k)))
            if k == 0:
                part = part * (score_scale * log2_e)
            qkv[at, k * width : (k + 1) * width] = part.astype(bf16)
        after(layer, s, "qkv")
        forward_attention(layer, s)

        @pl.when(layer == 0)
        def _():
            for copy in spill_copies(s, False, range(4)):
                copy.start()

    def ffn_part(s, layer, picks):
        at = seg_rows(s)

        def up(c):
            return mm(doa[0, at, :], mat(2, layer, slice(c * chunk, (c + 1) * chunk)))

        before = up(picks[0])
        for c in picks:
            cols = slice(c * chunk, (c + 1) * chunk)
            following = up(c + 1) if c + 1 in picks else None
            square = before * before
            gate = 0.5 + 0.5 * jnp.tanh(before * (gelu_c + (gelu_c * gelu_k) * square))
            act = before * gate
            slope[at, cols] = (gate + act * (1.0 - gate) * (2.0 * gelu_c + (6.0 * gelu_c * gelu_k) * square)).astype(bf16)
            act = act.astype(bf16)
            active[at, cols] = act
            part = mm(act, mat(3, layer, planes=slice(c, c + 1)))
            if c == 0:
                dn[at, :] = part
            else:
                dn[at, :] += part
            before = following

    def forward_ffn_a(layer, s):
        at = seg_rows(s)
        valid = valid_col(s)
        z = mm(obuf[at, :], mat(1, layer))
        add_stat(layer, 1, jnp.sum(z * z, axis=1, keepdims=True), valid)
        h = ub[at, :].astype(f32) + z
        hbuf[at, :] = h.astype(bf16)
        doa[0, at, :] = (h * lax.rsqrt(jnp.mean(h * h, axis=1, keepdims=True) + norm_eps) * gains[layer, 1]).astype(bf16)
        ffn_part(s, layer, range(ff // chunk // 2))
        after(layer, s, "ffna")

    def forward_ffn_b(layer, s):
        at = seg_rows(s)
        valid = valid_col(s)
        ffn_part(s, layer, range(ff // chunk // 2, ff // chunk))
        out = dn[at, :]
        add_stat(layer, 2, jnp.sum(out * out, axis=1, keepdims=True), valid)
        z = mm(obuf[at, :], mat(1, layer))
        result = (ub[at, :].astype(f32) + z + out).astype(bf16)

        @pl.when(layer == 0)
        def _():
            spill_copies(s, False, (7,))[0].wait()
            ub[at, :] = result

        @pl.when(layer == 1)
        def _():
            doa[1, at, :] = result

        @pl.when(layer == 0)
        def _():
            for copy in spill_copies(s, False, (4, 5, 6)):
                copy.start()

        after(layer, s, "ffnb")

    @pl.loop(0, 2)
    def _(layer):
        after(layer, 0, "open")
        need(layer, first_units)
        unpack_small(layer)

        @pl.loop(0, segs)
        def _(s):
            forward_attn(layer, s)

        after(layer, 0, "gate")
        need(layer, later_units)

        @pl.loop(0, segs)
        def _(s):
            forward_ffn_a(layer, s)

        after(layer, 0, "last")
        need(layer, last_units)

        @pl.loop(0, segs)
        def _(s):
            forward_ffn_b(layer, s)

    if routed:
        for n in range(len(units)):
            drain(n)
    for copies in y_copies:
        for copy in copies:
            copy.start()

    if routed:
        wqa_u, wo_u, wu_u, wd_u, wqb_u = range(5)
        half_cols = quads * 3 * lanes
        rs_cols = {wqa_u: slice(0, half_cols), wqb_u: slice(half_cols, 2 * half_cols + lanes)}
        rs_weight = (0, 1, 2, 3, 0)
        chunked = (wu_u, wd_u)
        fast = (wqa_u, wqb_u)
        plane_peers = [near_x, near_y, (core, place(z, 1 - y, 1 - x))]
        plane_spots = [(y, 1 - x), (1 - y, x), (1 - y, 1 - x)]
        chunks = ff // chunk

        def rs_copy(src, dst, layer, u, k, target):
            return pltpu.make_async_remote_copy(
                src_ref=src,
                dst_ref=dst,
                send_sem=rs_send.at[layer, u, k],
                recv_sem=rs_recv.at[layer, u, k],
                device_id=target,
                device_id_type=pl.DeviceIdType.MESH,
            )

        def chunk_cols(c):
            return slice(c * chunk, (c + 1) * chunk)

        def spot(layer, u, pz, py, px, c, piece=None):
            cols = rs_cols.get(u, every)
            if piece is not None and u == wd_u:
                pz = piece
            elif piece is not None:
                cols = chunk_cols(piece)
            return weight_buf[rs_weight[u]].at[layer + 1, pz, py, px, c, every, cols]

        def land_at(u, step, piece=None):
            ref = lands[u][step]
            if piece is None:
                return ref
            if u == wd_u:
                return ref.at[piece % 2 if step == 0 else piece]
            if step == 0:
                return ref.at[every, every, every, every, chunk_cols(piece % 2)]
            return ref.at[every, every, every, chunk_cols(piece)]

        def rs_copies(layer, u, step, y_first, piece=None):
            if step == 0:
                src = spot(layer, u, every, every, every, other, piece)
                return [rs_copy(src, land_at(u, 0, piece), layer, u, piece or 0, mate)]
            if step == 1 and u in fast:
                return [
                    rs_copy(spot(layer, u, every, *plane_spots[k], core), lands[u][1].at[k], layer, u, 4 + k, plane_peers[k])
                    for k in range(3)
                ]
            if step == 3 and u in fast:
                return [owner_copy(layer, u, k) for k in range(4)]
            if step == 1:
                at = (every, 1 - y, every) if y_first else (every, every, 1 - x)
                src = spot(layer, u, *at, core, piece)
                return [rs_copy(src, land_at(u, 1, piece), layer, u, 4 + (piece or 0), near_y if y_first else near_x)]
            if step == 2:
                at = (every, y, 1 - x) if y_first else (every, 1 - y, x)
                return [rs_copy(spot(layer, u, *at, core), lands[u][2], layer, u, 8, near_x if y_first else near_y)]
            if step == 3:
                return [
                    rs_copy(spot(layer, u, (z + k) % 4, y, x, core), lands[u][3].at[k - 1], layer, u, 8 + k, along_z[k - 1])
                    for k in range(1, 4)
                ]
            return [rs_copy(src, dst, layer, u, 12 + k, mate) for k, (src, dst) in enumerate(home_parts(layer, u))]

        def owner_copy(layer, u, k, half=None):
            away = (z + k + 1) % 4 if k < 3 else z
            half = core if half is None else half
            return pltpu.make_async_remote_copy(
                src_ref=spot(layer, u, away, y, x, core),
                dst_ref=lands[u][3].at[half, k],
                send_sem=rs_send.at[layer, u, 9 + k],
                recv_sem=rs_recv.at[layer, u, 9 + 4 * half + k],
                device_id=(layer, place(away, y, x)),
                device_id_type=pl.DeviceIdType.MESH,
            )

        def start_owner(layer, u):
            for k in range(3):
                owner_copy(layer, u, k).start()

            @pl.when(core != layer)
            def _():
                owner_copy(layer, u, 3).start()

        def merge_owner(layer, u):
            @pl.when(core == layer)
            def _():
                for k in range(3):
                    owner_copy(layer, u, k, layer).wait_recv()
                for k in range(4):
                    owner_copy(layer, u, k, 1 - layer).wait_recv()
                got = lands[u][3]
                cols = rs_cols[u]
                for half in range(2):
                    if half == layer:
                        total = weight_buf[0][layer + 1, z, y, x, half, :, cols].astype(f32)
                    else:
                        total = got[half, 3].astype(f32)
                    for k in range(3):
                        total = total + got[half, k].astype(f32)
                    if u == wqb_u:
                        small = total[:, :lanes].T
                        turned = jnp.concatenate([small[:8, :], jnp.zeros((8, lanes - small.shape[1]), f32)], axis=1)
                        fin[u][half, 0:8, 0:lanes] = turned
                        fin[u][half, :, lanes:] = total[:, lanes:]
                    else:
                        fin[u][half] = total
                for k, (src, dst) in enumerate(home_parts(layer, u)):
                    pltpu.make_async_copy(src, dst, sem_g.at[layer, u, k]).start()

        def home_parts(layer, u):
            if u not in rs_cols:
                return [(fin[u], grads_out[u].at[core])]
            base, q = (0, 0) if u == wqa_u else (lanes, 1)
            parts = [
                (
                    fin[u].at[:, :, base + k * quad : base + (k + 1) * quad],
                    grads_out[0].at[:, :, k * width + q * quad : k * width + (q + 1) * quad],
                )
                for k in range(3)
            ]
            if u == wqb_u:
                parts.append((fin[u].at[:, 0:8, 0:lanes], grads_out[4]))
            return parts

        def rs_route(u, act):
            for side in range(2):
                @pl.when(core == side)
                def _(side=side):
                    act((side + u) % 2 == 0)

        def on_route(u, step, act):
            if step in (1, 2):
                rs_route(u, act)
            else:
                act(True)

        def rs_pieces(u, step):
            return list(range(chunks)) if u in chunked and step < 2 else [None]

        def rs_start(layer, u, step, piece=None):
            if step == 3 and u in fast:
                start_owner(layer, u)
                return
            used = layer == 0 and not piece
            if step == 0 and u in chunked:
                used = layer == 0 or piece >= 2
            if used and step < 4:
                pl.semaphore_wait(rs_free.at[u, step], 3 if step == 3 or (step == 1 and u in fast) else 1)

            def act(y_first):
                for copy in rs_copies(layer, u, step, y_first, piece):
                    copy.start()

            on_route(u, step, act)

        def give_back(u, step):
            def act(y_first):
                if step == 0:
                    peers = [mate]
                elif step == 3:
                    peers = along_z
                elif u in fast:
                    peers = plane_peers
                else:
                    peers = [near_y if y_first == (step == 1) else near_x]
                for peer in peers:
                    pl.semaphore_signal(rs_free.at[u, step], inc=1, device_id=peer, device_id_type=pl.DeviceIdType.MESH)

            on_route(u, step, act)

        def rs_merge(layer, u, step, piece=None):
            if step == 3 and u in fast:
                merge_owner(layer, u)
                return

            def act(y_first):
                for wait_piece in [piece] if step == 0 else rs_pieces(u, step):
                    for copy in rs_copies(layer, u, step, y_first, wait_piece):
                        copy.wait_recv()

            on_route(u, step, act)
            slot = layer + 1
            buf, got = weight_buf[rs_weight[u]], lands[u][step]
            cols = rs_cols.get(u, every)
            if step == 3:
                if layer == 0:
                    rs_home(1, u)
                total = buf[slot, z, y, x, core, :, cols].astype(f32)
                for k in range(3):
                    total = total + got[k].astype(f32)
                fin[u][...] = total
                if layer == 1:
                    give_back(u, 3)

                @pl.when(core == layer)
                def _():
                    for k, (src, dst) in enumerate(home_parts(layer, u)):
                        pltpu.make_async_copy(src, dst, sem_g.at[layer, u, k]).start()

                @pl.when(core != layer)
                def _():
                    rs_start(layer, u, 4)

                return
            if step == 0 and piece is not None and u == wd_u:
                buf[slot, piece, :, :, core] += got[piece % 2]
            else:
                got_cols = every
                if step == 0 and piece is not None:
                    cols, got_cols = chunk_cols(piece), chunk_cols(piece % 2)

                @pl.loop(0, 4)
                def _(pz):
                    if step == 0:
                        buf[slot, pz, :, :, core, :, cols] += got[pz, :, :, :, got_cols]
                    elif u in fast:
                        total = buf[slot, pz, y, x, core, :, cols].astype(f32)
                        for k in range(3):
                            total = total + got[k, pz].astype(f32)
                        buf[slot, pz, y, x, core, :, cols] = total.astype(bf16)
                    elif step == 2:
                        buf[slot, pz, y, x, core, :, cols] += got[pz]
                    else:
                        def add(y_first):
                            if y_first:
                                buf[slot, pz, y, :, core, :, cols] += got[pz]
                            else:
                                buf[slot, pz, :, x, core, :, cols] += got[pz]

                        rs_route(u, add)

            if layer == 1 or (step == 0 and u in chunked and piece < 2):
                give_back(u, step)
            rs_start(layer, u, 3 if u in fast and step == 1 else step + 1, piece)

        def rs_home(layer, u):
            @pl.when(core == layer)
            def _():
                for k, (src, dst) in enumerate(home_parts(layer, u)):
                    pltpu.make_async_copy(src, dst, sem_g.at[layer, u, k]).wait()
                if u not in fast:
                    for copy in rs_copies(layer, u, 4, True):
                        copy.wait_recv()

            if u not in fast:
                @pl.when(core != layer)
                def _():
                    for copy in rs_copies(layer, u, 4, True):
                        copy.wait_send()

        def rs_finish(layer, u):
            if u in fast:
                for step in range(2):
                    for copy in rs_copies(layer, u, step, True):
                        copy.wait_send()
                for k in range(3):
                    owner_copy(layer, u, k).wait_send()

                @pl.when(core != layer)
                def _():
                    owner_copy(layer, u, 3).wait_send()

                return
            for step in range(4):
                def act(y_first, step=step):
                    for piece in rs_pieces(u, step):
                        for copy in rs_copies(layer, u, step, y_first, piece):
                            copy.wait_send()

                on_route(u, step, act)

        def stat_copy(step, k=0):
            target = (mate, near_y, near_x)[step] if step < 3 else along_z[k]
            place_at = step if step < 3 else 3 + z
            return pltpu.make_async_remote_copy(
                src_ref=stat_sum.at[step],
                dst_ref=stat_land.at[place_at],
                send_sem=stat_send.at[step + k],
                recv_sem=stat_recv.at[step + k],
                device_id=target,
                device_id_type=pl.DeviceIdType.MESH,
            )

        def stat_step(step):
            if step == 0:
                stat_sum[0] = stat_ref[...]
            elif step < 4:
                stat_copy(step - 1).wait()
                stat_sum[step] = stat_sum[step - 1] + stat_land[step - 1]
            if step < 3:
                stat_copy(step).start()
            elif step == 3:
                stat_land[3 + z] = stat_sum[3]
                for k in range(3):
                    stat_copy(3, k).start()
            else:
                for k in range(3):
                    stat_copy(3, k).wait()
                total = stat_land[3] + stat_land[4] + stat_land[5] + stat_land[6]
                stat_ref[...] = total
                stat_done()

        stat_step(0)
        names = dict(a=wqa_u, o=wo_u, u=wu_u, d=wd_u, b=wqb_u)

        def run_events(layer, text):
            for word in text.split():
                if word[0] == "t":
                    stat_step(int(word[1]))
                    continue
                at_layer = layer
                if word[0] == "p":
                    at_layer, word = layer + 1, word[1:]
                step, u = int(word[1]), names[word[2]]
                piece = int(word[3]) if len(word) > 3 else None
                (rs_start if word[0] == "S" else rs_merge)(at_layer, u, step, piece)

        back_points = {
            (1, "ffn0"): "t1 S0d0 S0u0",
            (1, "ffn1"): "t2 M0d0 M0u0 S0d1 S0u1",
            (1, "ffn2"): "t3 M0d1 M0u1 S0d2 S0u2",
            (1, "ffn3"): "t4 M0d2 M0u2 S0d3 S0u3",
            (1, "mid"): "M0d3 M0u3",
            (1, "wo"): "S0o",
            (1, "att00"): "M0o",
            (1, "att01"): "M1d M1u",
            (1, "wq0"): "S0a",
            (1, "att10"): "M0a M1o",
            (1, "att11"): "M2d M2u",
            (1, "wq1"): "S0b",
            (1, "in0"): "M0b M2o",
            (1, "in1"): "M1a",
            (0, "ffn0"): "S0d0 S0u0",
            (0, "ffn1"): "M0d0 M0u0 S0d1 S0u1 pM1b pM3d pM3u",
            (0, "ffn2"): "M0d1 M0u1 S0d2 S0u2 pM3o pM3a",
            (0, "ffn3"): "M0d2 M0u2 S0d3 S0u3 pM3b",
            (0, "mid"): "M0d3 M0u3",
            (0, "wo"): "S0o",
            (0, "att00"): "M0o",
            (0, "att01"): "M1d M1u",
            (0, "wq0"): "S0a",
            (0, "att10"): "M0a M1o",
            (0, "att11"): "M2d M2u",
            (0, "wq1"): "S0b M1a M0b",
            (0, "in0"): "M2o",
            (0, "end"): "M3d M3u M1b M3o M3a M3b",
        }
    else:
        back_points = {}

    def stat_done():
        totals = stat_ref[...]
        stat_out[...] = totals if not routed else jnp.sqrt(totals / (totals[0:1, 3:4, :] * width))

    if not routed:
        stat_done()

    def back_point(layer, point, s=None, at=None):
        for (at_layer, at_point), text in back_points.items():
            if at_point == point:
                here = layer == at_layer
                if s is not None:
                    here = here & (s == at)

                @pl.when(here)
                def _(at_layer=at_layer, text=text):
                    run_events(at_layer, text)

    def norm_back(x, gain, grad):
        inv = lax.rsqrt(jnp.mean(x * x, axis=1, keepdims=True) + norm_eps)
        hat = x * inv
        scaled = grad * gain
        return inv * (scaled - hat * jnp.mean(scaled * hat, axis=1, keepdims=True))

    def add_gain(k, d_weight, weight):
        for p in range(d_weight.shape[1] // lanes):
            cols = slice(p * lanes, (p + 1) * lanes)
            gain_sums[k] += d_weight[:, cols] * weight[:, cols].astype(f32)

    def pack_small(layer):
        turned = dbias[...].T
        for h in range(heads):
            ext[pl.ds(h, slots, stride=heads), :] = jnp.broadcast_to(turned[:slots, h : h + 1], (slots, lanes))
        lane = lax.broadcasted_iota(jnp.int32, (width, lanes), 1)
        gain = mat(0, layer, slice(0, lanes)).astype(f32)
        sums = [jnp.sum(gain_sums[k], axis=1, keepdims=True) for k in range(2)]
        safe = jnp.where(lane < 2, gain, 1.0)
        value = jnp.where(lane == 0, sums[0], jnp.where(lane == 1, sums[1], 0.0)) / safe
        value = jnp.where(lane == 2, ext[...], value)
        put_mat(0, layer + 1, value.astype(bf16), slice(3 * quad, 3 * quad + lanes))

    def backward_ffn(layer):
        slot = layer + 1

        @pl.loop(0, segs)
        def _(s):
            at = seg_rows(s)
            h = hbuf[at, :].astype(f32)
            doa[0, at, :] = (h * lax.rsqrt(jnp.mean(h * h, axis=1, keepdims=True) + norm_eps) * gains[layer, 1]).astype(bf16)

        dn[...] = jnp.zeros_like(dn)
        gain_sums[...] = jnp.zeros_like(gain_sums)
        dbias[...] = jnp.zeros_like(dbias)
        turned_cols = slice(0, segs * rows)
        put_mat(0, slot, doa[0].T, turned_cols)

        @pl.loop(0, ff // chunk)
        def _(c):
            cols = pl.ds(pl.multiple_of(c * chunk, chunk), chunk)
            planes = pl.ds(c, 1)
            d_pre = (nt(dy[...], mat(3, layer, planes=planes)) * slope[:, cols].astype(f32)).astype(bf16)
            put_mat(3, slot, tn(active[:, cols], dy[...]).astype(bf16), planes=planes)
            d_up = mm(mat(0, slot, turned_cols), d_pre)
            add_gain(1, d_up, mat(2, layer, cols))
            put_mat(2, slot, d_up.astype(bf16), cols)
            dn[...] += nt(d_pre, mat(2, layer, cols))
            for k in range(ff // chunk):
                back_point(layer, "ffn" + str(k), c, k)

    def backward_middle(layer, s):
        at = seg_rows(s)
        dh = norm_back(hbuf[at, :].astype(f32), gains[layer, 1], dn[at, :])
        dh = dh + dy[at, :].astype(f32)
        dn[at, :] = dh
        dz = dh.astype(bf16)
        dy[at, :] = dz
        do = nt(dz, mat(1, layer)) * ilbuf[at, :].astype(f32)
        prod = do.astype(bf16).astype(f32) * obuf[at, :].astype(f32)
        for p in range(pairs):
            cols = slice(p * lanes, (p + 1) * lanes)
            for side in range(2):
                own, marks = lane_marks(head_size, side)
                delta = -jnp.sum(prod[:, cols] * own, axis=1, keepdims=True)
                hi = delta.astype(bf16).astype(f32)
                fill = hi * marks[0] + (delta - hi) * marks[1]
                doa[side, at, cols] = (do[:, cols] * (1.0 - marks[0] - marks[1]) + fill).astype(bf16)

    def backward_attention(layer, q, s):
        at = seg_rows(s)
        for p in range(2):
            cols, kcols, vcols = (
                pl.ds(pl.multiple_of(k * width + q * quad + p * lanes, lanes), lanes) for k in range(3)
            )
            qp = qkv[at, cols]
            kp = qkv[at, kcols]
            vp = qkv[at, vcols]
            q_turned = qp.T
            dq, dk, dv = [], [], []
            for side in range(2):
                h = 4 * q + 2 * p + side
                own, marks = lane_marks(head_size, side)
                do_h = doa[side, at, cols]
                va = vp * own.astype(bf16) + (marks[0] + marks[1]).astype(bf16)
                weights = ebuf[s, h]
                d_scores = weights.astype(f32) * nt(do_h, va)
                dbias[pl.ds(h, 1), :] += jnp.sum(d_scores[:, :lanes], axis=0, keepdims=True)
                d_scores = d_scores.astype(bf16)
                half = slice(side * head_size, (side + 1) * head_size)
                dq.append(mm(d_scores, kp))
                dk.append(mm(q_turned[half, :], d_scores))
                dv.append(mm(do_h.T[half, :], weights))
            own, _ = lane_marks(head_size, 0)
            qkv[at, cols] = (jnp.where(own > 0, dq[0], dq[1]) * score_scale).astype(bf16)
            qkv[at, kcols] = (jnp.concatenate(dk, axis=0).T * (1.0 / log2_e)).astype(bf16)
            qkv[at, vcols] = jnp.concatenate(dv, axis=0).T.astype(bf16)

    def backward_input(layer, s):
        at = seg_rows(s)
        x = ub[at, :].astype(f32)
        du = norm_back(x, gains[layer, 0], nt(qkv[at, :], mat(0, layer, slice(lanes, lanes + 3 * width))))
        dy[at, :] = (du + dn[at, :]).astype(bf16)

    def grad_col(q, k):
        return q * (3 * quad + lanes) + k * quad

    def grad_copies(layer):
        return [
            pltpu.make_async_copy(buf.at[layer + 1], out.at[layer], sem_g.at[layer, k, 0])
            for k, (buf, out) in enumerate(zip(weight_buf, grads_out))
        ]

    @pl.loop(0, 2)
    def _(step):
        layer = 1 - step
        slot = layer + 1

        @pl.when(layer == 0)
        def _():
            for s in range(segs):
                for copy in spill_copies(s, True, (2, 3, 4, 5, 6)):
                    copy.wait()

        backward_ffn(layer)

        @pl.when(layer == 1)
        def _():
            for copies in y_copies:
                for copy in copies:
                    copy.wait()

        @pl.loop(0, segs)
        def _(s):
            backward_middle(layer, s)

        back_point(layer, "mid")
        put_mat(1, slot, tn(obuf[...], dy[...]).astype(bf16))
        back_point(layer, "wo")

        @pl.when(layer == 1)
        def _():
            for s in range(segs):
                for copy in spill_copies(s, True, (2, 3, 4, 5, 6)):
                    copy.start()

        @pl.loop(0, segs)
        def _(s):
            at = seg_rows(s)

            @pl.when(layer == 0)
            def _():
                spill_copies(s, True, (7,))[0].wait()

            v = ub[at, :].astype(f32)
            dy[at, :] = (v * lax.rsqrt(jnp.mean(v * v, axis=1, keepdims=True) + norm_eps) * gains[layer, 0]).astype(bf16)

        @pl.loop(0, quads)
        def _(q):
            @pl.loop(0, segs)
            def _(s):
                @pl.when((layer == 0) & (q == 0))
                def _():
                    for copy in spill_copies(s, True, (0, 1)):
                        copy.wait()

                backward_attention(layer, q, s)

                @pl.when((layer == 1) & (q == quads - 1))
                def _():
                    spill_copies(s, True, (1,))[0].start()

                for i in range(quads):
                    for k in range(segs):
                        back_point(layer, "att" + str(i) + str(k), q * segs + s, i * segs + k)

            for k in range(3):
                d_weight = tn(dy[...], qkv[:, pl.ds(pl.multiple_of(k * width + q * quad, quad), quad)])
                add_gain(0, d_weight, mat(0, layer, pl.ds(pl.multiple_of(lanes + k * width + q * quad, lanes), quad)))
                put_mat(0, slot, d_weight.astype(bf16), pl.ds(pl.multiple_of(grad_col(q, k), lanes), quad))

            @pl.when(q == quads - 1)
            def _():
                pack_small(layer)

            for i in range(quads):
                back_point(layer, "wq" + str(i), q, i)

        @pl.loop(0, segs)
        def _(s):
            backward_input(layer, s)
            for k in range(segs):
                back_point(layer, "in" + str(k), s, k)

        @pl.when(layer == 1)
        def _():
            for s in range(segs):
                for copy in spill_copies(s, True, (0, 7)):
                    copy.start()

        if not routed:
            for copy in grad_copies(layer):
                copy.start()
            for copy in grad_copies(layer):
                copy.wait()

    for copies in du_copies:
        for copy in copies:
            copy.start()
    back_point(0, "end")
    if routed:
        for layer in (1, 0):
            for u in range(5):
                rs_finish(layer, u)
    if routed:
        for u in range(5):
            rs_home(0, u)
        for u in (0, 4):
            rs_home(1, u)
    for copies in du_copies:
        for copy in copies:
            copy.wait()


def run_layers(dims, routed, doc_len, row_args, weights):
    segs, rows, width, ff, slots, heads, per_doc = dims
    all_rows = segs * rows
    vmem = pl.BlockSpec(memory_space=pltpu.VMEM)
    smem = pl.BlockSpec(memory_space=pltpu.SMEM)
    hbm = pl.BlockSpec(memory_space=pl.ANY)
    shape = jax.ShapeDtypeStruct
    dma = pltpu.SemaphoreType.DMA
    wide = (all_rows, width)
    tiles = [
        (width // 32, lanes + 3 * width),
        (width // 32, width),
        (width // 32, ff),
        (ff // 32, width),
    ]
    out_shape = [shape(part.shape, bf16) for part in row_args]
    if routed:
        out_shape += [shape((2, width // 32, 3 * width), f32)]
        out_shape += [shape((2, *tile), f32) for tile in tiles[1:]]
        out_shape += [shape((2, 8, lanes), f32)]
    else:
        out_shape += [shape((2, 4, 2, 2, 2, *tile), bf16) for tile in tiles]
    row_outs = len(out_shape)
    out_shape += [shape((2, 8, lanes), f32)]
    out_shape += [
        shape((all_rows, 3 * width), bf16),
        shape((segs, heads, rows, rows), bf16),
        shape(wide, bf16),
        shape(wide, bf16),
        shape((all_rows, ff), bf16),
        shape((all_rows, ff), bf16),
        shape(wide, bf16),
        shape(wide, bf16),
    ]
    unit_count = 16
    scratch = [pltpu.VMEM((3, 4, 2, 2, 2, *tile), bf16) for tile in tiles]
    scratch += [
        pltpu.VMEM(wide, bf16),
        pltpu.VMEM(wide, bf16),
        pltpu.VMEM((all_rows, 3 * width), bf16),
        pltpu.VMEM((segs, heads, rows, rows), bf16),
        pltpu.VMEM(wide, bf16),
        pltpu.VMEM(wide, bf16),
        pltpu.VMEM(wide, bf16),
        pltpu.VMEM((all_rows, ff), bf16),
        pltpu.VMEM((all_rows, ff), bf16),
        pltpu.VMEM((2, *wide), bf16),
        pltpu.VMEM(wide, f32),
        pltpu.VMEM((2, 2, 1, width), f32),
        pltpu.VMEM((heads, slots, lanes), f32),
        pltpu.VMEM((width, lanes), f32),
        pltpu.VMEM((2, width, lanes), f32),
        pltpu.VMEM((heads, lanes), f32),
        pltpu.VMEM((2, 8, lanes), f32),
        dma((segs, 8)),
        dma((segs, 8)),
        dma((2, 5, 4)),
        dma((8 * segs,)),
        dma((unit_count, 2)),
        dma((unit_count, 12)),
        dma((unit_count, 12)),
    ]
    params = dict(vmem_limit_bytes=127 * 2**19)
    if routed:
        params.update(collective_id=0, has_side_effects=True)
        half_cols = 3 * width // 2
        rs_tiles = [(width // 32, half_cols), *tiles[1:], (width // 32, half_cols + lanes)]
        first_tiles = [(4, 2, 2, *tile) for tile in rs_tiles]
        first_tiles[2] = (4, 2, 2, width // 32, 2 * chunk)
        first_tiles[3] = (2, 2, 2, ff // 32, width)
        for u, (first, tile) in enumerate(zip(first_tiles, rs_tiles)):
            leads = ((3, 4), (1,), (2, 4)) if u in (0, 4) else ((4, 2), (4,), (3,))
            scratch += [pltpu.VMEM(first, bf16)]
            scratch += [pltpu.VMEM((*lead, *tile), bf16) for lead in leads]
        scratch += [pltpu.VMEM((2, *tile) if u in (0, 4) else tile, f32) for u, tile in enumerate(rs_tiles)]
        scratch += [
            pltpu.VMEM((4, 2, 8, lanes), f32),
            pltpu.VMEM((7, 2, 8, lanes), f32),
            dma((2, 5, 17)),
            dma((2, 5, 17)),
            pltpu.SemaphoreType.REGULAR((5, 4)),
            dma((8 * segs,)),
            dma((8 * segs,)),
            dma((6,)),
            dma((6,)),
        ]
    return pl.pallas_call(
        partial(fused_layers, dims, routed),
        out_shape=out_shape,
        in_specs=[smem] + [hbm] * (len(row_args) + len(weights)),
        out_specs=[hbm] * row_outs + [vmem] + [hbm] * (len(out_shape) - row_outs - 1),
        scratch_shapes=scratch,
        compiler_params=pltpu.CompilerParams(**params),
    )(doc_len, *row_args, *weights)[: row_outs + 1]


def settle_kernel(*refs):
    count = (len(refs) - 7) // 3
    srcs, (small, stats) = refs[:count], refs[count : count + 2]
    dsts = refs[count + 2 : 2 * count + 2]
    vectors, rms = refs[2 * count + 2 : 2 * count + 5], refs[2 * count + 5]
    mids, sems = refs[2 * count + 6 : -1], refs[-1]
    inward = [pltpu.make_async_copy(src, mid, sems.at[0, k]) for k, (src, mid) in enumerate(zip(srcs, mids))]
    outward = [pltpu.make_async_copy(mid, dst, sems.at[1, k]) for k, (mid, dst) in enumerate(zip(mids, dsts))]
    for copy in inward:
        copy.start()
    for k, vector in enumerate(vectors):
        size = vector.shape[1] // 2
        vector[...] = jnp.concatenate([small[half, k : k + 1, :size] for half in range(2)], axis=1)
    lane = lax.broadcasted_iota(jnp.int32, (1, lanes), 1)
    for layer in range(2):
        row = sum(jnp.where(lane == k, stats[layer, k : k + 1, :], 0.0) for k in range(3))
        rms[layer : layer + 1, :] = row[:, :3]
    for into, out in zip(inward, outward):
        into.wait()
        out.start()
    for out in outward:
        out.wait()


def settle(big, small, stats):
    vmem = pl.BlockSpec(memory_space=pltpu.VMEM)
    hbm = pl.BlockSpec(memory_space=pl.ANY)
    shape = jax.ShapeDtypeStruct
    size = 2 * big[4].shape[1]
    return pl.pallas_call(
        settle_kernel,
        out_shape=[shape(part.shape, part.dtype) for part in big] + [shape((1, size), f32)] * 3 + [shape((2, 3), f32)],
        in_specs=[hbm] * len(big) + [vmem] * 2,
        out_specs=[hbm] * len(big) + [vmem] * 4,
        scratch_shapes=[pltpu.VMEM(part.shape, part.dtype) for part in big] + [pltpu.SemaphoreType.DMA((2, len(big)))],
    )(*big, small, stats)


def swap(block):
    return lax.ppermute(block, "section", [(0, 1), (1, 0)])


def body(
    tokens,
    memory,
    lengths,
    w_qkv,
    w_out,
    w_up,
    w_down,
    gain_attn,
    gain_ffn,
    forget_bias,
    grad_tokens,
    grad_memory,
):
    section = lax.axis_index("section")
    is_first = section == 0
    micro = tokens.shape[0]
    segs = micro // 2
    half_tok = tokens.shape[1]
    half_mem = memory.shape[1]
    slots = 2 * half_mem
    rows = slots + 2 * half_tok
    width = tokens.shape[2]
    ff = w_up.shape[2]
    heads = forget_bias.shape[1] * lax.axis_size("dp") // slots
    per_doc = micro // lengths.shape[0]
    dims = (segs, rows, width, ff, slots, heads, per_doc)
    small = jnp.stack([gain_attn, gain_ffn, forget_bias], axis=2)
    small = jnp.pad(small, ((0, 0), (0, 0), (0, lanes - 3)))

    if lax.axis_size("dp") == 16 and w_qkv.shape[1] == 32:
        pieces = (w_qkv, w_out, w_up, w_down, small)
        weights = [piece.reshape(2, -1, piece.shape[2]) for piece in pieces]
        row_args = (tokens, memory, grad_tokens, grad_memory)
        *outs, small_grads, stats = run_layers(dims, True, lengths, row_args, weights)
        outs = settle(outs, small_grads, stats)
        mats = [grad.reshape(1, -1, grad.shape[2]) for grad in outs[4:8]]
        return (*outs[:4], *mats, *outs[8:])

    own_len = lax.dynamic_slice_in_dim(lengths, section * segs // per_doc, segs // per_doc, 0)
    pieces = (jnp.concatenate([small, w_qkv], axis=2), w_out, w_up, w_down)

    def unpack(grads):
        mat = grads[0]
        half = 3 * width // 2
        parts = [mat[:, :, :half], mat[:, :, half + lanes :]]
        parts = [part.reshape(1, -1, 3, width // 2) for part in parts]
        whole = jnp.concatenate(parts, axis=3).reshape(1, -1, 3 * width)
        return (whole, *grads[1:], *(mat[:, :, half + k] for k in range(3)))

    def own_segs(halves):
        return lax.dynamic_slice_in_dim(halves, section * segs, segs, 0)

    def other_segs(halves):
        return lax.dynamic_slice_in_dim(halves, (1 - section) * segs, segs, 0)

    def both(kept, got):
        return jnp.concatenate(
            [jnp.where(is_first, kept, got), jnp.where(is_first, got, kept)], axis=1
        )

    inputs = (tokens, memory, grad_tokens, grad_memory)
    got = swap(tuple(other_segs(part) for part in inputs))
    full = [both(own_segs(part), other) for part, other in zip(inputs, got)]
    u0 = jnp.concatenate([full[1], full[0]], axis=1).reshape(segs * rows, width)
    dout = jnp.concatenate([full[3], full[2]], axis=1).reshape(segs * rows, width)

    def gather(piece):
        whole = lax.all_gather(piece, ("section", "dp"), axis=1, tiled=True)
        return whole.reshape(2, 4, 2, 2, 2, -1, piece.shape[2])

    y, du, *grads, stats = run_layers(dims, False, own_len, (u0, dout), [gather(piece) for piece in pieces])

    def scatter(grad):
        grad = grad.reshape(2, -1, grad.shape[-1])
        mine = lax.dynamic_index_in_dim(grad, section, 0, keepdims=True)
        other = lax.dynamic_index_in_dim(grad, 1 - section, 0, keepdims=True)
        chip = (mine.astype(f32) + swap(other).astype(f32)).astype(grad.dtype)
        return lax.psum_scatter(chip, "dp", scatter_dimension=1, tiled=True).astype(f32)

    shares = unpack([scatter(grad) for grad in grads])
    totals = lax.psum(stats[:, :4, 0], ("section", "dp"))
    rms = jnp.sqrt(totals[:, :3] / (totals[0, 3] * width))
    result = jnp.stack([y.reshape(segs, rows, width), du.reshape(segs, rows, width)])

    def half_of(which):
        tok = lax.dynamic_slice_in_dim(result, slots + which * half_tok, half_tok, 2)
        mem = lax.dynamic_slice_in_dim(result, which * half_mem, half_mem, 2)
        return tok, mem

    kept = half_of(section)
    got = swap(half_of(1 - section))

    def order(mine, other):
        return jnp.concatenate(
            [jnp.where(is_first, mine, other), jnp.where(is_first, other, mine)], axis=0
        )

    toks = [order(kept[0][k], got[0][k]) for k in range(2)]
    mems = [order(kept[1][k], got[1][k]) for k in range(2)]
    return (toks[0], mems[0], toks[1], mems[1], *shares, rms)


def solution(mesh):
    rows = P("dp", "section", None)
    mats = P("section", "dp", None)
    vecs = P("section", "dp")
    return jax.shard_map(
        body,
        mesh=mesh,
        in_specs=(rows, rows, P("dp"), mats, mats, mats, mats, vecs, vecs, vecs, rows, rows),
        out_specs=(rows, rows, rows, rows, mats, mats, mats, mats, vecs, vecs, vecs, P()),
        check_vma=False,
    )
```

```python
from functools import partial

import jax
import jax.numpy as jnp
from jax import lax
from jax.experimental import pallas as pl
from jax.experimental.pallas import tpu as pltpu
from jax.sharding import PartitionSpec as P

norm_eps = 1e-06
score_scale = 0.125
log2_e = 1.4426950408889634
masked_score = -1000000000.0
gelu_c = 0.7978845608028654
gelu_k = 0.044715
f32 = jnp.float32
bf16 = jnp.bfloat16
lanes = 128
chunk = 512


def mm(a, b, ca=1, cb=0):
    return lax.dot_general(a, b, (((ca,), (cb,)), ((), ())), preferred_element_type=f32)


def nt(a, b):
    return mm(a, b, 1, 1)


def tn(a, b):
    return mm(a, b, 0, 0)


def lane_marks(head_size, side):
    lane = lax.broadcasted_iota(jnp.int32, (1, lanes), 1)
    own = ((lane // head_size) == side).astype(f32)
    first = (1 - side) * head_size
    marks = [(lane == first + k).astype(f32) for k in range(3)]
    return own, marks


def fused_layers(dims, routed, *refs):
    segs, rows, width, ff, slots, heads, per_doc = dims
    refs = list(refs)

    def take(count):
        picked = refs[:count]
        del refs[:count]
        return picked

    (len_ref,) = take(1)
    rows_in = take(4 if routed else 2)
    weight_in = take(5 if routed else 4)
    rows_out = take(4 if routed else 2)
    grads_out = take(5 if routed else 4)
    (stat_out,) = take(1)
    spill_hbm = take(8)
    weight_buf = take(4)
    ub, dy, qkv, ebuf, obuf, ilbuf, hbuf, slope, active, doa, dn = take(11)
    gains, bias_rows, ext, gain_sums, dbias, stat_ref = take(6)
    sem_spill, sem_back, sem_g, sem_io, sem_send, sem_recv = take(6)
    if routed:
        lands = [take(4) for _ in range(5)]
        fin = take(5)
        stat_sum, stat_land = take(2)
        rs_send, rs_recv, rs_free, stat_send, stat_recv = take(5)
    head_size = width // heads
    pairs = width // lanes
    tok_rows = rows - slots
    quads = width // (2 * lanes)
    quad = 2 * lanes
    first_doc = lax.axis_index("section") * segs // per_doc if routed else 0
    every = slice(None)

    def wait_bytes(ref, sem):
        pltpu.make_async_copy(ref, ref, sem).wait()

    def units_of(layer):
        half_ff, half_deep = ff // 2, ff // 64
        lead = [
            (0, slice(0, lanes + width), every),
            (0, slice(lanes + width, lanes + 2 * width), every),
            (0, slice(lanes + 2 * width, lanes + 3 * width), every),
        ]
        rest = [(1, every, every)]
        rest += [(3, every, slice(k * half_deep, (k + 1) * half_deep)) for k in range(2)]
        rest += [(2, slice(k * half_ff, (k + 1) * half_ff), every) for k in range(2)]
        return [(layer, *unit) for unit in lead + rest]

    units = units_of(0) + units_of(1)
    first_units = [k for k, unit in enumerate(units) if unit[1] == 0]
    last_units = [7, 15]
    later_units = [k for k, unit in enumerate(units) if unit[1] != 0 and k not in last_units]
    plane_first = (11, 15)

    def view(n, z, y, x, c):
        layer, which, cols, part = units[n]
        return weight_buf[which].at[layer, z, y, x, c, part, cols]

    if routed:
        core = lax.axis_index("section")
        chip = lax.axis_index("dp")
        z, y, x = chip // 4, (chip // 2) % 2, chip % 2
        other = 1 - core

        def place(pz, py, px):
            return pz * 4 + py * 2 + px

        mate = (other, chip)
        near_x = (core, place(z, y, 1 - x))
        near_y = (core, place(z, 1 - y, x))
        along_z = [(core, place((z + k) % 4, y, x)) for k in range(1, 4)]

        def remote(src, dst, n, k, target):
            far = k in (4, 5, 9, 10) or (k in (0, 11) and n in plane_first)
            arrived = {0: 0, 11: 0, 1: 1, 2: 1, 3: 1, 4: 2, 5: 3, 6: 4, 7: 4, 8: 4, 9: 5, 10: 5}[k]
            return pltpu.make_async_remote_copy(
                src_ref=src,
                dst_ref=dst,
                send_sem=sem_send.at[n, int(far)],
                recv_sem=sem_recv.at[n, arrived],
                device_id=target,
                device_id_type=pl.DeviceIdType.MESH,
            )

        def some(n, shards, half):
            return view(n, slice(0, 3), y, x, half) if shards == 3 else view(n, slice(0, 3), every, every, half)

        def own_shards(n):
            layer, which, cols, part = units[n]
            home = weight_buf[which].at[layer, z, y, x]
            if which > 0:
                return [(weight_in[which].at[every, part, cols], home.at[every, part, cols], 0)]
            start = max(cols.start - lanes, 0)
            matrix = slice(start, cols.stop - lanes)
            pairs_of = [(weight_in[0].at[every, every, matrix], home.at[every, every, slice(start + lanes, cols.stop)], 0)]
            if cols.start == 0:
                pairs_of.append((weight_in[4], home.at[every, every, slice(0, lanes)], 11))
            return pairs_of

        def z_copy(n, k):
            where = view(n, z, every, every, core) if n in plane_first else view(n, z, y, x, core)
            return remote(where, where, n, k, along_z[k - 1])

        def plane_copy(n, k, x_first):
            planes = z if n in plane_first else every
            if k == 4:
                where = view(n, planes, y, x, core)
                return remote(where, where, n, 4, near_x if x_first else near_y)
            where = view(n, planes, y, every, core) if x_first else view(n, planes, every, x, core)
            return remote(where, where, n, 5, near_y if x_first else near_x)

        def mate_copy(n, k, x_first, half):
            planes = z if n in plane_first else every
            if k < 9:
                from_z = (z + 4 - (k - 5)) % 4
                where = view(n, from_z, every, every, half) if n in plane_first else view(n, from_z, y, x, half)
            elif k == 9:
                where = view(n, planes, y, 1 - x, half) if x_first else view(n, planes, 1 - y, x, half)
            else:
                where = view(n, planes, 1 - y, every, half) if x_first else view(n, planes, every, 1 - x, half)
            return remote(where, where, n, k, mate)

        def by_route(n, act):
            for side in range(2):
                @pl.when(core == side)
                def _(side=side):
                    act((side + n) % 2 == 0)

        def share_own(n):
            @pl.when(core == units[n][0])
            def _():
                for src, dst, k in own_shards(n):
                    pltpu.make_async_copy(src, dst, sem_recv.at[n, 0]).start()
                    remote(src, dst, n, k, mate).start()

        def start_z(n):
            wait_bytes(view(n, z, y, x, every), sem_recv.at[n, 0])
            if n in plane_first:
                by_route(n, lambda x_first: plane_copy(n, 4, x_first).start())
            else:
                for k in range(1, 4):
                    z_copy(n, k).start()

        def first_hop(n):
            if n not in plane_first:
                wait_bytes(some(n, 3, core), sem_recv.at[n, 1])

            def act(x_first):
                if n in plane_first:
                    plane_copy(n, 4, x_first).wait_recv()
                    plane_copy(n, 5, x_first).start()
                    mate_copy(n, 9, x_first, core).start()
                else:
                    plane_copy(n, 4, x_first).start()
                    for k in range(6, 9):
                        mate_copy(n, k, x_first, core).start()

            by_route(n, act)

        def second_hop(n):
            def act(x_first):
                if n in plane_first:
                    plane_copy(n, 5, x_first).wait_recv()
                    for k in range(1, 4):
                        z_copy(n, k).start()
                    mate_copy(n, 10, x_first, core).start()
                else:
                    plane_copy(n, 4, x_first).wait_recv()
                    plane_copy(n, 5, x_first).start()
                    mate_copy(n, 9, x_first, core).start()

            by_route(n, act)

        def last_share(n):
            def act(x_first):
                if n in plane_first:
                    wait_bytes(some(n, 12, core), sem_recv.at[n, 1])
                    for k in range(6, 9):
                        mate_copy(n, k, x_first, core).start()
                else:
                    plane_copy(n, 5, x_first).wait_recv()
                    mate_copy(n, 10, x_first, core).start()

            by_route(n, act)

        def complete(n):
            near, rest = (12, 3) if n in plane_first else (3, 12)
            wait_bytes(some(n, near, other), sem_recv.at[n, 4])
            wait_bytes(some(n, rest, other), sem_recv.at[n, 5])

        def drain(n):
            few, many = (1, 0) if n in plane_first else (0, 1)
            wait_bytes(view(n, slice(0, 3), every, every, every), sem_send.at[n, many])

            @pl.when(core == units[n][0])
            def _():
                wait_bytes(view(n, every, y, x, every), sem_send.at[n, few])

            @pl.when(core != units[n][0])
            def _():
                wait_bytes(view(n, slice(0, 3), y, x, every), sem_send.at[n, few])

        def hops(text):
            kinds = dict(z=start_z, f=first_hop, s=second_hop, l=last_share)
            for word in text:
                kinds[word[0]](int(word[1:]))

        opening = ("z0", "z1", "z2", "z3", "z4", "z5", "f0", "f1", "s0", "z6", "f2", "s1", "z7", "f3", "s2", "l0", "f4", "s3", "l1", "f5", "s4", "f6", "l2")
        hops_at = {
            (0, 0, "qkv"): ("s5", "f7", "z8", "z9", "z11", "z15"),
            (0, 0, "quad0"): ("s6", "z10", "z12", "l3"),
            (0, 0, "quad1"): ("f8", "z13", "f11"),
            (0, 1, "qkv"): ("s7", "f9", "l4"),
            (0, 1, "quad0"): ("s8", "f10", "z14", "f15", "l5"),
            (0, 1, "quad1"): ("l6", "s9", "s11"),
            (0, 0, "gate"): ("f12",),
            (0, 0, "ffna"): ("l7", "s10", "f13"),
            (0, 1, "ffna"): ("s12", "s15"),
            (0, 0, "ffnb"): ("l8", "s13", "f14"),
            (0, 1, "ffnb"): ("l9", "l10"),
            (1, 0, "quad0"): ("s14", "l11"),
            (1, 0, "quad1"): ("l12",),
            (1, 1, "qkv"): ("l13",),
            (1, 1, "quad0"): ("l14", "l15"),
        }
    else:
        hops_at = {}

        def weight_copy(n):
            layer, which, cols, part = units[n]
            src = weight_in[which].at[layer, every, every, every, every, part, cols]
            return pltpu.make_async_copy(src, view(n, every, every, every, every), sem_recv.at[n, 0])

        def complete(n):
            weight_copy(n).wait()

    def after(layer, s, point):
        for (at_layer, at_s, at_point), text in hops_at.items():
            if at_point == point:
                @pl.when((layer == at_layer) & (s == at_s))
                def _(text=text):
                    hops(text)

    def need(layer, picks):
        for at_layer in range(2):
            @pl.when(layer == at_layer)
            def _(at_layer=at_layer):
                for n in picks:
                    if units[n][0] == at_layer:
                        complete(n)

    def mat(which, slot, cols=every, planes=None):
        if planes is None:
            value = weight_buf[which][slot, :, :, :, :, :, cols]
        else:
            value = weight_buf[which][slot, planes, :, :, :, :, cols]
        deep = 1
        for size in value.shape[:-1]:
            deep *= size
        return value.reshape(deep, value.shape[-1])

    def put_mat(which, slot, value, cols=every, planes=None):
        buf = weight_buf[which]
        shape = buf.shape[1:-1]
        if planes is None:
            buf[slot, :, :, :, :, :, cols] = value.reshape(*shape, value.shape[-1])
        else:
            buf[slot, planes] = value.reshape(1, *shape[1:], value.shape[-1])

    def qkv_cols(k):
        return slice(lanes + k * width, lanes + (k + 1) * width)

    def seg_rows(s):
        return pl.ds(pl.multiple_of(s * rows, rows), rows)

    def spill_copies(s, back, picks=range(7)):
        at = seg_rows(s)
        kept = (qkv.at[at], ebuf.at[s], obuf.at[at], ilbuf.at[at], slope.at[at], active.at[at], hbuf.at[at], ub.at[at])
        pairs_of = [
            (vmem, hbm.at[s] if k == 1 else hbm.at[at])
            for k, (vmem, hbm) in enumerate(zip(kept, spill_hbm))
        ]
        if back:
            return [
                pltpu.make_async_copy(hbm, vmem, sem_back.at[s, k])
                for k, (vmem, hbm) in enumerate(pairs_of)
                if k in picks
            ]
        return [
            pltpu.make_async_copy(vmem, hbm, sem_spill.at[s, k])
            for k, (vmem, hbm) in enumerate(pairs_of)
            if k in picks
        ]

    def doc_end(s):
        return len_ref[first_doc + s // per_doc] - (s % per_doc) * tok_rows

    def valid_col(s):
        row = lax.broadcasted_iota(jnp.int32, (rows, 1), 0)
        return jnp.where(
            (row >= slots) & (row - slots < doc_end(s)), 1.0, 0.0
        ).astype(f32)

    def mask_col(s):
        row = lax.broadcasted_iota(jnp.int32, (rows, 1), 0)
        return jnp.where(
            (row >= slots) & (row - slots >= doc_end(s)), masked_score, 0.0
        ).astype(f32)

    if routed:
        half_tok, half_mem = tok_rows // 2, slots // 2

        def io_copies(buf, tok_ref, mem_ref, sems, outward):
            local, away = [], []
            own_sem, send_sem, recv_sem = (sem_io.at[k] for k in sems)
            for s in range(segs):
                mine, theirs = core * segs + s, other * segs + s
                for ref, base, size in ((tok_ref, slots, half_tok), (mem_ref, 0, half_mem)):
                    def rows_of(half):
                        return buf.at[pl.ds(pl.multiple_of(s * rows + base + half * size, 16), size)]

                    if outward:
                        local.append(pltpu.make_async_copy(rows_of(core), ref.at[mine], own_sem))
                        src, dst = rows_of(other), ref.at[mine]
                    else:
                        local.append(pltpu.make_async_copy(ref.at[mine], rows_of(core), own_sem))
                        src, dst = ref.at[theirs], rows_of(core)
                    away.append(
                        pltpu.make_async_remote_copy(
                            src_ref=src,
                            dst_ref=dst,
                            send_sem=send_sem,
                            recv_sem=recv_sem,
                            device_id=mate,
                            device_id_type=pl.DeviceIdType.MESH,
                        )
                    )
            return local, away

        def half_rows(buf):
            return buf.at[pl.ds(0, segs * rows // 2)]

        loads, shares = io_copies(ub, rows_in[0], rows_in[1], (0, 2, 0), False)
        more = io_copies(dy, rows_in[2], rows_in[3], (1, 2, 1), False)
        loads, shares = loads + more[0], shares + more[1]
        y_copies = io_copies(doa.at[1], rows_out[0], rows_out[1], (3, 4, 5), True)
        du_copies = io_copies(dy, rows_out[2], rows_out[3], (6, 7, 8), True)
    else:
        loads = [
            pltpu.make_async_copy(rows_in[0], ub, sem_io.at[0]),
            pltpu.make_async_copy(rows_in[1], dy, sem_io.at[1]),
        ]
        shares = []
        y_copies = [pltpu.make_async_copy(doa.at[1], rows_out[0], sem_io.at[3])], []
        du_copies = [pltpu.make_async_copy(dy, rows_out[1], sem_io.at[6])], []
    for copy in loads:
        copy.start()
    if routed:
        barrier = pltpu.get_barrier_semaphore()
        peers = [mate, near_x, near_y, (core, place(z, 1 - y, 1 - x)), *along_z]
        peers += [(other, place((z + k) % 4, y, x)) for k in range(1, 4)]
        for peer in peers:
            pl.semaphore_signal(barrier, inc=1, device_id=peer, device_id_type=pl.DeviceIdType.MESH)
        pl.semaphore_wait(barrier, len(peers))
        for n in range(8):
            share_own(n)
        for copy in shares:
            copy.start()
        for n in range(8, len(units)):
            share_own(n)
        hops(opening)
    else:
        for n in range(len(units)):
            weight_copy(n).start()
    stat_ref[...] = jnp.zeros_like(stat_ref)

    wait_bytes(ub, sem_io.at[0])
    wait_bytes(dy, sem_io.at[1])
    if routed:
        wait_bytes(ub, sem_io.at[2])

    def wait_rows(buf, first):
        if routed:
            for k in range(3):
                wait_bytes(half_rows(buf), sem_io.at[first + k])
        else:
            wait_bytes(buf, sem_io.at[first])

    def add_stat(layer, k, row_sums, valid):
        total = jnp.sum(row_sums * valid, axis=0, keepdims=True)
        stat_ref[layer, k : k + 1, :] += jnp.broadcast_to(total, (1, lanes))

    def forward_attention(layer, s):
        at = seg_rows(s)
        mask = mask_col(s)
        for p in range(pairs):
            cols = slice(p * lanes, (p + 1) * lanes)
            qp = qkv[at, cols]
            kp = qkv[at, slice(width + p * lanes, width + (p + 1) * lanes)]
            vp = qkv[at, slice(2 * width + p * lanes, 2 * width + (p + 1) * lanes)]
            outs = []
            for side in range(2):
                h = 2 * p + side
                own, marks = lane_marks(head_size, side)
                bias = bias_rows[h]
                hi = bias.astype(bf16).astype(f32)
                aux = jnp.concatenate([hi * marks[1] + (bias - hi) * marks[2], jnp.zeros((tok_rows, lanes), f32)], axis=0)
                aux = aux + mask * marks[0]
                extra = marks[0] + marks[1] + marks[2]
                ka = kp * own.astype(bf16) + aux.astype(bf16)
                qa = qp * (1.0 - extra).astype(bf16) + extra.astype(bf16)
                scores = nt(qa, ka)
                top = jnp.max(scores, axis=1, keepdims=True)
                weights = jnp.exp2(scores - top).astype(bf16)
                ebuf[s, h] = weights
                va = vp * own.astype(bf16) + (1.0 - own).astype(bf16)
                outs.append(mm(weights, va))
            own, _ = lane_marks(head_size, 0)
            raw = jnp.where(own > 0, outs[0], outs[1])
            sums = pltpu.roll(jnp.where(own > 0, outs[1], outs[0]), head_size, 1)
            inv = 1.0 / sums
            ilbuf[at, cols] = inv.astype(ilbuf.dtype)
            obuf[at, cols] = (raw * inv).astype(bf16)
            if p % 2 == 1:
                after(layer, s, "quad" + str(p // 2))

    def unpack_small(layer):
        ext[...] = mat(0, layer, slice(0, lanes)).astype(f32)
        turned = ext[...].T
        for k in range(2):
            gains[layer, k] = turned[k : k + 1, :]
        for h in range(heads):
            column = ext[pl.ds(h, slots, stride=heads), :][:, 2:3]
            bias_rows[h] = jnp.broadcast_to(column * log2_e, (slots, lanes))

    def forward_attn(layer, s):
        at = seg_rows(s)

        @pl.when(layer == 1)
        def _():
            for copy in spill_copies(s, False):
                copy.wait()

        @pl.when(layer == 0)
        def _():
            spill_copies(s, False, (7,))[0].start()

        valid = valid_col(s)
        x = ub[at, :].astype(f32)
        squares = jnp.sum(x * x, axis=1, keepdims=True)
        add_stat(layer, 0, squares, valid)
        add_stat(layer, 3, valid, valid)
        n1 = (x * lax.rsqrt(squares / width + norm_eps) * gains[layer, 0]).astype(bf16)
        for k in range(3):
            part = mm(n1, mat(0, layer, qkv_cols(k)))
            if k == 0:
                part = part * (score_scale * log2_e)
            qkv[at, k * width : (k + 1) * width] = part.astype(bf16)
        after(layer, s, "qkv")
        forward_attention(layer, s)

        @pl.when(layer == 0)
        def _():
            for copy in spill_copies(s, False, range(4)):
                copy.start()

    def ffn_part(s, layer, picks):
        at = seg_rows(s)

        def up(c):
            return mm(doa[0, at, :], mat(2, layer, slice(c * chunk, (c + 1) * chunk)))

        before = up(picks[0])
        for c in picks:
            cols = slice(c * chunk, (c + 1) * chunk)
            following = up(c + 1) if c + 1 in picks else None
            square = before * before
            gate = 0.5 + 0.5 * jnp.tanh(before * (gelu_c + (gelu_c * gelu_k) * square))
            act = before * gate
            slope[at, cols] = (gate + act * (1.0 - gate) * (2.0 * gelu_c + (6.0 * gelu_c * gelu_k) * square)).astype(bf16)
            act = act.astype(bf16)
            active[at, cols] = act
            part = mm(act, mat(3, layer, planes=slice(c, c + 1)))
            if c == 0:
                dn[at, :] = part
            else:
                dn[at, :] += part
            before = following

    def forward_ffn_a(layer, s):
        at = seg_rows(s)
        valid = valid_col(s)
        z = mm(obuf[at, :], mat(1, layer))
        add_stat(layer, 1, jnp.sum(z * z, axis=1, keepdims=True), valid)
        h = ub[at, :].astype(f32) + z
        hbuf[at, :] = h.astype(bf16)
        doa[0, at, :] = (h * lax.rsqrt(jnp.mean(h * h, axis=1, keepdims=True) + norm_eps) * gains[layer, 1]).astype(bf16)
        ffn_part(s, layer, range(ff // chunk // 2))
        after(layer, s, "ffna")

    def forward_ffn_b(layer, s):
        at = seg_rows(s)
        valid = valid_col(s)
        ffn_part(s, layer, range(ff // chunk // 2, ff // chunk))
        out = dn[at, :]
        add_stat(layer, 2, jnp.sum(out * out, axis=1, keepdims=True), valid)
        z = mm(obuf[at, :], mat(1, layer))
        result = (ub[at, :].astype(f32) + z + out).astype(bf16)

        @pl.when(layer == 0)
        def _():
            spill_copies(s, False, (7,))[0].wait()
            ub[at, :] = result

        @pl.when(layer == 1)
        def _():
            doa[1, at, :] = result

        @pl.when(layer == 0)
        def _():
            for copy in spill_copies(s, False, (4, 5, 6)):
                copy.start()

        after(layer, s, "ffnb")

    @pl.loop(0, 2)
    def _(layer):
        after(layer, 0, "open")
        need(layer, first_units)
        unpack_small(layer)

        @pl.loop(0, segs)
        def _(s):
            forward_attn(layer, s)

        after(layer, 0, "gate")
        need(layer, later_units)

        @pl.loop(0, segs)
        def _(s):
            forward_ffn_a(layer, s)

        after(layer, 0, "last")
        need(layer, last_units)

        @pl.loop(0, segs)
        def _(s):
            forward_ffn_b(layer, s)

    if routed:
        for n in range(len(units)):
            drain(n)
    for copies in y_copies:
        for copy in copies:
            copy.start()

    if routed:
        wqa_u, wo_u, wu_u, wd_u, wqb_u = range(5)
        half_cols = quads * 3 * lanes
        rs_cols = {wqa_u: slice(0, half_cols), wqb_u: slice(half_cols, 2 * half_cols + lanes)}
        rs_weight = (0, 1, 2, 3, 0)
        chunked = (wu_u, wd_u)
        fast = (wqa_u, wqb_u)
        plane_peers = [near_x, near_y, (core, place(z, 1 - y, 1 - x))]
        plane_spots = [(y, 1 - x), (1 - y, x), (1 - y, 1 - x)]
        chunks = ff // chunk

        def rs_copy(src, dst, u, step, k, target):
            return pltpu.make_async_remote_copy(
                src_ref=src,
                dst_ref=dst,
                send_sem=rs_send.at[u, step],
                recv_sem=rs_recv.at[u, k],
                device_id=target,
                device_id_type=pl.DeviceIdType.MESH,
            )

        def piece_cols(step, piece, u):
            size = chunk if step < 2 else ff // 2
            return slice(piece * size, (piece + 1) * size)

        def piece_planes(step, piece):
            return piece if step < 2 else slice(2 * piece, 2 * piece + 2)

        def spot(layer, u, pz, py, px, c, piece=None, step=0):
            cols = rs_cols.get(u, every)
            if piece is not None and u == wd_u:
                pz = piece_planes(step, piece)
            elif piece is not None:
                cols = piece_cols(step, piece, u)
            return weight_buf[rs_weight[u]].at[layer + 1, pz, py, px, c, every, cols]

        def land_at(u, step, piece=None):
            ref = lands[u][step]
            if piece is None:
                return ref
            ring = piece % 2 if step == 0 else piece
            if u == wd_u:
                return ref.at[piece_planes(step, ring)]
            lead = (every,) * (len(ref.shape) - 1)
            return ref.at[(*lead, piece_cols(step, ring, u))]

        def rs_copies(layer, u, step, y_first, piece=None):
            if step == 0:
                src = spot(layer, u, every, every, every, other, piece)
                return [rs_copy(src, land_at(u, 0, piece), u, 0, (piece or 0) % 2, mate)]
            if step == 1 and u in fast:
                return [
                    rs_copy(spot(layer, u, every, *plane_spots[k], core), lands[u][1].at[k], u, 1, 2, plane_peers[k])
                    for k in range(3)
                ]
            if step == 3 and u in fast:
                return [owner_copy(layer, u, k) for k in range(4)]
            if step == 1:
                at = (every, 1 - y, every) if y_first else (every, every, 1 - x)
                src = spot(layer, u, *at, core, piece)
                return [rs_copy(src, land_at(u, 1, piece), u, 1, 2 + (piece or 0) // 2, near_y if y_first else near_x)]
            if step == 2:
                at = (every, y, 1 - x) if y_first else (every, 1 - y, x)
                src = spot(layer, u, *at, core, piece, 2)
                return [rs_copy(src, land_at(u, 2, piece), u, 2, 4 + (piece or 0), near_x if y_first else near_y)]
            if step == 3:
                cols = piece_cols(3, piece, u) if piece is not None else every
                return [
                    rs_copy(
                        weight_buf[rs_weight[u]].at[layer + 1, (z + k) % 4, y, x, core, every, cols],
                        lands[u][3].at[k - 1, every, cols], u, 3, 6, along_z[k - 1],
                    )
                    for k in range(1, 4)
                ]
            return [rs_copy(src, dst, u, 4, 7, mate) for src, dst in home_parts(layer, u)]

        def owner_copy(layer, u, k):
            away = (z + k + 1) % 4 if k < 3 else z
            half = core
            return pltpu.make_async_remote_copy(
                src_ref=spot(layer, u, away, y, x, core),
                dst_ref=lands[u][3].at[half, k],
                send_sem=rs_send.at[u, 3],
                recv_sem=rs_recv.at[u, 6 + half],
                device_id=(layer, place(away, y, x)),
                device_id_type=pl.DeviceIdType.MESH,
            )

        def start_owner(layer, u):
            for k in range(3):
                owner_copy(layer, u, k).start()

            @pl.when(core != layer)
            def _():
                owner_copy(layer, u, 3).start()

        def merge_owner(layer, u):
            @pl.when(core == layer)
            def _():
                got = lands[u][3]
                wait_bytes(got.at[layer, pl.ds(0, 3)], rs_recv.at[u, 6 + layer])
                wait_bytes(got.at[1 - layer], rs_recv.at[u, 7 - layer])
                cols = rs_cols[u]
                for half in range(2):
                    if half == layer:
                        total = weight_buf[0][layer + 1, z, y, x, half, :, cols].astype(f32)
                    else:
                        total = got[half, 3].astype(f32)
                    for k in range(3):
                        total = total + got[half, k].astype(f32)
                    if u == wqb_u:
                        small = total[:, :lanes].T
                        turned = jnp.concatenate([small[:8, :], jnp.zeros((8, lanes - small.shape[1]), f32)], axis=1)
                        fin[u][half, 0:8, 0:lanes] = turned
                        fin[u][half, :, lanes:] = total[:, lanes:]
                    else:
                        fin[u][half] = total
                for k, (src, dst) in enumerate(home_parts(layer, u)):
                    pltpu.make_async_copy(src, dst, sem_g.at[5 if k == 3 else u]).start()

        def home_parts(layer, u):
            if u not in rs_cols:
                return [(fin[u], grads_out[u].at[core])]
            base, q = (0, 0) if u == wqa_u else (lanes, 1)
            parts = [
                (
                    fin[u].at[:, :, base + k * quad : base + (k + 1) * quad],
                    grads_out[0].at[:, :, k * width + q * quad : k * width + (q + 1) * quad],
                )
                for k in range(3)
            ]
            if u == wqb_u:
                parts.append((fin[u].at[:, 0:8, 0:lanes], grads_out[4]))
            return parts

        def rs_route(u, act):
            for side in range(2):
                @pl.when(core == side)
                def _(side=side):
                    act((side + u) % 2 == 0)

        def on_route(u, step, act):
            if step in (1, 2):
                rs_route(u, act)
            else:
                act(True)

        def rs_pieces(u, step):
            if u in chunked and step < 3:
                return list(range(chunks if step < 2 else 2))
            return [0, 1] if u == wu_u and step == 3 else [None]

        def rs_start(layer, u, step, piece=None):
            if layer == 0 and step < 4 and not piece:
                rs_sent(1, u, step)
            if step == 3 and u in fast:
                start_owner(layer, u)
                return
            used = layer == 0 and not piece
            if u in chunked and step < 3:
                used = (layer == 0 or piece >= 2, layer == 0 and piece % 2 == 0, layer == 0)[step]
            if used and step < 4:
                pl.semaphore_wait(rs_free.at[u, step], 3 if step == 3 or (step == 1 and u in fast) else 1)

            if u == wd_u and step == 3:
                for k, copy in enumerate(rs_copies(layer, u, 3, True)):
                    @pl.when((z + k + 1) % 4 // 2 == piece)
                    def _(copy=copy):
                        copy.start()

                return

            def act(y_first):
                for copy in rs_copies(layer, u, step, y_first, piece):
                    copy.start()

            on_route(u, step, act)

        def give_back(u, step):
            def act(y_first):
                if step == 0:
                    peers = [mate]
                elif step == 3:
                    peers = along_z
                elif u in fast:
                    peers = plane_peers
                else:
                    peers = [near_y if y_first == (step == 1) else near_x]
                for peer in peers:
                    pl.semaphore_signal(rs_free.at[u, step], inc=1, device_id=peer, device_id_type=pl.DeviceIdType.MESH)

            on_route(u, step, act)

        def rs_merge(layer, u, step, piece=None):
            if step == 3 and u in fast:
                merge_owner(layer, u)
                return

            got = lands[u][step]
            sem = (piece or 0) % 2 if step < 3 else 0
            wait_at = land_at(u, step, piece) if step in (0, 2) else got
            if u in chunked and step == 1:
                wait_at = got.at[piece_planes(2, piece)] if u == wd_u else got.at[:, :, :, piece_cols(2, piece, u)]
            wait_bytes(wait_at, rs_recv.at[u, 2 * step + sem])
            slot = layer + 1
            buf = weight_buf[rs_weight[u]]
            cols = rs_cols.get(u, every)
            if step == 3:
                if layer == 0:
                    rs_home(1, u)
                total = buf[slot, z, y, x, core, :, cols].astype(f32)
                for k in range(3):
                    total = total + got[k].astype(f32)
                fin[u][...] = total
                if layer == 1:
                    give_back(u, 3)

                @pl.when(core == layer)
                def _():
                    for src, dst in home_parts(layer, u):
                        pltpu.make_async_copy(src, dst, sem_g.at[u]).start()

                @pl.when(core != layer)
                def _():
                    rs_start(layer, u, 4)

                return
            if step == 0 and piece is not None and u == wd_u:
                buf[slot, piece, :, :, core] += got[piece % 2]
            else:
                got_cols, planes = every, (0, 4)
                if piece is not None and u == wd_u:
                    planes = (2 * piece, 2 * piece + 2)
                elif piece is not None:
                    cols = piece_cols(step if step != 1 else 2, piece, u)
                    got_cols = piece_cols(0, piece % 2, u) if step == 0 else cols

                @pl.loop(*planes)
                def _(pz):
                    if step == 0:
                        buf[slot, pz, :, :, core, :, cols] += got[pz, :, :, :, got_cols]
                    elif u in fast:
                        total = buf[slot, pz, y, x, core, :, cols].astype(f32)
                        for k in range(3):
                            total = total + got[k, pz].astype(f32)
                        buf[slot, pz, y, x, core, :, cols] = total.astype(bf16)
                    elif step == 2:
                        buf[slot, pz, y, x, core, :, cols] += got[pz, :, got_cols]
                    else:
                        def add(y_first):
                            if y_first:
                                buf[slot, pz, y, :, core, :, cols] += got[pz, :, :, got_cols]
                            else:
                                buf[slot, pz, :, x, core, :, cols] += got[pz, :, :, got_cols]

                        rs_route(u, add)

            if layer == 1 or (step == 0 and u in chunked and piece < 2):
                give_back(u, step)
            rs_start(layer, u, 3 if u in fast and step == 1 else step + 1, piece)

        def rs_home(layer, u):
            @pl.when(core == layer)
            def _():
                if u == wqb_u:
                    wait_bytes(fin[u].at[:, :, lanes:], sem_g.at[u])
                    wait_bytes(fin[u].at[:, 0:8, 0:lanes], sem_g.at[5])
                else:
                    wait_bytes(fin[u], sem_g.at[u])
                if u not in fast:
                    for copy in rs_copies(layer, u, 4, True):
                        copy.wait_recv()

            if u not in fast:
                @pl.when(core != layer)
                def _():
                    for copy in rs_copies(layer, u, 4, True):
                        copy.wait_send()

        def rs_sent(layer, u, step):
            three = slice(0, 3)
            if step == 0:
                wait_bytes(spot(layer, u, every, every, every, other), rs_send.at[u, 0])
            elif step == 1 and u in fast:
                wait_bytes(spot(layer, u, three, every, every, core), rs_send.at[u, 1])
            elif step == 1:
                wait_bytes(spot(layer, u, every, y, every, core), rs_send.at[u, 1])
            elif step == 2:
                wait_bytes(spot(layer, u, every, y, x, core), rs_send.at[u, 2])
            elif u not in fast:
                wait_bytes(spot(layer, u, three, y, x, core), rs_send.at[u, 3])
            else:
                @pl.when(core == layer)
                def _():
                    wait_bytes(spot(layer, u, three, y, x, core), rs_send.at[u, 3])

                @pl.when(core != layer)
                def _():
                    wait_bytes(spot(layer, u, every, y, x, core), rs_send.at[u, 3])

        def rs_finish(layer, u):
            for step in (0, 1, 3) if u in fast else range(4):
                rs_sent(layer, u, step)

        def stat_copy(step, k=0):
            target = (mate, near_y, near_x)[step] if step < 3 else along_z[k]
            place_at = step if step < 3 else 3 + z
            return pltpu.make_async_remote_copy(
                src_ref=stat_sum.at[step],
                dst_ref=stat_land.at[place_at],
                send_sem=stat_send.at[step],
                recv_sem=stat_recv.at[step],
                device_id=target,
                device_id_type=pl.DeviceIdType.MESH,
            )

        def stat_step(step):
            if step == 0:
                stat_sum[0] = stat_ref[...]
            elif step < 4:
                stat_copy(step - 1).wait()
                stat_sum[step] = stat_sum[step - 1] + stat_land[step - 1]
            if step < 3:
                stat_copy(step).start()
            elif step == 3:
                stat_land[3 + z] = stat_sum[3]
                for k in range(3):
                    stat_copy(3, k).start()
            else:
                wait_bytes(stat_land.at[pl.ds(3, 3)], stat_recv.at[3])
                wait_bytes(stat_land.at[pl.ds(3, 3)], stat_send.at[3])
                total = stat_land[3] + stat_land[4] + stat_land[5] + stat_land[6]
                stat_ref[...] = total
                stat_done()

        stat_step(0)
        names = dict(a=wqa_u, o=wo_u, u=wu_u, d=wd_u, b=wqb_u)

        def run_events(layer, text):
            for word in text:
                if word[0] == "t":
                    stat_step(int(word[1]))
                    continue
                at_layer = layer
                if word[0] == "p":
                    at_layer, word = layer + 1, word[1:]
                step, u = int(word[1]), names[word[2]]
                piece = int(word[3]) if len(word) > 3 else None
                (rs_start if word[0] == "S" else rs_merge)(at_layer, u, step, piece)

        back_points = {
            (1, "ffn0"): ("t1", "S0d0", "S0u0"),
            (1, "ffn1"): ("t2", "M0d0", "M0u0", "S0d1", "S0u1"),
            (1, "ffn2"): ("t3", "M0d1", "M0u1", "S0d2", "S0u2"),
            (1, "ffn3"): ("t4", "M0d2", "M0u2", "S0d3", "S0u3"),
            (1, "mid0"): ("M0d3", "M0u3"),
            (1, "wo"): ("S0o", "M1d0", "M1u0"),
            (1, "att00"): ("M0o", "M1d1", "M1u1"),
            (1, "att01"): ("M2d0", "M2u0"),
            (1, "wq0"): ("S0a",),
            (1, "att10"): ("M0a", "M1o", "M2d1", "M2u1"),
            (1, "wq1"): ("S0b",),
            (1, "in0"): ("M0b", "M2o"),
            (1, "in1"): ("M1a",),
            (0, "ffn0"): ("S0d0", "S0u0"),
            (0, "ffn1"): ("M0d0", "M0u0", "S0d1", "S0u1", "pM1b", "pM3d", "pM3u"),
            (0, "ffn2"): ("M0d1", "M0u1", "S0d2", "S0u2", "pM3o", "pM3a"),
            (0, "ffn3"): ("M0d2", "M0u2", "S0d3", "S0u3", "pM3b"),
            (0, "mid0"): ("M0d3", "M0u3"),
            (0, "wo"): ("S0o", "M1d0", "M1u0"),
            (0, "att00"): ("M0o", "M1d1", "M1u1"),
            (0, "att01"): ("M2d0", "M2u0"),
            (0, "wq0"): ("S0a",),
            (0, "att10"): ("M0a", "M1o", "M2d1", "M2u1"),
            (0, "wq1"): ("S0b", "M1a", "M0b"),
            (0, "in0"): ("M2o",),
            (0, "end"): ("M1b", "M3d", "M3u", "M3o", "M3a", "M3b"),
        }
    else:
        back_points = {}

    def stat_done():
        totals = stat_ref[...]
        stat_out[...] = totals if not routed else jnp.sqrt(totals / (totals[0:1, 3:4, :] * width))

    if not routed:
        stat_done()

    def back_point(layer, point, s=None, at=None):
        for (at_layer, at_point), text in back_points.items():
            if at_point == point:
                here = layer == at_layer
                if s is not None:
                    here = here & (s == at)

                @pl.when(here)
                def _(at_layer=at_layer, text=text):
                    run_events(at_layer, text)

    def norm_back(x, gain, grad):
        inv = lax.rsqrt(jnp.mean(x * x, axis=1, keepdims=True) + norm_eps)
        hat = x * inv
        scaled = grad * gain
        return inv * (scaled - hat * jnp.mean(scaled * hat, axis=1, keepdims=True))

    def add_gain(k, d_weight, weight):
        for p in range(d_weight.shape[1] // lanes):
            cols = slice(p * lanes, (p + 1) * lanes)
            gain_sums[k] += d_weight[:, cols] * weight[:, cols].astype(f32)

    def pack_small(layer):
        turned = dbias[...].T
        for h in range(heads):
            ext[pl.ds(h, slots, stride=heads), :] = jnp.broadcast_to(turned[:slots, h : h + 1], (slots, lanes))
        lane = lax.broadcasted_iota(jnp.int32, (width, lanes), 1)
        gain = mat(0, layer, slice(0, lanes)).astype(f32)
        sums = [jnp.sum(gain_sums[k], axis=1, keepdims=True) for k in range(2)]
        safe = jnp.where(lane < 2, gain, 1.0)
        value = jnp.where(lane == 0, sums[0], jnp.where(lane == 1, sums[1], 0.0)) / safe
        value = jnp.where(lane == 2, ext[...], value)
        put_mat(0, layer + 1, value.astype(bf16), slice(3 * quad, 3 * quad + lanes))

    def backward_ffn(layer):
        slot = layer + 1

        @pl.loop(0, segs)
        def _(s):
            at = seg_rows(s)
            h = hbuf[at, :].astype(f32)
            doa[0, at, :] = (h * lax.rsqrt(jnp.mean(h * h, axis=1, keepdims=True) + norm_eps) * gains[layer, 1]).astype(bf16)

        dn[...] = jnp.zeros_like(dn)
        gain_sums[...] = jnp.zeros_like(gain_sums)
        dbias[...] = jnp.zeros_like(dbias)
        turned_cols = slice(0, segs * rows)
        put_mat(0, slot, doa[0].T, turned_cols)

        @pl.loop(0, ff // chunk)
        def _(c):
            cols = pl.ds(pl.multiple_of(c * chunk, chunk), chunk)
            planes = pl.ds(c, 1)
            d_pre = (nt(dy[...], mat(3, layer, planes=planes)) * slope[:, cols].astype(f32)).astype(bf16)
            put_mat(3, slot, tn(active[:, cols], dy[...]).astype(bf16), planes=planes)
            d_up = mm(mat(0, slot, turned_cols), d_pre)
            add_gain(1, d_up, mat(2, layer, cols))
            put_mat(2, slot, d_up.astype(bf16), cols)
            dn[...] += nt(d_pre, mat(2, layer, cols))
            for k in range(ff // chunk):
                back_point(layer, "ffn" + str(k), c, k)

    def backward_middle(layer, s):
        at = seg_rows(s)
        dh = norm_back(hbuf[at, :].astype(f32), gains[layer, 1], dn[at, :])
        dh = dh + dy[at, :].astype(f32)
        dn[at, :] = dh
        dz = dh.astype(bf16)
        dy[at, :] = dz
        do = nt(dz, mat(1, layer)) * ilbuf[at, :].astype(f32)
        prod = do.astype(bf16).astype(f32) * obuf[at, :].astype(f32)
        for p in range(pairs):
            cols = slice(p * lanes, (p + 1) * lanes)
            for side in range(2):
                own, marks = lane_marks(head_size, side)
                delta = -jnp.sum(prod[:, cols] * own, axis=1, keepdims=True)
                hi = delta.astype(bf16).astype(f32)
                fill = hi * marks[0] + (delta - hi) * marks[1]
                doa[side, at, cols] = (do[:, cols] * (1.0 - marks[0] - marks[1]) + fill).astype(bf16)

    def backward_attention(layer, q, s):
        at = seg_rows(s)
        for p in range(2):
            cols, kcols, vcols = (
                pl.ds(pl.multiple_of(k * width + q * quad + p * lanes, lanes), lanes) for k in range(3)
            )
            qp = qkv[at, cols]
            kp = qkv[at, kcols]
            vp = qkv[at, vcols]
            q_turned = qp.T
            dq, dk, dv = [], [], []
            for side in range(2):
                h = 4 * q + 2 * p + side
                own, marks = lane_marks(head_size, side)
                do_h = doa[side, at, cols]
                va = vp * own.astype(bf16) + (marks[0] + marks[1]).astype(bf16)
                weights = ebuf[s, h]
                d_scores = weights.astype(f32) * nt(do_h, va)
                dbias[pl.ds(h, 1), :] += jnp.sum(d_scores[:, :lanes], axis=0, keepdims=True)
                d_scores = d_scores.astype(bf16)
                half = slice(side * head_size, (side + 1) * head_size)
                dq.append(mm(d_scores, kp))
                dk.append(mm(q_turned[half, :], d_scores))
                dv.append(mm(do_h.T[half, :], weights))
            own, _ = lane_marks(head_size, 0)
            qkv[at, cols] = (jnp.where(own > 0, dq[0], dq[1]) * score_scale).astype(bf16)
            qkv[at, kcols] = (jnp.concatenate(dk, axis=0).T * (1.0 / log2_e)).astype(bf16)
            qkv[at, vcols] = jnp.concatenate(dv, axis=0).T.astype(bf16)

    def backward_input(layer, s):
        at = seg_rows(s)
        x = ub[at, :].astype(f32)
        du = norm_back(x, gains[layer, 0], nt(qkv[at, :], mat(0, layer, slice(lanes, lanes + 3 * width))))
        dy[at, :] = (du + dn[at, :]).astype(bf16)

    def grad_col(q, k):
        return q * (3 * quad + lanes) + k * quad

    def grad_copies(layer):
        return [
            pltpu.make_async_copy(buf.at[layer + 1], out.at[layer], sem_g.at[k])
            for k, (buf, out) in enumerate(zip(weight_buf, grads_out))
        ]

    @pl.loop(0, 2)
    def _(step):
        layer = 1 - step
        slot = layer + 1

        @pl.when(layer == 0)
        def _():
            for s in range(segs):
                for copy in spill_copies(s, True, (2, 3, 4, 5, 6)):
                    copy.wait()

        backward_ffn(layer)

        @pl.when(layer == 1)
        def _():
            wait_rows(doa.at[1], 3)

        @pl.loop(0, segs)
        def _(s):
            backward_middle(layer, s)
            back_point(layer, "mid0", s, 0)

        put_mat(1, slot, tn(obuf[...], dy[...]).astype(bf16))
        back_point(layer, "wo")

        @pl.when(layer == 1)
        def _():
            for s in range(segs):
                for copy in spill_copies(s, True, (2, 3, 4, 5, 6)):
                    copy.start()

        @pl.loop(0, segs)
        def _(s):
            at = seg_rows(s)

            @pl.when(layer == 0)
            def _():
                spill_copies(s, True, (7,))[0].wait()

            v = ub[at, :].astype(f32)
            dy[at, :] = (v * lax.rsqrt(jnp.mean(v * v, axis=1, keepdims=True) + norm_eps) * gains[layer, 0]).astype(bf16)

        @pl.loop(0, quads)
        def _(q):
            @pl.loop(0, segs)
            def _(s):
                @pl.when((layer == 0) & (q == 0))
                def _():
                    for copy in spill_copies(s, True, (0, 1)):
                        copy.wait()

                backward_attention(layer, q, s)

                @pl.when((layer == 1) & (q == quads - 1))
                def _():
                    spill_copies(s, True, (1,))[0].start()

                for i in range(quads):
                    for k in range(segs):
                        back_point(layer, "att" + str(i) + str(k), q * segs + s, i * segs + k)

            for k in range(3):
                d_weight = tn(dy[...], qkv[:, pl.ds(pl.multiple_of(k * width + q * quad, quad), quad)])
                add_gain(0, d_weight, mat(0, layer, pl.ds(pl.multiple_of(lanes + k * width + q * quad, lanes), quad)))
                put_mat(0, slot, d_weight.astype(bf16), pl.ds(pl.multiple_of(grad_col(q, k), lanes), quad))

            @pl.when(q == quads - 1)
            def _():
                pack_small(layer)

            for i in range(quads):
                back_point(layer, "wq" + str(i), q, i)

        @pl.loop(0, segs)
        def _(s):
            backward_input(layer, s)
            for k in range(segs):
                back_point(layer, "in" + str(k), s, k)

        @pl.when(layer == 1)
        def _():
            for s in range(segs):
                for copy in spill_copies(s, True, (0, 7)):
                    copy.start()

        if not routed:
            for copy in grad_copies(layer):
                copy.start()
            for copy in grad_copies(layer):
                copy.wait()

    for copies in du_copies:
        for copy in copies:
            copy.start()
    back_point(0, "end")
    if routed:
        for u in range(5):
            rs_finish(0, u)
    if routed:
        for u in range(5):
            rs_home(0, u)
        for u in (0, 4):
            rs_home(1, u)
    wait_rows(dy, 6)


def run_layers(dims, routed, doc_len, row_args, weights):
    segs, rows, width, ff, slots, heads, per_doc = dims
    all_rows = segs * rows
    vmem = pl.BlockSpec(memory_space=pltpu.VMEM)
    smem = pl.BlockSpec(memory_space=pltpu.SMEM)
    hbm = pl.BlockSpec(memory_space=pl.ANY)
    shape = jax.ShapeDtypeStruct
    dma = pltpu.SemaphoreType.DMA
    wide = (all_rows, width)
    tiles = [
        (width // 32, lanes + 3 * width),
        (width // 32, width),
        (width // 32, ff),
        (ff // 32, width),
    ]
    out_shape = [shape(part.shape, bf16) for part in row_args]
    if routed:
        out_shape += [shape((2, width // 32, 3 * width), f32)]
        out_shape += [shape((2, *tile), f32) for tile in tiles[1:]]
        out_shape += [shape((2, 8, lanes), f32)]
    else:
        out_shape += [shape((2, 4, 2, 2, 2, *tile), bf16) for tile in tiles]
    row_outs = len(out_shape)
    out_shape += [shape((2, 8, lanes), f32)]
    out_shape += [
        shape((all_rows, 3 * width), bf16),
        shape((segs, heads, rows, rows), bf16),
        shape(wide, bf16),
        shape(wide, bf16),
        shape((all_rows, ff), bf16),
        shape((all_rows, ff), bf16),
        shape(wide, bf16),
        shape(wide, bf16),
    ]
    unit_count = 16
    scratch = [pltpu.VMEM((3, 4, 2, 2, 2, *tile), bf16) for tile in tiles]
    scratch += [
        pltpu.VMEM(wide, bf16),
        pltpu.VMEM(wide, bf16),
        pltpu.VMEM((all_rows, 3 * width), bf16),
        pltpu.VMEM((segs, heads, rows, rows), bf16),
        pltpu.VMEM(wide, bf16),
        pltpu.VMEM(wide, bf16),
        pltpu.VMEM(wide, bf16),
        pltpu.VMEM((all_rows, ff), bf16),
        pltpu.VMEM((all_rows, ff), bf16),
        pltpu.VMEM((2, *wide), bf16),
        pltpu.VMEM(wide, f32),
        pltpu.VMEM((2, 2, 1, width), f32),
        pltpu.VMEM((heads, slots, lanes), f32),
        pltpu.VMEM((width, lanes), f32),
        pltpu.VMEM((2, width, lanes), f32),
        pltpu.VMEM((heads, lanes), f32),
        pltpu.VMEM((2, 8, lanes), f32),
        dma((segs, 8)),
        dma((segs, 8)),
        dma((8,)),
        dma((9,)),
        dma((unit_count, 2)),
        dma((unit_count, 6)),
    ]
    params = dict(vmem_limit_bytes=127 * 2**19)
    if routed:
        params.update(collective_id=0, has_side_effects=True)
        half_cols = 3 * width // 2
        rs_tiles = [(width // 32, half_cols), *tiles[1:], (width // 32, half_cols + lanes)]
        first_tiles = [(4, 2, 2, *tile) for tile in rs_tiles]
        first_tiles[2] = (4, 2, 2, width // 32, 2 * chunk)
        first_tiles[3] = (2, 2, 2, ff // 32, width)
        for u, (first, tile) in enumerate(zip(first_tiles, rs_tiles)):
            leads = ((3, 4), (1,), (2, 4)) if u in (0, 4) else ((4, 2), (4,), (3,))
            scratch += [pltpu.VMEM(first, bf16)]
            scratch += [pltpu.VMEM((*lead, *tile), bf16) for lead in leads]
        scratch += [pltpu.VMEM((2, *tile) if u in (0, 4) else tile, f32) for u, tile in enumerate(rs_tiles)]
        scratch += [
            pltpu.VMEM((4, 2, 8, lanes), f32),
            pltpu.VMEM((7, 2, 8, lanes), f32),
            dma((5, 5)),
            dma((5, 8)),
            pltpu.SemaphoreType.REGULAR((5, 4)),
            dma((4,)),
            dma((4,)),
        ]
    return pl.pallas_call(
        partial(fused_layers, dims, routed),
        out_shape=out_shape,
        in_specs=[smem] + [hbm] * (len(row_args) + len(weights)),
        out_specs=[hbm] * row_outs + [vmem] + [hbm] * (len(out_shape) - row_outs - 1),
        scratch_shapes=scratch,
        compiler_params=pltpu.CompilerParams(**params),
    )(doc_len, *row_args, *weights)[: row_outs + 1]


def settle_kernel(*refs):
    count = (len(refs) - 7) // 3
    srcs, (small, stats) = refs[:count], refs[count : count + 2]
    dsts = refs[count + 2 : 2 * count + 2]
    vectors, rms = refs[2 * count + 2 : 2 * count + 5], refs[2 * count + 5]
    mids, sems = refs[2 * count + 6 : -1], refs[-1]
    inward = [pltpu.make_async_copy(src, mid, sems.at[0, k]) for k, (src, mid) in enumerate(zip(srcs, mids))]
    outward = [pltpu.make_async_copy(mid, dst, sems.at[1, k]) for k, (mid, dst) in enumerate(zip(mids, dsts))]
    for copy in inward:
        copy.start()
    for k, vector in enumerate(vectors):
        size = vector.shape[1] // 2
        vector[...] = jnp.concatenate([small[half, k : k + 1, :size] for half in range(2)], axis=1)
    lane = lax.broadcasted_iota(jnp.int32, (1, lanes), 1)
    for layer in range(2):
        row = sum(jnp.where(lane == k, stats[layer, k : k + 1, :], 0.0) for k in range(3))
        rms[layer : layer + 1, :] = row[:, :3]
    for into, out in zip(inward, outward):
        into.wait()
        out.start()
    for out in outward:
        out.wait()


def settle(big, small, stats):
    vmem = pl.BlockSpec(memory_space=pltpu.VMEM)
    hbm = pl.BlockSpec(memory_space=pl.ANY)
    shape = jax.ShapeDtypeStruct
    size = 2 * big[4].shape[1]
    return pl.pallas_call(
        settle_kernel,
        out_shape=[shape(part.shape, part.dtype) for part in big] + [shape((1, size), f32)] * 3 + [shape((2, 3), f32)],
        in_specs=[hbm] * len(big) + [vmem] * 2,
        out_specs=[hbm] * len(big) + [vmem] * 4,
        scratch_shapes=[pltpu.VMEM(part.shape, part.dtype) for part in big] + [pltpu.SemaphoreType.DMA((2, len(big)))],
    )(*big, small, stats)


def swap(block):
    return lax.ppermute(block, "section", [(0, 1), (1, 0)])


def body(
    tokens,
    memory,
    lengths,
    w_qkv,
    w_out,
    w_up,
    w_down,
    gain_attn,
    gain_ffn,
    forget_bias,
    grad_tokens,
    grad_memory,
):
    section = lax.axis_index("section")
    is_first = section == 0
    micro = tokens.shape[0]
    segs = micro // 2
    half_tok = tokens.shape[1]
    half_mem = memory.shape[1]
    slots = 2 * half_mem
    rows = slots + 2 * half_tok
    width = tokens.shape[2]
    ff = w_up.shape[2]
    heads = forget_bias.shape[1] * lax.axis_size("dp") // slots
    per_doc = micro // lengths.shape[0]
    dims = (segs, rows, width, ff, slots, heads, per_doc)
    small = jnp.stack([gain_attn, gain_ffn, forget_bias], axis=2)
    small = jnp.pad(small, ((0, 0), (0, 0), (0, lanes - 3)))

    if lax.axis_size("dp") == 16 and w_qkv.shape[1] == 32:
        pieces = (w_qkv, w_out, w_up, w_down, small)
        weights = [piece.reshape(2, -1, piece.shape[2]) for piece in pieces]
        row_args = (tokens, memory, grad_tokens, grad_memory)
        *outs, small_grads, stats = run_layers(dims, True, lengths, row_args, weights)
        outs = settle(outs, small_grads, stats)
        mats = [grad.reshape(1, -1, grad.shape[2]) for grad in outs[4:8]]
        return (*outs[:4], *mats, *outs[8:])

    own_len = lax.dynamic_slice_in_dim(lengths, section * segs // per_doc, segs // per_doc, 0)
    pieces = (jnp.concatenate([small, w_qkv], axis=2), w_out, w_up, w_down)

    def unpack(grads):
        mat = grads[0]
        half = 3 * width // 2
        parts = [mat[:, :, :half], mat[:, :, half + lanes :]]
        parts = [part.reshape(1, -1, 3, width // 2) for part in parts]
        whole = jnp.concatenate(parts, axis=3).reshape(1, -1, 3 * width)
        return (whole, *grads[1:], *(mat[:, :, half + k] for k in range(3)))

    def own_segs(halves):
        return lax.dynamic_slice_in_dim(halves, section * segs, segs, 0)

    def other_segs(halves):
        return lax.dynamic_slice_in_dim(halves, (1 - section) * segs, segs, 0)

    def both(kept, got):
        return jnp.concatenate(
            [jnp.where(is_first, kept, got), jnp.where(is_first, got, kept)], axis=1
        )

    inputs = (tokens, memory, grad_tokens, grad_memory)
    got = swap(tuple(other_segs(part) for part in inputs))
    full = [both(own_segs(part), other) for part, other in zip(inputs, got)]
    u0 = jnp.concatenate([full[1], full[0]], axis=1).reshape(segs * rows, width)
    dout = jnp.concatenate([full[3], full[2]], axis=1).reshape(segs * rows, width)

    def gather(piece):
        whole = lax.all_gather(piece, ("section", "dp"), axis=1, tiled=True)
        return whole.reshape(2, 4, 2, 2, 2, -1, piece.shape[2])

    y, du, *grads, stats = run_layers(dims, False, own_len, (u0, dout), [gather(piece) for piece in pieces])

    def scatter(grad):
        grad = grad.reshape(2, -1, grad.shape[-1])
        mine = lax.dynamic_index_in_dim(grad, section, 0, keepdims=True)
        other = lax.dynamic_index_in_dim(grad, 1 - section, 0, keepdims=True)
        chip = (mine.astype(f32) + swap(other).astype(f32)).astype(grad.dtype)
        return lax.psum_scatter(chip, "dp", scatter_dimension=1, tiled=True).astype(f32)

    shares = unpack([scatter(grad) for grad in grads])
    totals = lax.psum(stats[:, :4, 0], ("section", "dp"))
    rms = jnp.sqrt(totals[:, :3] / (totals[0, 3] * width))
    result = jnp.stack([y.reshape(segs, rows, width), du.reshape(segs, rows, width)])

    def half_of(which):
        tok = lax.dynamic_slice_in_dim(result, slots + which * half_tok, half_tok, 2)
        mem = lax.dynamic_slice_in_dim(result, which * half_mem, half_mem, 2)
        return tok, mem

    kept = half_of(section)
    got = swap(half_of(1 - section))

    def order(mine, other):
        return jnp.concatenate(
            [jnp.where(is_first, mine, other), jnp.where(is_first, other, mine)], axis=0
        )

    toks = [order(kept[0][k], got[0][k]) for k in range(2)]
    mems = [order(kept[1][k], got[1][k]) for k in range(2)]
    return (toks[0], mems[0], toks[1], mems[1], *shares, rms)


def solution(mesh):
    rows = P("dp", "section", None)
    mats = P("section", "dp", None)
    vecs = P("section", "dp")
    return jax.shard_map(
        body,
        mesh=mesh,
        in_specs=(rows, rows, P("dp"), mats, mats, mats, mats, vecs, vecs, vecs, rows, rows),
        out_specs=(rows, rows, rows, rows, mats, mats, mats, mats, vecs, vecs, vecs, P()),
        check_vma=False,
    )
```

```python
from functools import partial

import jax
import jax.numpy as jnp
from jax import lax
from jax.experimental import pallas as pl
from jax.experimental.pallas import tpu as pltpu
from jax.sharding import PartitionSpec as P

norm_eps = 1e-06
score_scale = 0.125
log2_e = 1.4426950408889634
masked_score = -1000000000.0
gelu_c = 0.7978845608028654
gelu_k = 0.044715
f32 = jnp.float32
bf16 = jnp.bfloat16
lanes = 128
chunk = 512


def mm(a, b, ca=1, cb=0):
    return lax.dot_general(a, b, (((ca,), (cb,)), ((), ())), preferred_element_type=f32)


def nt(a, b):
    return mm(a, b, 1, 1)


def tn(a, b):
    return mm(a, b, 0, 0)


def lane_marks(head_size, side):
    lane = lax.broadcasted_iota(jnp.int32, (1, lanes), 1)
    own = ((lane // head_size) == side).astype(f32)
    first = (1 - side) * head_size
    marks = [(lane == first + k).astype(f32) for k in range(3)]
    return own, marks


def fused_layers(dims, routed, *refs):
    segs, rows, width, ff, slots, heads, per_doc = dims
    refs = list(refs)

    def take(count):
        picked = refs[:count]
        del refs[:count]
        return picked

    (len_ref,) = take(1)
    rows_in = take(4 if routed else 2)
    weight_in = take(4)
    vectors_in = take(3) if routed else []
    rows_out = take(4 if routed else 2)
    grads_out = take(5 if routed else 4)
    (stat_out,) = take(1)
    spill_hbm = take(8)
    weight_buf = take(4)
    ub, dy, qkv, ebuf, obuf, ilbuf, hbuf, slope, active, doa, dn = take(11)
    gains, gain_sums, dbias, stat_ref = take(4)
    sem_spill, sem_g, sem_io, sem_send, sem_recv = take(5)
    if routed:
        lands = [take(4) for _ in range(5)]
        fin = take(5)
        stat_sum, stat_land, small_buf = take(3)
        weight_in = [*weight_in, small_buf]
        rs_send, rs_recv, rs_free, stat_send, stat_recv = take(5)
    head_size = width // heads
    pairs = width // lanes
    tok_rows = rows - slots
    quads = width // (2 * lanes)
    quad = 2 * lanes
    first_doc = lax.axis_index("section") * segs // per_doc if routed else 0
    every = slice(None)

    def wait_bytes(ref, sem):
        pltpu.make_async_copy(ref, ref, sem).wait()

    def units_of(layer):
        half_ff, half_deep = ff // 2, ff // 64
        lead = [
            (0, slice(0, lanes + width), every),
            (0, slice(lanes + width, lanes + 2 * width), every),
            (0, slice(lanes + 2 * width, lanes + 3 * width), every),
        ]
        rest = [(1, every, every)]
        rest += [(3, every, slice(k * half_deep, (k + 1) * half_deep)) for k in range(2)]
        rest += [(2, slice(k * half_ff, (k + 1) * half_ff), every) for k in range(2)]
        return [(layer, *unit) for unit in lead + rest]

    units = units_of(0) + units_of(1)
    first_units = [k for k, unit in enumerate(units) if unit[1] == 0]
    last_units = [7, 15]
    later_units = [k for k, unit in enumerate(units) if unit[1] != 0 and k not in last_units]
    plane_first = (11, 15)

    def view(n, z, y, x, c):
        layer, which, cols, part = units[n]
        return weight_buf[which].at[layer, z, y, x, c, part, cols]

    if routed:
        core = lax.axis_index("section")
        chip = lax.axis_index("dp")
        z, y, x = chip // 4, (chip // 2) % 2, chip % 2
        other = 1 - core

        def place(pz, py, px):
            return pz * 4 + py * 2 + px

        mate = (other, chip)
        near_x = (core, place(z, y, 1 - x))
        near_y = (core, place(z, 1 - y, x))
        along_z = [(core, place((z + k) % 4, y, x)) for k in range(1, 4)]

        def remote(src, dst, n, k, target):
            far = k in (4, 5, 9, 10) or (k in (0, 11) and n in plane_first)
            arrived = {0: 0, 11: 0, 1: 1, 2: 1, 3: 1, 4: 2, 5: 3, 6: 4, 7: 4, 8: 4, 9: 5, 10: 5}[k]
            return pltpu.make_async_remote_copy(
                src_ref=src,
                dst_ref=dst,
                send_sem=sem_send.at[n, int(far)],
                recv_sem=sem_recv.at[n, arrived],
                device_id=target,
                device_id_type=pl.DeviceIdType.MESH,
            )

        def some(n, shards, half):
            return view(n, slice(0, 3), y, x, half) if shards == 3 else view(n, slice(0, 3), every, every, half)

        def own_shards(n):
            layer, which, cols, part = units[n]
            home = weight_buf[which].at[layer, z, y, x]
            if which > 0:
                return [(weight_in[which].at[every, part, cols], home.at[every, part, cols], 0)]
            start = max(cols.start - lanes, 0)
            matrix = slice(start, cols.stop - lanes)
            pairs_of = [(weight_in[0].at[every, every, matrix], home.at[every, every, slice(start + lanes, cols.stop)], 0)]
            if cols.start == 0:
                pairs_of.append((weight_in[4], home.at[every, every, slice(0, lanes)], 11))
            return pairs_of

        def z_copy(n, k):
            where = view(n, z, every, every, core) if n in plane_first else view(n, z, y, x, core)
            return remote(where, where, n, k, along_z[k - 1])

        def plane_copy(n, k, x_first):
            planes = z if n in plane_first else every
            if k == 4:
                where = view(n, planes, y, x, core)
                return remote(where, where, n, 4, near_x if x_first else near_y)
            where = view(n, planes, y, every, core) if x_first else view(n, planes, every, x, core)
            return remote(where, where, n, 5, near_y if x_first else near_x)

        def mate_copy(n, k, x_first, half):
            planes = z if n in plane_first else every
            if k < 9:
                from_z = (z + 4 - (k - 5)) % 4
                where = view(n, from_z, every, every, half) if n in plane_first else view(n, from_z, y, x, half)
            elif k == 9:
                where = view(n, planes, y, 1 - x, half) if x_first else view(n, planes, 1 - y, x, half)
            else:
                where = view(n, planes, 1 - y, every, half) if x_first else view(n, planes, every, 1 - x, half)
            return remote(where, where, n, k, mate)

        def by_route(n, act):
            for side in range(2):
                @pl.when(core == side)
                def _(side=side):
                    act((side + n) % 2 == 0)

        def share_own(n):
            @pl.when(core == units[n][0])
            def _():
                for src, dst, k in own_shards(n):
                    pltpu.make_async_copy(src, dst, sem_recv.at[n, 0]).start()
                    remote(src, dst, n, k, mate).start()

        def start_z(n):
            wait_bytes(view(n, z, y, x, every), sem_recv.at[n, 0])
            if n in plane_first:
                by_route(n, lambda x_first: plane_copy(n, 4, x_first).start())
            else:
                for k in range(1, 4):
                    z_copy(n, k).start()

        def first_hop(n):
            if n not in plane_first:
                wait_bytes(some(n, 3, core), sem_recv.at[n, 1])

            def act(x_first):
                if n in plane_first:
                    plane_copy(n, 4, x_first).wait_recv()
                    plane_copy(n, 5, x_first).start()
                    mate_copy(n, 9, x_first, core).start()
                else:
                    plane_copy(n, 4, x_first).start()
                    for k in range(6, 9):
                        mate_copy(n, k, x_first, core).start()

            by_route(n, act)

        def second_hop(n):
            def act(x_first):
                if n in plane_first:
                    plane_copy(n, 5, x_first).wait_recv()
                    for k in range(1, 4):
                        z_copy(n, k).start()
                    mate_copy(n, 10, x_first, core).start()
                else:
                    plane_copy(n, 4, x_first).wait_recv()
                    plane_copy(n, 5, x_first).start()
                    mate_copy(n, 9, x_first, core).start()

            by_route(n, act)

        def last_share(n):
            def act(x_first):
                if n in plane_first:
                    wait_bytes(some(n, 12, core), sem_recv.at[n, 1])
                    for k in range(6, 9):
                        mate_copy(n, k, x_first, core).start()
                else:
                    plane_copy(n, 5, x_first).wait_recv()
                    mate_copy(n, 10, x_first, core).start()

            by_route(n, act)

        def complete(n):
            near, rest = (12, 3) if n in plane_first else (3, 12)
            wait_bytes(some(n, near, other), sem_recv.at[n, 4])
            wait_bytes(some(n, rest, other), sem_recv.at[n, 5])

        def drain(n):
            few, many = (1, 0) if n in plane_first else (0, 1)
            wait_bytes(view(n, slice(0, 3), every, every, every), sem_send.at[n, many])

            @pl.when(core == units[n][0])
            def _():
                wait_bytes(view(n, every, y, x, every), sem_send.at[n, few])

            @pl.when(core != units[n][0])
            def _():
                wait_bytes(view(n, slice(0, 3), y, x, every), sem_send.at[n, few])

        def hops(text):
            kinds = dict(z=start_z, f=first_hop, s=second_hop, l=last_share)
            for word in text:
                kinds[word[0]](int(word[1:]))

        opening = ("z0", "z1", "z2", "z3", "z4", "z5", "f0", "f1", "s0", "z6", "f2", "s1", "z7", "f3", "s2", "l0", "f4", "s3", "l1", "f5", "s4", "f6", "l2", "z8", "z9", "z11")
        hops_at = {
            (0, 0, "qkv"): ("s5", "f7", "z10", "z15"),
            (0, 0, "quad0"): ("s6", "z12", "l3"),
            (0, 0, "quad1"): ("f8", "f11", "z13"),
            (0, 1, "qkv"): ("s7", "f9", "l4"),
            (0, 1, "quad0"): ("f10", "s8", "z14", "f15", "l5"),
            (0, 1, "quad1"): ("l6", "s9", "s11"),
            (0, 0, "gate"): ("f12",),
            (0, 0, "ffna"): ("l7", "s10", "f13"),
            (0, 1, "ffna"): ("s15",),
            (0, 0, "ffnb"): ("s12", "l8", "f14"),
            (0, 1, "ffnb"): ("s13", "l9", "l10"),
            (1, 0, "quad0"): ("s14",),
            (1, 1, "qkv"): ("l12", "l13"),
            (1, 1, "quad0"): ("l11", "l14"),
            (1, 1, "quad1"): ("l15",),
        }
    else:
        hops_at = {}

        def weight_copy(n):
            layer, which, cols, part = units[n]
            src = weight_in[which].at[layer, every, every, every, every, part, cols]
            return pltpu.make_async_copy(src, view(n, every, every, every, every), sem_recv.at[n, 0])

        def complete(n):
            weight_copy(n).wait()

    def after(layer, s, point):
        for (at_layer, at_s, at_point), text in hops_at.items():
            if at_point == point:
                @pl.when((layer == at_layer) & (s == at_s))
                def _(text=text):
                    hops(text)

    def need(layer, picks):
        for at_layer in range(2):
            @pl.when(layer == at_layer)
            def _(at_layer=at_layer):
                for n in picks:
                    if units[n][0] == at_layer:
                        complete(n)

    def mat(which, slot, cols=every, planes=None):
        if planes is None:
            value = weight_buf[which][slot, :, :, :, :, :, cols]
        else:
            value = weight_buf[which][slot, planes, :, :, :, :, cols]
        deep = 1
        for size in value.shape[:-1]:
            deep *= size
        return value.reshape(deep, value.shape[-1])

    def put_mat(which, slot, value, cols=every, planes=None):
        buf = weight_buf[which]
        shape = buf.shape[1:-1]
        if planes is None:
            buf[slot, :, :, :, :, :, cols] = value.reshape(*shape, value.shape[-1])
        else:
            buf[slot, planes] = value.reshape(1, *shape[1:], value.shape[-1])

    def qkv_cols(k):
        return slice(lanes + k * width, lanes + (k + 1) * width)

    def seg_rows(s):
        return pl.ds(pl.multiple_of(s * rows, rows), rows)

    def spill_copies(s, back, picks=range(7)):
        at = seg_rows(s)
        kept = (qkv.at[at], ebuf.at[s], obuf.at[at], ilbuf.at[at], slope.at[at], active.at[at], hbuf.at[at], ub.at[at])
        pairs_of = [
            (vmem, hbm.at[s] if k == 1 else hbm.at[at])
            for k, (vmem, hbm) in enumerate(zip(kept, spill_hbm))
        ]
        if back:
            return [
                pltpu.make_async_copy(hbm, vmem, sem_spill.at[s, k])
                for k, (vmem, hbm) in enumerate(pairs_of)
                if k in picks
            ]
        return [
            pltpu.make_async_copy(vmem, hbm, sem_spill.at[s, k])
            for k, (vmem, hbm) in enumerate(pairs_of)
            if k in picks
        ]

    def doc_end(s):
        return len_ref[first_doc + s // per_doc] - (s % per_doc) * tok_rows

    def valid_rows(s):
        row = lax.broadcasted_iota(jnp.int32, (rows, lanes), 0)
        return jnp.where(
            (row >= slots) & (row - slots < doc_end(s)), 1.0, 0.0
        ).astype(f32)

    def mask_col(s):
        row = lax.broadcasted_iota(jnp.int32, (rows, 1), 0)
        return jnp.where(
            (row >= slots) & (row - slots >= doc_end(s)), masked_score, 0.0
        ).astype(f32)

    if routed:
        half_tok, half_mem = tok_rows // 2, slots // 2

        def io_copies(buf, tok_ref, mem_ref, sems, outward):
            local, away = [], []
            own_sem, send_sem, recv_sem = (sem_io.at[k] for k in sems)
            for s in range(segs):
                mine, theirs = core * segs + s, other * segs + s
                for ref, base, size in ((tok_ref, slots, half_tok), (mem_ref, 0, half_mem)):
                    def rows_of(half):
                        return buf.at[pl.ds(pl.multiple_of(s * rows + base + half * size, 16), size)]

                    if outward:
                        local.append(pltpu.make_async_copy(rows_of(core), ref.at[mine], own_sem))
                        src, dst = rows_of(other), ref.at[mine]
                    else:
                        local.append(pltpu.make_async_copy(ref.at[mine], rows_of(core), own_sem))
                        src, dst = ref.at[theirs], rows_of(core)
                    away.append(
                        pltpu.make_async_remote_copy(
                            src_ref=src,
                            dst_ref=dst,
                            send_sem=send_sem,
                            recv_sem=recv_sem,
                            device_id=mate,
                            device_id_type=pl.DeviceIdType.MESH,
                        )
                    )
            return local, away

        def half_rows(buf):
            return buf.at[pl.ds(0, segs * rows // 2)]

        loads, shares = io_copies(ub, rows_in[0], rows_in[1], (0, 2, 0), False)
        more = io_copies(dy, rows_in[2], rows_in[3], (1, 2, 1), False)
        loads, shares = loads + more[0], shares + more[1]
        y_copies = io_copies(doa.at[1], rows_out[0], rows_out[1], (3, 4, 5), True)
        du_copies = io_copies(dy, rows_out[2], rows_out[3], (6, 7, 8), True)
    else:
        loads = [
            pltpu.make_async_copy(rows_in[0], ub, sem_io.at[0]),
            pltpu.make_async_copy(rows_in[1], dy, sem_io.at[1]),
        ]
        shares = []
        y_copies = [pltpu.make_async_copy(doa.at[1], rows_out[0], sem_io.at[3])], []
        du_copies = [pltpu.make_async_copy(dy, rows_out[1], sem_io.at[6])], []
    for copy in loads:
        copy.start()
    if routed:
        vectors = [ref[...].astype(f32) for ref in vectors_in]
        count = vectors[0].shape[1]
        tile = jnp.concatenate([*vectors, jnp.zeros((5, count), f32)], axis=0)
        tile = jnp.concatenate([tile, jnp.zeros((8, lanes - count), f32)], axis=1).T[:count]
        tile = jnp.concatenate([tile, jnp.zeros((count, lanes - 8), f32)], axis=1)
        small_buf[...] = tile.astype(bf16).reshape(small_buf.shape)
        barrier = pltpu.get_barrier_semaphore()
        peers = [mate, near_x, near_y, (core, place(z, 1 - y, 1 - x)), *along_z]
        peers += [(other, place((z + k) % 4, y, x)) for k in range(1, 4)]
        for peer in peers:
            pl.semaphore_signal(barrier, inc=1, device_id=peer, device_id_type=pl.DeviceIdType.MESH)
        pl.semaphore_wait(barrier, len(peers))
        for n in range(8):
            share_own(n)
        for copy in shares:
            copy.start()
        for n in range(8, len(units)):
            share_own(n)
        hops(opening)
    else:
        for n in range(len(units)):
            weight_copy(n).start()
    stat_ref[...] = jnp.zeros_like(stat_ref)

    wait_bytes(ub, sem_io.at[0])
    wait_bytes(dy, sem_io.at[1])
    if routed:
        wait_bytes(ub, sem_io.at[2])

    def wait_rows(buf, first):
        if routed:
            for k in range(3):
                wait_bytes(half_rows(buf), sem_io.at[first + k])
        else:
            wait_bytes(buf, sem_io.at[first])

    def add_stat(layer, k, values, valid):
        total = jnp.zeros((1, lanes), f32)
        for p in range(values.shape[1] // lanes):
            part = values[:, p * lanes : (p + 1) * lanes]
            total = total + jnp.sum(part * part * valid, axis=0, keepdims=True)
        stat_ref[layer, k : k + 1, :] += total

    def forward_attention(layer, s):
        at = seg_rows(s)
        mask = mask_col(s)
        for p in range(pairs):
            cols = slice(p * lanes, (p + 1) * lanes)
            qp = qkv[at, cols]
            kp = qkv[at, slice(width + p * lanes, width + (p + 1) * lanes)]
            vp = qkv[at, slice(2 * width + p * lanes, 2 * width + (p + 1) * lanes)]
            outs = []
            for side in range(2):
                h = 2 * p + side
                own, marks = lane_marks(head_size, side)
                bias = gain_sums[0, h * slots : (h + 1) * slots]
                hi = bias.astype(bf16).astype(f32)
                aux = jnp.concatenate([hi * marks[1] + (bias - hi) * marks[2], jnp.zeros((tok_rows, lanes), f32)], axis=0)
                aux = aux + mask * marks[0]
                extra = marks[0] + marks[1] + marks[2]
                ka = kp * own.astype(bf16) + aux.astype(bf16)
                qa = qp * (1.0 - extra).astype(bf16) + extra.astype(bf16)
                scores = nt(qa, ka)
                top = jnp.max(scores, axis=1, keepdims=True)
                weights = jnp.exp2(scores - top).astype(bf16)
                ebuf[s, h] = weights
                va = vp * own.astype(bf16) + (1.0 - own).astype(bf16)
                outs.append(mm(weights, va))
            own, _ = lane_marks(head_size, 0)
            raw = jnp.where(own > 0, outs[0], outs[1])
            sums = pltpu.roll(jnp.where(own > 0, outs[1], outs[0]), head_size, 1)
            inv = 1.0 / sums
            ilbuf[at, cols] = inv.astype(ilbuf.dtype)
            obuf[at, cols] = (raw * inv).astype(bf16)
            if p % 2 == 1:
                after(layer, s, "quad" + str(p // 2))

    def unpack_small(layer):
        small = mat(0, layer, slice(0, lanes)).astype(f32)
        gain_sums[1] = small
        turned = small.T
        for k in range(2):
            gains[layer, k] = turned[k : k + 1, :]
        for h in range(heads):
            column = gain_sums[1, pl.ds(h, slots, stride=heads)][:, 2:3]
            gain_sums[0, h * slots : (h + 1) * slots] = jnp.broadcast_to(column * log2_e, (slots, lanes))

    def forward_attn(layer, s):
        at = seg_rows(s)

        @pl.when(layer == 1)
        def _():
            for copy in spill_copies(s, False):
                copy.wait()

        @pl.when(layer == 0)
        def _():
            spill_copies(s, False, (7,))[0].start()

        valid = valid_rows(s)
        x = ub[at, :].astype(f32)
        squares = jnp.sum(x * x, axis=1, keepdims=True)
        add_stat(layer, 0, x, valid)
        add_stat(layer, 3, valid, valid)
        n1 = (x * lax.rsqrt(squares / width + norm_eps) * gains[layer, 0]).astype(bf16)
        for k in range(3):
            part = mm(n1, mat(0, layer, qkv_cols(k)))
            if k == 0:
                part = part * (score_scale * log2_e)
            qkv[at, k * width : (k + 1) * width] = part.astype(bf16)
        after(layer, s, "qkv")
        forward_attention(layer, s)

        @pl.when(layer == 0)
        def _():
            for copy in spill_copies(s, False, range(4)):
                copy.start()

    def ffn_part(s, layer, picks):
        at = seg_rows(s)

        def up(c):
            return mm(doa[0, at, :], mat(2, layer, slice(c * chunk, (c + 1) * chunk)))

        before = up(picks[0])
        for c in picks:
            cols = slice(c * chunk, (c + 1) * chunk)
            following = up(c + 1) if c + 1 in picks else None
            square = before * before
            gate = 0.5 + 0.5 * jnp.tanh(before * (gelu_c + (gelu_c * gelu_k) * square))
            act = before * gate
            slope[at, cols] = (gate + act * (1.0 - gate) * (2.0 * gelu_c + (6.0 * gelu_c * gelu_k) * square)).astype(bf16)
            act = act.astype(bf16)
            active[at, cols] = act
            part = mm(act, mat(3, layer, planes=slice(c, c + 1)))
            if c == 0:
                dn[at, :] = part
            else:
                dn[at, :] += part
            before = following

    def forward_ffn_a(layer, s):
        at = seg_rows(s)
        valid = valid_rows(s)
        z = mm(obuf[at, :], mat(1, layer))
        add_stat(layer, 1, z, valid)
        h = ub[at, :].astype(f32) + z
        hbuf[at, :] = h.astype(bf16)
        doa[0, at, :] = (h * lax.rsqrt(jnp.mean(h * h, axis=1, keepdims=True) + norm_eps) * gains[layer, 1]).astype(bf16)
        ffn_part(s, layer, range(ff // chunk // 2))
        after(layer, s, "ffna")

    def forward_ffn_b(layer, s):
        at = seg_rows(s)
        valid = valid_rows(s)
        ffn_part(s, layer, range(ff // chunk // 2, ff // chunk))
        out = dn[at, :]
        add_stat(layer, 2, out, valid)
        result = (hbuf[at, :].astype(f32) + out).astype(bf16)

        @pl.when(layer == 0)
        def _():
            spill_copies(s, False, (7,))[0].wait()
            ub[at, :] = result

        @pl.when(layer == 1)
        def _():
            doa[1, at, :] = result

        @pl.when(layer == 0)
        def _():
            for copy in spill_copies(s, False, (4, 5, 6)):
                copy.start()

        after(layer, s, "ffnb")

    @pl.loop(0, 2)
    def _(layer):
        after(layer, 0, "open")
        need(layer, first_units)
        unpack_small(layer)

        @pl.loop(0, segs)
        def _(s):
            forward_attn(layer, s)

        after(layer, 0, "gate")
        need(layer, later_units)

        @pl.loop(0, segs)
        def _(s):
            forward_ffn_a(layer, s)

        after(layer, 0, "last")
        need(layer, last_units)

        @pl.loop(0, segs)
        def _(s):
            forward_ffn_b(layer, s)

    if routed:
        for n in range(len(units)):
            drain(n)
    for copies in y_copies:
        for copy in copies:
            copy.start()

    if routed:
        wqa_u, wo_u, wu_u, wd_u, wqb_u = range(5)
        half_cols = quads * 3 * lanes
        rs_cols = {wqa_u: slice(0, half_cols), wqb_u: slice(half_cols, 2 * half_cols + lanes)}
        rs_weight = (0, 1, 2, 3, 0)
        chunked = (wu_u, wd_u)
        fast = (wqa_u, wqb_u)
        plane_peers = [near_x, near_y, (core, place(z, 1 - y, 1 - x))]
        plane_spots = [(y, 1 - x), (1 - y, x), (1 - y, 1 - x)]
        chunks = ff // chunk

        def rs_copy(src, dst, u, step, k, target):
            return pltpu.make_async_remote_copy(
                src_ref=src,
                dst_ref=dst,
                send_sem=rs_send.at[u, step],
                recv_sem=rs_recv.at[u, k],
                device_id=target,
                device_id_type=pl.DeviceIdType.MESH,
            )

        def piece_cols(step, piece, u):
            size = chunk if step < 2 else ff // 2
            return slice(piece * size, (piece + 1) * size)

        def piece_planes(step, piece):
            return piece if step < 2 else slice(2 * piece, 2 * piece + 2)

        def spot(layer, u, pz, py, px, c, piece=None, step=0):
            cols = rs_cols.get(u, every)
            if piece is not None and u == wd_u:
                pz = piece_planes(step, piece)
            elif piece is not None:
                cols = piece_cols(step, piece, u)
            return weight_buf[rs_weight[u]].at[layer + 1, pz, py, px, c, every, cols]

        def land_at(u, step, piece=None):
            ref = lands[u][step]
            if piece is None:
                return ref
            ring = piece % 2 if step == 0 else piece
            if u == wd_u:
                return ref.at[piece_planes(step, ring)]
            lead = (every,) * (len(ref.shape) - 1)
            return ref.at[(*lead, piece_cols(step, ring, u))]

        def rs_copies(layer, u, step, y_first, piece=None):
            if step == 0:
                src = spot(layer, u, every, every, every, other, piece)
                return [rs_copy(src, land_at(u, 0, piece), u, 0, (piece or 0) % 2, mate)]
            if step == 1 and u in fast:
                return [
                    rs_copy(spot(layer, u, every, *plane_spots[k], core), lands[u][1].at[k], u, 1, 2, plane_peers[k])
                    for k in range(3)
                ]
            if step == 3 and u in fast:
                return [owner_copy(layer, u, k) for k in range(4)]
            if step == 1:
                at = (every, 1 - y, every) if y_first else (every, every, 1 - x)
                src = spot(layer, u, *at, core, piece)
                return [rs_copy(src, land_at(u, 1, piece), u, 1, 2 + (piece or 0) // 2, near_y if y_first else near_x)]
            if step == 2:
                at = (every, y, 1 - x) if y_first else (every, 1 - y, x)
                src = spot(layer, u, *at, core, piece, 2)
                return [rs_copy(src, land_at(u, 2, piece), u, 2, 4 + (piece or 0), near_x if y_first else near_y)]
            if step == 3:
                cols = piece_cols(3, piece, u) if piece is not None else every
                return [
                    rs_copy(
                        weight_buf[rs_weight[u]].at[layer + 1, (z + k) % 4, y, x, core, every, cols],
                        lands[u][3].at[k - 1, every, cols], u, 3, 6, along_z[k - 1],
                    )
                    for k in range(1, 4)
                ]
            return [rs_copy(src, dst, u, 4, 7, mate) for src, dst in home_parts(layer, u)]

        def owner_copy(layer, u, k):
            away = (z + k + 1) % 4 if k < 3 else z
            half = core
            return pltpu.make_async_remote_copy(
                src_ref=spot(layer, u, away, y, x, core),
                dst_ref=lands[u][3].at[half, k],
                send_sem=rs_send.at[u, 3],
                recv_sem=rs_recv.at[u, 6 + half],
                device_id=(layer, place(away, y, x)),
                device_id_type=pl.DeviceIdType.MESH,
            )

        def start_owner(layer, u):
            for k in range(3):
                owner_copy(layer, u, k).start()

            @pl.when(core != layer)
            def _():
                owner_copy(layer, u, 3).start()

        def merge_owner(layer, u):
            @pl.when(core == layer)
            def _():
                got = lands[u][3]
                wait_bytes(got.at[layer, pl.ds(0, 3)], rs_recv.at[u, 6 + layer])
                wait_bytes(got.at[1 - layer], rs_recv.at[u, 7 - layer])
                cols = rs_cols[u]
                for half in range(2):
                    if half == layer:
                        total = weight_buf[0][layer + 1, z, y, x, half, :, cols].astype(f32)
                    else:
                        total = got[half, 3].astype(f32)
                    for k in range(3):
                        total = total + got[half, k].astype(f32)
                    if u == wqb_u:
                        small = total[:, :lanes].T
                        turned = jnp.concatenate([small[:8, :], jnp.zeros((8, lanes - small.shape[1]), f32)], axis=1)
                        fin[u][half, 0:8, 0:lanes] = turned
                        fin[u][half, :, lanes:] = total[:, lanes:]
                    else:
                        fin[u][half] = total
                for k, (src, dst) in enumerate(home_parts(layer, u)):
                    pltpu.make_async_copy(src, dst, sem_g.at[5 if k == 3 else u]).start()

        def home_parts(layer, u):
            if u not in rs_cols:
                return [(fin[u], grads_out[u].at[core])]
            base, q = (0, 0) if u == wqa_u else (lanes, 1)
            parts = [
                (
                    fin[u].at[:, :, base + k * quad : base + (k + 1) * quad],
                    grads_out[0].at[:, :, k * width + q * quad : k * width + (q + 1) * quad],
                )
                for k in range(3)
            ]
            if u == wqb_u:
                parts.append((fin[u].at[:, 0:8, 0:lanes], grads_out[4]))
            return parts

        def rs_route(u, act):
            for side in range(2):
                @pl.when(core == side)
                def _(side=side):
                    act((side + u) % 2 == 0)

        def on_route(u, step, act):
            if step in (1, 2):
                rs_route(u, act)
            else:
                act(True)

        def rs_pieces(u, step):
            if u in chunked and step < 3:
                return list(range(chunks if step < 2 else 2))
            return [0, 1] if u == wu_u and step == 3 else [None]

        def rs_start(layer, u, step, piece=None):
            if layer == 0 and step < 4 and not piece:
                rs_sent(1, u, step)
            if step == 3 and u in fast:
                start_owner(layer, u)
                return
            used = layer == 0 and not piece
            if u in chunked and step < 3:
                used = (layer == 0 or piece >= 2, layer == 0 and piece % 2 == 0, layer == 0)[step]
            if used and step < 4:
                pl.semaphore_wait(rs_free.at[u, step], 3 if step == 3 or (step == 1 and u in fast) else 1)

            if u == wd_u and step == 3:
                for k, copy in enumerate(rs_copies(layer, u, 3, True)):
                    @pl.when((z + k + 1) % 4 // 2 == piece)
                    def _(copy=copy):
                        copy.start()

                return

            def act(y_first):
                for copy in rs_copies(layer, u, step, y_first, piece):
                    copy.start()

            on_route(u, step, act)

        def give_back(u, step):
            def act(y_first):
                if step == 0:
                    peers = [mate]
                elif step == 3:
                    peers = along_z
                elif u in fast:
                    peers = plane_peers
                else:
                    peers = [near_y if y_first == (step == 1) else near_x]
                for peer in peers:
                    pl.semaphore_signal(rs_free.at[u, step], inc=1, device_id=peer, device_id_type=pl.DeviceIdType.MESH)

            on_route(u, step, act)

        def rs_merge(layer, u, step, piece=None):
            if step == 3 and u in fast:
                merge_owner(layer, u)
                return

            got = lands[u][step]
            sem = (piece or 0) % 2 if step < 3 else 0
            wait_at = land_at(u, step, piece) if step in (0, 2) else got
            if u in chunked and step == 1:
                wait_at = got.at[piece_planes(2, piece)] if u == wd_u else got.at[:, :, :, piece_cols(2, piece, u)]
            wait_bytes(wait_at, rs_recv.at[u, 2 * step + sem])
            slot = layer + 1
            buf = weight_buf[rs_weight[u]]
            cols = rs_cols.get(u, every)
            if step == 3:
                if layer == 0:
                    rs_home(1, u)
                total = buf[slot, z, y, x, core, :, cols].astype(f32)
                for k in range(3):
                    total = total + got[k].astype(f32)
                fin[u][...] = total
                if layer == 1:
                    give_back(u, 3)

                @pl.when(core == layer)
                def _():
                    for src, dst in home_parts(layer, u):
                        pltpu.make_async_copy(src, dst, sem_g.at[u]).start()

                @pl.when(core != layer)
                def _():
                    rs_start(layer, u, 4)

                return
            if step == 0 and piece is not None and u == wd_u:
                buf[slot, piece, :, :, core] += got[piece % 2]
            else:
                got_cols, planes = every, (0, 4)
                if piece is not None and u == wd_u:
                    planes = (2 * piece, 2 * piece + 2)
                elif piece is not None:
                    cols = piece_cols(step if step != 1 else 2, piece, u)
                    got_cols = piece_cols(0, piece % 2, u) if step == 0 else cols

                @pl.loop(*planes)
                def _(pz):
                    if step == 0:
                        buf[slot, pz, :, :, core, :, cols] += got[pz, :, :, :, got_cols]
                    elif u in fast:
                        total = buf[slot, pz, y, x, core, :, cols].astype(f32)
                        for k in range(3):
                            total = total + got[k, pz].astype(f32)
                        buf[slot, pz, y, x, core, :, cols] = total.astype(bf16)
                    elif step == 2:
                        buf[slot, pz, y, x, core, :, cols] += got[pz, :, got_cols]
                    else:
                        def add(y_first):
                            if y_first:
                                buf[slot, pz, y, :, core, :, cols] += got[pz, :, :, got_cols]
                            else:
                                buf[slot, pz, :, x, core, :, cols] += got[pz, :, :, got_cols]

                        rs_route(u, add)

            if layer == 1 or (step == 0 and u in chunked and piece < 2):
                give_back(u, step)
            rs_start(layer, u, 3 if u in fast and step == 1 else step + 1, piece)

        def rs_home(layer, u):
            @pl.when(core == layer)
            def _():
                if u == wqb_u:
                    wait_bytes(fin[u].at[:, :, lanes:], sem_g.at[u])
                    wait_bytes(fin[u].at[:, 0:8, 0:lanes], sem_g.at[5])
                else:
                    wait_bytes(fin[u], sem_g.at[u])
                if u not in fast:
                    for copy in rs_copies(layer, u, 4, True):
                        copy.wait_recv()

            if u not in fast:
                @pl.when(core != layer)
                def _():
                    for copy in rs_copies(layer, u, 4, True):
                        copy.wait_send()

        def rs_sent(layer, u, step):
            three = slice(0, 3)
            if step == 0:
                wait_bytes(spot(layer, u, every, every, every, other), rs_send.at[u, 0])
            elif step == 1 and u in fast:
                wait_bytes(spot(layer, u, three, every, every, core), rs_send.at[u, 1])
            elif step == 1:
                wait_bytes(spot(layer, u, every, y, every, core), rs_send.at[u, 1])
            elif step == 2:
                wait_bytes(spot(layer, u, every, y, x, core), rs_send.at[u, 2])
            elif u not in fast:
                wait_bytes(spot(layer, u, three, y, x, core), rs_send.at[u, 3])
            else:
                @pl.when(core == layer)
                def _():
                    wait_bytes(spot(layer, u, three, y, x, core), rs_send.at[u, 3])

                @pl.when(core != layer)
                def _():
                    wait_bytes(spot(layer, u, every, y, x, core), rs_send.at[u, 3])

        def rs_finish(layer, u):
            for step in (0, 1, 3) if u in fast else range(4):
                rs_sent(layer, u, step)

        def stat_copy(step, k=0):
            target = (mate, near_y, near_x)[step] if step < 3 else along_z[k]
            place_at = step if step < 3 else 3 + z
            return pltpu.make_async_remote_copy(
                src_ref=stat_sum.at[step],
                dst_ref=stat_land.at[place_at],
                send_sem=stat_send.at[step],
                recv_sem=stat_recv.at[step],
                device_id=target,
                device_id_type=pl.DeviceIdType.MESH,
            )

        def stat_step(step):
            if step == 0:
                stat_sum[0] = stat_ref[...]
            elif step < 4:
                stat_copy(step - 1).wait()
                stat_sum[step] = stat_sum[step - 1] + stat_land[step - 1]
            if step < 3:
                stat_copy(step).start()
            elif step == 3:
                stat_land[3 + z] = stat_sum[3]
                for k in range(3):
                    stat_copy(3, k).start()
            else:
                wait_bytes(stat_land.at[pl.ds(3, 3)], stat_recv.at[3])
                wait_bytes(stat_land.at[pl.ds(3, 3)], stat_send.at[3])
                total = stat_land[3] + stat_land[4] + stat_land[5] + stat_land[6]
                stat_ref[...] = total
                stat_done()

        stat_step(0)
        names = dict(a=wqa_u, o=wo_u, u=wu_u, d=wd_u, b=wqb_u)

        def run_events(layer, text):
            for word in text:
                if word[0] == "t":
                    stat_step(int(word[1]))
                    continue
                at_layer = layer
                if word[0] == "p":
                    at_layer, word = layer + 1, word[1:]
                step, u = int(word[1]), names[word[2]]
                piece = int(word[3]) if len(word) > 3 else None
                (rs_start if word[0] == "S" else rs_merge)(at_layer, u, step, piece)

        back_points = {
            (1, "ffn0"): ("S0d0", "S0u0"),
            (1, "ffn1"): ("t1", "M0d0", "M0u0", "S0d1", "S0u1"),
            (1, "ffn2"): ("M0d1", "M0u1", "S0d2", "S0u2"),
            (1, "ffn3"): ("t2", "M0d2", "M0u2", "S0d3", "S0u3"),
            (1, "mid0"): ("M0d3", "M0u3"),
            (1, "wo"): ("t3", "S0o", "M1d0", "M1u0"),
            (1, "att00"): ("M0o", "M1d1", "M1u1"),
            (1, "att01"): ("t4", "M2d0", "M2u0"),
            (1, "wq0"): ("S0a",),
            (1, "att10"): ("M0a", "M1o", "M2d1", "M2u1"),
            (1, "wq1"): ("S0b",),
            (1, "in0"): ("M0b",),
            (0, "ffn0"): ("S0d0", "S0u0", "pM1a", "pM2o"),
            (0, "ffn1"): ("M0d0", "M0u0", "S0d1", "S0u1", "pM1b"),
            (0, "ffn2"): ("M0d1", "M0u1", "S0d2", "S0u2", "pM3d", "pM3u"),
            (0, "ffn3"): ("M0d2", "M0u2", "S0d3", "S0u3", "pM3o", "pM3a"),
            (0, "mid0"): ("M0d3", "M0u3", "pM3b"),
            (0, "wo"): ("S0o", "M1d0", "M1u0"),
            (0, "att00"): ("M0o", "M1d1", "M1u1"),
            (0, "att01"): ("M2d0", "M2u0"),
            (0, "wq0"): ("S0a",),
            (0, "att10"): ("M0a", "M1o", "M2d1", "M2u1"),
            (0, "wq1"): ("S0b", "M1a", "M0b"),
            (0, "in0"): ("M2o",),
            (0, "end"): ("M1b", "M3d", "M3u", "M3o", "M3a", "M3b"),
        }
    else:
        back_points = {}

    def stat_done():
        totals = stat_ref[...]
        stat_out[...] = totals if not routed else jnp.broadcast_to(
            jnp.sqrt(jnp.sum(totals, axis=2, keepdims=True) / (totals[0:1, 3:4, 0:1] * width)), totals.shape
        )

    if not routed:
        stat_done()

    def back_point(layer, point, s=None, at=None):
        for (at_layer, at_point), text in back_points.items():
            if at_point == point:
                here = layer == at_layer
                if s is not None:
                    here = here & (s == at)

                @pl.when(here)
                def _(at_layer=at_layer, text=text):
                    run_events(at_layer, text)

    def norm_back(x, gain, grad):
        inv = lax.rsqrt(jnp.mean(x * x, axis=1, keepdims=True) + norm_eps)
        hat = x * inv
        scaled = grad * gain
        return inv * (scaled - hat * jnp.mean(scaled * hat, axis=1, keepdims=True))

    def add_gain(k, d_weight, weight):
        total = gain_sums[k]
        for p in range(d_weight.shape[1] // lanes):
            cols = slice(p * lanes, (p + 1) * lanes)
            total = total + d_weight[:, cols] * weight[:, cols].astype(f32)
        gain_sums[k] = total

    def pack_small(layer):
        sums = [jnp.sum(gain_sums[k], axis=1, keepdims=True) for k in range(2)]
        turned = dbias[...].T
        for h in range(heads):
            gain_sums[1, pl.ds(h, slots, stride=heads)] = jnp.broadcast_to(turned[:slots, h : h + 1], (slots, lanes))
        lane = lax.broadcasted_iota(jnp.int32, (width, lanes), 1)
        gain = mat(0, layer, slice(0, lanes)).astype(f32)
        safe = jnp.where(lane < 2, gain, 1.0)
        value = jnp.where(lane == 0, sums[0], jnp.where(lane == 1, sums[1], 0.0)) / safe
        value = jnp.where(lane == 2, gain_sums[1], value)
        put_mat(0, layer + 1, value.astype(bf16), slice(3 * quad, 3 * quad + lanes))

    def backward_ffn(layer):
        slot = layer + 1

        @pl.loop(0, segs)
        def _(s):
            at = seg_rows(s)
            h = hbuf[at, :].astype(f32)
            doa[0, at, :] = (h * lax.rsqrt(jnp.mean(h * h, axis=1, keepdims=True) + norm_eps) * gains[layer, 1]).astype(bf16)

        gain_sums[...] = jnp.zeros_like(gain_sums)
        dbias[...] = jnp.zeros_like(dbias)
        turned_cols = slice(0, segs * rows)
        put_mat(0, slot, doa[0].T, turned_cols)

        @pl.loop(0, ff // chunk)
        def _(c):
            cols = pl.ds(pl.multiple_of(c * chunk, chunk), chunk)
            planes = pl.ds(c, 1)
            d_pre = nt(dy[...], mat(3, layer, planes=planes)).astype(bf16) * slope[:, cols]
            slope[:, cols] = d_pre
            put_mat(3, slot, tn(active[:, cols], dy[...]).astype(bf16), planes=planes)
            d_up = mm(mat(0, slot, turned_cols), d_pre)
            add_gain(1, d_up, mat(2, layer, cols))
            put_mat(2, slot, d_up.astype(bf16), cols)
            for k in range(ff // chunk):
                back_point(layer, "ffn" + str(k), c, k)

    def backward_middle(layer, s):
        at = seg_rows(s)
        dh = norm_back(hbuf[at, :].astype(f32), gains[layer, 1], nt(slope[at, :], mat(2, layer)))
        v = ub[at, :].astype(f32)
        hbuf[at, :] = (v * lax.rsqrt(jnp.mean(v * v, axis=1, keepdims=True) + norm_eps) * gains[layer, 0]).astype(bf16)
        dh = dh + dy[at, :].astype(f32)
        dn[at, :] = dh
        dz = dh.astype(bf16)
        dy[at, :] = dz
        do = nt(dz, mat(1, layer)) * ilbuf[at, :].astype(f32)
        prod = do.astype(bf16).astype(f32) * obuf[at, :].astype(f32)
        lane = lax.broadcasted_iota(jnp.int32, (1, quad), 1) % head_size
        side = lax.broadcasted_iota(jnp.int32, (1, quad), 1) // head_size % 2
        hi_at, lo_at = (lane == 0).astype(f32), (lane == 1).astype(f32)
        free = 1.0 - hi_at - lo_at
        head_of = lax.broadcasted_iota(jnp.int32, (quad, quad), 0) // head_size
        gets = lax.broadcasted_iota(jnp.int32, (quad, quad), 1) // head_size
        swap_sum = jnp.where(head_of == gets + 1 - 2 * (gets % 2), -1.0, 0.0).astype(bf16)
        for q in range(quads):
            cols = slice(q * quad, (q + 1) * quad)
            upper = prod[:, cols].astype(bf16)
            delta = mm(upper, swap_sum) + mm((prod[:, cols] - upper.astype(f32)).astype(bf16), swap_sum)
            hi = delta.astype(bf16).astype(f32)
            filled = do[:, cols] * free + hi * hi_at + (delta - hi) * lo_at
            for k in range(2):
                doa[k, at, cols] = jnp.where(side == k, do[:, cols], filled).astype(bf16)

    def backward_attention(layer, q, s):
        at = seg_rows(s)
        for p in range(2):
            cols, kcols, vcols = (
                pl.ds(pl.multiple_of(k * width + q * quad + p * lanes, lanes), lanes) for k in range(3)
            )
            qp = qkv[at, cols]
            kp = qkv[at, kcols]
            vp = qkv[at, vcols]
            q_turned = qp.T
            dq, dk, dv = [], [], []
            for side in range(2):
                h = 4 * q + 2 * p + side
                own, marks = lane_marks(head_size, side)
                do_h = doa[side, at, cols]
                va = vp * own.astype(bf16) + (marks[0] + marks[1]).astype(bf16)
                weights = ebuf[s, h]
                d_scores = weights * nt(do_h, va).astype(bf16)
                dbias[pl.ds(h, 1), :] += jnp.sum(d_scores[:, :lanes].astype(f32), axis=0, keepdims=True)
                half = slice(side * head_size, (side + 1) * head_size)
                dq.append(mm(d_scores, kp))
                dk.append(mm(q_turned[half, :], d_scores))
                dv.append(mm(do_h.T[half, :], weights))
            own, _ = lane_marks(head_size, 0)
            qkv[at, cols] = (jnp.where(own > 0, dq[0], dq[1]) * score_scale).astype(bf16)
            qkv[at, kcols] = (jnp.concatenate(dk, axis=0).T * (1.0 / log2_e)).astype(bf16)
            qkv[at, vcols] = jnp.concatenate(dv, axis=0).T.astype(bf16)

    def backward_input(layer, s):
        at = seg_rows(s)
        x = ub[at, :].astype(f32)
        du = norm_back(x, gains[layer, 0], nt(qkv[at, :], mat(0, layer, slice(lanes, lanes + 3 * width))))
        dy[at, :] = (du + dn[at, :]).astype(bf16)

    def grad_col(q, k):
        return q * (3 * quad + lanes) + k * quad

    def grad_copies(layer):
        return [
            pltpu.make_async_copy(buf.at[layer + 1], out.at[layer], sem_g.at[k])
            for k, (buf, out) in enumerate(zip(weight_buf, grads_out))
        ]

    @pl.loop(0, 2)
    def _(step):
        layer = 1 - step
        slot = layer + 1

        @pl.when(layer == 0)
        def _():
            for s in range(segs):
                for copy in spill_copies(s, True, (2, 3, 4, 5, 6)):
                    copy.wait()

        backward_ffn(layer)

        @pl.when(layer == 1)
        def _():
            wait_rows(doa.at[1], 3)

        @pl.when(layer == 0)
        def _():
            for s in range(segs):
                spill_copies(s, True, (7,))[0].wait()

        @pl.loop(0, segs)
        def _(s):
            backward_middle(layer, s)
            back_point(layer, "mid0", s, 0)

        put_mat(1, slot, tn(obuf[...], dy[...]).astype(bf16))
        back_point(layer, "wo")

        @pl.when(layer == 1)
        def _():
            for s in range(segs):
                for copy in spill_copies(s, True, (2, 3, 4, 5)):
                    copy.start()

        @pl.loop(0, quads)
        def _(q):
            @pl.loop(0, segs)
            def _(s):
                @pl.when((layer == 0) & (q == 0))
                def _():
                    for copy in spill_copies(s, True, (0, 1)):
                        copy.wait()

                backward_attention(layer, q, s)

                for i in range(quads):
                    for k in range(segs):
                        back_point(layer, "att" + str(i) + str(k), q * segs + s, i * segs + k)

            for k in range(3):
                d_weight = tn(hbuf[...], qkv[:, pl.ds(pl.multiple_of(k * width + q * quad, quad), quad)])
                add_gain(0, d_weight, mat(0, layer, pl.ds(pl.multiple_of(lanes + k * width + q * quad, lanes), quad)))
                put_mat(0, slot, d_weight.astype(bf16), pl.ds(pl.multiple_of(grad_col(q, k), lanes), quad))

            @pl.when((layer == 1) & (q == quads - 1))
            def _():
                for k in (6, 1):
                    for s in range(segs):
                        spill_copies(s, True, (k,))[0].start()

            @pl.when(q == quads - 1)
            def _():
                pack_small(layer)

            for i in range(quads):
                back_point(layer, "wq" + str(i), q, i)

        @pl.loop(0, segs)
        def _(s):
            backward_input(layer, s)
            for k in range(segs):
                back_point(layer, "in" + str(k), s, k)


        @pl.when(layer == 1)
        def _():
            for s in range(segs):
                for copy in spill_copies(s, True, (7, 0)):
                    copy.start()

        if not routed:
            for copy in grad_copies(layer):
                copy.start()
            for copy in grad_copies(layer):
                copy.wait()

    for copies in du_copies:
        for copy in copies:
            copy.start()
    back_point(0, "end")
    if routed:
        for u in range(5):
            rs_finish(0, u)
    if routed:
        for u in range(5):
            rs_home(0, u)
        for u in (0, 4):
            rs_home(1, u)
    wait_rows(dy, 6)


def run_layers(dims, routed, doc_len, row_args, weights):
    segs, rows, width, ff, slots, heads, per_doc = dims
    all_rows = segs * rows
    vmem = pl.BlockSpec(memory_space=pltpu.VMEM)
    smem = pl.BlockSpec(memory_space=pltpu.SMEM)
    hbm = pl.BlockSpec(memory_space=pl.ANY)
    shape = jax.ShapeDtypeStruct
    dma = pltpu.SemaphoreType.DMA
    wide = (all_rows, width)
    tiles = [
        (width // 32, lanes + 3 * width),
        (width // 32, width),
        (width // 32, ff),
        (ff // 32, width),
    ]
    out_shape = [shape(part.shape, bf16) for part in row_args]
    if routed:
        out_shape += [shape((2, width // 32, 3 * width), f32)]
        out_shape += [shape((2, *tile), f32) for tile in tiles[1:]]
        out_shape += [shape((2, 8, lanes), f32)]
    else:
        out_shape += [shape((2, 4, 2, 2, 2, *tile), bf16) for tile in tiles]
    row_outs = len(out_shape)
    out_shape += [shape((2, 8, lanes), f32)]
    out_shape += [
        shape((all_rows, 3 * width), bf16),
        shape((segs, heads, rows, rows), bf16),
        shape(wide, bf16),
        shape(wide, bf16),
        shape((all_rows, ff), bf16),
        shape((all_rows, ff), bf16),
        shape(wide, bf16),
        shape(wide, bf16),
    ]
    unit_count = 16
    scratch = [pltpu.VMEM((3, 4, 2, 2, 2, *tile), bf16) for tile in tiles]
    scratch += [
        pltpu.VMEM(wide, bf16),
        pltpu.VMEM(wide, bf16),
        pltpu.VMEM((all_rows, 3 * width), bf16),
        pltpu.VMEM((segs, heads, rows, rows), bf16),
        pltpu.VMEM(wide, bf16),
        pltpu.VMEM(wide, bf16),
        pltpu.VMEM(wide, bf16),
        pltpu.VMEM((all_rows, ff), bf16),
        pltpu.VMEM((all_rows, ff), bf16),
        pltpu.VMEM((2, *wide), bf16),
        pltpu.VMEM(wide, f32),
        pltpu.VMEM((2, 2, 1, width), f32),
        pltpu.VMEM((2, width, lanes), f32),
        pltpu.VMEM((heads, lanes), f32),
        pltpu.VMEM((2, 8, lanes), f32),
        dma((segs, 8)),
        dma((8,)),
        dma((9,)),
        dma((unit_count, 2)),
        dma((unit_count, 6)),
    ]
    params = dict(vmem_limit_bytes=127 * 2**19)
    if routed:
        params.update(collective_id=0, has_side_effects=True)
        half_cols = 3 * width // 2
        rs_tiles = [(width // 32, half_cols), *tiles[1:], (width // 32, half_cols + lanes)]
        first_tiles = [(4, 2, 2, *tile) for tile in rs_tiles]
        first_tiles[2] = (4, 2, 2, width // 32, 2 * chunk)
        first_tiles[3] = (2, 2, 2, ff // 32, width)
        for u, (first, tile) in enumerate(zip(first_tiles, rs_tiles)):
            leads = ((3, 4), (1,), (2, 4)) if u in (0, 4) else ((4, 2), (4,), (3,))
            scratch += [pltpu.VMEM(first, bf16)]
            scratch += [pltpu.VMEM((*lead, *tile), bf16) for lead in leads]
        scratch += [pltpu.VMEM((2, *tile) if u in (0, 4) else tile, f32) for u, tile in enumerate(rs_tiles)]
        scratch += [
            pltpu.VMEM((4, 2, 8, lanes), f32),
            pltpu.VMEM((7, 2, 8, lanes), f32),
            pltpu.VMEM((2, width // 32, lanes), bf16),
            dma((5, 5)),
            dma((5, 8)),
            pltpu.SemaphoreType.REGULAR((5, 4)),
            dma((4,)),
            dma((4,)),
        ]
    return pl.pallas_call(
        partial(fused_layers, dims, routed),
        out_shape=out_shape,
        in_specs=[smem] + [hbm] * (len(row_args) + 4) + [vmem] * (len(weights) - 4),
        out_specs=[hbm] * row_outs + [vmem] + [hbm] * (len(out_shape) - row_outs - 1),
        scratch_shapes=scratch,
        compiler_params=pltpu.CompilerParams(**params),
    )(doc_len, *row_args, *weights)[: row_outs + 1]


def settle_kernel(*refs):
    count = (len(refs) - 7) // 3
    srcs, (small, stats) = refs[:count], refs[count : count + 2]
    dsts = refs[count + 2 : 2 * count + 2]
    vectors, rms = refs[2 * count + 2 : 2 * count + 5], refs[2 * count + 5]
    mids, sems = refs[2 * count + 6 : -1], refs[-1]
    inward = [pltpu.make_async_copy(src, mid, sems.at[0, k]) for k, (src, mid) in enumerate(zip(srcs, mids))]
    outward = [pltpu.make_async_copy(mid, dst, sems.at[1, k]) for k, (mid, dst) in enumerate(zip(mids, dsts))]
    for copy in inward:
        copy.start()
    for k, vector in enumerate(vectors):
        size = vector.shape[1] // 2
        vector[...] = jnp.concatenate([small[half, k : k + 1, :size] for half in range(2)], axis=1)
    lane = lax.broadcasted_iota(jnp.int32, (1, lanes), 1)
    for layer in range(2):
        row = sum(jnp.where(lane == k, stats[layer, k : k + 1, :], 0.0) for k in range(3))
        rms[layer : layer + 1, :] = row[:, :3]
    for into, out in zip(inward, outward):
        into.wait()
        out.start()
    for out in outward:
        out.wait()


def settle(big, small, stats):
    vmem = pl.BlockSpec(memory_space=pltpu.VMEM)
    hbm = pl.BlockSpec(memory_space=pl.ANY)
    shape = jax.ShapeDtypeStruct
    size = 2 * big[4].shape[1]
    return pl.pallas_call(
        settle_kernel,
        out_shape=[shape(part.shape, part.dtype) for part in big] + [shape((1, size), f32)] * 3 + [shape((2, 3), f32)],
        in_specs=[hbm] * len(big) + [vmem] * 2,
        out_specs=[hbm] * len(big) + [vmem] * 4,
        scratch_shapes=[pltpu.VMEM(part.shape, part.dtype) for part in big] + [pltpu.SemaphoreType.DMA((2, len(big)))],
    )(*big, small, stats)


def swap(block):
    return lax.ppermute(block, "section", [(0, 1), (1, 0)])


def body(
    tokens,
    memory,
    lengths,
    w_qkv,
    w_out,
    w_up,
    w_down,
    gain_attn,
    gain_ffn,
    forget_bias,
    grad_tokens,
    grad_memory,
):
    section = lax.axis_index("section")
    is_first = section == 0
    micro = tokens.shape[0]
    segs = micro // 2
    half_tok = tokens.shape[1]
    half_mem = memory.shape[1]
    slots = 2 * half_mem
    rows = slots + 2 * half_tok
    width = tokens.shape[2]
    ff = w_up.shape[2]
    heads = forget_bias.shape[1] * lax.axis_size("dp") // slots
    per_doc = micro // lengths.shape[0]
    dims = (segs, rows, width, ff, slots, heads, per_doc)
    if lax.axis_size("dp") == 16 and w_qkv.shape[1] == 32:
        weights = [piece.reshape(2, -1, piece.shape[2]) for piece in (w_qkv, w_out, w_up, w_down)]
        weights += [gain_attn, gain_ffn, forget_bias]
        row_args = (tokens, memory, grad_tokens, grad_memory)
        *outs, small_grads, stats = run_layers(dims, True, lengths, row_args, weights)
        outs = settle(outs, small_grads, stats)
        mats = [grad.reshape(1, -1, grad.shape[2]) for grad in outs[4:8]]
        return (*outs[:4], *mats, *outs[8:])

    own_len = lax.dynamic_slice_in_dim(lengths, section * segs // per_doc, segs // per_doc, 0)
    small = jnp.stack([gain_attn, gain_ffn, forget_bias], axis=2)
    small = jnp.pad(small, ((0, 0), (0, 0), (0, lanes - 3)))
    pieces = (jnp.concatenate([small, w_qkv], axis=2), w_out, w_up, w_down)

    def unpack(grads):
        mat = grads[0]
        half = 3 * width // 2
        parts = [mat[:, :, :half], mat[:, :, half + lanes :]]
        parts = [part.reshape(1, -1, 3, width // 2) for part in parts]
        whole = jnp.concatenate(parts, axis=3).reshape(1, -1, 3 * width)
        return (whole, *grads[1:], *(mat[:, :, half + k] for k in range(3)))

    def own_segs(halves):
        return lax.dynamic_slice_in_dim(halves, section * segs, segs, 0)

    def other_segs(halves):
        return lax.dynamic_slice_in_dim(halves, (1 - section) * segs, segs, 0)

    def both(kept, got):
        return jnp.concatenate(
            [jnp.where(is_first, kept, got), jnp.where(is_first, got, kept)], axis=1
        )

    inputs = (tokens, memory, grad_tokens, grad_memory)
    got = swap(tuple(other_segs(part) for part in inputs))
    full = [both(own_segs(part), other) for part, other in zip(inputs, got)]
    u0 = jnp.concatenate([full[1], full[0]], axis=1).reshape(segs * rows, width)
    dout = jnp.concatenate([full[3], full[2]], axis=1).reshape(segs * rows, width)

    def gather(piece):
        whole = lax.all_gather(piece, ("section", "dp"), axis=1, tiled=True)
        return whole.reshape(2, 4, 2, 2, 2, -1, piece.shape[2])

    y, du, *grads, stats = run_layers(dims, False, own_len, (u0, dout), [gather(piece) for piece in pieces])

    def scatter(grad):
        grad = grad.reshape(2, -1, grad.shape[-1])
        mine = lax.dynamic_index_in_dim(grad, section, 0, keepdims=True)
        other = lax.dynamic_index_in_dim(grad, 1 - section, 0, keepdims=True)
        chip = (mine.astype(f32) + swap(other).astype(f32)).astype(grad.dtype)
        return lax.psum_scatter(chip, "dp", scatter_dimension=1, tiled=True).astype(f32)

    shares = unpack([scatter(grad) for grad in grads])
    totals = lax.psum(stats[:, :4], ("section", "dp"))
    rms = jnp.sqrt(jnp.sum(totals[:, :3], axis=2) / (totals[0, 3, 0] * width))
    result = jnp.stack([y.reshape(segs, rows, width), du.reshape(segs, rows, width)])

    def half_of(which):
        tok = lax.dynamic_slice_in_dim(result, slots + which * half_tok, half_tok, 2)
        mem = lax.dynamic_slice_in_dim(result, which * half_mem, half_mem, 2)
        return tok, mem

    kept = half_of(section)
    got = swap(half_of(1 - section))

    def order(mine, other):
        return jnp.concatenate(
            [jnp.where(is_first, mine, other), jnp.where(is_first, other, mine)], axis=0
        )

    toks = [order(kept[0][k], got[0][k]) for k in range(2)]
    mems = [order(kept[1][k], got[1][k]) for k in range(2)]
    return (toks[0], mems[0], toks[1], mems[1], *shares, rms)


def solution(mesh):
    rows = P("dp", "section", None)
    mats = P("section", "dp", None)
    vecs = P("section", "dp")
    return jax.shard_map(
        body,
        mesh=mesh,
        in_specs=(rows, rows, P("dp"), mats, mats, mats, mats, vecs, vecs, vecs, rows, rows),
        out_specs=(rows, rows, rows, rows, mats, mats, mats, mats, vecs, vecs, vecs, P()),
        check_vma=False,
    )
```

```python
from functools import partial

import jax
import jax.numpy as jnp
from jax import lax
from jax.experimental import pallas as pl
from jax.experimental.pallas import tpu as pltpu
from jax.sharding import PartitionSpec as P

norm_eps = 1e-06
score_scale = 0.125
log2_e = 1.4426950408889634
masked_score = -1000000000.0
gelu_c = 0.7978845608028654
gelu_k = 0.044715
f32 = jnp.float32
bf16 = jnp.bfloat16
lanes = 128
chunk = 512


def mm(a, b, ca=1, cb=0):
    return lax.dot_general(a, b, (((ca,), (cb,)), ((), ())), preferred_element_type=f32)


def nt(a, b):
    return mm(a, b, 1, 1)


def tn(a, b):
    return mm(a, b, 0, 0)


def lane_marks(head_size, side):
    lane = lax.broadcasted_iota(jnp.int32, (1, lanes), 1)
    own = ((lane // head_size) == side).astype(f32)
    first = (1 - side) * head_size
    marks = [(lane == first + k).astype(f32) for k in range(3)]
    return own, marks


def fused_layers(dims, routed, *refs):
    segs, rows, width, ff, slots, heads, per_doc = dims
    refs = list(refs)

    def take(count):
        picked = refs[:count]
        del refs[:count]
        return picked

    (len_ref,) = take(1)
    rows_in = take(4 if routed else 2)
    weight_in = take(4)
    vectors_in = take(3) if routed else []
    rows_out = take(4 if routed else 2)
    grads_out = take(5 if routed else 4)
    (stat_out,) = take(1)
    spill_hbm = take(8)
    weight_buf = take(4)
    ub, dy, qkv, ebuf, obuf, ilbuf, hbuf, slope, active, doa, dn = take(11)
    gains, gain_sums, dbias, stat_ref = take(4)
    sem_spill, sem_g, sem_io, sem_send, sem_recv = take(5)
    if routed:
        lands = [take(4) for _ in range(5)]
        fin = take(5)
        stat_sum, stat_land, small_buf = take(3)
        weight_in = [*weight_in, small_buf]
        rs_send, rs_recv, rs_free, stat_send, stat_recv = take(5)
    head_size = width // heads
    pairs = width // lanes
    tok_rows = rows - slots
    quads = width // (2 * lanes)
    quad = 2 * lanes
    first_doc = lax.axis_index("section") * segs // per_doc if routed else 0
    every = slice(None)

    def wait_bytes(ref, sem):
        pltpu.make_async_copy(ref, ref, sem).wait()

    def units_of(layer):
        half_ff, half_deep = ff // 2, ff // 64
        lead = [
            (0, slice(0, lanes + width), every),
            (0, slice(lanes + width, lanes + 2 * width), every),
            (0, slice(lanes + 2 * width, lanes + 3 * width), every),
        ]
        rest = [(1, every, every)]
        rest += [(3, every, slice(k * half_deep, (k + 1) * half_deep)) for k in range(2)]
        rest += [(2, slice(k * half_ff, (k + 1) * half_ff), every) for k in range(2)]
        return [(layer, *unit) for unit in lead + rest]

    units = units_of(0) + units_of(1)
    first_units = [k for k, unit in enumerate(units) if unit[1] == 0]
    last_units = [7, 15]
    later_units = [k for k, unit in enumerate(units) if unit[1] != 0 and k not in last_units]
    plane_first = (11, 15)

    def view(n, z, y, x, c):
        layer, which, cols, part = units[n]
        return weight_buf[which].at[layer, z, y, x, c, part, cols]

    if routed:
        core = lax.axis_index("section")
        chip = lax.axis_index("dp")
        z, y, x = chip // 4, (chip // 2) % 2, chip % 2
        other = 1 - core

        def place(pz, py, px):
            return pz * 4 + py * 2 + px

        mate = (other, chip)
        near_x = (core, place(z, y, 1 - x))
        near_y = (core, place(z, 1 - y, x))
        along_z = [(core, place((z + k) % 4, y, x)) for k in range(1, 4)]

        def remote(src, dst, n, k, target):
            far = k in (4, 5, 9, 10) or (k in (0, 11) and n in plane_first)
            arrived = {0: 0, 11: 0, 1: 1, 2: 1, 3: 1, 4: 2, 5: 3, 6: 4, 7: 4, 8: 4, 9: 5, 10: 5}[k]
            return pltpu.make_async_remote_copy(
                src_ref=src,
                dst_ref=dst,
                send_sem=sem_send.at[n, int(far)],
                recv_sem=sem_recv.at[n, arrived],
                device_id=target,
                device_id_type=pl.DeviceIdType.MESH,
            )

        def some(n, shards, half):
            return view(n, slice(0, 3), y, x, half) if shards == 3 else view(n, slice(0, 3), every, every, half)

        def own_shards(n):
            layer, which, cols, part = units[n]
            home = weight_buf[which].at[layer, z, y, x]
            if which > 0:
                return [(weight_in[which].at[every, part, cols], home.at[every, part, cols], 0)]
            start = max(cols.start - lanes, 0)
            matrix = slice(start, cols.stop - lanes)
            pairs_of = [(weight_in[0].at[every, every, matrix], home.at[every, every, slice(start + lanes, cols.stop)], 0)]
            if cols.start == 0:
                pairs_of.append((weight_in[4], home.at[every, every, slice(0, lanes)], 11))
            return pairs_of

        def z_copy(n, k):
            where = view(n, z, every, every, core) if n in plane_first else view(n, z, y, x, core)
            return remote(where, where, n, k, along_z[k - 1])

        def plane_copy(n, k, x_first):
            planes = z if n in plane_first else every
            if k == 4:
                where = view(n, planes, y, x, core)
                return remote(where, where, n, 4, near_x if x_first else near_y)
            where = view(n, planes, y, every, core) if x_first else view(n, planes, every, x, core)
            return remote(where, where, n, 5, near_y if x_first else near_x)

        def mate_copy(n, k, x_first, half):
            planes = z if n in plane_first else every
            if k < 9:
                from_z = (z + 4 - (k - 5)) % 4
                where = view(n, from_z, every, every, half) if n in plane_first else view(n, from_z, y, x, half)
            elif k == 9:
                where = view(n, planes, y, 1 - x, half) if x_first else view(n, planes, 1 - y, x, half)
            else:
                where = view(n, planes, 1 - y, every, half) if x_first else view(n, planes, every, 1 - x, half)
            return remote(where, where, n, k, mate)

        def by_route(n, act):
            for side in range(2):
                @pl.when(core == side)
                def _(side=side):
                    act((side + n) % 2 == 0)

        def share_own(n):
            @pl.when(core == units[n][0])
            def _():
                for src, dst, k in own_shards(n):
                    pltpu.make_async_copy(src, dst, sem_recv.at[n, 0]).start()
                    remote(src, dst, n, k, mate).start()

        def start_z(n):
            wait_bytes(view(n, z, y, x, every), sem_recv.at[n, 0])
            if n in plane_first:
                by_route(n, lambda x_first: plane_copy(n, 4, x_first).start())
            else:
                for k in range(1, 4):
                    z_copy(n, k).start()

        def first_hop(n):
            if n not in plane_first:
                wait_bytes(some(n, 3, core), sem_recv.at[n, 1])

            def act(x_first):
                if n in plane_first:
                    plane_copy(n, 4, x_first).wait_recv()
                    plane_copy(n, 5, x_first).start()
                    mate_copy(n, 9, x_first, core).start()
                else:
                    plane_copy(n, 4, x_first).start()
                    for k in range(6, 9):
                        mate_copy(n, k, x_first, core).start()

            by_route(n, act)

        def second_hop(n):
            def act(x_first):
                if n in plane_first:
                    plane_copy(n, 5, x_first).wait_recv()
                    for k in range(1, 4):
                        z_copy(n, k).start()
                    mate_copy(n, 10, x_first, core).start()
                else:
                    plane_copy(n, 4, x_first).wait_recv()
                    plane_copy(n, 5, x_first).start()
                    mate_copy(n, 9, x_first, core).start()

            by_route(n, act)

        def last_share(n):
            def act(x_first):
                if n in plane_first:
                    wait_bytes(some(n, 12, core), sem_recv.at[n, 1])
                    for k in range(6, 9):
                        mate_copy(n, k, x_first, core).start()
                else:
                    plane_copy(n, 5, x_first).wait_recv()
                    mate_copy(n, 10, x_first, core).start()

            by_route(n, act)

        def complete(n):
            near, rest = (12, 3) if n in plane_first else (3, 12)
            wait_bytes(some(n, near, other), sem_recv.at[n, 4])
            wait_bytes(some(n, rest, other), sem_recv.at[n, 5])

        def drain(n):
            few, many = (1, 0) if n in plane_first else (0, 1)
            wait_bytes(view(n, slice(0, 3), every, every, every), sem_send.at[n, many])

            @pl.when(core == units[n][0])
            def _():
                wait_bytes(view(n, every, y, x, every), sem_send.at[n, few])

            @pl.when(core != units[n][0])
            def _():
                wait_bytes(view(n, slice(0, 3), y, x, every), sem_send.at[n, few])

        def hops(text):
            kinds = dict(z=start_z, f=first_hop, s=second_hop, l=last_share, u=take_small)
            for word in text:
                kinds[word[0]](int(word[1:]))

        opening = ("z0", "z1", "z2", "z3", "z4", "z5", "f0", "f1", "s0", "z6", "f2", "s1", "z7", "f3", "s2", "l0", "f4", "s3", "l1", "f5", "u0", "l2", "s4", "f6", "z8", "z9", "z11")
        hops_at = {
            (0, 0, "qkv"): ("s5", "f7", "z10", "z15"),
            (0, 0, "quad0"): ("s6", "z12", "l3"),
            (0, 0, "quad1"): ("f8", "f11", "z13"),
            (0, 1, "qkv"): ("s7", "f9", "l4"),
            (0, 1, "quad0"): ("f10", "s8", "z14", "f15", "l5"),
            (0, 1, "quad1"): ("l6", "s11"),
            (0, 0, "gate"): ("f12",),
            (0, 0, "ffna"): ("l7", "s9", "s10", "f13"),
            (0, 1, "ffna"): ("s15",),
            (0, 0, "ffnb"): ("s12", "l8", "f14"),
            (0, 1, "ffnb"): ("s13", "l9", "l10"),
            (1, 0, "qkv"): ("s14",),
            (1, 1, "qkv"): ("l12", "l13"),
            (1, 1, "quad0"): ("l11", "l14"),
            (1, 1, "quad1"): ("l15",),
        }
    else:
        hops_at = {}

        def weight_copy(n):
            layer, which, cols, part = units[n]
            src = weight_in[which].at[layer, every, every, every, every, part, cols]
            return pltpu.make_async_copy(src, view(n, every, every, every, every), sem_recv.at[n, 0])

        def complete(n):
            weight_copy(n).wait()

    def after(layer, s, point):
        for (at_layer, at_s, at_point), text in hops_at.items():
            if at_point == point:
                @pl.when((layer == at_layer) & (s == at_s))
                def _(text=text):
                    hops(text)

    def need(layer, picks):
        for at_layer in range(2):
            @pl.when(layer == at_layer)
            def _(at_layer=at_layer):
                for n in picks:
                    if units[n][0] == at_layer:
                        complete(n)

    def mat(which, slot, cols=every, planes=None):
        if planes is None:
            value = weight_buf[which][slot, :, :, :, :, :, cols]
        else:
            value = weight_buf[which][slot, planes, :, :, :, :, cols]
        deep = 1
        for size in value.shape[:-1]:
            deep *= size
        return value.reshape(deep, value.shape[-1])

    def put_mat(which, slot, value, cols=every, planes=None):
        buf = weight_buf[which]
        shape = buf.shape[1:-1]
        if planes is None:
            buf[slot, :, :, :, :, :, cols] = value.reshape(*shape, value.shape[-1])
        else:
            buf[slot, planes] = value.reshape(1, *shape[1:], value.shape[-1])

    def qkv_cols(k):
        return slice(lanes + k * width, lanes + (k + 1) * width)

    def seg_rows(s):
        return pl.ds(pl.multiple_of(s * rows, rows), rows)

    def spill_copies(s, back, picks=range(7)):
        at = seg_rows(s)
        kept = (qkv.at[at], ebuf.at[s], obuf.at[at], ilbuf.at[at], slope.at[at], active.at[at], hbuf.at[at], ub.at[at])
        pairs_of = [
            (vmem, hbm.at[s] if k == 1 else hbm.at[at])
            for k, (vmem, hbm) in enumerate(zip(kept, spill_hbm))
        ]
        if back:
            return [
                pltpu.make_async_copy(hbm, vmem, sem_spill.at[s, k])
                for k, (vmem, hbm) in enumerate(pairs_of)
                if k in picks
            ]
        return [
            pltpu.make_async_copy(vmem, hbm, sem_spill.at[s, k])
            for k, (vmem, hbm) in enumerate(pairs_of)
            if k in picks
        ]

    def doc_end(s):
        return len_ref[first_doc + s // per_doc] - (s % per_doc) * tok_rows

    def valid_rows(s):
        row = lax.broadcasted_iota(jnp.int32, (rows, lanes), 0)
        return jnp.where(
            (row >= slots) & (row - slots < doc_end(s)), 1.0, 0.0
        ).astype(f32)

    def mask_col(s):
        row = lax.broadcasted_iota(jnp.int32, (rows, 1), 0)
        return jnp.where(
            (row >= slots) & (row - slots >= doc_end(s)), masked_score, 0.0
        ).astype(f32)

    if routed:
        half_tok, half_mem = tok_rows // 2, slots // 2

        def io_copies(buf, tok_ref, mem_ref, sems, outward):
            local, away = [], []
            own_sem, send_sem, recv_sem = (sem_io.at[k] for k in sems)
            for s in range(segs):
                mine, theirs = core * segs + s, other * segs + s
                for ref, base, size in ((tok_ref, slots, half_tok), (mem_ref, 0, half_mem)):
                    def rows_of(half):
                        return buf.at[pl.ds(pl.multiple_of(s * rows + base + half * size, 16), size)]

                    if outward:
                        local.append(pltpu.make_async_copy(rows_of(core), ref.at[mine], own_sem))
                        src, dst = rows_of(other), ref.at[mine]
                    else:
                        local.append(pltpu.make_async_copy(ref.at[mine], rows_of(core), own_sem))
                        src, dst = ref.at[theirs], rows_of(core)
                    away.append(
                        pltpu.make_async_remote_copy(
                            src_ref=src,
                            dst_ref=dst,
                            send_sem=send_sem,
                            recv_sem=recv_sem,
                            device_id=mate,
                            device_id_type=pl.DeviceIdType.MESH,
                        )
                    )
            return local, away

        def half_rows(buf):
            return buf.at[pl.ds(0, segs * rows // 2)]

        loads, shares = io_copies(ub, rows_in[0], rows_in[1], (0, 2, 0), False)
        more = io_copies(dy, rows_in[2], rows_in[3], (1, 2, 1), False)
        loads, shares = loads + more[0], shares + more[1]
        y_copies = io_copies(doa.at[1], rows_out[0], rows_out[1], (3, 4, 5), True)
        du_copies = io_copies(dy, rows_out[2], rows_out[3], (6, 7, 8), True)
    else:
        loads = [
            pltpu.make_async_copy(rows_in[0], ub, sem_io.at[0]),
            pltpu.make_async_copy(rows_in[1], dy, sem_io.at[1]),
        ]
        shares = []
        y_copies = [pltpu.make_async_copy(doa.at[1], rows_out[0], sem_io.at[3])], []
        du_copies = [pltpu.make_async_copy(dy, rows_out[1], sem_io.at[6])], []
    for copy in loads:
        copy.start()
    if routed:
        vectors = [ref[...].astype(f32) for ref in vectors_in]
        count = vectors[0].shape[1]
        tile = jnp.concatenate([*vectors, jnp.zeros((5, count), f32)], axis=0)
        tile = jnp.concatenate([tile, jnp.zeros((8, lanes - count), f32)], axis=1).T[:count]
        tile = jnp.concatenate([tile, jnp.zeros((count, lanes - 8), f32)], axis=1)
        small_buf[...] = tile.astype(bf16).reshape(small_buf.shape)
        barrier = pltpu.get_barrier_semaphore()
        peers = [mate, near_x, near_y, (core, place(z, 1 - y, 1 - x)), *along_z]
        peers += [(other, place((z + k) % 4, y, x)) for k in range(1, 4)]
        for peer in peers:
            pl.semaphore_signal(barrier, inc=1, device_id=peer, device_id_type=pl.DeviceIdType.MESH)
        pl.semaphore_wait(barrier, len(peers))
        for n in range(8):
            share_own(n)
        for copy in shares:
            copy.start()
        for n in range(8, len(units)):
            share_own(n)
    else:
        for n in range(len(units)):
            weight_copy(n).start()
    stat_ref[...] = jnp.zeros_like(stat_ref)


    def wait_rows(buf, first):
        if routed:
            for k in range(3):
                wait_bytes(half_rows(buf), sem_io.at[first + k])
        else:
            wait_bytes(buf, sem_io.at[first])

    def add_stat(layer, k, values, valid):
        total = jnp.zeros((1, lanes), f32)
        for p in range(values.shape[1] // lanes):
            part = values[:, p * lanes : (p + 1) * lanes]
            total = total + jnp.sum(part * part * valid, axis=0, keepdims=True)
        stat_ref[layer, k : k + 1, :] += total

    def forward_attention(layer, s):
        at = seg_rows(s)
        mask = mask_col(s)

        def pair_cols(k, p):
            return slice(k * width + p * lanes, k * width + (p + 1) * lanes)

        def scores_of(h):
            p, side = h // 2, h % 2
            qp, kp = qkv[at, pair_cols(0, p)], qkv[at, pair_cols(1, p)]
            own, marks = lane_marks(head_size, side)
            bias = gain_sums[0, h * slots : (h + 1) * slots]
            hi = bias.astype(bf16).astype(f32)
            aux = jnp.concatenate([hi * marks[1] + (bias - hi) * marks[2], jnp.zeros((tok_rows, lanes), f32)], axis=0)
            aux = aux + mask * marks[0]
            extra = marks[0] + marks[1] + marks[2]
            ka = kp * own.astype(bf16) + aux.astype(bf16)
            qa = qp * (1.0 - extra).astype(bf16) + extra.astype(bf16)
            return nt(qa, ka)

        scores, outs = scores_of(0), []
        for h in range(heads):
            p, side = h // 2, h % 2
            following = scores_of(h + 1) if h + 1 < heads else None
            top = jnp.max(scores, axis=1, keepdims=True)
            weights = jnp.exp2(scores - top).astype(bf16)
            ebuf[s, h] = weights
            own, _ = lane_marks(head_size, side)
            va = qkv[at, pair_cols(2, p)] * own.astype(bf16) + (1.0 - own).astype(bf16)
            outs.append(mm(weights, va))
            scores = following
            if side == 0:
                continue
            own, _ = lane_marks(head_size, 0)
            raw = jnp.where(own > 0, outs[-2], outs[-1])
            sums = pltpu.roll(jnp.where(own > 0, outs[-1], outs[-2]), head_size, 1)
            inv = 1.0 / sums
            cols = pair_cols(0, p)
            ilbuf[at, cols] = inv.astype(ilbuf.dtype)
            obuf[at, cols] = (raw * inv).astype(bf16)
            if p % 2 == 1:
                after(layer, s, "quad" + str(p // 2))

    def unpack_small(layer):
        small = mat(0, layer, slice(0, lanes)).astype(f32)
        gain_sums[1] = small
        turned = small.T
        for k in range(2):
            gains[layer, k] = turned[k : k + 1, :]
        for h in range(heads):
            column = gain_sums[1, pl.ds(h, slots, stride=heads)][:, 2:3]
            gain_sums[0, h * slots : (h + 1) * slots] = jnp.broadcast_to(column * log2_e, (slots, lanes))

    def take_small(layer):
        complete(8 * layer)
        unpack_small(layer)

    def forward_attn(layer, s):
        at = seg_rows(s)

        @pl.when(layer == 1)
        def _():
            for copy in spill_copies(s, False):
                copy.wait()

        @pl.when(layer == 0)
        def _():
            spill_copies(s, False, (7,))[0].start()

        valid = valid_rows(s)
        x = ub[at, :].astype(f32)
        squares = jnp.sum(x * x, axis=1, keepdims=True)
        add_stat(layer, 0, x, valid)
        add_stat(layer, 3, valid, valid)
        n1 = (x * lax.rsqrt(squares / width + norm_eps) * gains[layer, 0]).astype(bf16)
        for k in range(3):
            part = mm(n1, mat(0, layer, qkv_cols(k)))
            if k == 0:
                part = part * (score_scale * log2_e)
            qkv[at, k * width : (k + 1) * width] = part.astype(bf16)
        after(layer, s, "qkv")
        forward_attention(layer, s)

        @pl.when(layer == 0)
        def _():
            for copy in spill_copies(s, False, range(4)):
                copy.start()

    def ffn_part(s, layer, picks):
        at = seg_rows(s)

        def up(c):
            return mm(doa[0, at, :], mat(2, layer, slice(c * chunk, (c + 1) * chunk)))

        before = up(picks[0])
        for c in picks:
            cols = slice(c * chunk, (c + 1) * chunk)
            following = up(c + 1) if c + 1 in picks else None
            square = before * before
            gate = 0.5 + 0.5 * jnp.tanh(before * (gelu_c + (gelu_c * gelu_k) * square))
            act = before * gate
            slope[at, cols] = (gate + act * (1.0 - gate) * (2.0 * gelu_c + (6.0 * gelu_c * gelu_k) * square)).astype(bf16)
            act = act.astype(bf16)
            active[at, cols] = act
            part = mm(act, mat(3, layer, planes=slice(c, c + 1)))
            if c == 0:
                dn[at, :] = part
            else:
                dn[at, :] += part
            before = following

    def forward_mid(layer, s):
        at = seg_rows(s)
        valid = valid_rows(s)
        z = mm(obuf[at, :], mat(1, layer))
        add_stat(layer, 1, z, valid)
        h = ub[at, :].astype(f32) + z
        hbuf[at, :] = h.astype(bf16)
        doa[0, at, :] = (h * lax.rsqrt(jnp.mean(h * h, axis=1, keepdims=True) + norm_eps) * gains[layer, 1]).astype(bf16)

    def forward_ffn_a(layer, s):
        ffn_part(s, layer, range(ff // chunk // 2))
        after(layer, s, "ffna")

    def forward_ffn_b(layer, s):
        at = seg_rows(s)
        valid = valid_rows(s)
        ffn_part(s, layer, range(ff // chunk // 2, ff // chunk))
        out = dn[at, :]
        add_stat(layer, 2, out, valid)
        result = (hbuf[at, :].astype(f32) + out).astype(bf16)

        @pl.when(layer == 0)
        def _():
            spill_copies(s, False, (7,))[0].wait()
            ub[at, :] = result

        @pl.when(layer == 1)
        def _():
            doa[1, at, :] = result

        @pl.when(layer == 0)
        def _():
            for copy in spill_copies(s, False, (4, 5, 6)):
                copy.start()

        after(layer, s, "ffnb")

    if routed:
        hops(opening)
        wait_bytes(ub, sem_io.at[2])
    wait_bytes(ub, sem_io.at[0])
    wait_bytes(dy, sem_io.at[1])

    @pl.loop(0, 2)
    def _(layer):
        after(layer, 0, "open")
        for at_layer in range(2):
            if at_layer == 1 or not routed:
                @pl.when(layer == at_layer)
                def _(at_layer=at_layer):
                    take_small(at_layer)

        need(layer, [n for n in first_units if n % 8 > 0])

        @pl.loop(0, segs)
        def _(s):
            forward_attn(layer, s)

        after(layer, 0, "gate")
        need(layer, later_units)
        for s in range(segs):
            forward_mid(layer, s)

        @pl.loop(0, segs)
        def _(s):
            forward_ffn_a(layer, s)

        after(layer, 0, "last")
        need(layer, last_units)

        @pl.loop(0, segs)
        def _(s):
            forward_ffn_b(layer, s)

    if routed:
        for n in range(len(units)):
            drain(n)
    for copies in y_copies:
        for copy in copies:
            copy.start()

    if routed:
        wqa_u, wo_u, wu_u, wd_u, wqb_u = range(5)
        half_cols = quads * 3 * lanes
        rs_cols = {wqa_u: slice(0, half_cols), wqb_u: slice(half_cols, 2 * half_cols + lanes)}
        rs_weight = (0, 1, 2, 3, 0)
        chunked = (wu_u, wd_u)
        fast = (wqa_u, wqb_u)
        plane_peers = [near_x, near_y, (core, place(z, 1 - y, 1 - x))]
        plane_spots = [(y, 1 - x), (1 - y, x), (1 - y, 1 - x)]
        chunks = ff // chunk

        def rs_copy(src, dst, u, step, k, target):
            return pltpu.make_async_remote_copy(
                src_ref=src,
                dst_ref=dst,
                send_sem=rs_send.at[u, step],
                recv_sem=rs_recv.at[u, k],
                device_id=target,
                device_id_type=pl.DeviceIdType.MESH,
            )

        def piece_cols(step, piece, u):
            size = chunk if step < 2 else ff // 2
            return slice(piece * size, (piece + 1) * size)

        def piece_planes(step, piece):
            return piece if step < 2 else slice(2 * piece, 2 * piece + 2)

        def spot(layer, u, pz, py, px, c, piece=None, step=0):
            cols = rs_cols.get(u, every)
            if piece is not None and u == wd_u:
                pz = piece_planes(step, piece)
            elif piece is not None:
                cols = piece_cols(step, piece, u)
            return weight_buf[rs_weight[u]].at[layer + 1, pz, py, px, c, every, cols]

        def land_at(u, step, piece=None):
            ref = lands[u][step]
            if piece is None:
                return ref
            ring = piece % 2 if step == 0 else piece
            if u == wd_u:
                return ref.at[piece_planes(step, ring)]
            lead = (every,) * (len(ref.shape) - 1)
            return ref.at[(*lead, piece_cols(step, ring, u))]

        def rs_copies(layer, u, step, y_first, piece=None):
            if step == 0:
                src = spot(layer, u, every, every, every, other, piece)
                return [rs_copy(src, land_at(u, 0, piece), u, 0, (piece or 0) % 2, mate)]
            if step == 1 and u in fast:
                return [
                    rs_copy(spot(layer, u, every, *plane_spots[k], core), lands[u][1].at[k], u, 1, 2, plane_peers[k])
                    for k in range(3)
                ]
            if step == 3 and u in fast:
                return [owner_copy(layer, u, k) for k in range(4)]
            if step == 1:
                at = (every, 1 - y, every) if y_first else (every, every, 1 - x)
                src = spot(layer, u, *at, core, piece)
                return [rs_copy(src, land_at(u, 1, piece), u, 1, 2 + (piece or 0) // 2, near_y if y_first else near_x)]
            if step == 2:
                at = (every, y, 1 - x) if y_first else (every, 1 - y, x)
                src = spot(layer, u, *at, core, piece, 2)
                return [rs_copy(src, land_at(u, 2, piece), u, 2, 4 + (piece or 0), near_x if y_first else near_y)]
            if step == 3:
                cols = piece_cols(3, piece, u) if piece is not None else every
                return [
                    rs_copy(
                        weight_buf[rs_weight[u]].at[layer + 1, (z + k) % 4, y, x, core, every, cols],
                        lands[u][3].at[k - 1, every, cols], u, 3, 6, along_z[k - 1],
                    )
                    for k in range(1, 4)
                ]
            return [rs_copy(src, dst, u, 4, 7, mate) for src, dst in home_parts(layer, u)]

        def owner_copy(layer, u, k):
            away = (z + k + 1) % 4 if k < 3 else z
            half = core
            return pltpu.make_async_remote_copy(
                src_ref=spot(layer, u, away, y, x, core),
                dst_ref=lands[u][3].at[half, k],
                send_sem=rs_send.at[u, 3],
                recv_sem=rs_recv.at[u, 6 + half],
                device_id=(layer, place(away, y, x)),
                device_id_type=pl.DeviceIdType.MESH,
            )

        def start_owner(layer, u):
            for k in range(3):
                owner_copy(layer, u, k).start()

            @pl.when(core != layer)
            def _():
                owner_copy(layer, u, 3).start()

        def merge_owner(layer, u):
            @pl.when(core == layer)
            def _():
                got = lands[u][3]
                wait_bytes(got.at[layer, pl.ds(0, 3)], rs_recv.at[u, 6 + layer])
                wait_bytes(got.at[1 - layer], rs_recv.at[u, 7 - layer])
                cols = rs_cols[u]
                for half in range(2):
                    if half == layer:
                        total = weight_buf[0][layer + 1, z, y, x, half, :, cols].astype(f32)
                    else:
                        total = got[half, 3].astype(f32)
                    for k in range(3):
                        total = total + got[half, k].astype(f32)
                    if u == wqb_u:
                        small = total[:, :lanes].T
                        turned = jnp.concatenate([small[:8, :], jnp.zeros((8, lanes - small.shape[1]), f32)], axis=1)
                        fin[u][half, 0:8, 0:lanes] = turned
                        fin[u][half, :, lanes:] = total[:, lanes:]
                    else:
                        fin[u][half] = total
                for k, (src, dst) in enumerate(home_parts(layer, u)):
                    pltpu.make_async_copy(src, dst, sem_g.at[5 if k == 3 else u]).start()

        def home_parts(layer, u):
            if u not in rs_cols:
                return [(fin[u], grads_out[u].at[core])]
            base, q = (0, 0) if u == wqa_u else (lanes, 1)
            parts = [
                (
                    fin[u].at[:, :, base + k * quad : base + (k + 1) * quad],
                    grads_out[0].at[:, :, k * width + q * quad : k * width + (q + 1) * quad],
                )
                for k in range(3)
            ]
            if u == wqb_u:
                parts.append((fin[u].at[:, 0:8, 0:lanes], grads_out[4]))
            return parts

        def rs_route(u, act):
            for side in range(2):
                @pl.when(core == side)
                def _(side=side):
                    act((side + u) % 2 == 0)

        def on_route(u, step, act):
            if step in (1, 2):
                rs_route(u, act)
            else:
                act(True)

        def rs_pieces(u, step):
            if u in chunked and step < 3:
                return list(range(chunks if step < 2 else 2))
            return [0, 1] if u == wu_u and step == 3 else [None]

        def rs_start(layer, u, step, piece=None):
            if layer == 0 and step < 4 and not piece:
                rs_sent(1, u, step)
            if step == 3 and u in fast:
                start_owner(layer, u)
                return
            used = layer == 0 and not piece
            if u in chunked and step < 3:
                used = (layer == 0 or piece >= 2, layer == 0 and piece % 2 == 0, layer == 0)[step]
            if used and step < 4:
                pl.semaphore_wait(rs_free.at[u, step], 3 if step == 3 or (step == 1 and u in fast) else 1)

            if u == wd_u and step == 3:
                for k, copy in enumerate(rs_copies(layer, u, 3, True)):
                    @pl.when((z + k + 1) % 4 // 2 == piece)
                    def _(copy=copy):
                        copy.start()

                return

            def act(y_first):
                for copy in rs_copies(layer, u, step, y_first, piece):
                    copy.start()

            on_route(u, step, act)

        def give_back(u, step):
            def act(y_first):
                if step == 0:
                    peers = [mate]
                elif step == 3:
                    peers = along_z
                elif u in fast:
                    peers = plane_peers
                else:
                    peers = [near_y if y_first == (step == 1) else near_x]
                for peer in peers:
                    pl.semaphore_signal(rs_free.at[u, step], inc=1, device_id=peer, device_id_type=pl.DeviceIdType.MESH)

            on_route(u, step, act)

        def rs_merge(layer, u, step, piece=None):
            if step == 3 and u in fast:
                merge_owner(layer, u)
                return

            got = lands[u][step]
            sem = (piece or 0) % 2 if step < 3 else 0
            wait_at = land_at(u, step, piece) if step in (0, 2) else got
            if u in chunked and step == 1:
                wait_at = got.at[piece_planes(2, piece)] if u == wd_u else got.at[:, :, :, piece_cols(2, piece, u)]
            wait_bytes(wait_at, rs_recv.at[u, 2 * step + sem])
            slot = layer + 1
            buf = weight_buf[rs_weight[u]]
            cols = rs_cols.get(u, every)
            if step == 3:
                if layer == 0:
                    rs_home(1, u)
                total = buf[slot, z, y, x, core, :, cols].astype(f32)
                for k in range(3):
                    total = total + got[k].astype(f32)
                fin[u][...] = total
                if layer == 1:
                    give_back(u, 3)

                @pl.when(core == layer)
                def _():
                    for src, dst in home_parts(layer, u):
                        pltpu.make_async_copy(src, dst, sem_g.at[u]).start()

                @pl.when(core != layer)
                def _():
                    rs_start(layer, u, 4)

                return
            if step == 0 and piece is not None and u == wd_u:
                buf[slot, piece, :, :, core] += got[piece % 2]
            else:
                got_cols, planes = every, (0, 4)
                if piece is not None and u == wd_u:
                    planes = (2 * piece, 2 * piece + 2)
                elif piece is not None:
                    cols = piece_cols(step if step != 1 else 2, piece, u)
                    got_cols = piece_cols(0, piece % 2, u) if step == 0 else cols

                @pl.loop(*planes)
                def _(pz):
                    if step == 0:
                        buf[slot, pz, :, :, core, :, cols] += got[pz, :, :, :, got_cols]
                    elif u in fast:
                        total = buf[slot, pz, y, x, core, :, cols].astype(f32)
                        for k in range(3):
                            total = total + got[k, pz].astype(f32)
                        buf[slot, pz, y, x, core, :, cols] = total.astype(bf16)
                    elif step == 2:
                        buf[slot, pz, y, x, core, :, cols] += got[pz, :, got_cols]
                    else:
                        def add(y_first):
                            if y_first:
                                buf[slot, pz, y, :, core, :, cols] += got[pz, :, :, got_cols]
                            else:
                                buf[slot, pz, :, x, core, :, cols] += got[pz, :, :, got_cols]

                        rs_route(u, add)

            if layer == 1 or (step == 0 and u in chunked and piece < 2):
                give_back(u, step)
            rs_start(layer, u, 3 if u in fast and step == 1 else step + 1, piece)

        def rs_home(layer, u):
            @pl.when(core == layer)
            def _():
                if u == wqb_u:
                    wait_bytes(fin[u].at[:, :, lanes:], sem_g.at[u])
                    wait_bytes(fin[u].at[:, 0:8, 0:lanes], sem_g.at[5])
                else:
                    wait_bytes(fin[u], sem_g.at[u])
                if u not in fast:
                    for copy in rs_copies(layer, u, 4, True):
                        copy.wait_recv()

            if u not in fast:
                @pl.when(core != layer)
                def _():
                    for copy in rs_copies(layer, u, 4, True):
                        copy.wait_send()

        def rs_sent(layer, u, step):
            three = slice(0, 3)
            if step == 0:
                wait_bytes(spot(layer, u, every, every, every, other), rs_send.at[u, 0])
            elif step == 1 and u in fast:
                wait_bytes(spot(layer, u, three, every, every, core), rs_send.at[u, 1])
            elif step == 1:
                wait_bytes(spot(layer, u, every, y, every, core), rs_send.at[u, 1])
            elif step == 2:
                wait_bytes(spot(layer, u, every, y, x, core), rs_send.at[u, 2])
            elif u not in fast:
                wait_bytes(spot(layer, u, three, y, x, core), rs_send.at[u, 3])
            else:
                @pl.when(core == layer)
                def _():
                    wait_bytes(spot(layer, u, three, y, x, core), rs_send.at[u, 3])

                @pl.when(core != layer)
                def _():
                    wait_bytes(spot(layer, u, every, y, x, core), rs_send.at[u, 3])

        def rs_finish(layer, u):
            for step in (0, 1, 3) if u in fast else range(4):
                rs_sent(layer, u, step)

        def stat_copy(step, k=0):
            target = (mate, near_y, near_x)[step] if step < 3 else along_z[k]
            place_at = step if step < 3 else 3 + z
            return pltpu.make_async_remote_copy(
                src_ref=stat_sum.at[step],
                dst_ref=stat_land.at[place_at],
                send_sem=stat_send.at[step],
                recv_sem=stat_recv.at[step],
                device_id=target,
                device_id_type=pl.DeviceIdType.MESH,
            )

        def stat_step(step):
            if step == 0:
                stat_sum[0] = stat_ref[...]
            elif step < 4:
                stat_copy(step - 1).wait()
                stat_sum[step] = stat_sum[step - 1] + stat_land[step - 1]
            if step < 3:
                stat_copy(step).start()
            elif step == 3:
                stat_land[3 + z] = stat_sum[3]
                for k in range(3):
                    stat_copy(3, k).start()
            else:
                wait_bytes(stat_land.at[pl.ds(3, 3)], stat_recv.at[3])
                wait_bytes(stat_land.at[pl.ds(3, 3)], stat_send.at[3])
                total = stat_land[3] + stat_land[4] + stat_land[5] + stat_land[6]
                stat_ref[...] = total
                stat_done()

        stat_step(0)
        names = dict(a=wqa_u, o=wo_u, u=wu_u, d=wd_u, b=wqb_u)

        def run_events(layer, text):
            for word in text:
                if word[0] == "t":
                    stat_step(int(word[1]))
                    continue
                at_layer = layer
                if word[0] == "p":
                    at_layer, word = layer + 1, word[1:]
                step, u = int(word[1]), names[word[2]]
                piece = int(word[3]) if len(word) > 3 else None
                (rs_start if word[0] == "S" else rs_merge)(at_layer, u, step, piece)

        back_points = {
            (1, "ffn0"): ("S0d0", "S0u0"),
            (1, "ffn1"): ("t1", "M0d0", "M0u0", "S0d1", "S0u1"),
            (1, "ffn2"): ("M0d1", "M0u1", "S0d2", "S0u2"),
            (1, "ffn3"): ("t2", "M0d2", "M0u2", "S0d3", "S0u3"),
            (1, "mid0"): ("M0d3", "M0u3"),
            (1, "wo"): ("t3", "S0o", "M1d0", "M1u0"),
            (1, "att00"): ("M0o", "M1d1", "M1u1"),
            (1, "att01"): ("t4", "M2d0", "M2u0"),
            (1, "wq0"): ("S0a",),
            (1, "att10"): ("M0a", "M1o", "M2d1", "M2u1"),
            (1, "wq1"): ("S0b",),
            (1, "in0"): ("M0b",),
            (0, "ffn0"): ("S0d0", "S0u0", "pM1a", "pM2o"),
            (0, "ffn1"): ("M0d0", "M0u0", "S0d1", "S0u1", "pM1b"),
            (0, "ffn2"): ("M0d1", "M0u1", "S0d2", "S0u2", "pM3d", "pM3u"),
            (0, "ffn3"): ("M0d2", "M0u2", "S0d3", "S0u3", "pM3o", "pM3a"),
            (0, "mid0"): ("M0d3", "M0u3", "pM3b"),
            (0, "wo"): ("S0o", "M1d0", "M1u0"),
            (0, "att00"): ("M0o", "M1d1", "M1u1"),
            (0, "att01"): ("M2d0", "M2u0"),
            (0, "wq0"): ("S0a",),
            (0, "att10"): ("M0a", "M1o", "M2d1", "M2u1"),
            (0, "wq1"): ("S0b", "M1a", "M0b"),
            (0, "in0"): ("M2o",),
            (0, "end"): ("M1b", "M3d", "M3u", "M3o", "M3a", "M3b"),
        }
    else:
        back_points = {}

    def stat_done():
        totals = stat_ref[...]
        stat_out[...] = totals if not routed else jnp.broadcast_to(
            jnp.sqrt(jnp.sum(totals, axis=2, keepdims=True) / (totals[0:1, 3:4, 0:1] * width)), totals.shape
        )

    if not routed:
        stat_done()

    def back_point(layer, point, s=None, at=None):
        for (at_layer, at_point), text in back_points.items():
            if at_point == point:
                here = layer == at_layer
                if s is not None:
                    here = here & (s == at)

                @pl.when(here)
                def _(at_layer=at_layer, text=text):
                    run_events(at_layer, text)

    def norm_back(x, gain, grad):
        inv = lax.rsqrt(jnp.mean(x * x, axis=1, keepdims=True) + norm_eps)
        hat = x * inv
        scaled = grad * gain
        return inv * (scaled - hat * jnp.mean(scaled * hat, axis=1, keepdims=True))

    def add_gain(k, d_weight, weight):
        total = gain_sums[k]
        for p in range(d_weight.shape[1] // lanes):
            cols = slice(p * lanes, (p + 1) * lanes)
            total = total + d_weight[:, cols] * weight[:, cols].astype(f32)
        gain_sums[k] = total

    def pack_small(layer):
        sums = [jnp.sum(gain_sums[k], axis=1, keepdims=True) for k in range(2)]
        turned = dbias[...].T
        for h in range(heads):
            gain_sums[1, pl.ds(h, slots, stride=heads)] = jnp.broadcast_to(turned[:slots, h : h + 1], (slots, lanes))
        lane = lax.broadcasted_iota(jnp.int32, (width, lanes), 1)
        gain = mat(0, layer, slice(0, lanes)).astype(f32)
        safe = jnp.where(lane < 2, gain, 1.0)
        value = jnp.where(lane == 0, sums[0], jnp.where(lane == 1, sums[1], 0.0)) / safe
        value = jnp.where(lane == 2, gain_sums[1], value)
        put_mat(0, layer + 1, value.astype(bf16), slice(3 * quad, 3 * quad + lanes))

    def backward_ffn(layer):
        slot = layer + 1

        @pl.loop(0, segs)
        def _(s):
            at = seg_rows(s)
            h = hbuf[at, :].astype(f32)
            doa[0, at, :] = (h * lax.rsqrt(jnp.mean(h * h, axis=1, keepdims=True) + norm_eps) * gains[layer, 1]).astype(bf16)

        gain_sums[...] = jnp.zeros_like(gain_sums)
        dbias[...] = jnp.zeros_like(dbias)
        turned_cols = slice(0, segs * rows)
        put_mat(0, slot, doa[0].T, turned_cols)

        @pl.loop(0, ff // chunk)
        def _(c):
            cols = pl.ds(pl.multiple_of(c * chunk, chunk), chunk)
            planes = pl.ds(c, 1)
            d_act = nt(dy[...], mat(3, layer, planes=planes)).astype(bf16)
            put_mat(3, slot, tn(active[:, cols], dy[...]).astype(bf16), planes=planes)
            d_pre = d_act * slope[:, cols]
            slope[:, cols] = d_pre
            d_up = mm(mat(0, slot, turned_cols), d_pre)
            add_gain(1, d_up, mat(2, layer, cols))
            put_mat(2, slot, d_up.astype(bf16), cols)
            for k in range(ff // chunk):
                back_point(layer, "ffn" + str(k), c, k)

    def backward_middle(layer, s):
        at = seg_rows(s)
        dh = norm_back(hbuf[at, :].astype(f32), gains[layer, 1], nt(slope[at, :], mat(2, layer)))
        v = ub[at, :].astype(f32)
        hbuf[at, :] = (v * lax.rsqrt(jnp.mean(v * v, axis=1, keepdims=True) + norm_eps) * gains[layer, 0]).astype(bf16)
        dh = dh + dy[at, :].astype(f32)
        dn[at, :] = dh
        dz = dh.astype(bf16)
        dy[at, :] = dz
        do = nt(dz, mat(1, layer)) * ilbuf[at, :].astype(f32)
        prod = do.astype(bf16).astype(f32) * obuf[at, :].astype(f32)
        lane = lax.broadcasted_iota(jnp.int32, (1, quad), 1) % head_size
        side = lax.broadcasted_iota(jnp.int32, (1, quad), 1) // head_size % 2
        hi_at, lo_at = (lane == 0).astype(f32), (lane == 1).astype(f32)
        free = 1.0 - hi_at - lo_at
        head_of = lax.broadcasted_iota(jnp.int32, (quad, quad), 0) // head_size
        gets = lax.broadcasted_iota(jnp.int32, (quad, quad), 1) // head_size
        swap_sum = jnp.where(head_of == gets + 1 - 2 * (gets % 2), -1.0, 0.0).astype(bf16)
        for q in range(quads):
            cols = slice(q * quad, (q + 1) * quad)
            upper = prod[:, cols].astype(bf16)
            delta = mm(upper, swap_sum) + mm((prod[:, cols] - upper.astype(f32)).astype(bf16), swap_sum)
            hi = delta.astype(bf16).astype(f32)
            filled = do[:, cols] * free + hi * hi_at + (delta - hi) * lo_at
            for k in range(2):
                doa[k, at, cols] = jnp.where(side == k, do[:, cols], filled).astype(bf16)

    def backward_attention(layer, q, s):
        at = seg_rows(s)

        def pair_cols(k, p):
            return pl.ds(pl.multiple_of(k * width + q * quad + p * lanes, lanes), lanes)

        def d_probs_of(h):
            p, side = h // 2, h % 2
            own, marks = lane_marks(head_size, side)
            do_h = doa[side, at, pair_cols(0, p)]
            va = qkv[at, pair_cols(2, p)] * own.astype(bf16) + (marks[0] + marks[1]).astype(bf16)
            return do_h, nt(do_h, va)

        do_h, d_probs = d_probs_of(0)
        dq, dk, dv = [], [], []
        for h in range(4):
            p, side = h // 2, h % 2
            head = 4 * q + h
            following = d_probs_of(h + 1) if h < 3 else (None, None)
            qp, kp = qkv[at, pair_cols(0, p)], qkv[at, pair_cols(1, p)]
            half = slice(side * head_size, (side + 1) * head_size)
            weights = ebuf[s, head]
            dv.append(mm(do_h.T[half, :], weights))
            d_scores = weights * d_probs.astype(bf16)
            dbias[pl.ds(head, 1), :] += jnp.sum(d_scores[:, :lanes].astype(f32), axis=0, keepdims=True)
            dq.append(mm(d_scores, kp))
            dk.append(mm(qp.T[half, :], d_scores))
            do_h, d_probs = following
            if side == 0:
                continue
            own, _ = lane_marks(head_size, 0)
            qkv[at, pair_cols(0, p)] = (jnp.where(own > 0, dq[-2], dq[-1]) * score_scale).astype(bf16)
            qkv[at, pair_cols(1, p)] = (jnp.concatenate(dk[-2:], axis=0).T * (1.0 / log2_e)).astype(bf16)
            qkv[at, pair_cols(2, p)] = jnp.concatenate(dv[-2:], axis=0).T.astype(bf16)

    def backward_input(layer, s):
        at = seg_rows(s)
        x = ub[at, :].astype(f32)
        du = norm_back(x, gains[layer, 0], nt(qkv[at, :], mat(0, layer, slice(lanes, lanes + 3 * width))))
        dy[at, :] = (du + dn[at, :]).astype(bf16)

    def grad_col(q, k):
        return q * (3 * quad + lanes) + k * quad

    def grad_copies(layer):
        return [
            pltpu.make_async_copy(buf.at[layer + 1], out.at[layer], sem_g.at[k])
            for k, (buf, out) in enumerate(zip(weight_buf, grads_out))
        ]

    @pl.loop(0, 2)
    def _(step):
        layer = 1 - step
        slot = layer + 1

        @pl.when(layer == 0)
        def _():
            for s in range(segs):
                for copy in spill_copies(s, True, (2, 3, 4, 5, 6)):
                    copy.wait()

        backward_ffn(layer)

        @pl.when(layer == 1)
        def _():
            wait_rows(doa.at[1], 3)

        @pl.when(layer == 0)
        def _():
            for s in range(segs):
                spill_copies(s, True, (7,))[0].wait()

        @pl.loop(0, segs)
        def _(s):
            backward_middle(layer, s)
            back_point(layer, "mid0", s, 0)

        put_mat(1, slot, tn(obuf[...], dy[...]).astype(bf16))
        back_point(layer, "wo")

        @pl.when(layer == 1)
        def _():
            for s in range(segs):
                for copy in spill_copies(s, True, (2, 3, 4, 5)):
                    copy.start()

        @pl.loop(0, quads)
        def _(q):
            @pl.loop(0, segs)
            def _(s):
                @pl.when((layer == 0) & (q == 0))
                def _():
                    for copy in spill_copies(s, True, (0, 1)):
                        copy.wait()

                backward_attention(layer, q, s)

                for i in range(quads):
                    for k in range(segs):
                        back_point(layer, "att" + str(i) + str(k), q * segs + s, i * segs + k)

            for k in range(3):
                d_weight = tn(hbuf[...], qkv[:, pl.ds(pl.multiple_of(k * width + q * quad, quad), quad)])
                add_gain(0, d_weight, mat(0, layer, pl.ds(pl.multiple_of(lanes + k * width + q * quad, lanes), quad)))
                put_mat(0, slot, d_weight.astype(bf16), pl.ds(pl.multiple_of(grad_col(q, k), lanes), quad))

            @pl.when((layer == 1) & (q == quads - 1))
            def _():
                for k in (6, 1):
                    for s in range(segs):
                        spill_copies(s, True, (k,))[0].start()

            @pl.when(q == quads - 1)
            def _():
                pack_small(layer)

            for i in range(quads):
                back_point(layer, "wq" + str(i), q, i)

        @pl.loop(0, segs)
        def _(s):
            backward_input(layer, s)
            for k in range(segs):
                back_point(layer, "in" + str(k), s, k)


        @pl.when(layer == 1)
        def _():
            for s in range(segs):
                for copy in spill_copies(s, True, (7, 0)):
                    copy.start()

        if not routed:
            for copy in grad_copies(layer):
                copy.start()
            for copy in grad_copies(layer):
                copy.wait()

    for copies in du_copies:
        for copy in copies:
            copy.start()
    back_point(0, "end")
    if routed:
        for u in range(5):
            rs_finish(0, u)
    if routed:
        for u in range(5):
            rs_home(0, u)
        for u in (0, 4):
            rs_home(1, u)
    wait_rows(dy, 6)


def run_layers(dims, routed, doc_len, row_args, weights):
    segs, rows, width, ff, slots, heads, per_doc = dims
    all_rows = segs * rows
    vmem = pl.BlockSpec(memory_space=pltpu.VMEM)
    smem = pl.BlockSpec(memory_space=pltpu.SMEM)
    hbm = pl.BlockSpec(memory_space=pl.ANY)
    shape = jax.ShapeDtypeStruct
    dma = pltpu.SemaphoreType.DMA
    wide = (all_rows, width)
    tiles = [
        (width // 32, lanes + 3 * width),
        (width // 32, width),
        (width // 32, ff),
        (ff // 32, width),
    ]
    out_shape = [shape(part.shape, bf16) for part in row_args]
    if routed:
        out_shape += [shape((2, width // 32, 3 * width), f32)]
        out_shape += [shape((2, *tile), f32) for tile in tiles[1:]]
        out_shape += [shape((2, 8, lanes), f32)]
    else:
        out_shape += [shape((2, 4, 2, 2, 2, *tile), bf16) for tile in tiles]
    row_outs = len(out_shape)
    out_shape += [shape((2, 8, lanes), f32)]
    out_shape += [
        shape((all_rows, 3 * width), bf16),
        shape((segs, heads, rows, rows), bf16),
        shape(wide, bf16),
        shape(wide, bf16),
        shape((all_rows, ff), bf16),
        shape((all_rows, ff), bf16),
        shape(wide, bf16),
        shape(wide, bf16),
    ]
    unit_count = 16
    scratch = [pltpu.VMEM((3, 4, 2, 2, 2, *tile), bf16) for tile in tiles]
    scratch += [
        pltpu.VMEM(wide, bf16),
        pltpu.VMEM(wide, bf16),
        pltpu.VMEM((all_rows, 3 * width), bf16),
        pltpu.VMEM((segs, heads, rows, rows), bf16),
        pltpu.VMEM(wide, bf16),
        pltpu.VMEM(wide, bf16),
        pltpu.VMEM(wide, bf16),
        pltpu.VMEM((all_rows, ff), bf16),
        pltpu.VMEM((all_rows, ff), bf16),
        pltpu.VMEM((2, *wide), bf16),
        pltpu.VMEM(wide, f32),
        pltpu.VMEM((2, 2, 1, width), f32),
        pltpu.VMEM((2, width, lanes), f32),
        pltpu.VMEM((heads, lanes), f32),
        pltpu.VMEM((2, 8, lanes), f32),
        dma((segs, 8)),
        dma((8,)),
        dma((9,)),
        dma((unit_count, 2)),
        dma((unit_count, 6)),
    ]
    params = dict(vmem_limit_bytes=127 * 2**19)
    if routed:
        params.update(collective_id=0, has_side_effects=True)
        half_cols = 3 * width // 2
        rs_tiles = [(width // 32, half_cols), *tiles[1:], (width // 32, half_cols + lanes)]
        first_tiles = [(4, 2, 2, *tile) for tile in rs_tiles]
        first_tiles[2] = (4, 2, 2, width // 32, 2 * chunk)
        first_tiles[3] = (2, 2, 2, ff // 32, width)
        for u, (first, tile) in enumerate(zip(first_tiles, rs_tiles)):
            leads = ((3, 4), (1,), (2, 4)) if u in (0, 4) else ((4, 2), (4,), (3,))
            scratch += [pltpu.VMEM(first, bf16)]
            scratch += [pltpu.VMEM((*lead, *tile), bf16) for lead in leads]
        scratch += [pltpu.VMEM((2, *tile) if u in (0, 4) else tile, f32) for u, tile in enumerate(rs_tiles)]
        scratch += [
            pltpu.VMEM((4, 2, 8, lanes), f32),
            pltpu.VMEM((7, 2, 8, lanes), f32),
            pltpu.VMEM((2, width // 32, lanes), bf16),
            dma((5, 5)),
            dma((5, 8)),
            pltpu.SemaphoreType.REGULAR((5, 4)),
            dma((4,)),
            dma((4,)),
        ]
    return pl.pallas_call(
        partial(fused_layers, dims, routed),
        out_shape=out_shape,
        in_specs=[smem] + [hbm] * (len(row_args) + 4) + [vmem] * (len(weights) - 4),
        out_specs=[hbm] * row_outs + [vmem] + [hbm] * (len(out_shape) - row_outs - 1),
        scratch_shapes=scratch,
        compiler_params=pltpu.CompilerParams(**params),
    )(doc_len, *row_args, *weights)[: row_outs + 1]


def settle_kernel(*refs):
    count = (len(refs) - 7) // 3
    srcs, (small, stats) = refs[:count], refs[count : count + 2]
    dsts = refs[count + 2 : 2 * count + 2]
    vectors, rms = refs[2 * count + 2 : 2 * count + 5], refs[2 * count + 5]
    mids, sems = refs[2 * count + 6 : -1], refs[-1]
    inward = [pltpu.make_async_copy(src, mid, sems.at[0, k]) for k, (src, mid) in enumerate(zip(srcs, mids))]
    outward = [pltpu.make_async_copy(mid, dst, sems.at[1, k]) for k, (mid, dst) in enumerate(zip(mids, dsts))]
    for copy in inward:
        copy.start()
    for k, vector in enumerate(vectors):
        size = vector.shape[1] // 2
        vector[...] = jnp.concatenate([small[half, k : k + 1, :size] for half in range(2)], axis=1)
    lane = lax.broadcasted_iota(jnp.int32, (1, lanes), 1)
    for layer in range(2):
        row = sum(jnp.where(lane == k, stats[layer, k : k + 1, :], 0.0) for k in range(3))
        rms[layer : layer + 1, :] = row[:, :3]
    for into, out in zip(inward, outward):
        into.wait()
        out.start()
    for out in outward:
        out.wait()


def settle(big, small, stats):
    vmem = pl.BlockSpec(memory_space=pltpu.VMEM)
    hbm = pl.BlockSpec(memory_space=pl.ANY)
    shape = jax.ShapeDtypeStruct
    size = 2 * big[4].shape[1]
    return pl.pallas_call(
        settle_kernel,
        out_shape=[shape(part.shape, part.dtype) for part in big] + [shape((1, size), f32)] * 3 + [shape((2, 3), f32)],
        in_specs=[hbm] * len(big) + [vmem] * 2,
        out_specs=[hbm] * len(big) + [vmem] * 4,
        scratch_shapes=[pltpu.VMEM(part.shape, part.dtype) for part in big] + [pltpu.SemaphoreType.DMA((2, len(big)))],
    )(*big, small, stats)


def swap(block):
    return lax.ppermute(block, "section", [(0, 1), (1, 0)])


def body(
    tokens,
    memory,
    lengths,
    w_qkv,
    w_out,
    w_up,
    w_down,
    gain_attn,
    gain_ffn,
    forget_bias,
    grad_tokens,
    grad_memory,
):
    section = lax.axis_index("section")
    is_first = section == 0
    micro = tokens.shape[0]
    segs = micro // 2
    half_tok = tokens.shape[1]
    half_mem = memory.shape[1]
    slots = 2 * half_mem
    rows = slots + 2 * half_tok
    width = tokens.shape[2]
    ff = w_up.shape[2]
    heads = forget_bias.shape[1] * lax.axis_size("dp") // slots
    per_doc = micro // lengths.shape[0]
    dims = (segs, rows, width, ff, slots, heads, per_doc)
    if lax.axis_size("dp") == 16 and w_qkv.shape[1] == 32:
        weights = [piece.reshape(2, -1, piece.shape[2]) for piece in (w_qkv, w_out, w_up, w_down)]
        weights += [gain_attn, gain_ffn, forget_bias]
        row_args = (tokens, memory, grad_tokens, grad_memory)
        *outs, small_grads, stats = run_layers(dims, True, lengths, row_args, weights)
        outs = settle(outs, small_grads, stats)
        mats = [grad.reshape(1, -1, grad.shape[2]) for grad in outs[4:8]]
        return (*outs[:4], *mats, *outs[8:])

    own_len = lax.dynamic_slice_in_dim(lengths, section * segs // per_doc, segs // per_doc, 0)
    small = jnp.stack([gain_attn, gain_ffn, forget_bias], axis=2)
    small = jnp.pad(small, ((0, 0), (0, 0), (0, lanes - 3)))
    pieces = (jnp.concatenate([small, w_qkv], axis=2), w_out, w_up, w_down)

    def unpack(grads):
        mat = grads[0]
        half = 3 * width // 2
        parts = [mat[:, :, :half], mat[:, :, half + lanes :]]
        parts = [part.reshape(1, -1, 3, width // 2) for part in parts]
        whole = jnp.concatenate(parts, axis=3).reshape(1, -1, 3 * width)
        return (whole, *grads[1:], *(mat[:, :, half + k] for k in range(3)))

    def own_segs(halves):
        return lax.dynamic_slice_in_dim(halves, section * segs, segs, 0)

    def other_segs(halves):
        return lax.dynamic_slice_in_dim(halves, (1 - section) * segs, segs, 0)

    def both(kept, got):
        return jnp.concatenate(
            [jnp.where(is_first, kept, got), jnp.where(is_first, got, kept)], axis=1
        )

    inputs = (tokens, memory, grad_tokens, grad_memory)
    got = swap(tuple(other_segs(part) for part in inputs))
    full = [both(own_segs(part), other) for part, other in zip(inputs, got)]
    u0 = jnp.concatenate([full[1], full[0]], axis=1).reshape(segs * rows, width)
    dout = jnp.concatenate([full[3], full[2]], axis=1).reshape(segs * rows, width)

    def gather(piece):
        whole = lax.all_gather(piece, ("section", "dp"), axis=1, tiled=True)
        return whole.reshape(2, 4, 2, 2, 2, -1, piece.shape[2])

    y, du, *grads, stats = run_layers(dims, False, own_len, (u0, dout), [gather(piece) for piece in pieces])

    def scatter(grad):
        grad = grad.reshape(2, -1, grad.shape[-1])
        mine = lax.dynamic_index_in_dim(grad, section, 0, keepdims=True)
        other = lax.dynamic_index_in_dim(grad, 1 - section, 0, keepdims=True)
        chip = (mine.astype(f32) + swap(other).astype(f32)).astype(grad.dtype)
        return lax.psum_scatter(chip, "dp", scatter_dimension=1, tiled=True).astype(f32)

    shares = unpack([scatter(grad) for grad in grads])
    totals = lax.psum(stats[:, :4], ("section", "dp"))
    rms = jnp.sqrt(jnp.sum(totals[:, :3], axis=2) / (totals[0, 3, 0] * width))
    result = jnp.stack([y.reshape(segs, rows, width), du.reshape(segs, rows, width)])

    def half_of(which):
        tok = lax.dynamic_slice_in_dim(result, slots + which * half_tok, half_tok, 2)
        mem = lax.dynamic_slice_in_dim(result, which * half_mem, half_mem, 2)
        return tok, mem

    kept = half_of(section)
    got = swap(half_of(1 - section))

    def order(mine, other):
        return jnp.concatenate(
            [jnp.where(is_first, mine, other), jnp.where(is_first, other, mine)], axis=0
        )

    toks = [order(kept[0][k], got[0][k]) for k in range(2)]
    mems = [order(kept[1][k], got[1][k]) for k in range(2)]
    return (toks[0], mems[0], toks[1], mems[1], *shares, rms)


def solution(mesh):
    rows = P("dp", "section", None)
    mats = P("section", "dp", None)
    vecs = P("section", "dp")
    return jax.shard_map(
        body,
        mesh=mesh,
        in_specs=(rows, rows, P("dp"), mats, mats, mats, mats, vecs, vecs, vecs, rows, rows),
        out_specs=(rows, rows, rows, rows, mats, mats, mats, mats, vecs, vecs, vecs, P()),
        check_vma=False,
    )
```

```python
from functools import partial

import jax
import jax.numpy as jnp
from jax import lax
from jax.experimental import pallas as pl
from jax.experimental.pallas import tpu as pltpu
from jax.sharding import PartitionSpec as P

norm_eps = 1e-06
score_scale = 0.125
log2_e = 1.4426950408889634
masked_score = -1000000000.0
gelu_c = 0.7978845608028654
gelu_k = 0.044715
f32 = jnp.float32
bf16 = jnp.bfloat16
lanes = 128
chunk = 512


def mm(a, b, ca=1, cb=0):
    return lax.dot_general(a, b, (((ca,), (cb,)), ((), ())), preferred_element_type=f32)


def nt(a, b):
    return mm(a, b, 1, 1)


def tn(a, b):
    return mm(a, b, 0, 0)


def lane_marks(head_size, side):
    lane = lax.broadcasted_iota(jnp.int32, (1, lanes), 1)
    own = ((lane // head_size) == side).astype(f32)
    first = (1 - side) * head_size
    marks = [(lane == first + k).astype(f32) for k in range(3)]
    return own, marks


def fused_layers(dims, routed, *refs):
    segs, rows, width, ff, slots, heads, per_doc = dims
    refs = list(refs)

    def take(count):
        picked = refs[:count]
        del refs[:count]
        return picked

    (len_ref,) = take(1)
    rows_in = take(4 if routed else 2)
    weight_in = take(4)
    vectors_in = take(3) if routed else []
    rows_out = take(4 if routed else 2)
    grads_out = take(5 if routed else 4)
    (stat_out,) = take(1)
    spill_hbm = take(8)
    weight_buf = take(4)
    ub, dy, qkv, ebuf, obuf, ilbuf, hbuf, slope, active, doa, dn = take(11)
    gains, gain_sums, dbias, stat_ref = take(4)
    sem_spill, sem_g, sem_io, sem_send, sem_recv = take(5)
    if routed:
        lands = [take(4) for _ in range(5)]
        fin = take(5)
        stat_sum, stat_land, small_buf = take(3)
        weight_in = [*weight_in, small_buf]
        rs_recv, rs_free, stat_recv = take(3)
    head_size = width // heads
    pairs = width // lanes
    tok_rows = rows - slots
    quads = width // (2 * lanes)
    quad = 2 * lanes
    first_doc = lax.axis_index("section") * segs // per_doc if routed else 0
    every = slice(None)

    def sent_sem(k):
        return sem_send.at[k // 2, k % 2]

    def wait_bytes(ref, sem):
        pltpu.make_async_copy(ref, ref, sem).wait()

    def units_of(layer):
        half_ff, half_deep = ff // 2, ff // 64
        lead = [
            (0, slice(0, lanes + width), every),
            (0, slice(lanes + width, lanes + 2 * width), every),
            (0, slice(lanes + 2 * width, lanes + 3 * width), every),
        ]
        rest = [(1, every, every)]
        rest += [(3, every, slice(k * half_deep, (k + 1) * half_deep)) for k in range(2)]
        rest += [(2, slice(k * half_ff, (k + 1) * half_ff), every) for k in range(2)]
        return [(layer, *unit) for unit in lead + rest]

    units = units_of(0) + units_of(1)
    first_units = [k for k, unit in enumerate(units) if unit[1] == 0]
    last_units = [7, 15]
    later_units = [k for k, unit in enumerate(units) if unit[1] != 0 and k not in last_units]
    plane_first = (11, 15)

    def view(n, z, y, x, c):
        layer, which, cols, part = units[n]
        return weight_buf[which].at[layer, z, y, x, c, part, cols]

    if routed:
        core = lax.axis_index("section")
        chip = lax.axis_index("dp")
        z, y, x = chip // 4, (chip // 2) % 2, chip % 2
        other = 1 - core

        def place(pz, py, px):
            return pz * 4 + py * 2 + px

        mate = (other, chip)
        near_x = (core, place(z, y, 1 - x))
        near_y = (core, place(z, 1 - y, x))
        along_z = [(core, place((z + k) % 4, y, x)) for k in range(1, 4)]

        def remote(src, dst, n, k, target):
            far = k in (4, 5, 9, 10) or (k in (0, 11) and n in plane_first)
            arrived = {0: 0, 11: 0, 1: 1, 2: 1, 3: 1, 4: 2, 5: 3, 6: 4, 7: 4, 8: 4, 9: 5, 10: 5}[k]
            return pltpu.make_async_remote_copy(
                src_ref=src,
                dst_ref=dst,
                send_sem=sem_send.at[n, int(far)],
                recv_sem=sem_recv.at[n, arrived],
                device_id=target,
                device_id_type=pl.DeviceIdType.MESH,
            )

        def some(n, shards, half):
            return view(n, slice(0, 3), y, x, half) if shards == 3 else view(n, slice(0, 3), every, every, half)

        def own_shards(n):
            layer, which, cols, part = units[n]
            home = weight_buf[which].at[layer, z, y, x]
            if which > 0:
                return [(weight_in[which].at[every, part, cols], home.at[every, part, cols], 0)]
            start = max(cols.start - lanes, 0)
            matrix = slice(start, cols.stop - lanes)
            pairs_of = [(weight_in[0].at[every, every, matrix], home.at[every, every, slice(start + lanes, cols.stop)], 0)]
            if cols.start == 0:
                pairs_of.append((weight_in[4], home.at[every, every, slice(0, lanes)], 11))
            return pairs_of

        def z_copy(n, k):
            where = view(n, z, every, every, core) if n in plane_first else view(n, z, y, x, core)
            return remote(where, where, n, k, along_z[k - 1])

        def plane_copy(n, k, x_first):
            planes = z if n in plane_first else every
            if k == 4:
                where = view(n, planes, y, x, core)
                return remote(where, where, n, 4, near_x if x_first else near_y)
            where = view(n, planes, y, every, core) if x_first else view(n, planes, every, x, core)
            return remote(where, where, n, 5, near_y if x_first else near_x)

        def mate_copy(n, k, x_first, half):
            planes = z if n in plane_first else every
            if k < 9:
                from_z = (z + 4 - (k - 5)) % 4
                where = view(n, from_z, every, every, half) if n in plane_first else view(n, from_z, y, x, half)
            elif k == 9:
                where = view(n, planes, y, 1 - x, half) if x_first else view(n, planes, 1 - y, x, half)
            else:
                where = view(n, planes, 1 - y, every, half) if x_first else view(n, planes, every, 1 - x, half)
            return remote(where, where, n, k, mate)

        def by_route(n, act):
            for side in range(2):
                @pl.when(core == side)
                def _(side=side):
                    act((side + n) % 2 == 0)

        def share_own(n):
            @pl.when(core == units[n][0])
            def _():
                for src, dst, k in own_shards(n):
                    pltpu.make_async_copy(src, dst, sem_recv.at[n, 0]).start()
                    remote(src, dst, n, k, mate).start()

        def start_z(n):
            wait_bytes(view(n, z, y, x, every), sem_recv.at[n, 0])
            if n in plane_first:
                by_route(n, lambda x_first: plane_copy(n, 4, x_first).start())
            else:
                for k in range(1, 4):
                    z_copy(n, k).start()

        def first_hop(n):
            if n not in plane_first:
                wait_bytes(some(n, 3, core), sem_recv.at[n, 1])

            def act(x_first):
                if n in plane_first:
                    plane_copy(n, 4, x_first).wait_recv()
                    plane_copy(n, 5, x_first).start()
                    mate_copy(n, 9, x_first, core).start()
                else:
                    plane_copy(n, 4, x_first).start()
                    for k in range(6, 9):
                        mate_copy(n, k, x_first, core).start()

            by_route(n, act)

        def second_hop(n):
            def act(x_first):
                if n in plane_first:
                    plane_copy(n, 5, x_first).wait_recv()
                    for k in range(1, 4):
                        z_copy(n, k).start()
                    mate_copy(n, 10, x_first, core).start()
                else:
                    plane_copy(n, 4, x_first).wait_recv()
                    plane_copy(n, 5, x_first).start()
                    mate_copy(n, 9, x_first, core).start()

            by_route(n, act)

        def last_share(n):
            def act(x_first):
                if n in plane_first:
                    wait_bytes(some(n, 12, core), sem_recv.at[n, 1])
                    for k in range(6, 9):
                        mate_copy(n, k, x_first, core).start()
                else:
                    plane_copy(n, 5, x_first).wait_recv()
                    mate_copy(n, 10, x_first, core).start()

            by_route(n, act)

        def complete(n):
            near, rest = (12, 3) if n in plane_first else (3, 12)
            wait_bytes(some(n, near, other), sem_recv.at[n, 4])
            wait_bytes(some(n, rest, other), sem_recv.at[n, 5])

        def drain(n):
            few, many = (1, 0) if n in plane_first else (0, 1)
            wait_bytes(view(n, slice(0, 3), every, every, every), sem_send.at[n, many])

            @pl.when(core == units[n][0])
            def _():
                wait_bytes(view(n, every, y, x, every), sem_send.at[n, few])

            @pl.when(core != units[n][0])
            def _():
                wait_bytes(view(n, slice(0, 3), y, x, every), sem_send.at[n, few])

        def hops(text):
            kinds = dict(z=start_z, f=first_hop, s=second_hop, l=last_share, u=take_small)
            for word in text:
                kinds[word[0]](int(word[1:]))

        opening = ("z0", "z1", "z2", "z3", "z4", "z5", "f0", "f1", "s0", "z6", "f2", "s1", "z7", "f3", "s2", "l0", "f4", "s3", "l1", "f5", "u0", "l2", "s4", "f6", "z8", "z9", "z11")
        hops_at = {
            (0, 0, "qkv"): ("s5", "f7", "z10", "z15"),
            (0, 0, "quad0"): ("s6", "z12", "l3"),
            (0, 0, "quad1"): ("f8", "f11", "z13"),
            (0, 1, "qkv"): ("s7", "f9", "l4"),
            (0, 1, "quad0"): ("f10", "s8", "z14", "f15", "l5"),
            (0, 1, "quad1"): ("l6", "s11"),
            (0, 0, "gate"): ("f12",),
            (0, 0, "ffna"): ("l7", "s9", "s10", "f13"),
            (0, 1, "ffna"): ("s15",),
            (0, 0, "ffnb"): ("s12", "l8", "f14"),
            (0, 1, "ffnb"): ("s13", "l9", "l10"),
            (1, 0, "qkv"): ("s14",),
            (1, 1, "qkv"): ("l12", "l13"),
            (1, 1, "quad0"): ("l11", "l14"),
            (1, 1, "quad1"): ("l15",),
        }
    else:
        hops_at = {}

        def weight_copy(n):
            layer, which, cols, part = units[n]
            src = weight_in[which].at[layer, every, every, every, every, part, cols]
            return pltpu.make_async_copy(src, view(n, every, every, every, every), sem_recv.at[n, 0])

        def complete(n):
            weight_copy(n).wait()

    def after(layer, s, point):
        for (at_layer, at_s, at_point), text in hops_at.items():
            if at_point == point:
                @pl.when((layer == at_layer) & (s == at_s))
                def _(text=text):
                    hops(text)

    def need(layer, picks):
        for at_layer in range(2):
            @pl.when(layer == at_layer)
            def _(at_layer=at_layer):
                for n in picks:
                    if units[n][0] == at_layer:
                        complete(n)

    def mat(which, slot, cols=every, planes=None):
        if planes is None:
            value = weight_buf[which][slot, :, :, :, :, :, cols]
        else:
            value = weight_buf[which][slot, planes, :, :, :, :, cols]
        deep = 1
        for size in value.shape[:-1]:
            deep *= size
        return value.reshape(deep, value.shape[-1])

    def put_mat(which, slot, value, cols=every, planes=None):
        buf = weight_buf[which]
        shape = buf.shape[1:-1]
        if planes is None:
            buf[slot, :, :, :, :, :, cols] = value.reshape(*shape, value.shape[-1])
        else:
            buf[slot, planes] = value.reshape(1, *shape[1:], value.shape[-1])

    def qkv_cols(k):
        return slice(lanes + k * width, lanes + (k + 1) * width)

    def seg_rows(s):
        return pl.ds(pl.multiple_of(s * rows, rows), rows)

    def spill_copies(s, back, picks=range(7)):
        at = seg_rows(s)
        kept = (qkv.at[at], ebuf.at[s], obuf.at[at], ilbuf.at[at], slope.at[at], active.at[at], hbuf.at[at], ub.at[at])
        pairs_of = [
            (vmem, hbm.at[s] if k == 1 else hbm.at[at])
            for k, (vmem, hbm) in enumerate(zip(kept, spill_hbm))
        ]
        if back:
            return [
                pltpu.make_async_copy(hbm, vmem, sem_spill.at[s, k])
                for k, (vmem, hbm) in enumerate(pairs_of)
                if k in picks
            ]
        return [
            pltpu.make_async_copy(vmem, hbm, sem_spill.at[s, k])
            for k, (vmem, hbm) in enumerate(pairs_of)
            if k in picks
        ]

    def doc_end(s):
        return len_ref[first_doc + s // per_doc] - (s % per_doc) * tok_rows

    def valid_rows(s):
        row = lax.broadcasted_iota(jnp.int32, (rows, lanes), 0)
        return jnp.where(
            (row >= slots) & (row - slots < doc_end(s)), 1.0, 0.0
        ).astype(f32)

    def mask_col(s):
        row = lax.broadcasted_iota(jnp.int32, (rows, 1), 0)
        return jnp.where(
            (row >= slots) & (row - slots >= doc_end(s)), masked_score, 0.0
        ).astype(f32)

    if routed:
        half_tok, half_mem = tok_rows // 2, slots // 2

        def io_copies(buf, tok_ref, mem_ref, sems, outward):
            local, away = [], []
            own_sem, send_sem, recv_sem = (sem_io.at[k] for k in sems)
            for s in range(segs):
                mine, theirs = core * segs + s, other * segs + s
                for ref, base, size in ((tok_ref, slots, half_tok), (mem_ref, 0, half_mem)):
                    def rows_of(half):
                        return buf.at[pl.ds(pl.multiple_of(s * rows + base + half * size, 16), size)]

                    if outward:
                        local.append(pltpu.make_async_copy(rows_of(core), ref.at[mine], own_sem))
                        src, dst = rows_of(other), ref.at[mine]
                    else:
                        local.append(pltpu.make_async_copy(ref.at[mine], rows_of(core), own_sem))
                        src, dst = ref.at[theirs], rows_of(core)
                    away.append(
                        pltpu.make_async_remote_copy(
                            src_ref=src,
                            dst_ref=dst,
                            send_sem=send_sem,
                            recv_sem=recv_sem,
                            device_id=mate,
                            device_id_type=pl.DeviceIdType.MESH,
                        )
                    )
            return local, away

        def half_rows(buf):
            return buf.at[pl.ds(0, segs * rows // 2)]

        loads, shares = io_copies(ub, rows_in[0], rows_in[1], (0, 2, 0), False)
        more = io_copies(dy, rows_in[2], rows_in[3], (1, 2, 1), False)
        loads, shares = loads + more[0], shares + more[1]
        y_copies = io_copies(doa.at[1], rows_out[0], rows_out[1], (3, 4, 5), True)
        du_copies = io_copies(dy, rows_out[2], rows_out[3], (6, 7, 8), True)
    else:
        loads = [
            pltpu.make_async_copy(rows_in[0], ub, sem_io.at[0]),
            pltpu.make_async_copy(rows_in[1], dy, sem_io.at[1]),
        ]
        shares = []
        y_copies = [pltpu.make_async_copy(doa.at[1], rows_out[0], sem_io.at[3])], []
        du_copies = [pltpu.make_async_copy(dy, rows_out[1], sem_io.at[6])], []
    for copy in loads:
        copy.start()
    if routed:
        vectors = [ref[...].astype(f32) for ref in vectors_in]
        count = vectors[0].shape[1]
        tile = jnp.concatenate([*vectors, jnp.zeros((5, count), f32)], axis=0)
        tile = jnp.concatenate([tile, jnp.zeros((8, lanes - count), f32)], axis=1).T[:count]
        tile = jnp.concatenate([tile, jnp.zeros((count, lanes - 8), f32)], axis=1)
        small_buf[...] = tile.astype(bf16).reshape(small_buf.shape)
        barrier = pltpu.get_barrier_semaphore()
        peers = [mate, near_x, near_y, (core, place(z, 1 - y, 1 - x)), *along_z]
        peers += [(other, place((z + k) % 4, y, x)) for k in range(1, 4)]
        for peer in peers:
            pl.semaphore_signal(barrier, inc=1, device_id=peer, device_id_type=pl.DeviceIdType.MESH)
        pl.semaphore_wait(barrier, len(peers))
        for n in range(8):
            share_own(n)
        for copy in shares:
            copy.start()
        for n in range(8, len(units)):
            share_own(n)
    else:
        for n in range(len(units)):
            weight_copy(n).start()
    stat_ref[...] = jnp.zeros_like(stat_ref)


    def wait_rows(buf, first):
        if routed:
            for k in range(3):
                wait_bytes(half_rows(buf), sem_io.at[first + k])
        else:
            wait_bytes(buf, sem_io.at[first])

    def add_stat(layer, k, values, valid):
        total = jnp.zeros((1, lanes), f32)
        for p in range(values.shape[1] // lanes):
            part = values[:, p * lanes : (p + 1) * lanes]
            total = total + jnp.sum(part * part * valid, axis=0, keepdims=True)
        stat_ref[layer, k : k + 1, :] += total

    def forward_attention(layer, s):
        at = seg_rows(s)
        mask = mask_col(s)

        def pair_cols(k, p):
            return slice(k * width + p * lanes, k * width + (p + 1) * lanes)

        def scores_of(h):
            p, side = h // 2, h % 2
            qp, kp = qkv[at, pair_cols(0, p)], qkv[at, pair_cols(1, p)]
            own, marks = lane_marks(head_size, side)
            bias = gain_sums[0, h * slots : (h + 1) * slots]
            hi = bias.astype(bf16).astype(f32)
            aux = jnp.concatenate([hi * marks[1] + (bias - hi) * marks[2], jnp.zeros((tok_rows, lanes), f32)], axis=0)
            aux = aux + mask * marks[0]
            extra = marks[0] + marks[1] + marks[2]
            ka = kp * own.astype(bf16) + aux.astype(bf16)
            qa = qp * (1.0 - extra).astype(bf16) + extra.astype(bf16)
            return nt(qa, ka)

        scores, outs = scores_of(0), []
        for h in range(heads):
            p, side = h // 2, h % 2
            following = scores_of(h + 1) if h + 1 < heads else None
            top = jnp.max(scores, axis=1, keepdims=True)
            weights = jnp.exp2(scores - top).astype(bf16)
            ebuf[s, h] = weights
            own, _ = lane_marks(head_size, side)
            va = qkv[at, pair_cols(2, p)] * own.astype(bf16) + (1.0 - own).astype(bf16)
            outs.append(mm(weights, va))
            scores = following
            if side == 0:
                continue
            own, _ = lane_marks(head_size, 0)
            raw = jnp.where(own > 0, outs[-2], outs[-1])
            sums = pltpu.roll(jnp.where(own > 0, outs[-1], outs[-2]), head_size, 1)
            inv = 1.0 / sums
            cols = pair_cols(0, p)
            ilbuf[at, cols] = inv.astype(ilbuf.dtype)
            obuf[at, cols] = (raw * inv).astype(bf16)
            if p % 2 == 1:
                after(layer, s, "quad" + str(p // 2))

    def unpack_small(layer):
        small = mat(0, layer, slice(0, lanes)).astype(f32)
        gain_sums[1] = small
        turned = small.T
        for k in range(2):
            gains[layer, k] = turned[k : k + 1, :]
        for h in range(heads):
            column = gain_sums[1, pl.ds(h, slots, stride=heads)][:, 2:3]
            gain_sums[0, h * slots : (h + 1) * slots] = jnp.broadcast_to(column * log2_e, (slots, lanes))

    def take_small(layer):
        complete(8 * layer)
        unpack_small(layer)

    def forward_attn(layer, s):
        at = seg_rows(s)

        @pl.when(layer == 1)
        def _():
            for copy in spill_copies(s, False):
                copy.wait()

        @pl.when(layer == 0)
        def _():
            spill_copies(s, False, (7,))[0].start()

        valid = valid_rows(s)
        x = ub[at, :].astype(f32)
        squares = jnp.sum(x * x, axis=1, keepdims=True)
        add_stat(layer, 0, x, valid)
        add_stat(layer, 3, valid, valid)
        n1 = (x * lax.rsqrt(squares / width + norm_eps) * gains[layer, 0]).astype(bf16)
        for k in range(3):
            part = mm(n1, mat(0, layer, qkv_cols(k)))
            if k == 0:
                part = part * (score_scale * log2_e)
            qkv[at, k * width : (k + 1) * width] = part.astype(bf16)
        after(layer, s, "qkv")
        forward_attention(layer, s)

        @pl.when(layer == 0)
        def _():
            for copy in spill_copies(s, False, range(4)):
                copy.start()

    def ffn_part(s, layer, picks):
        at = seg_rows(s)

        def up(c):
            return mm(doa[0, at, :], mat(2, layer, slice(c * chunk, (c + 1) * chunk)))

        before = up(picks[0])
        for c in picks:
            cols = slice(c * chunk, (c + 1) * chunk)
            following = up(c + 1) if c + 1 in picks else None
            square = before * before
            gate = 0.5 + 0.5 * jnp.tanh(before * (gelu_c + (gelu_c * gelu_k) * square))
            act = before * gate
            slope[at, cols] = (gate + act * (1.0 - gate) * (2.0 * gelu_c + (6.0 * gelu_c * gelu_k) * square)).astype(bf16)
            act = act.astype(bf16)
            active[at, cols] = act
            part = mm(act, mat(3, layer, planes=slice(c, c + 1)))
            if c == 0:
                dn[at, :] = part
            else:
                dn[at, :] += part
            before = following

    def forward_mid(layer, s):
        at = seg_rows(s)
        valid = valid_rows(s)
        z = mm(obuf[at, :], mat(1, layer))
        add_stat(layer, 1, z, valid)
        h = ub[at, :].astype(f32) + z
        hbuf[at, :] = h.astype(bf16)
        doa[0, at, :] = (h * lax.rsqrt(jnp.mean(h * h, axis=1, keepdims=True) + norm_eps) * gains[layer, 1]).astype(bf16)

    def forward_ffn_a(layer, s):
        ffn_part(s, layer, range(ff // chunk // 2))
        after(layer, s, "ffna")

    def forward_ffn_b(layer, s):
        at = seg_rows(s)
        valid = valid_rows(s)
        ffn_part(s, layer, range(ff // chunk // 2, ff // chunk))
        out = dn[at, :]
        add_stat(layer, 2, out, valid)
        result = (hbuf[at, :].astype(f32) + out).astype(bf16)

        @pl.when(layer == 0)
        def _():
            spill_copies(s, False, (7,))[0].wait()
            ub[at, :] = result

        @pl.when(layer == 1)
        def _():
            doa[1, at, :] = result

        @pl.when(layer == 0)
        def _():
            for copy in spill_copies(s, False, (4, 5, 6)):
                copy.start()

        after(layer, s, "ffnb")

    if routed:
        hops(opening)
        wait_bytes(ub, sem_io.at[2])
    wait_bytes(ub, sem_io.at[0])
    wait_bytes(dy, sem_io.at[1])

    @pl.loop(0, 2)
    def _(layer):
        after(layer, 0, "open")
        for at_layer in range(2):
            if at_layer == 1 or not routed:
                @pl.when(layer == at_layer)
                def _(at_layer=at_layer):
                    take_small(at_layer)

        need(layer, [n for n in first_units if n % 8 > 0])

        @pl.loop(0, segs)
        def _(s):
            forward_attn(layer, s)

        after(layer, 0, "gate")
        need(layer, later_units)
        for s in range(segs):
            forward_mid(layer, s)

        @pl.loop(0, segs)
        def _(s):
            forward_ffn_a(layer, s)

        after(layer, 0, "last")
        need(layer, last_units)

        @pl.loop(0, segs)
        def _(s):
            forward_ffn_b(layer, s)

    if routed:
        for n in range(len(units)):
            drain(n)
    for copies in y_copies:
        for copy in copies:
            copy.start()

    if routed:
        wqa_u, wo_u, wu_u, wd_u, wqb_u = range(5)
        half_cols = quads * 3 * lanes
        rs_cols = {wqa_u: slice(0, half_cols), wqb_u: slice(half_cols, 2 * half_cols + lanes)}
        rs_weight = (0, 1, 2, 3, 0)
        chunked = (wu_u, wd_u)
        fast = (wqa_u, wqb_u)
        plane_peers = [near_x, near_y, (core, place(z, 1 - y, 1 - x))]
        plane_spots = [(y, 1 - x), (1 - y, x), (1 - y, 1 - x)]
        chunks = ff // chunk

        def rs_copy(src, dst, u, step, k, target):
            return pltpu.make_async_remote_copy(
                src_ref=src,
                dst_ref=dst,
                send_sem=sent_sem(5 * u + step),
                recv_sem=rs_recv.at[u, k],
                device_id=target,
                device_id_type=pl.DeviceIdType.MESH,
            )

        def piece_cols(step, piece, u):
            size = chunk if step < 2 else ff // 2
            return slice(piece * size, (piece + 1) * size)

        def piece_planes(step, piece):
            return piece if step < 2 else slice(2 * piece, 2 * piece + 2)

        def spot(layer, u, pz, py, px, c, piece=None, step=0):
            cols = rs_cols.get(u, every)
            if piece is not None and u == wd_u:
                pz = piece_planes(step, piece)
            elif piece is not None:
                cols = piece_cols(step, piece, u)
            return weight_buf[rs_weight[u]].at[layer + 1, pz, py, px, c, every, cols]

        def land_at(u, step, piece=None):
            ref = lands[u][step]
            if piece is None:
                return ref
            ring = piece % 2 if step == 0 else piece
            if u == wd_u:
                return ref.at[piece_planes(step, ring)]
            lead = (every,) * (len(ref.shape) - 1)
            return ref.at[(*lead, piece_cols(step, ring, u))]

        def rs_copies(layer, u, step, y_first, piece=None):
            if step == 0:
                src = spot(layer, u, every, every, every, other, piece)
                return [rs_copy(src, land_at(u, 0, piece), u, 0, (piece or 0) % 2, mate)]
            if step == 1 and u in fast:
                return [
                    rs_copy(spot(layer, u, every, *plane_spots[k], core), lands[u][1].at[k], u, 1, 2, plane_peers[k])
                    for k in range(3)
                ]
            if step == 3 and u in fast:
                return [owner_copy(layer, u, k) for k in range(4)]
            if step == 1:
                at = (every, 1 - y, every) if y_first else (every, every, 1 - x)
                src = spot(layer, u, *at, core, piece)
                return [rs_copy(src, land_at(u, 1, piece), u, 1, 2 + (piece or 0) // 2, near_y if y_first else near_x)]
            if step == 2:
                at = (every, y, 1 - x) if y_first else (every, 1 - y, x)
                src = spot(layer, u, *at, core, piece, 2)
                return [rs_copy(src, land_at(u, 2, piece), u, 2, 4 + (piece or 0), near_x if y_first else near_y)]
            if step == 3:
                cols = piece_cols(3, piece, u) if piece is not None else every
                return [
                    rs_copy(
                        weight_buf[rs_weight[u]].at[layer + 1, (z + k) % 4, y, x, core, every, cols],
                        lands[u][3].at[k - 1, every, cols], u, 3, 6, along_z[k - 1],
                    )
                    for k in range(1, 4)
                ]
            return [rs_copy(src, dst, u, 4, 7, mate) for src, dst in home_parts(layer, u)]

        def owner_copy(layer, u, k):
            away = (z + k + 1) % 4 if k < 3 else z
            half = core
            return pltpu.make_async_remote_copy(
                src_ref=spot(layer, u, away, y, x, core),
                dst_ref=lands[u][3].at[half, k],
                send_sem=sent_sem(5 * u + 3),
                recv_sem=rs_recv.at[u, 6 + half],
                device_id=(layer, place(away, y, x)),
                device_id_type=pl.DeviceIdType.MESH,
            )

        def start_owner(layer, u):
            for k in range(3):
                owner_copy(layer, u, k).start()

            @pl.when(core != layer)
            def _():
                owner_copy(layer, u, 3).start()

        def merge_owner(layer, u):
            @pl.when(core == layer)
            def _():
                got = lands[u][3]
                wait_bytes(got.at[layer, pl.ds(0, 3)], rs_recv.at[u, 6 + layer])
                wait_bytes(got.at[1 - layer], rs_recv.at[u, 7 - layer])
                cols = rs_cols[u]
                for half in range(2):
                    if half == layer:
                        total = weight_buf[0][layer + 1, z, y, x, half, :, cols].astype(f32)
                    else:
                        total = got[half, 3].astype(f32)
                    for k in range(3):
                        total = total + got[half, k].astype(f32)
                    if u == wqb_u:
                        small = total[:, :lanes].T
                        turned = jnp.concatenate([small[:8, :], jnp.zeros((8, lanes - small.shape[1]), f32)], axis=1)
                        fin[u][half, 0:8, 0:lanes] = turned
                        fin[u][half, :, lanes:] = total[:, lanes:]
                    else:
                        fin[u][half] = total
                for k, (src, dst) in enumerate(home_parts(layer, u)):
                    pltpu.make_async_copy(src, dst, sem_g.at[5 if k == 3 else u]).start()

        def home_parts(layer, u):
            if u not in rs_cols:
                return [(fin[u], grads_out[u].at[core])]
            base, q = (0, 0) if u == wqa_u else (lanes, 1)
            parts = [
                (
                    fin[u].at[:, :, base + k * quad : base + (k + 1) * quad],
                    grads_out[0].at[:, :, k * width + q * quad : k * width + (q + 1) * quad],
                )
                for k in range(3)
            ]
            if u == wqb_u:
                parts.append((fin[u].at[:, 0:8, 0:lanes], grads_out[4]))
            return parts

        def rs_route(u, act):
            for side in range(2):
                @pl.when(core == side)
                def _(side=side):
                    act((side + u) % 2 == 0)

        def on_route(u, step, act):
            if step in (1, 2):
                rs_route(u, act)
            else:
                act(True)

        def rs_pieces(u, step):
            if u in chunked and step < 3:
                return list(range(chunks if step < 2 else 2))
            return [0, 1] if u == wu_u and step == 3 else [None]

        def rs_start(layer, u, step, piece=None):
            if layer == 0 and step < 4 and not piece:
                rs_sent(1, u, step)
            if step == 3 and u in fast:
                start_owner(layer, u)
                return
            used = layer == 0 and not piece
            if u in chunked and step < 3:
                used = (layer == 0 or piece >= 2, layer == 0 and piece % 2 == 0, layer == 0)[step]
            if used and step < 4:
                pl.semaphore_wait(rs_free.at[u, step], 3 if step == 3 or (step == 1 and u in fast) else 1)

            if u == wd_u and step == 3:
                for k, copy in enumerate(rs_copies(layer, u, 3, True)):
                    @pl.when((z + k + 1) % 4 // 2 == piece)
                    def _(copy=copy):
                        copy.start()

                return

            def act(y_first):
                for copy in rs_copies(layer, u, step, y_first, piece):
                    copy.start()

            on_route(u, step, act)

        def give_back(u, step):
            def act(y_first):
                if step == 0:
                    peers = [mate]
                elif step == 3:
                    peers = along_z
                elif u in fast:
                    peers = plane_peers
                else:
                    peers = [near_y if y_first == (step == 1) else near_x]
                for peer in peers:
                    pl.semaphore_signal(rs_free.at[u, step], inc=1, device_id=peer, device_id_type=pl.DeviceIdType.MESH)

            on_route(u, step, act)

        def rs_merge(layer, u, step, piece=None):
            if step == 3 and u in fast:
                merge_owner(layer, u)
                return

            got = lands[u][step]
            sem = (piece or 0) % 2 if step < 3 else 0
            wait_at = land_at(u, step, piece) if step in (0, 2) else got
            if u in chunked and step == 1:
                wait_at = got.at[piece_planes(2, piece)] if u == wd_u else got.at[:, :, :, piece_cols(2, piece, u)]
            wait_bytes(wait_at, rs_recv.at[u, 2 * step + sem])
            slot = layer + 1
            buf = weight_buf[rs_weight[u]]
            cols = rs_cols.get(u, every)
            if step == 3:
                if layer == 0:
                    rs_home(1, u)
                total = buf[slot, z, y, x, core, :, cols].astype(f32)
                for k in range(3):
                    total = total + got[k].astype(f32)
                fin[u][...] = total
                if layer == 1:
                    give_back(u, 3)

                @pl.when(core == layer)
                def _():
                    for src, dst in home_parts(layer, u):
                        pltpu.make_async_copy(src, dst, sem_g.at[u]).start()

                @pl.when(core != layer)
                def _():
                    rs_start(layer, u, 4)

                return
            if step == 0 and piece is not None and u == wd_u:
                buf[slot, piece, :, :, core] += got[piece % 2]
            else:
                got_cols, planes = every, (0, 4)
                if piece is not None and u == wd_u:
                    planes = (2 * piece, 2 * piece + 2)
                elif piece is not None:
                    cols = piece_cols(step if step != 1 else 2, piece, u)
                    got_cols = piece_cols(0, piece % 2, u) if step == 0 else cols

                @pl.loop(*planes)
                def _(pz):
                    if step == 0:
                        buf[slot, pz, :, :, core, :, cols] += got[pz, :, :, :, got_cols]
                    elif u in fast:
                        total = buf[slot, pz, y, x, core, :, cols].astype(f32)
                        for k in range(3):
                            total = total + got[k, pz].astype(f32)
                        buf[slot, pz, y, x, core, :, cols] = total.astype(bf16)
                    elif step == 2:
                        buf[slot, pz, y, x, core, :, cols] += got[pz, :, got_cols]
                    else:
                        def add(y_first):
                            if y_first:
                                buf[slot, pz, y, :, core, :, cols] += got[pz, :, :, got_cols]
                            else:
                                buf[slot, pz, :, x, core, :, cols] += got[pz, :, :, got_cols]

                        rs_route(u, add)

            if layer == 1 or (step == 0 and u in chunked and piece < 2):
                give_back(u, step)
            rs_start(layer, u, 3 if u in fast and step == 1 else step + 1, piece)

        def rs_home(layer, u):
            @pl.when(core == layer)
            def _():
                if u == wqb_u:
                    wait_bytes(fin[u].at[:, :, lanes:], sem_g.at[u])
                    wait_bytes(fin[u].at[:, 0:8, 0:lanes], sem_g.at[5])
                else:
                    wait_bytes(fin[u], sem_g.at[u])
                if u not in fast:
                    for copy in rs_copies(layer, u, 4, True):
                        copy.wait_recv()

            if u not in fast:
                @pl.when(core != layer)
                def _():
                    for copy in rs_copies(layer, u, 4, True):
                        copy.wait_send()

        def rs_sent(layer, u, step):
            three = slice(0, 3)
            if step == 0:
                wait_bytes(spot(layer, u, every, every, every, other), sent_sem(5 * u + 0))
            elif step == 1 and u in fast:
                wait_bytes(spot(layer, u, three, every, every, core), sent_sem(5 * u + 1))
            elif step == 1:
                wait_bytes(spot(layer, u, every, y, every, core), sent_sem(5 * u + 1))
            elif step == 2:
                wait_bytes(spot(layer, u, every, y, x, core), sent_sem(5 * u + 2))
            elif u not in fast:
                wait_bytes(spot(layer, u, three, y, x, core), sent_sem(5 * u + 3))
            else:
                @pl.when(core == layer)
                def _():
                    wait_bytes(spot(layer, u, three, y, x, core), sent_sem(5 * u + 3))

                @pl.when(core != layer)
                def _():
                    wait_bytes(spot(layer, u, every, y, x, core), sent_sem(5 * u + 3))

        def rs_finish(layer, u):
            for step in (0, 1, 3) if u in fast else range(4):
                rs_sent(layer, u, step)

        def stat_copy(step, k=0):
            target = (mate, near_y, near_x)[step] if step < 3 else along_z[k]
            place_at = step if step < 3 else 3 + z
            return pltpu.make_async_remote_copy(
                src_ref=stat_sum.at[step],
                dst_ref=stat_land.at[place_at],
                send_sem=sent_sem(25 + step),
                recv_sem=stat_recv.at[step],
                device_id=target,
                device_id_type=pl.DeviceIdType.MESH,
            )

        def stat_step(step):
            if step == 0:
                stat_sum[0] = stat_ref[...]
            elif step < 4:
                stat_copy(step - 1).wait()
                stat_sum[step] = stat_sum[step - 1] + stat_land[step - 1]
            if step < 3:
                stat_copy(step).start()
            elif step == 3:
                stat_land[3 + z] = stat_sum[3]
                for k in range(3):
                    stat_copy(3, k).start()
            else:
                wait_bytes(stat_land.at[pl.ds(3, 3)], stat_recv.at[3])
                wait_bytes(stat_land.at[pl.ds(3, 3)], sent_sem(25 + 3))
                total = stat_land[3] + stat_land[4] + stat_land[5] + stat_land[6]
                stat_ref[...] = total
                stat_done()

        stat_step(0)
        names = dict(a=wqa_u, o=wo_u, u=wu_u, d=wd_u, b=wqb_u)

        def run_events(layer, text):
            for word in text:
                if word[0] == "t":
                    stat_step(int(word[1]))
                    continue
                at_layer = layer
                if word[0] == "p":
                    at_layer, word = layer + 1, word[1:]
                step, u = int(word[1]), names[word[2]]
                piece = int(word[3]) if len(word) > 3 else None
                (rs_start if word[0] == "S" else rs_merge)(at_layer, u, step, piece)

        back_points = {
            (1, "ffn0"): ("S0d0", "S0u0"),
            (1, "ffn1"): ("t1", "M0d0", "M0u0", "S0d1", "S0u1"),
            (1, "ffn2"): ("M0d1", "M0u1", "S0d2", "S0u2"),
            (1, "ffn3"): ("t2", "M0d2", "M0u2", "S0d3", "S0u3"),
            (1, "mid0"): ("M0d3", "M0u3"),
            (1, "wo"): ("t3", "S0o", "M1d0", "M1u0"),
            (1, "att00"): ("M0o", "M1d1", "M1u1"),
            (1, "att01"): ("t4", "M2d0", "M2u0"),
            (1, "wq0"): ("S0a",),
            (1, "att10"): ("M0a", "M1o", "M2d1", "M2u1"),
            (1, "wq1"): ("S0b",),
            (1, "in0"): ("M0b",),
            (0, "ffn0"): ("S0d0", "S0u0", "pM1a", "pM2o"),
            (0, "ffn1"): ("M0d0", "M0u0", "S0d1", "S0u1", "pM1b"),
            (0, "ffn2"): ("M0d1", "M0u1", "S0d2", "S0u2", "pM3d", "pM3u"),
            (0, "ffn3"): ("M0d2", "M0u2", "S0d3", "S0u3", "pM3o", "pM3a"),
            (0, "mid0"): ("M0d3", "M0u3", "pM3b"),
            (0, "wo"): ("S0o", "M1d0", "M1u0"),
            (0, "att00"): ("M0o", "M1d1", "M1u1"),
            (0, "att01"): ("M2d0", "M2u0"),
            (0, "wq0"): ("S0a",),
            (0, "att10"): ("M0a", "M1o", "M2d1", "M2u1"),
            (0, "wq1"): ("S0b", "M1a", "M0b"),
            (0, "in0"): ("M2o",),
            (0, "end"): ("M1b", "M3d", "M3u", "M3o", "M3a", "M3b"),
        }
    else:
        back_points = {}

    def stat_done():
        totals = stat_ref[...]
        stat_out[...] = totals if not routed else jnp.broadcast_to(
            jnp.sqrt(jnp.sum(totals, axis=2, keepdims=True) / (totals[0:1, 3:4, 0:1] * width)), totals.shape
        )

    if not routed:
        stat_done()

    def back_point(layer, point, s=None, at=None):
        for (at_layer, at_point), text in back_points.items():
            if at_point == point:
                here = layer == at_layer
                if s is not None:
                    here = here & (s == at)

                @pl.when(here)
                def _(at_layer=at_layer, text=text):
                    run_events(at_layer, text)

    def norm_back(x, gain, grad):
        inv = lax.rsqrt(jnp.mean(x * x, axis=1, keepdims=True) + norm_eps)
        hat = x * inv
        scaled = grad * gain
        return inv * (scaled - hat * jnp.mean(scaled * hat, axis=1, keepdims=True))

    def add_gain(k, d_weight, weight):
        total = gain_sums[k]
        for p in range(d_weight.shape[1] // lanes):
            cols = slice(p * lanes, (p + 1) * lanes)
            total = total + d_weight[:, cols] * weight[:, cols].astype(f32)
        gain_sums[k] = total

    def pack_small(layer):
        sums = [jnp.sum(gain_sums[k], axis=1, keepdims=True) for k in range(2)]
        turned = dbias[...].T
        for h in range(heads):
            gain_sums[1, pl.ds(h, slots, stride=heads)] = jnp.broadcast_to(turned[:slots, h : h + 1], (slots, lanes))
        lane = lax.broadcasted_iota(jnp.int32, (width, lanes), 1)
        gain = mat(0, layer, slice(0, lanes)).astype(f32)
        safe = jnp.where(lane < 2, gain, 1.0)
        value = jnp.where(lane == 0, sums[0], jnp.where(lane == 1, sums[1], 0.0)) / safe
        value = jnp.where(lane == 2, gain_sums[1], value)
        put_mat(0, layer + 1, value.astype(bf16), slice(3 * quad, 3 * quad + lanes))

    def backward_ffn(layer):
        slot = layer + 1

        @pl.loop(0, segs)
        def _(s):
            at = seg_rows(s)
            h = hbuf[at, :].astype(f32)
            doa[0, at, :] = (h * lax.rsqrt(jnp.mean(h * h, axis=1, keepdims=True) + norm_eps) * gains[layer, 1]).astype(bf16)

        gain_sums[...] = jnp.zeros_like(gain_sums)
        dbias[...] = jnp.zeros_like(dbias)
        turned_cols = slice(0, segs * rows)
        put_mat(0, slot, doa[0].T, turned_cols)

        @pl.loop(0, ff // chunk)
        def _(c):
            cols = pl.ds(pl.multiple_of(c * chunk, chunk), chunk)
            planes = pl.ds(c, 1)
            d_act = nt(dy[...], mat(3, layer, planes=planes)).astype(bf16)
            put_mat(3, slot, tn(active[:, cols], dy[...]).astype(bf16), planes=planes)
            d_pre = d_act * slope[:, cols]
            slope[:, cols] = d_pre
            d_up = mm(mat(0, slot, turned_cols), d_pre)
            add_gain(1, d_up, mat(2, layer, cols))
            put_mat(2, slot, d_up.astype(bf16), cols)
            for k in range(ff // chunk):
                back_point(layer, "ffn" + str(k), c, k)

    def backward_middle(layer, s):
        at = seg_rows(s)
        dh = norm_back(hbuf[at, :].astype(f32), gains[layer, 1], nt(slope[at, :], mat(2, layer)))
        v = ub[at, :].astype(f32)
        hbuf[at, :] = (v * lax.rsqrt(jnp.mean(v * v, axis=1, keepdims=True) + norm_eps) * gains[layer, 0]).astype(bf16)
        dh = dh + dy[at, :].astype(f32)
        dn[at, :] = dh
        dz = dh.astype(bf16)
        dy[at, :] = dz
        do = nt(dz, mat(1, layer)) * ilbuf[at, :].astype(f32)
        prod = do.astype(bf16) * obuf[at, :]
        lane = lax.broadcasted_iota(jnp.int32, (1, quad), 1) % head_size
        side = lax.broadcasted_iota(jnp.int32, (1, quad), 1) // head_size % 2
        hi_at, lo_at = (lane == 0).astype(f32), (lane == 1).astype(f32)
        free = 1.0 - hi_at - lo_at
        head_of = lax.broadcasted_iota(jnp.int32, (quad, quad), 0) // head_size
        gets = lax.broadcasted_iota(jnp.int32, (quad, quad), 1) // head_size
        swap_sum = jnp.where(head_of == gets + 1 - 2 * (gets % 2), -1.0, 0.0).astype(bf16)
        for q in range(quads):
            cols = slice(q * quad, (q + 1) * quad)
            delta = mm(prod[:, cols], swap_sum)
            hi = delta.astype(bf16).astype(f32)
            filled = do[:, cols] * free + hi * hi_at + (delta - hi) * lo_at
            for k in range(2):
                doa[k, at, cols] = jnp.where(side == k, do[:, cols], filled).astype(bf16)

    def backward_attention(layer, q, s):
        at = seg_rows(s)

        def pair_cols(k, p):
            return pl.ds(pl.multiple_of(k * width + q * quad + p * lanes, lanes), lanes)

        def d_probs_of(h):
            p, side = h // 2, h % 2
            own, marks = lane_marks(head_size, side)
            do_h = doa[side, at, pair_cols(0, p)]
            va = qkv[at, pair_cols(2, p)] * own.astype(bf16) + (marks[0] + marks[1]).astype(bf16)
            return do_h, nt(do_h, va)

        do_h, d_probs = d_probs_of(0)
        dq, dk, dv = [], [], []
        for h in range(4):
            p, side = h // 2, h % 2
            head = 4 * q + h
            following = d_probs_of(h + 1) if h < 3 else (None, None)
            qp, kp = qkv[at, pair_cols(0, p)], qkv[at, pair_cols(1, p)]
            half = slice(side * head_size, (side + 1) * head_size)
            weights = ebuf[s, head]
            dv.append(mm(do_h.T[half, :], weights))
            d_scores = weights * d_probs.astype(bf16)
            dbias[pl.ds(head, 1), :] += jnp.sum(d_scores[:, :lanes].astype(f32), axis=0, keepdims=True)
            dq.append(mm(d_scores, kp))
            dk.append(mm(qp.T[half, :], d_scores))
            do_h, d_probs = following
            if side == 0:
                continue
            own, _ = lane_marks(head_size, 0)
            qkv[at, pair_cols(0, p)] = (jnp.where(own > 0, dq[-2], dq[-1]) * score_scale).astype(bf16)
            qkv[at, pair_cols(1, p)] = (jnp.concatenate(dk[-2:], axis=0).T * (1.0 / log2_e)).astype(bf16)
            qkv[at, pair_cols(2, p)] = jnp.concatenate(dv[-2:], axis=0).T.astype(bf16)

    def backward_input(layer, s):
        at = seg_rows(s)
        x = ub[at, :].astype(f32)
        du = norm_back(x, gains[layer, 0], nt(qkv[at, :], mat(0, layer, slice(lanes, lanes + 3 * width))))
        dy[at, :] = (du + dn[at, :]).astype(bf16)

    def grad_col(q, k):
        return q * (3 * quad + lanes) + k * quad

    def grad_copies(layer):
        return [
            pltpu.make_async_copy(buf.at[layer + 1], out.at[layer], sem_g.at[k])
            for k, (buf, out) in enumerate(zip(weight_buf, grads_out))
        ]

    @pl.loop(0, 2)
    def _(step):
        layer = 1 - step
        slot = layer + 1

        @pl.when(layer == 0)
        def _():
            for s in range(segs):
                for copy in spill_copies(s, True, (2, 3, 4, 5, 6)):
                    copy.wait()

        backward_ffn(layer)

        @pl.when(layer == 1)
        def _():
            wait_rows(doa.at[1], 3)

        @pl.when(layer == 0)
        def _():
            for s in range(segs):
                spill_copies(s, True, (7,))[0].wait()

        @pl.loop(0, segs)
        def _(s):
            backward_middle(layer, s)
            back_point(layer, "mid0", s, 0)

        put_mat(1, slot, tn(obuf[...], dy[...]).astype(bf16))
        back_point(layer, "wo")

        @pl.when(layer == 1)
        def _():
            for s in range(segs):
                for copy in spill_copies(s, True, (2, 3, 4, 5)):
                    copy.start()

        @pl.loop(0, quads)
        def _(q):
            @pl.loop(0, segs)
            def _(s):
                @pl.when((layer == 0) & (q == 0))
                def _():
                    for copy in spill_copies(s, True, (0, 1)):
                        copy.wait()

                backward_attention(layer, q, s)

                for i in range(quads):
                    for k in range(segs):
                        back_point(layer, "att" + str(i) + str(k), q * segs + s, i * segs + k)

            for k in range(3):
                d_weight = tn(hbuf[...], qkv[:, pl.ds(pl.multiple_of(k * width + q * quad, quad), quad)])
                add_gain(0, d_weight, mat(0, layer, pl.ds(pl.multiple_of(lanes + k * width + q * quad, lanes), quad)))
                put_mat(0, slot, d_weight.astype(bf16), pl.ds(pl.multiple_of(grad_col(q, k), lanes), quad))

            @pl.when((layer == 1) & (q == quads - 1))
            def _():
                for k in (6, 1):
                    for s in range(segs):
                        spill_copies(s, True, (k,))[0].start()

            @pl.when(q == quads - 1)
            def _():
                pack_small(layer)

            for i in range(quads):
                back_point(layer, "wq" + str(i), q, i)

        @pl.loop(0, segs)
        def _(s):
            backward_input(layer, s)
            for k in range(segs):
                back_point(layer, "in" + str(k), s, k)


        @pl.when(layer == 1)
        def _():
            for s in range(segs):
                for copy in spill_copies(s, True, (7, 0)):
                    copy.start()

        if not routed:
            for copy in grad_copies(layer):
                copy.start()
            for copy in grad_copies(layer):
                copy.wait()

    for copies in du_copies:
        for copy in copies:
            copy.start()
    back_point(0, "end")
    if routed:
        for u in range(5):
            rs_finish(0, u)
    if routed:
        for u in range(5):
            rs_home(0, u)
        for u in (0, 4):
            rs_home(1, u)
    wait_rows(dy, 6)


def run_layers(dims, routed, doc_len, row_args, weights):
    segs, rows, width, ff, slots, heads, per_doc = dims
    all_rows = segs * rows
    vmem = pl.BlockSpec(memory_space=pltpu.VMEM)
    smem = pl.BlockSpec(memory_space=pltpu.SMEM)
    hbm = pl.BlockSpec(memory_space=pl.ANY)
    shape = jax.ShapeDtypeStruct
    dma = pltpu.SemaphoreType.DMA
    wide = (all_rows, width)
    tiles = [
        (width // 32, lanes + 3 * width),
        (width // 32, width),
        (width // 32, ff),
        (ff // 32, width),
    ]
    out_shape = [shape(part.shape, bf16) for part in row_args]
    if routed:
        out_shape += [shape((2, width // 32, 3 * width), f32)]
        out_shape += [shape((2, *tile), f32) for tile in tiles[1:]]
        out_shape += [shape((2, 8, lanes), f32)]
    else:
        out_shape += [shape((2, 4, 2, 2, 2, *tile), bf16) for tile in tiles]
    row_outs = len(out_shape)
    out_shape += [shape((2, 8, lanes), f32)]
    out_shape += [
        shape((all_rows, 3 * width), bf16),
        shape((segs, heads, rows, rows), bf16),
        shape(wide, bf16),
        shape(wide, bf16),
        shape((all_rows, ff), bf16),
        shape((all_rows, ff), bf16),
        shape(wide, bf16),
        shape(wide, bf16),
    ]
    unit_count = 16
    scratch = [pltpu.VMEM((3, 4, 2, 2, 2, *tile), bf16) for tile in tiles]
    scratch += [
        pltpu.VMEM(wide, bf16),
        pltpu.VMEM(wide, bf16),
        pltpu.VMEM((all_rows, 3 * width), bf16),
        pltpu.VMEM((segs, heads, rows, rows), bf16),
        pltpu.VMEM(wide, bf16),
        pltpu.VMEM(wide, bf16),
        pltpu.VMEM(wide, bf16),
        pltpu.VMEM((all_rows, ff), bf16),
        pltpu.VMEM((all_rows, ff), bf16),
        pltpu.VMEM((2, *wide), bf16),
        pltpu.VMEM(wide, f32),
        pltpu.VMEM((2, 2, 1, width), f32),
        pltpu.VMEM((2, width, lanes), f32),
        pltpu.VMEM((heads, lanes), f32),
        pltpu.VMEM((2, 8, lanes), f32),
        dma((segs, 8)),
        dma((8,)),
        dma((9,)),
        dma((unit_count, 2)),
        dma((unit_count, 6)),
    ]
    params = dict(vmem_limit_bytes=127 * 2**19)
    if routed:
        params.update(collective_id=0, has_side_effects=True)
        half_cols = 3 * width // 2
        rs_tiles = [(width // 32, half_cols), *tiles[1:], (width // 32, half_cols + lanes)]
        first_tiles = [(4, 2, 2, *tile) for tile in rs_tiles]
        first_tiles[2] = (4, 2, 2, width // 32, 2 * chunk)
        first_tiles[3] = (2, 2, 2, ff // 32, width)
        for u, (first, tile) in enumerate(zip(first_tiles, rs_tiles)):
            leads = ((3, 4), (1,), (2, 4)) if u in (0, 4) else ((4, 2), (4,), (3,))
            scratch += [pltpu.VMEM(first, bf16)]
            scratch += [pltpu.VMEM((*lead, *tile), bf16) for lead in leads]
        scratch += [pltpu.VMEM((2, *tile) if u in (0, 4) else tile, f32) for u, tile in enumerate(rs_tiles)]
        scratch += [
            pltpu.VMEM((4, 2, 8, lanes), f32),
            pltpu.VMEM((7, 2, 8, lanes), f32),
            pltpu.VMEM((2, width // 32, lanes), bf16),
            dma((5, 8)),
            pltpu.SemaphoreType.REGULAR((5, 4)),
            dma((4,)),
        ]
    return pl.pallas_call(
        partial(fused_layers, dims, routed),
        out_shape=out_shape,
        in_specs=[smem] + [hbm] * (len(row_args) + 4) + [vmem] * (len(weights) - 4),
        out_specs=[hbm] * row_outs + [vmem] + [hbm] * (len(out_shape) - row_outs - 1),
        scratch_shapes=scratch,
        compiler_params=pltpu.CompilerParams(**params),
    )(doc_len, *row_args, *weights)[: row_outs + 1]


def settle_kernel(*refs):
    count = (len(refs) - 7) // 3
    srcs, (small, stats) = refs[:count], refs[count : count + 2]
    dsts = refs[count + 2 : 2 * count + 2]
    vectors, rms = refs[2 * count + 2 : 2 * count + 5], refs[2 * count + 5]
    mids, sems = refs[2 * count + 6 : -1], refs[-1]
    inward = [pltpu.make_async_copy(src, mid, sems.at[0, k]) for k, (src, mid) in enumerate(zip(srcs, mids))]
    outward = [pltpu.make_async_copy(mid, dst, sems.at[1, k]) for k, (mid, dst) in enumerate(zip(mids, dsts))]
    for copy in inward:
        copy.start()
    for k, vector in enumerate(vectors):
        size = vector.shape[1] // 2
        vector[...] = jnp.concatenate([small[half, k : k + 1, :size] for half in range(2)], axis=1)
    lane = lax.broadcasted_iota(jnp.int32, (1, lanes), 1)
    for layer in range(2):
        row = sum(jnp.where(lane == k, stats[layer, k : k + 1, :], 0.0) for k in range(3))
        rms[layer : layer + 1, :] = row[:, :3]
    for into, out in zip(inward, outward):
        into.wait()
        out.start()
    for out in outward:
        out.wait()


def settle(big, small, stats):
    vmem = pl.BlockSpec(memory_space=pltpu.VMEM)
    hbm = pl.BlockSpec(memory_space=pl.ANY)
    shape = jax.ShapeDtypeStruct
    size = 2 * big[4].shape[1]
    return pl.pallas_call(
        settle_kernel,
        out_shape=[shape(part.shape, part.dtype) for part in big] + [shape((1, size), f32)] * 3 + [shape((2, 3), f32)],
        in_specs=[hbm] * len(big) + [vmem] * 2,
        out_specs=[hbm] * len(big) + [vmem] * 4,
        scratch_shapes=[pltpu.VMEM(part.shape, part.dtype) for part in big] + [pltpu.SemaphoreType.DMA((2, len(big)))],
    )(*big, small, stats)


def swap(block):
    return lax.ppermute(block, "section", [(0, 1), (1, 0)])


def body(
    tokens,
    memory,
    lengths,
    w_qkv,
    w_out,
    w_up,
    w_down,
    gain_attn,
    gain_ffn,
    forget_bias,
    grad_tokens,
    grad_memory,
):
    section = lax.axis_index("section")
    is_first = section == 0
    micro = tokens.shape[0]
    segs = micro // 2
    half_tok = tokens.shape[1]
    half_mem = memory.shape[1]
    slots = 2 * half_mem
    rows = slots + 2 * half_tok
    width = tokens.shape[2]
    ff = w_up.shape[2]
    heads = forget_bias.shape[1] * lax.axis_size("dp") // slots
    per_doc = micro // lengths.shape[0]
    dims = (segs, rows, width, ff, slots, heads, per_doc)
    if lax.axis_size("dp") == 16 and w_qkv.shape[1] == 32:
        weights = [piece.reshape(2, -1, piece.shape[2]) for piece in (w_qkv, w_out, w_up, w_down)]
        weights += [gain_attn, gain_ffn, forget_bias]
        row_args = (tokens, memory, grad_tokens, grad_memory)
        *outs, small_grads, stats = run_layers(dims, True, lengths, row_args, weights)
        outs = settle(outs, small_grads, stats)
        mats = [grad.reshape(1, -1, grad.shape[2]) for grad in outs[4:8]]
        return (*outs[:4], *mats, *outs[8:])

    own_len = lax.dynamic_slice_in_dim(lengths, section * segs // per_doc, segs // per_doc, 0)
    small = jnp.stack([gain_attn, gain_ffn, forget_bias], axis=2)
    small = jnp.pad(small, ((0, 0), (0, 0), (0, lanes - 3)))
    pieces = (jnp.concatenate([small, w_qkv], axis=2), w_out, w_up, w_down)

    def unpack(grads):
        mat = grads[0]
        half = 3 * width // 2
        parts = [mat[:, :, :half], mat[:, :, half + lanes :]]
        parts = [part.reshape(1, -1, 3, width // 2) for part in parts]
        whole = jnp.concatenate(parts, axis=3).reshape(1, -1, 3 * width)
        return (whole, *grads[1:], *(mat[:, :, half + k] for k in range(3)))

    def own_segs(halves):
        return lax.dynamic_slice_in_dim(halves, section * segs, segs, 0)

    def other_segs(halves):
        return lax.dynamic_slice_in_dim(halves, (1 - section) * segs, segs, 0)

    def both(kept, got):
        return jnp.concatenate(
            [jnp.where(is_first, kept, got), jnp.where(is_first, got, kept)], axis=1
        )

    inputs = (tokens, memory, grad_tokens, grad_memory)
    got = swap(tuple(other_segs(part) for part in inputs))
    full = [both(own_segs(part), other) for part, other in zip(inputs, got)]
    u0 = jnp.concatenate([full[1], full[0]], axis=1).reshape(segs * rows, width)
    dout = jnp.concatenate([full[3], full[2]], axis=1).reshape(segs * rows, width)

    def gather(piece):
        whole = lax.all_gather(piece, ("section", "dp"), axis=1, tiled=True)
        return whole.reshape(2, 4, 2, 2, 2, -1, piece.shape[2])

    y, du, *grads, stats = run_layers(dims, False, own_len, (u0, dout), [gather(piece) for piece in pieces])

    def scatter(grad):
        grad = grad.reshape(2, -1, grad.shape[-1])
        mine = lax.dynamic_index_in_dim(grad, section, 0, keepdims=True)
        other = lax.dynamic_index_in_dim(grad, 1 - section, 0, keepdims=True)
        chip = (mine.astype(f32) + swap(other).astype(f32)).astype(grad.dtype)
        return lax.psum_scatter(chip, "dp", scatter_dimension=1, tiled=True).astype(f32)

    shares = unpack([scatter(grad) for grad in grads])
    totals = lax.psum(stats[:, :4], ("section", "dp"))
    rms = jnp.sqrt(jnp.sum(totals[:, :3], axis=2) / (totals[0, 3, 0] * width))
    result = jnp.stack([y.reshape(segs, rows, width), du.reshape(segs, rows, width)])

    def half_of(which):
        tok = lax.dynamic_slice_in_dim(result, slots + which * half_tok, half_tok, 2)
        mem = lax.dynamic_slice_in_dim(result, which * half_mem, half_mem, 2)
        return tok, mem

    kept = half_of(section)
    got = swap(half_of(1 - section))

    def order(mine, other):
        return jnp.concatenate(
            [jnp.where(is_first, mine, other), jnp.where(is_first, other, mine)], axis=0
        )

    toks = [order(kept[0][k], got[0][k]) for k in range(2)]
    mems = [order(kept[1][k], got[1][k]) for k in range(2)]
    return (toks[0], mems[0], toks[1], mems[1], *shares, rms)


def solution(mesh):
    rows = P("dp", "section", None)
    mats = P("section", "dp", None)
    vecs = P("section", "dp")
    return jax.shard_map(
        body,
        mesh=mesh,
        in_specs=(rows, rows, P("dp"), mats, mats, mats, mats, vecs, vecs, vecs, rows, rows),
        out_specs=(rows, rows, rows, rows, mats, mats, mats, mats, vecs, vecs, vecs, P()),
        check_vma=False,
    )
```
